32 devices in a mesh: seq: 8 (over z, y), batch: 4 (over x, core).
Axes of the slice: x: 2, y: 2, z: 4, core: 2. Of those that a mesh axis runs over, the one named last changes fastest.
Arguments:
- inputs: bfloat16 [2048, 4, 1024], P('seq', 'batch'), may hold values from -6 to 6
- lengths: int32 [4], P('batch'), may hold values from 1024 to 2048, as said below
- w_query: bfloat16 [1024, 1024], P(('seq', 'batch')), may hold values from -0.1875 to 0.1875
- key_weight: bfloat16 [1024, 512], P(('seq', 'batch')), may hold values from -0.1875 to 0.1875
- value_weight: bfloat16 [1024, 512], P(('seq', 'batch')), may hold values from -0.1875 to 0.1875
- w_out: bfloat16 [1024, 1024], P(('seq', 'batch')), may hold values from -3 to 3
- w_gate: bfloat16 [1024, 4608], P(('seq', 'batch')), may hold values from -0.1875 to 0.1875
- w_up: bfloat16 [1024, 4608], P(('seq', 'batch')), may hold values from -0.1875 to 0.1875
- w_down: bfloat16 [4608, 1024], P(('seq', 'batch')), may hold values from -0.09375 to 0.09375
- gain_attn: float32 [1024], replicated, may hold values from 0.1 to 1.9
- gain_ffn: float32 [1024], replicated, may hold values from 0.1 to 1.9
- gain_query: float32 [64], replicated, may hold values from 0.1 to 1.9
- gain_key: float32 [64], replicated, may hold values from 0.1 to 1.9
- cotangent: bfloat16 [2048, 4, 1024], P('seq', 'batch'), may hold values from -6 to 6
Outputs:
- output: bfloat16 [2048, 4, 1024], P('seq', 'batch')
- grad_inputs: bfloat16 [2048, 4, 1024], P('seq', 'batch')
- grad_query: float32 [1024, 1024], P(('seq', 'batch'))
- grad_key: float32 [1024, 512], P(('seq', 'batch'))
- grad_value: float32 [1024, 512], P(('seq', 'batch'))
- grad_out: float32 [1024, 1024], P(('seq', 'batch'))
- grad_gate: float32 [1024, 4608], P(('seq', 'batch'))
- grad_up: float32 [1024, 4608], P(('seq', 'batch'))
- grad_down: float32 [4608, 1024], P(('seq', 'batch'))
- grad_gain_attn: float32 [1024], replicated
- grad_gain_ffn: float32 [1024], replicated
- grad_gain_query: float32 [64], replicated
- grad_gain_key: float32 [64], replicated
The draws below stay inside these ranges and needn't reach their ends.
Inputs may be any that keep to these rules, and one draw needn't show every extreme that they name: `lengths`: in each aligned block of 1 entries (the sequences of one index of batch) at least one length equals 2048.
All inputs are finite; a program needn't handle non-finite values.
Results may differ from the reference program's by a relative error of at most 0.025.
Values may be sent and summed in bfloat16 or wider, within the bound.
A program may use at most 256 MiB of HBM per device.

```python
import jax
import jax.numpy as jnp
from jax import lax

MODEL_WIDTH = 1024
QUERY_HEADS = 16
KEY_VALUE_HEADS = 8
HEAD_SIZE = 64
FF = 4608
SEQS = 1
SEQUENCE_SLOTS = 2048
SEQUENCE_TOTAL = 4


def draw_lengths(key, part):
    key = jax.random.fold_in(key, 5)
    first, second = jax.random.split(key)
    base = jax.random.randint(first, (SEQUENCE_TOTAL,), SEQUENCE_SLOTS // 2, SEQUENCE_SLOTS + 1)
    chosen = jax.random.randint(second, (SEQUENCE_TOTAL // SEQS,), 0, SEQS)
    places = jnp.arange(SEQUENCE_TOTAL, dtype=jnp.int32)
    full_slot = chosen[places // SEQS]
    return jnp.where(places % SEQS == full_slot, SEQUENCE_SLOTS, base).astype(jnp.int32)


def levels(own_key, extent, pieces, least, largest):
    def one(position, shards_of):
        draws = jax.random.uniform(jax.random.fold_in(jax.random.fold_in(own_key, 6), position), (shards_of,), jnp.float32, least / len(pieces), largest / len(pieces))
        return jnp.repeat(jnp.exp(draws), extent[position] // shards_of).reshape((-1,) + (1,) * (len(extent) - position - 1))

    loudness = one(*pieces[0])
    for cut in pieces[1:]:
        loudness = loudness * one(*cut)
    return loudness


def normal_values(stream_key, shape, deviation, reach, cuts=(), held_as=jnp.bfloat16):
    values = deviation * jax.random.normal(stream_key, shape, jnp.float32)
    if cuts:
        values = values * levels(stream_key, shape, cuts, -0.22, 0.18)
    return jnp.clip(values, -reach, reach).astype(held_as)


def setup_inputs(seed: int = 0) -> dict:
    key_list = jax.random.split(jax.random.key(seed), 15)
    inputs = normal_values(key_list[0], (SEQUENCE_SLOTS, SEQUENCE_TOTAL, MODEL_WIDTH), 1.0, 6.0, ((0, 8), (1, 4)))
    lengths = draw_lengths(jax.random.fold_in(key_list[14], 71), 0)
    w_query = normal_values(key_list[2], (MODEL_WIDTH, QUERY_HEADS * HEAD_SIZE), MODEL_WIDTH ** -0.5, 0.1875, ((0, 32),))
    key_weight = normal_values(key_list[3], (MODEL_WIDTH, KEY_VALUE_HEADS * HEAD_SIZE), MODEL_WIDTH ** -0.5, 0.1875, ((0, 32),))
    value_weight = normal_values(key_list[4], (MODEL_WIDTH, KEY_VALUE_HEADS * HEAD_SIZE), MODEL_WIDTH ** -0.5, 0.1875, ((0, 32),))
    w_out = normal_values(key_list[5], (QUERY_HEADS * HEAD_SIZE, MODEL_WIDTH), (max(1, QUERY_HEADS * HEAD_SIZE * 8 // SEQUENCE_SLOTS)) ** -0.5, 3.0, ((0, 32),))
    w_gate = normal_values(key_list[6], (MODEL_WIDTH, FF), MODEL_WIDTH ** -0.5, 0.1875, ((0, 32),))
    w_up = normal_values(key_list[7], (MODEL_WIDTH, FF), MODEL_WIDTH ** -0.5, 0.1875, ((0, 32),))
    w_down = normal_values(key_list[8], (FF, MODEL_WIDTH), FF ** -0.5, 0.09375, ((0, 32),))
    gain_attn = jnp.clip(1.0 + 0.18 * jax.random.normal(key_list[9], (MODEL_WIDTH,), jnp.float32), 0.1, 1.9)
    gain_ffn = jnp.clip(1.0 + 0.18 * jax.random.normal(key_list[10], (MODEL_WIDTH,), jnp.float32), 0.1, 1.9)
    gain_query = jnp.clip(1.0 + 0.18 * jax.random.normal(key_list[11], (HEAD_SIZE,), jnp.float32), 0.1, 1.9)
    gain_key = jnp.clip(1.0 + 0.18 * jax.random.normal(key_list[12], (HEAD_SIZE,), jnp.float32), 0.1, 1.9)
    cotangent = normal_values(key_list[13], (SEQUENCE_SLOTS, SEQUENCE_TOTAL, MODEL_WIDTH), 1.0, 6.0, ((0, 8), (1, 4)))
    return dict(inputs=inputs, lengths=lengths, w_query=w_query, key_weight=key_weight, value_weight=value_weight, w_out=w_out, w_gate=w_gate, w_up=w_up, w_down=w_down, gain_attn=gain_attn, gain_ffn=gain_ffn, gain_query=gain_query, gain_key=gain_key, cotangent=cotangent)


@jax.custom_vjp
def low(v):
    return lax.optimization_barrier(v.astype(jnp.bfloat16)).astype(jnp.float32)

@jax.custom_vjp
def low_back(v):
    return v

def low_keep(v):
    return (low(v), None)

def low_pass(kept, grad):
    return (grad,)

def back_keep(v):
    return (v, None)

def back_low(kept, grad):
    return (low(grad),)
low.defvjp(low_keep, low_pass)
low_back.defvjp(back_keep, back_low)
eps = 1e-05
theta = 1000000.0

def matrix_multiply(left, right):
    return jnp.dot(left, right, precision=lax.Precision.HIGHEST)

def rms_factor(v):
    return lax.rsqrt(lax.optimization_barrier(jnp.mean(v * v, axis=-1, keepdims=True)) + eps)

def rotary_tables(positions, width):
    half = width // 2
    freqs = theta ** (-(jnp.arange(half, dtype=jnp.float32) * 2.0) / width)
    angles = positions.astype(jnp.float32)[:, None] * freqs[None, :]
    cosine = jnp.concatenate([jnp.cos(angles), jnp.cos(angles)], axis=-1)
    sine = jnp.concatenate([jnp.sin(angles), jnp.sin(angles)], axis=-1)
    return (cosine, sine)

def rotate(v, cosine, sine):
    half = v.shape[-1] // 2
    turned = jnp.concatenate([-v[..., half:], v[..., :half]], axis=-1)
    return v * cosine + turned * sine

def attend(query, keys, value_rows, length):
    sequence_group = QUERY_HEADS // KEY_VALUE_HEADS
    keys = jnp.repeat(keys, sequence_group, axis=1)
    value_rows = jnp.repeat(value_rows, sequence_group, axis=1)
    scores = jnp.einsum('qhd,khd->hqk', query, keys, precision=lax.Precision.HIGHEST) * HEAD_SIZE ** (-0.5)
    scores = low_back(scores)
    places = jnp.arange(SEQUENCE_SLOTS, dtype=jnp.int32)
    valid = (places[None, :] <= places[:, None]) & (places[None, :] < length)
    scores = jnp.where(valid[None, :, :], scores, -jnp.inf)
    top = lax.optimization_barrier(jnp.max(scores, axis=-1, keepdims=True))
    weights = jnp.exp(scores - top)
    weights = weights / lax.optimization_barrier(jnp.sum(weights, axis=-1, keepdims=True))
    return jnp.einsum('hqk,khd->qhd', low(weights), value_rows, precision=lax.Precision.HIGHEST)

def reference(inputs, lengths, w_query, key_weight, value_weight, w_out, w_gate, w_up, w_down, gain_attn, gain_ffn, gain_query, gain_key, cotangent):
    cosine, sine = rotary_tables(jnp.arange(SEQUENCE_SLOTS, dtype=jnp.int32), HEAD_SIZE)
    cosine = cosine[:, None, None, :]
    sine = sine[:, None, None, :]
    checked = jax.checkpoint(attend)

    def forward(x, wq, key_matrix, value_matrix, wo, wg, wu, wd, g_one, g_two, g_query, g_key):
        normalized_input = low(x * rms_factor(x) * g_one)
        query_pre = low_back(matrix_multiply(normalized_input, wq)).reshape(SEQUENCE_SLOTS, SEQUENCE_TOTAL, QUERY_HEADS, HEAD_SIZE)
        key_before_rotation = low_back(matrix_multiply(normalized_input, key_matrix)).reshape(SEQUENCE_SLOTS, SEQUENCE_TOTAL, KEY_VALUE_HEADS, HEAD_SIZE)
        value_rows = low(low_back(matrix_multiply(normalized_input, value_matrix))).reshape(SEQUENCE_SLOTS, SEQUENCE_TOTAL, KEY_VALUE_HEADS, HEAD_SIZE)
        query = low(low_back(rotate(query_pre * rms_factor(query_pre) * g_query, cosine, sine)))
        keys = low(low_back(rotate(key_before_rotation * rms_factor(key_before_rotation) * g_key, cosine, sine)))

        def one_sequence(items):
            return checked(items[0], items[1], items[2], items[3])
        mixed = lax.map(one_sequence, (jnp.moveaxis(query, 1, 0), jnp.moveaxis(keys, 1, 0), jnp.moveaxis(value_rows, 1, 0), lengths))
        mixed = jnp.moveaxis(mixed, 0, 1).reshape(SEQUENCE_SLOTS, SEQUENCE_TOTAL, QUERY_HEADS * HEAD_SIZE)
        mixed = low(low_back(mixed))
        middle = x + low_back(matrix_multiply(mixed, wo))
        normed_two = low(middle * rms_factor(middle) * g_two)
        gate = low_back(matrix_multiply(normed_two, wg))
        up_part = low_back(matrix_multiply(normed_two, wu))
        hidden = low(jax.nn.silu(gate) * up_part)
        return middle + low_back(matrix_multiply(hidden, wd))
    floats = (inputs.astype(jnp.float32), w_query.astype(jnp.float32), key_weight.astype(jnp.float32), value_weight.astype(jnp.float32), w_out.astype(jnp.float32), w_gate.astype(jnp.float32), w_up.astype(jnp.float32), w_down.astype(jnp.float32), gain_attn, gain_ffn, gain_query, gain_key)
    result, pullback = jax.vjp(forward, *floats)
    grads = pullback(cotangent.astype(jnp.float32))
    return (result.astype(jnp.bfloat16), grads[0].astype(jnp.bfloat16), grads[1], grads[2], grads[3], grads[4], grads[5], grads[6], grads[7], grads[8], grads[9], grads[10], grads[11])
```

```python
import functools

import jax
import jax.numpy as jnp
from jax import lax
from jax.experimental import pallas as pl
from jax.experimental.pallas import tpu as pltpu
from jax.sharding import PartitionSpec as P

MESH = pl.DeviceIdType.MESH
F32 = jnp.float32
BF16 = jnp.bfloat16
eps = 1e-05
theta = 1000000.0
VMEM = pl.BlockSpec(memory_space=pltpu.VMEM)
ANY = pl.BlockSpec(memory_space=pl.ANY)


def nn(left, right):
    return lax.dot_general(left, right, (((1,), (0,)), ((), ())), preferred_element_type=F32)


def nt(left, right):
    return lax.dot_general(left, right, (((1,), (1,)), ((), ())), preferred_element_type=F32)


def tn(left, right):
    return lax.dot_general(left, right, (((0,), (0,)), ((), ())), preferred_element_type=F32)


def rms_factor(v):
    return lax.rsqrt(jnp.mean(v * v, axis=-1, keepdims=True) + eps)


def norm_back(grad, value, factor):
    return factor * (
        grad - value * factor * factor * jnp.mean(grad * value, axis=-1, keepdims=True)
    )


def lanes(shape):
    return lax.broadcasted_iota(jnp.int32, shape, len(shape) - 1)


def rows_of(shape):
    return lax.broadcasted_iota(jnp.int32, shape, len(shape) - 2)


def head_mean(v):
    first = lanes(v.shape) < 64
    low = jnp.sum(jnp.where(first, v, 0.0), axis=-1, keepdims=True)
    high = jnp.sum(jnp.where(first, 0.0, v), axis=-1, keepdims=True)
    return jnp.where(first, low, high) * (1.0 / 64.0)


def rope(u, cosine, sine):
    early = lax.rem(lanes(u.shape), 64) < 32
    turned = jnp.where(early, -pltpu.roll(u, 96, 1), pltpu.roll(u, 32, 1))
    return u * cosine + turned * sine


def rope_back(u, cosine, sine):
    early = lax.rem(lanes(u.shape), 64) < 32
    w = u * sine
    return u * cosine + jnp.where(early, pltpu.roll(w, 96, 1), -pltpu.roll(w, 32, 1))


class Place:
    def __init__(self, send_sem, recv_sem, local_sem):
        self.s = lax.axis_index("seq")
        self.b = lax.axis_index("batch")
        self.z = self.s // 2
        self.y = lax.rem(self.s, 2)
        self.core = self.b + 1 - 2 * lax.rem(self.b, 2)
        self.across = lax.rem(self.b + 2, 4)
        self.far = 3 - self.b
        self.flip = 2 * self.z + 1 - self.y
        self.send_sem, self.recv_sem, self.local_sem = send_sem, recv_sem, local_sem
        self.used = 0
        self.used_local = 0
        self.sent = []

    def up(self, k):
        return lax.rem(self.z + k, 4)

    def down(self, k):
        return lax.rem(self.z + 4 - k, 4)

    def greet(self):
        barrier = pltpu.get_barrier_semaphore()
        for k in (1, 2, 3):
            pl.semaphore_signal(
                barrier, inc=1, device_id=(self.s, lax.rem(self.b + k, 4)), device_id_type=MESH
            )
        for k in range(1, 8):
            pl.semaphore_signal(
                barrier, inc=1, device_id=(lax.rem(self.s + k, 8), self.b), device_id_type=MESH
            )
        pl.semaphore_wait(barrier, 10)

    def slots(self, count):
        first = self.used
        self.used += count
        return first

    def copy(self, src, dst, device, out, into=None):
        return pltpu.make_async_remote_copy(
            src_ref=src,
            dst_ref=dst,
            send_sem=self.send_sem.at[out],
            recv_sem=self.recv_sem.at[out if into is None else into],
            device_id=device,
            device_id_type=MESH,
        )

    def post(self, src, dst, device):
        index = self.slots(1)
        made = self.copy(src, dst, device, index)
        made.start()
        self.sent.append(made)
        return index

    def landed(self, index, ref):
        self.copy(ref, ref, (self.s, self.core), index).wait_recv()

    def local(self, src, dst):
        index = self.used_local
        self.used_local += 1
        made = pltpu.make_async_copy(src, dst, self.local_sem.at[index])
        made.start()
        return made

    def drain(self):
        for made in self.sent:
            made.wait_send()
        self.sent = []


def forward_kernel(
    x, dy, length, wqkv_in, wgu_in, wd_in, wo_in, cos, sin, gain_q, gain_k, gain_a, gain_f,
    wgu, wd, wo, wqkv, norm, pre, unit, unit_out, lse, mix, norm_two, middle, dy_all, length_all,
    xa, pack, kv, vt, send_sem, recv_sem, local_sem,
):
    p = Place(send_sem, recv_sem, local_sem)
    s, b, z, y = p.s, p.b, p.z, p.y
    my_rows = pl.ds(pl.multiple_of(32 * b, 32), 32)
    own = [
        p.local(wqkv_in.at[b], wqkv.at[s, my_rows]),
        p.local(x, xa.at[b]),
        p.local(length, length_all.at[b]),
        p.local(wo_in, wo.at[s, b]),
    ]
    own_gu = p.local(wgu_in.at[b], wgu.at[s, :, my_rows])
    own_d = p.local(wd_in, wd.at[s])
    own_dy = p.local(dy, dy_all.at[b])
    p.greet()

    got = []
    for k in (1, 2, 3):
        to = lax.rem(b + k, 4)
        got.append(p.post(wqkv_in.at[to], wqkv.at[s, my_rows], (s, to)))
    x_core = p.post(x, xa.at[b], (s, p.core))
    x_across = p.post(x, xa.at[b], (s, p.across))
    got_len = []
    for k in (1, 2, 3):
        to = lax.rem(b + k, 4)
        got_len.append(p.post(length, length_all.at[b], (s, to)))
    for made in own:
        made.wait()
    for k in (1, 2, 3):
        p.landed(got[k - 1], wqkv.at[s, my_rows])
    z_qkv = [p.post(wqkv.at[s], wqkv.at[s], (2 * p.up(k) + y, b)) for k in (1, 2, 3)]
    y_qkv = [p.post(wqkv.at[s], wqkv.at[s], (p.flip, b))]
    z_wo = [p.post(wo.at[s, b], wo.at[s, b], (2 * p.up(k) + y, b)) for k in (1, 2, 3)]
    y_wo = [p.post(wo.at[s, b], wo.at[s, b], (p.flip, b))]
    got_gu = []
    for k in (1, 2, 3):
        to = lax.rem(b + k, 4)
        got_gu.append(p.post(wgu_in.at[to], wgu.at[s, :, my_rows], (s, to)))
    p.landed(x_across, xa.at[p.across])
    x_far = p.post(xa.at[p.across], xa.at[p.across], (s, p.core))
    for k in (1, 2, 3):
        slot = 2 * p.down(k) + y
        p.landed(z_qkv[k - 1], wqkv.at[slot])
        y_qkv.append(p.post(wqkv.at[slot], wqkv.at[slot], (p.flip, b)))
    p.landed(x_core, xa.at[p.core])
    p.landed(x_far, xa.at[p.far])
    for k in (1, 2, 3):
        p.landed(got_len[k - 1], length_all.at[lax.rem(b + 4 - k, 4)])

    def normalize(g, carry):
        xg = xa[g].astype(F32)
        norm[g] = (xg * rms_factor(xg) * gain_a[...]).astype(BF16)
        return carry

    lax.fori_loop(0, 4, normalize, 0)
    p.landed(y_qkv[0], wqkv.at[p.flip])
    for k in (1, 2, 3):
        p.landed(y_qkv[k], wqkv.at[2 * p.down(k) + 1 - y])

    own_gu.wait()
    own_d.wait()
    own_dy.wait()
    for k in (1, 2, 3):
        p.landed(got_gu[k - 1], wgu.at[s, :, my_rows])
    first_ffn = p.used
    z_gu, z_d = [], []
    for k in (1, 2, 3):
        z_gu.append(p.post(wgu.at[s], wgu.at[s], (2 * p.up(k) + y, b)))
        z_d.append(p.post(wd.at[s], wd.at[s], (2 * p.up(k) + y, b)))
    y_gu = [p.post(wgu.at[s], wgu.at[s], (p.flip, b))]
    y_d = [p.post(wd.at[s], wd.at[s], (p.flip, b))]

    first_unit = p.slots(8)

    def project(t, carry):
        g = lax.rem(z + 1 + t, 4)
        whole = nn(norm[g], wqkv[...].reshape(1024, 512))
        pre[g] = whole
        for kk in (0, 1):
            q = whole[:, 256 * kk : 256 * kk + 128]
            kvp = whole[:, 256 * kk + 128 : 256 * kk + 256]
            qn = q * lax.rsqrt(head_mean(q * q) + eps) * gain_q[...]
            kn = kvp * lax.rsqrt(head_mean(kvp * kvp) + eps) * gain_k[...]
            qr = rope(qn, cos[...], sin[...]) * 0.125
            kr = rope(kn, cos[...], sin[...])
            pack[2 * g + kk, :, 0:128] = qr.astype(BF16)
            pack[2 * g + kk, :, 128:256] = jnp.where(lanes(kr.shape) < 64, kr, kvp).astype(BF16)

        @pl.when(t < 3)
        def _():
            for kk in (0, 1):
                to = 2 * g + kk
                p.copy(
                    pack.at[to], unit.at[s], (to, b), first_unit + 2 * t + kk, first_unit + 2 * t + y
                ).start()

        @pl.when(t == 3)
        def _():
            p.copy(pack.at[p.flip], unit.at[s], (p.flip, b), first_unit + 6).start()

        return carry

    lax.fori_loop(0, 4, project, 0)
    own_unit = p.local(pack.at[s], unit.at[s])

    for k in (1, 2, 3):
        slot = 2 * p.down(k) + y
        p.landed(z_wo[k - 1], wo.at[slot, b])
        y_wo.append(p.post(wo.at[slot, b], wo.at[slot, b], (p.flip, b)))
    dy_core = p.post(dy, dy_all.at[b], (s, p.core))
    dy_across = p.post(dy, dy_all.at[b], (s, p.across))
    p.landed(y_wo[0], wo.at[p.flip, b])
    for k in (1, 2, 3):
        p.landed(y_wo[k], wo.at[2 * p.down(k) + 1 - y, b])
    wo_core = p.post(wo.at[:, b], wo.at[:, b], (s, p.core))
    wo_across = p.post(wo.at[:, b], wo.at[:, b], (s, p.across))

    for t in range(3):
        for other in (0, 1):
            src = 2 * lax.rem(z + 3 - t, 4) + other
            p.landed(first_unit + 2 * t + other, unit.at[src])
    p.landed(first_unit + 6, unit.at[p.flip])
    own_unit.wait()
    for t in range(3):
        for kk in (0, 1):
            p.copy(pack.at[s], unit.at[s], (p.flip, b), first_unit + 2 * t + kk).wait_send()
    p.copy(pack.at[s], unit.at[s], (p.flip, b), first_unit + 6).wait_send()

    def prepare(j, carry):
        live = j * 256 + rows_of((256, 128)) < length_all[z][0:1, :]
        masked = jnp.where(live, unit[j, :, 128:256].astype(F32), 0.0)
        kv[j] = masked.astype(BF16)
        vt[j, 0:64] = jnp.transpose(masked)[64:128].astype(BF16)
        alive = j * 256 + lanes((16, 256)) < length_all[z][0:1, 0:1]
        vt[j, 64:80] = jnp.where(alive, 1.0, 0.0).astype(BF16)
        return carry

    lax.fori_loop(0, 8, prepare, 0)
    p.landed(wo_across, wo.at[:, p.across])
    wo_far = p.post(wo.at[:, p.across], wo.at[:, p.across], (s, p.core))
    p.landed(dy_across, dy_all.at[p.across])
    dy_far = p.post(dy_all.at[p.across], dy_all.at[p.across], (s, p.core))
    first_mix = p.slots(8)

    def attend(t, carry):
        i = lax.rem(s + 1 + t, 8)
        qt = jnp.transpose(unit[i, :, 0:128].astype(F32)).astype(BF16)
        both = jnp.concatenate([qt[0:64], qt[64:128]], axis=1)
        right = jnp.concatenate([both, jnp.zeros((64, 512), BF16)], axis=0)

        def block(j, acc):
            return acc + nn(vt[j], jnp.exp(nn(kv[j], right)).astype(BF16))

        acc = lax.fori_loop(0, i, block, jnp.zeros((80, 512), F32))
        causal = rows_of((256, 512)) <= lax.rem(lanes((256, 512)), 256)
        edge = jnp.where(causal, jnp.exp(nn(kv[i], right)), 0.0).astype(BF16)
        acc = acc + nn(vt[i], edge)
        total = acc[64:65]
        out = acc[0:64] / total
        out = jnp.concatenate([out[:, 0:256], out[:, 256:512]], axis=0)
        unit_out[i] = jnp.transpose(out).astype(BF16)
        lse[i] = jnp.broadcast_to(jnp.log(total), (8, 512))

        @pl.when(t < 7)
        def _():
            p.copy(unit_out.at[i], mix.at[b, s], (i, b), first_mix + t).start()

        return carry

    lax.fori_loop(0, 8, attend, 0)
    own_mix = p.local(unit_out.at[s], mix.at[b, s])
    for k in (1, 2, 3):
        slot = 2 * p.down(k) + y
        p.landed(z_gu[k - 1], wgu.at[slot])
        p.landed(z_d[k - 1], wd.at[slot])
        y_gu.append(p.post(wgu.at[slot], wgu.at[slot], (p.flip, b)))
        y_d.append(p.post(wd.at[slot], wd.at[slot], (p.flip, b)))
    for t in range(7):
        p.landed(first_mix + t, mix.at[b, lax.rem(s + 7 - t, 8)])
        p.copy(unit_out.at[s], mix.at[b, s], (p.flip, b), first_mix + t).wait_send()
    own_mix.wait()
    mix_across = p.post(mix.at[b], mix.at[b], (s, p.across))
    mix_core = p.post(mix.at[b], mix.at[b], (s, p.core))
    p.landed(mix_across, mix.at[p.across])
    mix_far = p.post(mix.at[p.across], mix.at[p.across], (s, p.core))
    p.landed(wo_core, wo.at[:, p.core])
    p.landed(wo_far, wo.at[:, p.far])
    p.landed(dy_core, dy_all.at[p.core])
    p.landed(dy_far, dy_all.at[p.far])
    p.landed(mix_core, mix.at[p.core])
    p.landed(mix_far, mix.at[p.far])

    def project_out(g, carry):
        mixed = jnp.concatenate([mix[c, 2 * g + kk] for c in range(4) for kk in (0, 1)], axis=1)
        mid = xa[g].astype(F32) + nn(mixed, wo[...].reshape(1024, 1024))
        norm_two[g] = (mid * rms_factor(mid) * gain_f[...]).astype(BF16)

        @pl.when(g == b)
        def _():
            middle[...] = mid

        return carry

    lax.fori_loop(0, 4, project_out, 0)
    p.landed(y_gu[0], wgu.at[p.flip])
    p.landed(y_d[0], wd.at[p.flip])
    for k in (1, 2, 3):
        p.landed(y_gu[k], wgu.at[2 * p.down(k) + 1 - y])
        p.landed(y_d[k], wd.at[2 * p.down(k) + 1 - y])
    p.drain()


def chip_sum_post(p, t, parts, recv, first):
    @pl.when(t == 0)
    def _():
        p.copy(parts.at[p.far], recv.at[0], (p.s, p.core), first).start()

    @pl.when(t == 1)
    def _():
        p.copy(parts.at[p.core], recv.at[1], (p.s, p.core), first + 1).start()


def chip_sum_across(p, parts, recv, first):
    p.copy(recv.at[0], recv.at[0], (p.s, p.core), first).wait_recv()
    parts[p.across] = (parts[p.across].astype(F32) + recv[0].astype(F32)).astype(BF16)
    p.copy(parts.at[p.across], recv.at[2], (p.s, p.across), first + 2).start()


def chip_sum_rest(p, parts, recv, first):
    p.copy(recv.at[1], recv.at[1], (p.s, p.core), first + 1).wait_recv()
    p.copy(recv.at[2], recv.at[2], (p.s, p.core), first + 2).wait_recv()
    for k in range(3):
        p.copy(parts.at[p.b], recv.at[k], (p.s, p.core), first + k).wait_send()
    return recv[1].astype(F32) + recv[2].astype(F32)


def batch_order(p, t):
    return jnp.where(t == 0, p.far, jnp.where(t == 1, p.core, jnp.where(t == 2, p.across, p.b)))


def feed_kernel(
    norm_two, dy_all, wgu, wd, middle,
    output, dn2, ggu, gd,
    hid, dgate, dup, parts_n, recv_n, parts_o, recv_o, keep_n, keep_o, send_sem, recv_sem, local_sem,
):
    p = Place(send_sem, recv_sem, local_sem)
    p.greet()
    first_n, first_o = p.slots(3), p.slots(3)

    def gated(t, carry):
        g = batch_order(p, t)
        rows = pl.ds(pl.multiple_of(g * 256, 256), 256)
        n2 = norm_two[g]
        gate = nn(n2, wgu[:, 0].reshape(1024, 1152))
        up = nn(n2, wgu[:, 1].reshape(1024, 1152))
        dh = nt(dy_all[g], wd[...].reshape(1152, 1024))
        sg = 1.0 / (1.0 + jnp.exp(-gate))
        swish = gate * sg
        hid[rows] = (swish * up).astype(BF16)
        dg = (dh * up * sg * (1.0 + gate * (1.0 - sg))).astype(BF16)
        du = (dh * swish).astype(BF16)
        dgate[rows] = dg
        dup[rows] = du
        part = nt(dg, wgu[:, 0].reshape(1024, 1152)) + nt(du, wgu[:, 1].reshape(1024, 1152))
        parts_n[g] = part.astype(BF16)

        @pl.when(t == 3)
        def _():
            keep_n[...] = part

        chip_sum_post(p, t, parts_n, recv_n, first_n)
        return carry

    lax.fori_loop(0, 4, gated, 0)
    chip_sum_across(p, parts_n, recv_n, first_n)

    def down(t, carry):
        g = batch_order(p, t)
        part = nn(hid[pl.ds(pl.multiple_of(g * 256, 256), 256)], wd[...].reshape(1152, 1024))
        parts_o[g] = part.astype(BF16)

        @pl.when(t == 3)
        def _():
            keep_o[...] = part

        chip_sum_post(p, t, parts_o, recv_o, first_o)
        return carry

    lax.fori_loop(0, 4, down, 0)
    chip_sum_across(p, parts_o, recv_o, first_o)

    def down_rows(c, carry):
        at = pl.multiple_of(128 * c, 128)
        gd[pl.ds(at, 128)] = tn(hid[:, pl.ds(at, 128)], dy_all[...].reshape(1024, 1024)).astype(BF16)
        return carry

    lax.fori_loop(0, 9, down_rows, 0)

    def gate_rows(c, carry):
        at = pl.multiple_of(128 * c, 128)
        left = norm_two[:, :, pl.ds(at, 128)].reshape(1024, 128)
        ggu[c, 0] = tn(left, dgate[...]).astype(BF16)
        ggu[c, 1] = tn(left, dup[...]).astype(BF16)
        return carry

    lax.fori_loop(0, 8, gate_rows, 0)
    dn2[...] = keep_n[...] + chip_sum_rest(p, parts_n, recv_n, first_n)
    total = keep_o[...] + chip_sum_rest(p, parts_o, recv_o, first_o)
    output[...] = (middle[...] + total).astype(BF16)


class SeqSum:
    def __init__(self, p, y_recv, z_recv):
        self.p, self.y_recv, self.z_recv = p, y_recv, z_recv

    def start(self, source, mine=None):
        p = self.p
        self.index = p.post(source.at[:, 1 - p.y], self.y_recv, (p.flip, p.b))
        self.load = None
        if mine is None:
            self.mine = lambda i: source.at[i, p.y]
        else:
            self.load = p.local(source.at[:, p.y], mine)
            self.mine = lambda i: mine.at[i]

    def middle(self):
        p = self.p
        if self.load is not None:
            self.load.wait()
        p.landed(self.index, self.y_recv)
        self.far = []
        for k in (1, 2, 3):
            i = p.up(k)
            self.y_recv[i] = (self.y_recv[i].astype(F32) + self.mine(i)[...].astype(F32)).astype(BF16)
            self.far.append(p.post(self.y_recv.at[i], self.z_recv.at[k - 1], (2 * i + p.y, p.b)))

    def finish(self):
        p = self.p
        total = self.y_recv[p.z].astype(F32) + self.mine(p.z)[...].astype(F32)
        for k in (1, 2, 3):
            p.landed(self.far[k - 1], self.z_recv.at[k - 1])
            total = total + self.z_recv[k - 1].astype(F32)
        return total


def backward_kernel(
    dn2, middle, x, dy, wo, mix, unit, unit_out, lse, length_all, pre, norm, wqkv,
    cos, sin, gain_q, gain_k, gain_a, gain_f, ggu, gd,
    dx, rqkv, rgu, rd, ro, gains_out,
    dmid, dox, doq, dou, dbr, kv, kt, q_right, do_right, q_left, do_left, delta, dk2, dv2, back, dqr,
    dpre, parts, recv, keep, gqkv, go, mixt,
    y_d, m_d, z_d, y_g, m_g, z_g, y_u, m_u, z_u, y_q, z_q, y_o, z_o, fin_g, fin_u, fin_q,
    gain_sum, gain_batch, gain_seq,
    send_sem, recv_sem, local_sem,
):
    p = Place(send_sem, recv_sem, local_sem)
    s, b, z, y = p.s, p.b, p.z, p.y
    p.greet()
    sum_d, sum_g, sum_u = SeqSum(p, y_d, z_d), SeqSum(p, y_g, z_g), SeqSum(p, y_u, z_u)
    sum_d.start(gd, m_d)
    sum_g.start(ggu.at[:, :, 0], m_g)
    sum_u.start(ggu.at[:, :, 1], m_u)

    mid = middle[...]
    r2 = rms_factor(mid)
    grad_two = dn2[...]
    gain_sum[...] = jnp.zeros((8, 1024), F32)
    gain_sum[1:2] = jnp.sum(grad_two * mid * r2, axis=0, keepdims=True)
    dm = dy[...].astype(F32) + norm_back(grad_two * gain_f[...], mid, r2)
    dmid[...] = dm
    dbr[b] = dm.astype(BF16)
    for c in range(4):
        for kk in (0, 1):
            h = 2 * c + kk
            dox[c, kk] = nt(dbr[b], wo[h].reshape(128, 1024)).astype(BF16)
    got_do = []
    for k in (1, 2, 3):
        to = lax.rem(b + k, 4)
        got_do.append(p.post(dox.at[to], doq.at[pl.ds(2 * b, 2)], (s, to)))
    doq[pl.ds(2 * b, 2)] = dox[b]
    dbr_across = p.post(dbr.at[b], dbr.at[b], (s, p.across))
    dbr_core = p.post(dbr.at[b], dbr.at[b], (s, p.core))
    for k in (1, 2, 3):
        p.landed(got_do[k - 1], doq.at[pl.ds(2 * lax.rem(b + 4 - k, 4), 2)])
    got_unit = []
    for k in range(1, 8):
        to = lax.rem(s + k, 8)
        got_unit.append(p.post(doq.at[to], dou.at[s], (to, b)))
    dou[s] = doq[s]

    def prepare(i, carry):
        live = i * 256 + rows_of((256, 128)) < length_all[z][0:1, :]
        masked = jnp.where(live, unit[i, :, 128:256].astype(F32), 0.0)
        kv[i] = masked.astype(BF16)
        kt[i] = jnp.transpose(masked)[0:64].astype(BF16)
        q = unit[i, :, 0:128].astype(F32)
        qt = jnp.transpose(q).astype(BF16)
        q_right[i, 0:64] = jnp.concatenate([qt[0:64], qt[64:128]], axis=1)
        q_right[i, 64:128] = jnp.zeros((64, 512), BF16)
        first = lanes(q.shape) < 64
        q_left[i, 0:256] = jnp.where(first, q, 0.0).astype(BF16)
        q_left[i, 256:512] = jnp.where(first, 0.0, q).astype(BF16)
        dk2[i] = jnp.zeros((256, 128), F32)
        dv2[i] = jnp.zeros((256, 128), F32)
        return carry

    lax.fori_loop(0, 8, prepare, 0)
    sum_d.middle()
    p.landed(dbr_across, dbr.at[p.across])
    dbr_far = p.post(dbr.at[p.across], dbr.at[p.across], (s, p.core))
    for k in range(1, 8):
        p.landed(got_unit[k - 1], dou.at[lax.rem(s + 8 - k, 8)])

    def prepare_grad(i, carry):
        do = dou[i].astype(F32)
        dot = jnp.transpose(do)
        do_right[i, 0:64] = jnp.zeros((64, 512), BF16)
        do_right[i, 64:128] = jnp.concatenate([dot[0:64], dot[64:128]], axis=1).astype(BF16)
        first = lanes(do.shape) < 64
        do_left[i, 0:256] = jnp.where(first, do, 0.0).astype(BF16)
        do_left[i, 256:512] = jnp.where(first, 0.0, do).astype(BF16)
        both = dot * jnp.transpose(unit_out[i].astype(F32))
        low = jnp.sum(both[0:64], axis=0, keepdims=True)
        high = jnp.sum(both[64:128], axis=0, keepdims=True)
        delta[i] = jnp.broadcast_to(jnp.concatenate([low, high], axis=1), (8, 512))
        return carry

    lax.fori_loop(0, 8, prepare_grad, 0)

    def queries(t, carry):
        i = 7 - t
        qr, dr, ql, dl = q_right[i], do_right[i], q_left[i], do_left[i]
        log_total = lse[i][0:1]
        shift = delta[i][0:1]

        def block(j, probs):
            ds = (probs * (nn(kv[j], dr) - shift)).astype(BF16)
            dv2[j] += nn(probs.astype(BF16), dl)
            dk2[j] += nn(ds, ql)
            return nn(kt[j], ds)

        def step(j, acc):
            return acc + block(j, jnp.exp(nn(kv[j], qr) - log_total))

        acc = lax.fori_loop(0, i, step, jnp.zeros((64, 512), F32))
        causal = rows_of((256, 512)) <= lax.rem(lanes((256, 512)), 256)
        acc = acc + block(i, jnp.where(causal, jnp.exp(nn(kv[i], qr) - log_total), 0.0))
        dq = jnp.concatenate([acc[:, 0:256], acc[:, 256:512]], axis=0) * 0.125
        back[i, :, 0:128] = jnp.transpose(dq).astype(BF16)
        live = i * 256 + rows_of((256, 128)) < length_all[z][0:1, :]
        dk, dv = dk2[i], dv2[i]
        dk = dk + pltpu.roll(dk, 64, 1)
        dv = dv + pltpu.roll(dv, 64, 1)
        dkv = jnp.where(lanes((256, 128)) < 64, dk, dv)
        back[i, :, 128:256] = jnp.where(live, dkv, 0.0).astype(BF16)
        return carry

    lax.fori_loop(0, 3, queries, 0)
    sum_g.middle()
    lax.fori_loop(3, 8, queries, 0)
    got_back = []
    for k in range(1, 8):
        to = lax.rem(s + k, 8)
        got_back.append(p.post(back.at[to], dqr.at[s], (to, b)))
    dqr[s] = back[s]

    p.landed(dbr_core, dbr.at[p.core])
    p.landed(dbr_far, dbr.at[p.far])

    def turn(e, carry):
        for g in range(4):
            mixt[:, 256 * g : 256 * g + 256] = jnp.transpose(
                mix[e // 2, 2 * g + lax.rem(e, 2)].astype(F32)
            ).astype(BF16)
        left = mixt[pl.ds(pl.multiple_of(32 * b, 32), 32)]
        go[e // 2, lax.rem(e, 2)] = nn(left, dbr[...].reshape(1024, 1024)).astype(BF16)
        return carry

    lax.fori_loop(0, 8, turn, 0)
    sum_o = SeqSum(p, y_o, z_o)
    sum_o.start(go)
    sum_u.middle()
    for k in range(1, 8):
        p.landed(got_back[k - 1], dqr.at[lax.rem(s + 8 - k, 8)])

    first_n = p.slots(3)
    zero_row = jnp.zeros((1, 128), F32)

    def heads(t, carry):
        sum_q, sum_k = carry
        g = batch_order(p, t)
        for kk in (0, 1):
            at = 256 * kk
            q, k = pre[g, :, at : at + 128], pre[g, :, at + 128 : at + 256]
            rq = lax.rsqrt(head_mean(q * q) + eps)
            rk = lax.rsqrt(head_mean(k * k) + eps)
            dq = rope_back(dqr[2 * g + kk, :, 0:128].astype(F32), cos[...], sin[...])
            dkv = dqr[2 * g + kk, :, 128:256].astype(F32)
            dk = rope_back(dkv, cos[...], sin[...])
            sum_q = sum_q + jnp.sum(dq * q * rq, axis=0, keepdims=True)
            sum_k = sum_k + jnp.sum(dk * k * rk, axis=0, keepdims=True)
            dq = dq * gain_q[...]
            dk = dk * gain_k[...]
            dq = rq * (dq - q * rq * rq * head_mean(dq * q))
            dk = rk * (dk - k * rk * rk * head_mean(dk * k))
            dpre[g, :, at : at + 128] = dq.astype(BF16)
            dpre[g, :, at + 128 : at + 256] = jnp.where(lanes(dk.shape) < 64, dk, dkv).astype(BF16)
        part = nt(dpre[g], wqkv[...].reshape(1024, 512))
        parts[g] = part.astype(BF16)

        @pl.when(t == 3)
        def _():
            keep[...] = part

        chip_sum_post(p, t, parts, recv, first_n)
        return (sum_q, sum_k)

    sum_q, sum_k = lax.fori_loop(0, 4, heads, (zero_row, zero_row))
    gain_sum[2:3, 0:128] = sum_q
    gain_sum[3:4, 0:128] = sum_k
    chip_sum_across(p, parts, recv, first_n)

    def qkv_rows(c, carry):
        at = pl.multiple_of(128 * c, 128)
        left = norm[:, :, pl.ds(at, 128)].reshape(1024, 128)
        gqkv[c // 2, lax.rem(c, 2)] = tn(left, dpre[...].reshape(1024, 512)).astype(BF16)
        return carry

    lax.fori_loop(0, 8, qkv_rows, 0)
    sum_qkv = SeqSum(p, y_q, z_q)
    sum_qkv.start(gqkv)
    sum_o.middle()

    dn1 = keep[...] + chip_sum_rest(p, parts, recv, first_n)
    xf = x[...].astype(F32)
    r1 = rms_factor(xf)
    gain_sum[0:1] = jnp.sum(dn1 * xf * r1, axis=0, keepdims=True)
    dx[...] = (dmid[...] + norm_back(dn1 * gain_a[...], xf, r1)).astype(BF16)
    got_gain = [p.post(gain_sum, gain_batch.at[b], (s, lax.rem(b + k, 4))) for k in (1, 2, 3)]
    gain_batch[b] = gain_sum[...]
    sum_qkv.middle()

    rd[...] = sum_d.finish()

    def exchange(total, fin, dst):
        fin[...] = total.astype(BF16)
        got = []
        for k in (1, 2, 3):
            to = lax.rem(b + k, 4)
            rows = pl.ds(pl.multiple_of(32 * to, 32), 32)
            got.append(p.post(fin.at[rows], dst(b), (s, to)))
        dst(b)[...] = fin[pl.ds(pl.multiple_of(32 * b, 32), 32)]
        return got

    def arrive(got, dst):
        for k in (1, 2, 3):
            p.landed(got[k - 1], dst(lax.rem(b + 4 - k, 4)))

    dst_g, dst_u, dst_q = (lambda i: rgu.at[i, 0]), (lambda i: rgu.at[i, 1]), (lambda i: rqkv.at[i])
    got_g = exchange(sum_g.finish(), fin_g, dst_g)
    for k in (1, 2, 3):
        p.landed(got_gain[k - 1], gain_batch.at[lax.rem(b + 4 - k, 4)])
    gain_seq[s] = (gain_batch[0] + gain_batch[1]) + (gain_batch[2] + gain_batch[3])
    got_all = [p.post(gain_seq.at[s], gain_seq.at[s], (lax.rem(s + k, 8), b)) for k in range(1, 8)]
    got_u = exchange(sum_u.finish(), fin_u, dst_u)
    ro[...] = sum_o.finish()
    got_q = exchange(sum_qkv.finish(), fin_q, dst_q)
    for k in range(1, 8):
        p.landed(got_all[k - 1], gain_seq.at[lax.rem(s + 8 - k, 8)])
    total = gain_seq[0]
    for k in range(1, 8):
        total = total + gain_seq[k]
    gains_out[...] = total
    arrive(got_g, dst_g)
    arrive(got_u, dst_u)
    arrive(got_q, dst_q)
    p.drain()


def call(kernel, outs, in_specs, out_specs, scratch, cid, sems=(64, 16)):
    return pl.pallas_call(
        kernel,
        out_shape=[jax.ShapeDtypeStruct(shape, dtype) for shape, dtype in outs],
        in_specs=in_specs,
        out_specs=out_specs,
        scratch_shapes=[pltpu.VMEM(shape, dtype) for shape, dtype in scratch]
        + [
            pltpu.SemaphoreType.DMA((sems[0],)),
            pltpu.SemaphoreType.DMA((sems[0],)),
            pltpu.SemaphoreType.DMA((sems[1],)),
        ],
        compiler_params=pltpu.CompilerParams(
            collective_id=cid, has_side_effects=True, vmem_limit_bytes=60 * 2**20
        ),
    )


def body(
    inputs, lengths, w_query, key_weight, value_weight, w_out, w_gate, w_up, w_down,
    gain_attn, gain_ffn, gain_query, gain_key, cotangent,
):
    x = inputs.reshape(256, 1024)
    dy = cotangent.reshape(256, 1024)
    positions = lax.axis_index("seq") * 256 + jnp.arange(256, dtype=jnp.int32)
    freqs = theta ** (-(jnp.arange(32, dtype=F32) * 2.0) / 64)
    angles = positions.astype(F32)[:, None] * freqs[None, :]
    cosine = jnp.tile(jnp.cos(angles), (1, 4))
    sine = jnp.tile(jnp.sin(angles), (1, 4))
    length = jnp.broadcast_to(lengths[:, None], (8, 128))
    wqkv_in = jnp.concatenate(
        [
            w_query.reshape(32, 4, 2, 128),
            key_weight.reshape(32, 4, 2, 64),
            value_weight.reshape(32, 4, 2, 64),
        ],
        axis=-1,
    )
    wqkv_in = jnp.transpose(wqkv_in.reshape(32, 4, 512), (1, 0, 2))
    wgu_in = jnp.stack([w_gate, w_up]).reshape(2, 32, 8, 4, 144)
    wgu_in = jnp.transpose(wgu_in, (3, 0, 1, 2, 4)).reshape(4, 2, 32, 1152)
    gain_q = jnp.tile(gain_query, 2)[None]
    gain_k = jnp.tile(gain_key, 2)[None]
    gain_a = gain_attn[None]
    gain_f = gain_ffn[None]

    (wgu, wd, wo, wqkv, norm, pre, unit, unit_out, lse, mix, norm_two, middle, dy_all, length_all) = call(
        forward_kernel,
        [
            ((8, 2, 128, 1152), BF16), ((8, 144, 1024), BF16), ((8, 4, 32, 1024), BF16),
            ((8, 128, 512), BF16), ((4, 256, 1024), BF16), ((4, 256, 512), F32),
            ((8, 256, 256), BF16), ((8, 256, 128), BF16), ((8, 8, 512), F32),
            ((4, 8, 256, 128), BF16), ((4, 256, 1024), BF16), ((256, 1024), F32),
            ((4, 256, 1024), BF16), ((4, 8, 128), jnp.int32),
        ],
        [VMEM, ANY, VMEM, VMEM, ANY, ANY, VMEM] + [VMEM] * 6,
        [ANY, ANY] + [VMEM] * 10 + [ANY, VMEM],
        [
            ((4, 256, 1024), BF16), ((8, 256, 256), BF16), ((8, 256, 128), BF16), ((8, 80, 256), BF16),
        ],
        0,
        sems=(96, 16),
    )(x, dy, length, wqkv_in, wgu_in, w_down, w_out, cosine, sine, gain_q, gain_k, gain_a, gain_f)

    output, dn2, ggu, gd = call(
        feed_kernel,
        [
            ((256, 1024), BF16), ((256, 1024), F32), ((8, 2, 128, 1152), BF16), ((1152, 1024), BF16),
        ],
        [VMEM] * 5,
        [VMEM] * 4,
        [
            ((1024, 1152), BF16), ((1024, 1152), BF16), ((1024, 1152), BF16),
            ((4, 256, 1024), BF16), ((3, 256, 1024), BF16), ((4, 256, 1024), BF16),
            ((3, 256, 1024), BF16), ((256, 1024), F32), ((256, 1024), F32),
        ],
        1,
    )(norm_two, dy_all, wgu, wd, middle)

    dx, rqkv, rgu, rd, ro, gains = call(
        backward_kernel,
        [
            ((256, 1024), BF16), ((4, 32, 512), BF16), ((4, 2, 32, 1152), BF16),
            ((144, 1024), F32), ((32, 1024), F32), ((8, 1024), F32),
        ],
        [VMEM] * 19 + [ANY] * 2,
        [VMEM] * 6,
        [
            ((256, 1024), F32), ((4, 2, 256, 128), BF16), ((8, 256, 128), BF16), ((8, 256, 128), BF16),
            ((4, 256, 1024), BF16), ((8, 256, 128), BF16), ((8, 64, 256), BF16), ((8, 128, 512), BF16),
            ((8, 128, 512), BF16), ((8, 512, 128), BF16), ((8, 512, 128), BF16), ((8, 8, 512), F32),
            ((8, 256, 128), F32), ((8, 256, 128), F32), ((8, 256, 256), BF16), ((8, 256, 256), BF16),
            ((4, 256, 512), BF16), ((4, 256, 1024), BF16), ((3, 256, 1024), BF16), ((256, 1024), F32),
            ((4, 2, 128, 512), BF16), ((4, 2, 32, 1024), BF16), ((128, 1024), BF16),
            ((4, 144, 1024), BF16), ((4, 144, 1024), BF16), ((3, 144, 1024), BF16),
            ((4, 128, 1152), BF16), ((4, 128, 1152), BF16), ((3, 128, 1152), BF16),
            ((4, 128, 1152), BF16), ((4, 128, 1152), BF16), ((3, 128, 1152), BF16),
            ((4, 128, 512), BF16), ((3, 128, 512), BF16), ((4, 32, 1024), BF16), ((3, 32, 1024), BF16),
            ((128, 1152), BF16), ((128, 1152), BF16), ((128, 512), BF16),
            ((8, 1024), F32), ((4, 8, 1024), F32), ((8, 8, 1024), F32),
        ],
        2,
        sems=(96, 16),
    )(
        dn2, middle, x, dy, wo, mix, unit, unit_out, lse, length_all, pre, norm, wqkv,
        cosine, sine, gain_q, gain_k, gain_a, gain_f,
        ggu.reshape(4, 2, 2, 128, 1152), gd.reshape(4, 2, 144, 1024),
    )

    rows = jnp.transpose(rqkv, (1, 0, 2)).reshape(32, 8, 256).astype(F32)
    grad_query = rows[:, :, 0:128].reshape(32, 1024)
    grad_key = rows[:, :, 128:192].reshape(32, 512)
    grad_value = rows[:, :, 192:256].reshape(32, 512)
    wide = jnp.transpose(rgu.reshape(4, 2, 32, 8, 144), (1, 2, 3, 0, 4)).reshape(2, 32, 4608).astype(F32)
    return (
        output.reshape(256, 1, 1024),
        dx.reshape(256, 1, 1024),
        grad_query,
        grad_key,
        grad_value,
        ro,
        wide[0],
        wide[1],
        rd,
        gains[0],
        gains[1],
        gains[2, 0:64] + gains[2, 64:128],
        gains[3, 0:64],
    )


def rotary_tables(positions, width):
    half = width // 2
    freqs = theta ** (-(jnp.arange(half, dtype=jnp.float32) * 2.0) / width)
    angles = positions.astype(jnp.float32)[:, None] * freqs[None, :]
    cosine = jnp.concatenate([jnp.cos(angles), jnp.cos(angles)], axis=-1)
    sine = jnp.concatenate([jnp.sin(angles), jnp.sin(angles)], axis=-1)
    return (cosine, sine)


def rotate(v, cosine, sine):
    half = v.shape[-1] // 2
    turned = jnp.concatenate([-v[..., half:], v[..., :half]], axis=-1)
    return v * cosine + turned * sine


def rotate_back(grad, cosine, sine):
    half = grad.shape[-1] // 2
    moved = grad * sine
    return grad * cosine + jnp.concatenate([moved[..., half:], -moved[..., :half]], axis=-1)


def product(left, right):
    return jnp.dot(left, right, preferred_element_type=jnp.float32)


def left_product(left, right):
    return jnp.einsum("rd,rn->dn", left, right, preferred_element_type=jnp.float32)


def right_product(left, right):
    return jnp.einsum("rn,dn->rd", left, right, preferred_element_type=jnp.float32)


def rounded(v):
    return v.astype(jnp.bfloat16)


def split_rows(term, seq_size, batch_size):
    return term.reshape(
        seq_size, batch_size, term.shape[0] // (seq_size * batch_size), term.shape[1]
    )


def fold_sources(piece):
    return jnp.sum(piece, axis=1).reshape(-1, piece.shape[-1])


def general_body(
    inputs,
    lengths,
    w_query,
    key_weight,
    value_weight,
    w_out,
    w_gate,
    w_up,
    w_down,
    gain_attn,
    gain_ffn,
    gain_query,
    gain_key,
    cotangent,
):
    slice_len, seq_count, width = inputs.shape
    rows = slice_len * seq_count
    head_dim = gain_query.shape[0]
    kv_width = key_weight.shape[1]
    kv_heads = kv_width // head_dim
    q_heads = w_query.shape[1] // head_dim
    sequence_group = q_heads // kv_heads
    scale = head_dim ** (-0.5)
    cycle_size = lax.axis_size("seq")
    batch_size = lax.axis_size("batch")
    positions = lax.axis_index("seq") * slice_len + jnp.arange(slice_len, dtype=jnp.int32)
    cosine, sine = rotary_tables(positions, head_dim)
    cosine = cosine[:, None, None, :]
    sine = sine[:, None, None, :]
    shards = (w_query, key_weight, value_weight, w_out, w_gate, w_up, w_down)
    wq, key_matrix, value_matrix, wo, wg, wu, wd = (
        lax.all_gather(shards[0], ("seq", "batch"), axis=0, tiled=True),
        lax.all_gather(shards[1], ("seq", "batch"), axis=0, tiled=True),
        lax.all_gather(shards[2], ("seq", "batch"), axis=0, tiled=True),
        lax.all_gather(shards[3], ("seq", "batch"), axis=0, tiled=True),
        lax.all_gather(shards[4], ("seq", "batch"), axis=0, tiled=True),
        lax.all_gather(shards[5], ("seq", "batch"), axis=0, tiled=True),
        lax.all_gather(shards[6], ("seq", "batch"), axis=0, tiled=True),
    )
    stream = inputs.reshape(rows, width).astype(jnp.float32)
    factor_one = rms_factor(stream)
    normalized_input = rounded(stream * factor_one * gain_attn)
    query_pre = product(normalized_input, wq).reshape(slice_len, seq_count, q_heads, head_dim)
    key_before_rotation = product(normalized_input, key_matrix).reshape(
        slice_len, seq_count, kv_heads, head_dim
    )
    value_b = rounded(product(normalized_input, value_matrix)).reshape(
        slice_len, seq_count, kv_width
    )
    factor_q = rms_factor(query_pre)
    factor_k = rms_factor(key_before_rotation)
    query_b = rounded(rotate(query_pre * factor_q * gain_query, cosine, sine))
    key_b = rounded(rotate(key_before_rotation * factor_k * gain_key, cosine, sine)).reshape(
        slice_len, seq_count, kv_width
    )
    query_five = query_b.reshape(slice_len, seq_count, kv_heads, sequence_group, head_dim)

    def scores_of(keys, start):
        count = keys.shape[0]
        raw = (
            jnp.einsum(
                "tsgrd,csgd->sgrtc",
                query_five,
                keys.reshape(count, seq_count, kv_heads, head_dim),
                preferred_element_type=jnp.float32,
            )
            * scale
        )
        key_pos = start + jnp.arange(count, dtype=jnp.int32)
        causal = key_pos[None, :] <= positions[:, None]
        inside = key_pos[None, :] < lengths[:, None]
        valid = causal[None, :, :] & inside[:, None, :]
        return (raw, valid[:, None, None, :, :])

    state_shape = (seq_count, kv_heads, sequence_group, slice_len)
    shard_ids = jnp.arange(cycle_size, dtype=jnp.int32)
    top = jnp.full(state_shape, -1e30, jnp.float32)
    keys = lax.all_gather(key_b, "seq", axis=0, tiled=True)
    value_rows = lax.all_gather(value_b, "seq", axis=0, tiled=True)
    count = keys.shape[0]
    raw, valid = scores_of(keys, jnp.int32(0))
    masked = jnp.where(valid, raw, -jnp.inf)
    new_top = jnp.maximum(top, jnp.max(masked, axis=-1))
    probs = jnp.exp(masked - new_top[..., None])
    total = jnp.sum(probs, axis=-1)
    acc = jnp.einsum(
        "sgrtc,csgd->sgrtd",
        rounded(probs),
        value_rows.reshape(count, seq_count, kv_heads, head_dim),
        preferred_element_type=jnp.float32,
    )
    state = (new_top, total, acc)
    top, total, acc = state
    attn_out = acc / total[..., None]
    log_total = top + jnp.log(total)
    mixed_b = rounded(jnp.transpose(attn_out, (3, 0, 1, 2, 4)).reshape(rows, q_heads * head_dim))
    middle = stream + product(mixed_b, wo)
    factor_two = rms_factor(middle)
    normed_two = rounded(middle * factor_two * gain_ffn)
    gate = product(normed_two, wg)
    up_part = product(normed_two, wu)
    sigma = jax.nn.sigmoid(gate)
    swish = gate * sigma
    hidden_b = rounded(swish * up_part)
    result = middle + product(hidden_b, wd)
    output = rounded(result).reshape(slice_len, seq_count, width)
    wq, key_matrix, value_matrix, wo, wg, wu, wd = (
        lax.all_gather(shards[0], ("seq", "batch"), axis=0, tiled=True),
        lax.all_gather(shards[1], ("seq", "batch"), axis=0, tiled=True),
        lax.all_gather(shards[2], ("seq", "batch"), axis=0, tiled=True),
        lax.all_gather(shards[3], ("seq", "batch"), axis=0, tiled=True),
        lax.all_gather(shards[4], ("seq", "batch"), axis=0, tiled=True),
        lax.all_gather(shards[5], ("seq", "batch"), axis=0, tiled=True),
        lax.all_gather(shards[6], ("seq", "batch"), axis=0, tiled=True),
    )
    grad_res = cotangent.reshape(rows, width).astype(jnp.float32)
    grad_ffo = rounded(grad_res)
    grad_wd = left_product(hidden_b, grad_ffo)
    grad_hidden = right_product(grad_ffo, wd)
    grad_gate = rounded(grad_hidden * up_part * sigma * (1.0 + gate * (1.0 - sigma)))
    grad_up = rounded(grad_hidden * swish)
    grad_wg = left_product(normed_two, grad_gate)
    grad_wu = left_product(normed_two, grad_up)
    grad_normed_two = right_product(grad_gate, wg) + right_product(grad_up, wu)
    grad_gain_ffn = jnp.sum(grad_normed_two * middle * factor_two, axis=0)
    grad_middle = grad_res + norm_back(grad_normed_two * gain_ffn, middle, factor_two)
    grad_branch = rounded(grad_middle)
    grad_wo = left_product(mixed_b, grad_branch)
    grad_mixed = rounded(right_product(grad_branch, wo))
    grad_five = grad_mixed.reshape(slice_len, seq_count, kv_heads, sequence_group, head_dim)
    delta = jnp.sum(
        jnp.transpose(grad_five, (1, 2, 3, 0, 4)).astype(jnp.float32) * attn_out, axis=-1
    )
    gathered = (
        lax.all_gather(key_b, "seq", axis=0, tiled=True),
        lax.all_gather(value_b, "seq", axis=0, tiled=True),
    )

    def back_step(grad_query, item):
        index, keys, value_rows = item
        raw, valid = scores_of(keys, index * slice_len)
        probs = jnp.where(valid, jnp.exp(raw - log_total[..., None]), 0.0)
        key_four = keys.reshape(slice_len, seq_count, kv_heads, head_dim)
        value_four = value_rows.reshape(slice_len, seq_count, kv_heads, head_dim)
        grad_probs = jnp.einsum(
            "tsgrd,csgd->sgrtc", grad_five, value_four, preferred_element_type=jnp.float32
        )
        grad_score = rounded(probs * (grad_probs - delta[..., None]))
        grad_query = (
            grad_query
            + jnp.einsum(
                "sgrtc,csgd->tsgrd", grad_score, key_four, preferred_element_type=jnp.float32
            )
            * scale
        )
        key_term = (
            jnp.einsum(
                "sgrtc,tsgrd->csgd", grad_score, query_five, preferred_element_type=jnp.float32
            )
            * scale
        )
        value_term = jnp.einsum(
            "sgrtc,tsgrd->csgd", rounded(probs), grad_five, preferred_element_type=jnp.float32
        )
        return (
            grad_query,
            (
                key_term.reshape(slice_len, seq_count, kv_width),
                value_term.reshape(slice_len, seq_count, kv_width),
            ),
        )

    items = (
        shard_ids,
        gathered[0].reshape(cycle_size, slice_len, seq_count, kv_width),
        gathered[1].reshape(cycle_size, slice_len, seq_count, kv_width),
    )
    grad_query, terms = lax.scan(
        back_step,
        jnp.zeros((slice_len, seq_count, kv_heads, sequence_group, head_dim), jnp.float32),
        items,
    )
    key_terms = terms[0].reshape(cycle_size * slice_len, seq_count, kv_width)
    value_terms = terms[1].reshape(cycle_size * slice_len, seq_count, kv_width)
    grad_key, grad_value = (
        lax.psum_scatter(
            key_terms.astype(jnp.bfloat16), "seq", scatter_dimension=0, tiled=True
        ).astype(jnp.float32),
        lax.psum_scatter(
            value_terms.astype(jnp.bfloat16), "seq", scatter_dimension=0, tiled=True
        ).astype(jnp.float32),
    )
    grad_qr = (
        rounded(grad_query).astype(jnp.float32).reshape(slice_len, seq_count, q_heads, head_dim)
    )
    grad_qn = rotate_back(grad_qr, cosine, sine)
    grad_gain_query = jnp.sum(grad_qn * query_pre * factor_q, axis=(0, 1, 2))
    grad_qp = rounded(
        norm_back(grad_qn * gain_query, query_pre, factor_q).reshape(rows, q_heads * head_dim)
    )
    grad_kr = (
        rounded(grad_key).astype(jnp.float32).reshape(slice_len, seq_count, kv_heads, head_dim)
    )
    grad_kn = rotate_back(grad_kr, cosine, sine)
    grad_gain_key = jnp.sum(grad_kn * key_before_rotation * factor_k, axis=(0, 1, 2))
    grad_kp = rounded(
        norm_back(grad_kn * gain_key, key_before_rotation, factor_k).reshape(rows, kv_width)
    )
    grad_vp = rounded(grad_value).reshape(rows, kv_width)
    grad_wq = left_product(normalized_input, grad_qp)
    grad_wk = left_product(normalized_input, grad_kp)
    grad_wv = left_product(normalized_input, grad_vp)
    grad_normed = (
        right_product(grad_qp, wq)
        + right_product(grad_kp, key_matrix)
        + right_product(grad_vp, value_matrix)
    )
    grad_gain_attn = jnp.sum(grad_normed * stream * factor_one, axis=0)
    grad_stream = grad_middle + norm_back(grad_normed * gain_attn, stream, factor_one)
    spread = (
        lax.all_to_all(
            split_rows(grad_wq, cycle_size, batch_size).astype(jnp.bfloat16),
            "batch",
            split_axis=1,
            concat_axis=1,
            tiled=True,
        ).astype(jnp.float32),
        lax.all_to_all(
            split_rows(grad_wk, cycle_size, batch_size).astype(jnp.bfloat16),
            "batch",
            split_axis=1,
            concat_axis=1,
            tiled=True,
        ).astype(jnp.float32),
        lax.all_to_all(
            split_rows(grad_wv, cycle_size, batch_size).astype(jnp.bfloat16),
            "batch",
            split_axis=1,
            concat_axis=1,
            tiled=True,
        ).astype(jnp.float32),
        lax.all_to_all(
            split_rows(grad_wo, cycle_size, batch_size).astype(jnp.bfloat16),
            "batch",
            split_axis=1,
            concat_axis=1,
            tiled=True,
        ).astype(jnp.float32),
        lax.all_to_all(
            split_rows(grad_wg, cycle_size, batch_size).astype(jnp.bfloat16),
            "batch",
            split_axis=1,
            concat_axis=1,
            tiled=True,
        ).astype(jnp.float32),
        lax.all_to_all(
            split_rows(grad_wu, cycle_size, batch_size).astype(jnp.bfloat16),
            "batch",
            split_axis=1,
            concat_axis=1,
            tiled=True,
        ).astype(jnp.float32),
        lax.all_to_all(
            split_rows(grad_wd, cycle_size, batch_size).astype(jnp.bfloat16),
            "batch",
            split_axis=1,
            concat_axis=1,
            tiled=True,
        ).astype(jnp.float32),
    )
    partial_sums = [fold_sources(piece) for piece in spread]
    summed = (
        lax.psum_scatter(
            partial_sums[0].astype(jnp.bfloat16), "seq", scatter_dimension=0, tiled=True
        ).astype(jnp.float32),
        lax.psum_scatter(
            partial_sums[1].astype(jnp.bfloat16), "seq", scatter_dimension=0, tiled=True
        ).astype(jnp.float32),
        lax.psum_scatter(
            partial_sums[2].astype(jnp.bfloat16), "seq", scatter_dimension=0, tiled=True
        ).astype(jnp.float32),
        lax.psum_scatter(
            partial_sums[3].astype(jnp.bfloat16), "seq", scatter_dimension=0, tiled=True
        ).astype(jnp.float32),
        lax.psum_scatter(
            partial_sums[4].astype(jnp.bfloat16), "seq", scatter_dimension=0, tiled=True
        ).astype(jnp.float32),
        lax.psum_scatter(
            partial_sums[5].astype(jnp.bfloat16), "seq", scatter_dimension=0, tiled=True
        ).astype(jnp.float32),
        lax.psum_scatter(
            partial_sums[6].astype(jnp.bfloat16), "seq", scatter_dimension=0, tiled=True
        ).astype(jnp.float32),
    )
    gains = lax.psum(
        (grad_gain_attn, grad_gain_ffn, grad_gain_query, grad_gain_key), ("seq", "batch")
    )
    grad_inputs = rounded(grad_stream).reshape(slice_len, seq_count, width)
    return (
        output,
        grad_inputs,
        summed[0],
        summed[1],
        summed[2],
        summed[3],
        summed[4],
        summed[5],
        summed[6],
        gains[0],
        gains[1],
        gains[2],
        gains[3],
    )


def solution(mesh):
    sharded = P(("seq", "batch"), None)
    stream = P("seq", "batch", None)
    in_specs = (stream, P("batch")) + (sharded,) * 7 + (P(),) * 4 + (stream,)
    out_specs = (stream, stream) + (sharded,) * 7 + (P(),) * 4
    grouped = mesh.shape["seq"] == 8 and mesh.shape["batch"] == 4
    step = body if grouped else general_body
    return jax.shard_map(step, mesh=mesh, in_specs=in_specs, out_specs=out_specs, check_vma=False)
```

```python
import functools

import jax
import jax.numpy as jnp
from jax import lax
from jax.experimental import pallas as pl
from jax.experimental.pallas import tpu as pltpu
from jax.sharding import PartitionSpec as P

MESH = pl.DeviceIdType.MESH
F32 = jnp.float32
BF16 = jnp.bfloat16
eps = 1e-05
theta = 1000000.0
VMEM = pl.BlockSpec(memory_space=pltpu.VMEM)
ANY = pl.BlockSpec(memory_space=pl.ANY)


def nn(left, right):
    return lax.dot_general(left, right, (((1,), (0,)), ((), ())), preferred_element_type=F32)


def nt(left, right):
    return lax.dot_general(left, right, (((1,), (1,)), ((), ())), preferred_element_type=F32)


def tn(left, right):
    return lax.dot_general(left, right, (((0,), (0,)), ((), ())), preferred_element_type=F32)


def rms_factor(v):
    return lax.rsqrt(jnp.mean(v * v, axis=-1, keepdims=True) + eps)


def norm_back(grad, value, factor):
    return factor * (
        grad - value * factor * factor * jnp.mean(grad * value, axis=-1, keepdims=True)
    )


def lanes(shape):
    return lax.broadcasted_iota(jnp.int32, shape, len(shape) - 1)


def rows_of(shape):
    return lax.broadcasted_iota(jnp.int32, shape, len(shape) - 2)


def head_mean(v):
    first = lanes(v.shape) < 64
    low = jnp.sum(jnp.where(first, v, 0.0), axis=-1, keepdims=True)
    high = jnp.sum(jnp.where(first, 0.0, v), axis=-1, keepdims=True)
    return jnp.where(first, low, high) * (1.0 / 64.0)


def rope(u, cosine, sine):
    early = lax.rem(lanes(u.shape), 64) < 32
    turned = jnp.where(early, -pltpu.roll(u, 96, 1), pltpu.roll(u, 32, 1))
    return u * cosine + turned * sine


def rope_back(u, cosine, sine):
    early = lax.rem(lanes(u.shape), 64) < 32
    w = u * sine
    return u * cosine + jnp.where(early, pltpu.roll(w, 96, 1), -pltpu.roll(w, 32, 1))


class Place:
    def __init__(self, send_sem, recv_sem, local_sem):
        self.s = lax.axis_index("seq")
        self.b = lax.axis_index("batch")
        self.z = self.s // 2
        self.y = lax.rem(self.s, 2)
        self.core = self.b + 1 - 2 * lax.rem(self.b, 2)
        self.across = lax.rem(self.b + 2, 4)
        self.far = 3 - self.b
        self.flip = 2 * self.z + 1 - self.y
        self.inner = jnp.logical_or(self.z == 1, self.z == 2)
        self.pair = self.z + 1 - 2 * lax.rem(self.z, 2)
        self.there = jnp.where(self.z < 2, 2, 1)
        self.beyond = jnp.where(self.z < 2, 3, 0)
        self.send_sem, self.recv_sem, self.local_sem = send_sem, recv_sem, local_sem
        self.used = 0
        self.used_local = 0
        self.sent = []

    def up(self, k):
        return lax.rem(self.z + k, 4)

    def down(self, k):
        return lax.rem(self.z + 4 - k, 4)

    def greet(self):
        barrier = pltpu.get_barrier_semaphore()
        for k in (1, 2, 3):
            pl.semaphore_signal(
                barrier, inc=1, device_id=(self.s, lax.rem(self.b + k, 4)), device_id_type=MESH
            )
        for k in range(1, 8):
            pl.semaphore_signal(
                barrier, inc=1, device_id=(lax.rem(self.s + k, 8), self.b), device_id_type=MESH
            )
        pl.semaphore_wait(barrier, 10)

    def slots(self, count):
        first = self.used
        self.used += count
        return first

    def copy(self, src, dst, device, out, into=None):
        return pltpu.make_async_remote_copy(
            src_ref=src,
            dst_ref=dst,
            send_sem=self.send_sem.at[out],
            recv_sem=self.recv_sem.at[out if into is None else into],
            device_id=device,
            device_id_type=MESH,
        )

    def post(self, src, dst, device):
        index = self.slots(1)
        made = self.copy(src, dst, device, index)
        made.start()
        self.sent.append(made)
        return index

    def landed(self, index, ref):
        self.copy(ref, ref, (self.s, self.core), index).wait_recv()

    def local(self, src, dst):
        index = self.used_local
        self.used_local += 1
        made = pltpu.make_async_copy(src, dst, self.local_sem.at[index])
        made.start()
        return made

    def drain(self):
        for made in self.sent:
            made.wait_send()
        self.sent = []


class Spread:
    def __init__(self, p, slot):
        self.p, self.slot = p, slot
        self.first = p.slots(8)
        self.from_z = (p.pair, p.there, p.beyond)

    def send(self, s, device, out, into):
        self.p.copy(self.slot(s), self.slot(s), device, self.first + out, self.first + into).start()

    def start(self):
        p = self.p
        self.send(p.s, (2 * p.pair + p.y, p.b), 0, 0)
        self.send(p.s, (2 * p.there + p.y, p.b), 1, jnp.where(p.inner, 1, 2))
        self.send(p.s, (p.flip, p.b), 4, 3)

    def land(self, j):
        p = self.p
        s = 2 * self.from_z[j] + p.y
        p.landed(self.first + j, self.slot(s))
        if j > 0:

            @pl.when(p.inner)
            def _():
                self.send(s, (2 * p.pair + p.y, p.b), 1 + j, j)

        self.send(s, (p.flip, p.b), 5 + j, 4 + j)

    def land_inner(self):
        @pl.when(self.p.inner)
        def _():
            self.land(1)
            self.land(2)

    def land_end(self):
        @pl.when(jnp.logical_not(self.p.inner))
        def _():
            self.land(1)
            self.land(2)

    def finish(self):
        p = self.p
        p.landed(self.first + 3, self.slot(p.flip))
        for j in range(3):
            p.landed(self.first + 4 + j, self.slot(2 * self.from_z[j] + 1 - p.y))

    def drain(self):
        p = self.p

        def sent(out):
            p.copy(self.slot(p.s), self.slot(p.s), (p.flip, p.b), self.first + out).wait_send()

        for out in (0, 1, 4, 5, 6, 7):
            sent(out)

        @pl.when(p.inner)
        def _():
            sent(2)
            sent(3)


def forward_kernel(
    x, dy, length, wqkv_in, wgu_in, wd_in, wo_in, cos, sin, gain_q, gain_k, gain_a, gain_f,
    wgu, wd, wo, wqkv, norm, pre, unit, unit_out, lse, mix, norm_two, middle, dy_all, length_all,
    xa, pack, kv, vt, send_sem, recv_sem, local_sem,
):
    p = Place(send_sem, recv_sem, local_sem)
    s, b, z, y = p.s, p.b, p.z, p.y
    my_rows = pl.ds(pl.multiple_of(32 * b, 32), 32)
    own = [
        p.local(wqkv_in.at[b], wqkv.at[s, my_rows]),
        p.local(x, xa.at[b]),
        p.local(length, length_all.at[b]),
        p.local(wo_in, wo.at[s, b]),
    ]
    own_gu = p.local(wgu_in.at[b], wgu.at[s, :, my_rows])
    own_d = p.local(wd_in, wd.at[s])
    own_dy = p.local(dy, dy_all.at[b])
    p.greet()

    got = []
    for k in (1, 2, 3):
        to = lax.rem(b + k, 4)
        got.append(p.post(wqkv_in.at[to], wqkv.at[s, my_rows], (s, to)))
    x_core = p.post(x, xa.at[b], (s, p.core))
    x_across = p.post(x, xa.at[b], (s, p.across))
    got_len = []
    for k in (1, 2, 3):
        to = lax.rem(b + k, 4)
        got_len.append(p.post(length, length_all.at[b], (s, to)))
    for made in own:
        made.wait()
    for k in (1, 2, 3):
        p.landed(got[k - 1], wqkv.at[s, my_rows])
    z_qkv = [p.post(wqkv.at[s], wqkv.at[s], (2 * p.up(k) + y, b)) for k in (1, 2, 3)]
    y_qkv = [p.post(wqkv.at[s], wqkv.at[s], (p.flip, b))]
    z_wo = [p.post(wo.at[s, b], wo.at[s, b], (2 * p.up(k) + y, b)) for k in (1, 2, 3)]
    y_wo = [p.post(wo.at[s, b], wo.at[s, b], (p.flip, b))]
    got_gu = []
    for k in (1, 2, 3):
        to = lax.rem(b + k, 4)
        got_gu.append(p.post(wgu_in.at[to], wgu.at[s, :, my_rows], (s, to)))
    p.landed(x_across, xa.at[p.across])
    x_far = p.post(xa.at[p.across], xa.at[p.across], (s, p.core))
    for k in (1, 2, 3):
        slot = 2 * p.down(k) + y
        p.landed(z_qkv[k - 1], wqkv.at[slot])
        y_qkv.append(p.post(wqkv.at[slot], wqkv.at[slot], (p.flip, b)))
    own_d.wait()
    spread_d = Spread(p, lambda i: wd.at[i])
    spread_g = Spread(p, lambda i: wgu.at[i, 0])
    spread_u = Spread(p, lambda i: wgu.at[i, 1])
    spread_d.start()
    p.landed(x_core, xa.at[p.core])
    p.landed(x_far, xa.at[p.far])
    for k in (1, 2, 3):
        p.landed(got_len[k - 1], length_all.at[lax.rem(b + 4 - k, 4)])

    def normalize(g, carry):
        xg = xa[g].astype(F32)
        norm[g] = (xg * rms_factor(xg) * gain_a[...]).astype(BF16)
        return carry

    lax.fori_loop(0, 4, normalize, 0)
    p.landed(y_qkv[0], wqkv.at[p.flip])
    for k in (1, 2, 3):
        p.landed(y_qkv[k], wqkv.at[2 * p.down(k) + 1 - y])

    own_gu.wait()
    own_dy.wait()
    for k in (1, 2, 3):
        p.landed(got_gu[k - 1], wgu.at[s, :, my_rows])
    spread_g.start()
    spread_u.start()

    first_unit = p.slots(8)

    def project(t, carry):
        g = lax.rem(z + 1 + t, 4)
        whole = nn(norm[g], wqkv[...].reshape(1024, 512))
        pre[g] = whole
        for kk in (0, 1):
            q = whole[:, 256 * kk : 256 * kk + 128]
            kvp = whole[:, 256 * kk + 128 : 256 * kk + 256]
            qn = q * lax.rsqrt(head_mean(q * q) + eps) * gain_q[...]
            kn = kvp * lax.rsqrt(head_mean(kvp * kvp) + eps) * gain_k[...]
            qr = rope(qn, cos[...], sin[...]) * 0.125
            kr = rope(kn, cos[...], sin[...])
            pack[2 * g + kk, :, 0:128] = qr.astype(BF16)
            pack[2 * g + kk, :, 128:256] = jnp.where(lanes(kr.shape) < 64, kr, kvp).astype(BF16)

        @pl.when(t < 3)
        def _():
            for kk in (0, 1):
                to = 2 * g + kk
                p.copy(
                    pack.at[to], unit.at[s], (to, b), first_unit + 2 * t + kk, first_unit + 2 * t + y
                ).start()

        @pl.when(t == 3)
        def _():
            p.copy(pack.at[p.flip], unit.at[s], (p.flip, b), first_unit + 6).start()

        return carry

    lax.fori_loop(0, 4, project, 0)
    own_unit = p.local(pack.at[s], unit.at[s])
    spread_d.land(0)
    spread_d.land_inner()

    for k in (1, 2, 3):
        slot = 2 * p.down(k) + y
        p.landed(z_wo[k - 1], wo.at[slot, b])
        y_wo.append(p.post(wo.at[slot, b], wo.at[slot, b], (p.flip, b)))
    dy_core = p.post(dy, dy_all.at[b], (s, p.core))
    dy_across = p.post(dy, dy_all.at[b], (s, p.across))
    p.landed(y_wo[0], wo.at[p.flip, b])
    for k in (1, 2, 3):
        p.landed(y_wo[k], wo.at[2 * p.down(k) + 1 - y, b])
    wo_core = p.post(wo.at[:, b], wo.at[:, b], (s, p.core))
    wo_across = p.post(wo.at[:, b], wo.at[:, b], (s, p.across))
    spread_d.land_end()
    spread_g.land(0)
    spread_u.land(0)
    spread_g.land_inner()
    spread_u.land_inner()

    for t in range(3):
        for other in (0, 1):
            src = 2 * lax.rem(z + 3 - t, 4) + other
            p.landed(first_unit + 2 * t + other, unit.at[src])
    p.landed(first_unit + 6, unit.at[p.flip])
    own_unit.wait()
    for t in range(3):
        for kk in (0, 1):
            p.copy(pack.at[s], unit.at[s], (p.flip, b), first_unit + 2 * t + kk).wait_send()
    p.copy(pack.at[s], unit.at[s], (p.flip, b), first_unit + 6).wait_send()

    def prepare(j, carry):
        live = j * 256 + rows_of((256, 128)) < length_all[z][0:1, :]
        masked = jnp.where(live, unit[j, :, 128:256].astype(F32), 0.0)
        kv[j] = masked.astype(BF16)
        vt[j, 0:64] = jnp.transpose(masked)[64:128].astype(BF16)
        alive = j * 256 + lanes((16, 256)) < length_all[z][0:1, 0:1]
        vt[j, 64:80] = jnp.where(alive, 1.0, 0.0).astype(BF16)
        return carry

    lax.fori_loop(0, 8, prepare, 0)
    p.landed(wo_across, wo.at[:, p.across])
    wo_far = p.post(wo.at[:, p.across], wo.at[:, p.across], (s, p.core))
    p.landed(dy_across, dy_all.at[p.across])
    dy_far = p.post(dy_all.at[p.across], dy_all.at[p.across], (s, p.core))
    first_mix, first_across, first_core = p.slots(8), p.slots(8), p.slots(8)

    def mix_send(src, t):
        p.copy(mix.at[b, src], mix.at[b, src], (s, p.across), first_across + t).start()
        p.copy(mix.at[b, src], mix.at[b, src], (s, p.core), first_core + t).start()

    def mix_arrived(t):
        src = lax.rem(s + 7 - t, 8)
        p.landed(first_mix + t, mix.at[b, src])
        mix_send(src, t)

    def attend(t, carry):
        i = lax.rem(s + 1 + t, 8)
        qt = jnp.transpose(unit[i, :, 0:128].astype(F32)).astype(BF16)
        both = jnp.concatenate([qt[0:64], qt[64:128]], axis=1)
        right = jnp.concatenate([both, jnp.zeros((64, 512), BF16)], axis=0)

        def block(j, acc):
            return acc + nn(vt[j], jnp.exp(nn(kv[j], right)).astype(BF16))

        acc = lax.fori_loop(0, i, block, jnp.zeros((80, 512), F32))
        causal = rows_of((256, 512)) <= lax.rem(lanes((256, 512)), 256)
        edge = jnp.where(causal, jnp.exp(nn(kv[i], right)), 0.0).astype(BF16)
        acc = acc + nn(vt[i], edge)
        total = acc[64:65]
        out = acc[0:64] / total
        out = jnp.concatenate([out[:, 0:256], out[:, 256:512]], axis=0)
        unit_out[i] = jnp.transpose(out).astype(BF16)
        lse[i] = jnp.broadcast_to(jnp.log(total), (8, 512))

        @pl.when(t < 7)
        def _():
            p.copy(unit_out.at[i], mix.at[b, s], (i, b), first_mix + t).start()

        @pl.when(t == 2)
        def _():
            spread_g.land_end()

        @pl.when(t == 4)
        def _():
            spread_u.land_end()

        @pl.when(t >= 4)
        def _():
            mix_arrived(t - 4)

        return carry

    lax.fori_loop(0, 8, attend, 0)
    own_mix = p.local(unit_out.at[s], mix.at[b, s])
    own_mix.wait()
    mix_send(s, 7)
    for t in range(4, 7):
        mix_arrived(t)
    for t in range(7):
        p.copy(unit_out.at[s], mix.at[b, s], (p.flip, b), first_mix + t).wait_send()
    p.landed(wo_core, wo.at[:, p.core])
    p.landed(wo_far, wo.at[:, p.far])
    p.landed(dy_core, dy_all.at[p.core])
    p.landed(dy_far, dy_all.at[p.far])
    for t in range(8):
        p.landed(first_across + t, mix.at[p.across, lax.rem(s + 7 - t, 8)])
    mix_far = p.post(mix.at[p.across], mix.at[p.across], (s, p.core))
    for t in range(8):
        p.landed(first_core + t, mix.at[p.core, lax.rem(s + 7 - t, 8)])
        p.copy(mix.at[b, s], mix.at[b, s], (s, p.across), first_across + t).wait_send()
        p.copy(mix.at[b, s], mix.at[b, s], (s, p.core), first_core + t).wait_send()
    p.landed(mix_far, mix.at[p.far])

    def project_out(g, carry):
        mixed = jnp.concatenate([mix[c, 2 * g + kk] for c in range(4) for kk in (0, 1)], axis=1)
        mid = xa[g].astype(F32) + nn(mixed, wo[...].reshape(1024, 1024))
        norm_two[g] = (mid * rms_factor(mid) * gain_f[...]).astype(BF16)

        @pl.when(g == b)
        def _():
            middle[...] = mid

        return carry

    lax.fori_loop(0, 4, project_out, 0)
    for spread in (spread_d, spread_g, spread_u):
        spread.finish()
        spread.drain()
    p.drain()


def chip_sum_post(p, t, parts, recv, first):
    @pl.when(t == 0)
    def _():
        p.copy(parts.at[p.far], recv.at[0], (p.s, p.core), first).start()

    @pl.when(t == 1)
    def _():
        p.copy(parts.at[p.core], recv.at[1], (p.s, p.core), first + 1).start()


def chip_sum_across(p, parts, recv, first):
    p.copy(recv.at[0], recv.at[0], (p.s, p.core), first).wait_recv()
    parts[p.across] = (parts[p.across].astype(F32) + recv[0].astype(F32)).astype(BF16)
    p.copy(parts.at[p.across], recv.at[2], (p.s, p.across), first + 2).start()


def chip_sum_rest(p, parts, recv, first):
    p.copy(recv.at[1], recv.at[1], (p.s, p.core), first + 1).wait_recv()
    p.copy(recv.at[2], recv.at[2], (p.s, p.core), first + 2).wait_recv()
    for k in range(3):
        p.copy(parts.at[p.b], recv.at[k], (p.s, p.core), first + k).wait_send()
    return recv[1].astype(F32) + recv[2].astype(F32)


def batch_order(p, t):
    return jnp.where(t == 0, p.far, jnp.where(t == 1, p.core, jnp.where(t == 2, p.across, p.b)))


def feed_kernel(
    norm_two, dy_all, wgu, wd, middle,
    output, dn2, ggu, gd, gd_other,
    hid, dgate, dup, parts_n, recv_n, parts_o, recv_o, keep_n, keep_o, send_sem, recv_sem, local_sem,
):
    p = Place(send_sem, recv_sem, local_sem)
    p.greet()
    first_n, first_o = p.slots(3), p.slots(3)

    def gated(t, carry):
        g = batch_order(p, t)
        rows = pl.ds(pl.multiple_of(g * 256, 256), 256)
        n2 = norm_two[g]
        gate = nn(n2, wgu[:, 0].reshape(1024, 1152))
        up = nn(n2, wgu[:, 1].reshape(1024, 1152))
        dh = nt(dy_all[g], wd[...].reshape(1152, 1024))
        sg = 1.0 / (1.0 + jnp.exp(-gate))
        swish = gate * sg
        hid[rows] = (swish * up).astype(BF16)
        dg = (dh * up * sg * (1.0 + gate * (1.0 - sg))).astype(BF16)
        du = (dh * swish).astype(BF16)
        dgate[rows] = dg
        dup[rows] = du
        part = nt(dg, wgu[:, 0].reshape(1024, 1152)) + nt(du, wgu[:, 1].reshape(1024, 1152))
        parts_n[g] = part.astype(BF16)

        @pl.when(t == 3)
        def _():
            keep_n[...] = part

        chip_sum_post(p, t, parts_n, recv_n, first_n)
        return carry

    lax.fori_loop(0, 4, gated, 0)
    chip_sum_across(p, parts_n, recv_n, first_n)

    def down_rows(c, carry):
        at = pl.multiple_of(128 * c, 128)
        gd[pl.ds(at, 128)] = tn(hid[:, pl.ds(at, 128)], dy_all[...].reshape(1024, 1024)).astype(BF16)
        return carry

    lax.fori_loop(0, 9, down_rows, 0)
    sent_d = []
    for i in range(4):
        rows = pl.ds(pl.multiple_of(144 * (2 * i + 1 - p.y), 16), 144)
        sent_d.append(p.post(gd.at[rows], gd_other.at[i], (p.flip, p.b)))

    def down(t, carry):
        g = batch_order(p, t)
        part = nn(hid[pl.ds(pl.multiple_of(g * 256, 256), 256)], wd[...].reshape(1152, 1024))
        parts_o[g] = part.astype(BF16)

        @pl.when(t == 3)
        def _():
            keep_o[...] = part

        chip_sum_post(p, t, parts_o, recv_o, first_o)
        return carry

    lax.fori_loop(0, 4, down, 0)
    chip_sum_across(p, parts_o, recv_o, first_o)

    def gate_rows(c, carry):
        at = pl.multiple_of(128 * c, 128)
        left = norm_two[:, :, pl.ds(at, 128)].reshape(1024, 128)
        ggu[c, 0] = tn(left, dgate[...]).astype(BF16)
        ggu[c, 1] = tn(left, dup[...]).astype(BF16)
        return carry

    lax.fori_loop(0, 8, gate_rows, 0)
    dn2[...] = keep_n[...] + chip_sum_rest(p, parts_n, recv_n, first_n)
    total = keep_o[...] + chip_sum_rest(p, parts_o, recv_o, first_o)
    output[...] = (middle[...] + total).astype(BF16)
    for i in range(4):
        p.landed(sent_d[i], gd_other.at[i])
    p.drain()


class SeqTree:
    def __init__(self, p, mine, y_recv, relayed, z_recv, sums=None):
        self.p, self.mine, self.y_recv, self.relayed, self.z_recv = p, mine, y_recv, relayed, z_recv
        self.sums = y_recv if sums is None else sums
        self.first = p.slots(6)
        self.started = False

    def start(self):
        p = self.p
        self.started = True
        p.copy(self.mine.at[:, 1 - p.y], self.y_recv, (p.flip, p.b), self.first + 4).start()

    def send(self, i, dst, z, out, into):
        p = self.p
        p.copy(self.sums.at[i], dst, (2 * z + p.y, p.b), self.first + out, self.first + into).start()

    def reduce(self):
        p = self.p
        if self.started:
            p.landed(self.first + 4, self.y_recv)

        def add(i):
            self.sums[i] = (self.y_recv[i].astype(F32) + self.mine[i, p.y].astype(F32)).astype(BF16)

        add(p.there)
        add(p.beyond)

        @pl.when(jnp.logical_not(p.inner))
        def _():
            self.send(p.there, self.relayed.at[0], p.pair, 1, 1)
            self.send(p.beyond, self.relayed.at[1], p.pair, 2, 2)

        add(p.pair)
        self.send(p.pair, self.z_recv.at[0], p.pair, 0, 0)

    def relay(self):
        p = self.p

        @pl.when(p.inner)
        def _():
            for k, i in ((0, p.there), (1, p.beyond)):
                p.landed(self.first + 1 + k, self.relayed.at[k])
                self.sums[i] = (self.sums[i].astype(F32) + self.relayed[k].astype(F32)).astype(BF16)
                self.send(i, self.z_recv.at[1], i, 1 + k, 3)

    def finish(self):
        p = self.p
        total = self.y_recv[p.z].astype(F32) + self.mine[p.z, p.y].astype(F32)
        p.landed(self.first, self.z_recv.at[0])
        total = total + self.z_recv[0].astype(F32)
        p.landed(self.first + 3, self.z_recv.at[1])
        for out in range(3):
            p.copy(self.z_recv.at[0], self.z_recv.at[0], (p.flip, p.b), self.first + out).wait_send()
        if self.started:
            p.copy(self.y_recv, self.y_recv, (p.flip, p.b), self.first + 4).wait_send()
        return total + self.z_recv[1].astype(F32)


class SeqSum:
    def __init__(self, p, y_recv, z_recv):
        self.p, self.y_recv, self.z_recv = p, y_recv, z_recv

    def start(self, source, mine=None):
        p = self.p
        self.index = p.post(source.at[:, 1 - p.y], self.y_recv, (p.flip, p.b))
        self.load = None
        if mine is None:
            self.mine = lambda i: source.at[i, p.y]
        else:
            self.load = p.local(source.at[:, p.y], mine)
            self.mine = lambda i: mine.at[i]

    def middle(self):
        p = self.p
        if self.load is not None:
            self.load.wait()
        p.landed(self.index, self.y_recv)
        self.far = []
        for k in (1, 2, 3):
            i = p.up(k)
            self.y_recv[i] = (self.y_recv[i].astype(F32) + self.mine(i)[...].astype(F32)).astype(BF16)
            self.far.append(p.post(self.y_recv.at[i], self.z_recv.at[k - 1], (2 * i + p.y, p.b)))

    def finish(self):
        p = self.p
        total = self.y_recv[p.z].astype(F32) + self.mine(p.z)[...].astype(F32)
        for k in (1, 2, 3):
            p.landed(self.far[k - 1], self.z_recv.at[k - 1])
            total = total + self.z_recv[k - 1].astype(F32)
        return total


def backward_kernel(
    dn2, middle, x, dy, wo, mix, unit, unit_out, lse, length_all, pre, norm, wqkv,
    cos, sin, gain_q, gain_k, gain_a, gain_f, ggu, gd, y_d,
    dx, rqkv, rgu, rd, ro, gains_out,
    dmid, dox, doq, dou, dbr, kv, kt, q_right, do_right, q_left, do_left, delta, dk2, dv2, back, dqr,
    dpre, parts, recv, keep, gqkv, go, mixt,
    s_d, t_d, z_d, y_g, t_g, z_g, y_u, t_u, z_u, y_q, z_q, y_o, z_o, fin_g, fin_u, fin_q,
    gain_sum, gain_batch, gain_seq,
    send_sem, recv_sem, local_sem,
):
    p = Place(send_sem, recv_sem, local_sem)
    s, b, z, y = p.s, p.b, p.z, p.y
    p.greet()
    sum_d = SeqTree(p, gd, y_d, t_d, z_d, s_d)
    sum_g = SeqTree(p, ggu.at[:, :, 0], y_g, t_g, z_g)
    sum_u = SeqTree(p, ggu.at[:, :, 1], y_u, t_u, z_u)
    sum_g.start()
    sum_d.reduce()

    mid = middle[...]
    r2 = rms_factor(mid)
    grad_two = dn2[...]
    gain_sum[...] = jnp.zeros((8, 1024), F32)
    gain_sum[1:2] = jnp.sum(grad_two * mid * r2, axis=0, keepdims=True)
    dm = dy[...].astype(F32) + norm_back(grad_two * gain_f[...], mid, r2)
    dmid[...] = dm
    dbr[b] = dm.astype(BF16)
    for c in range(4):
        for kk in (0, 1):
            h = 2 * c + kk
            dox[c, kk] = nt(dbr[b], wo[h].reshape(128, 1024)).astype(BF16)
    got_do = []
    for k in (1, 2, 3):
        to = lax.rem(b + k, 4)
        got_do.append(p.post(dox.at[to], doq.at[pl.ds(2 * b, 2)], (s, to)))
    doq[pl.ds(2 * b, 2)] = dox[b]
    dbr_across = p.post(dbr.at[b], dbr.at[b], (s, p.across))
    dbr_core = p.post(dbr.at[b], dbr.at[b], (s, p.core))
    for k in (1, 2, 3):
        p.landed(got_do[k - 1], doq.at[pl.ds(2 * lax.rem(b + 4 - k, 4), 2)])
    got_unit = []
    for k in range(1, 8):
        to = lax.rem(s + k, 8)
        got_unit.append(p.post(doq.at[to], dou.at[s], (to, b)))
    dou[s] = doq[s]

    def prepare(i, carry):
        live = i * 256 + rows_of((256, 128)) < length_all[z][0:1, :]
        masked = jnp.where(live, unit[i, :, 128:256].astype(F32), 0.0)
        kv[i] = masked.astype(BF16)
        kt[i] = jnp.transpose(masked)[0:64].astype(BF16)
        q = unit[i, :, 0:128].astype(F32)
        qt = jnp.transpose(q).astype(BF16)
        q_right[i, 0:64] = jnp.concatenate([qt[0:64], qt[64:128]], axis=1)
        q_right[i, 64:128] = jnp.zeros((64, 512), BF16)
        first = lanes(q.shape) < 64
        q_left[i, 0:256] = jnp.where(first, q, 0.0).astype(BF16)
        q_left[i, 256:512] = jnp.where(first, 0.0, q).astype(BF16)
        dk2[i] = jnp.zeros((256, 128), F32)
        dv2[i] = jnp.zeros((256, 128), F32)
        return carry

    lax.fori_loop(0, 8, prepare, 0)
    sum_d.relay()
    p.landed(dbr_across, dbr.at[p.across])
    dbr_far = p.post(dbr.at[p.across], dbr.at[p.across], (s, p.core))
    for k in range(1, 8):
        p.landed(got_unit[k - 1], dou.at[lax.rem(s + 8 - k, 8)])

    def prepare_grad(i, carry):
        do = dou[i].astype(F32)
        dot = jnp.transpose(do)
        do_right[i, 0:64] = jnp.zeros((64, 512), BF16)
        do_right[i, 64:128] = jnp.concatenate([dot[0:64], dot[64:128]], axis=1).astype(BF16)
        first = lanes(do.shape) < 64
        do_left[i, 0:256] = jnp.where(first, do, 0.0).astype(BF16)
        do_left[i, 256:512] = jnp.where(first, 0.0, do).astype(BF16)
        both = dot * jnp.transpose(unit_out[i].astype(F32))
        low = jnp.sum(both[0:64], axis=0, keepdims=True)
        high = jnp.sum(both[64:128], axis=0, keepdims=True)
        delta[i] = jnp.broadcast_to(jnp.concatenate([low, high], axis=1), (8, 512))
        return carry

    lax.fori_loop(0, 8, prepare_grad, 0)

    def queries(t, carry):
        i = 7 - t
        qr, dr, ql, dl = q_right[i], do_right[i], q_left[i], do_left[i]
        log_total = lse[i][0:1]
        shift = delta[i][0:1]

        def block(j, probs):
            ds = (probs * (nn(kv[j], dr) - shift)).astype(BF16)
            dv2[j] += nn(probs.astype(BF16), dl)
            dk2[j] += nn(ds, ql)
            return nn(kt[j], ds)

        def step(j, acc):
            return acc + block(j, jnp.exp(nn(kv[j], qr) - log_total))

        acc = lax.fori_loop(0, i, step, jnp.zeros((64, 512), F32))
        causal = rows_of((256, 512)) <= lax.rem(lanes((256, 512)), 256)
        acc = acc + block(i, jnp.where(causal, jnp.exp(nn(kv[i], qr) - log_total), 0.0))
        dq = jnp.concatenate([acc[:, 0:256], acc[:, 256:512]], axis=0) * 0.125
        back[i, :, 0:128] = jnp.transpose(dq).astype(BF16)
        live = i * 256 + rows_of((256, 128)) < length_all[z][0:1, :]
        dk, dv = dk2[i], dv2[i]
        dk = dk + pltpu.roll(dk, 64, 1)
        dv = dv + pltpu.roll(dv, 64, 1)
        dkv = jnp.where(lanes((256, 128)) < 64, dk, dv)
        back[i, :, 128:256] = jnp.where(live, dkv, 0.0).astype(BF16)
        return carry

    lax.fori_loop(0, 1, queries, 0)
    sum_g.reduce()
    sum_u.start()
    lax.fori_loop(1, 4, queries, 0)
    sum_g.relay()
    lax.fori_loop(4, 8, queries, 0)
    got_back = []
    for k in range(1, 8):
        to = lax.rem(s + k, 8)
        got_back.append(p.post(back.at[to], dqr.at[s], (to, b)))
    dqr[s] = back[s]

    p.landed(dbr_core, dbr.at[p.core])
    p.landed(dbr_far, dbr.at[p.far])

    def turn(e, carry):
        for g in range(4):
            mixt[:, 256 * g : 256 * g + 256] = jnp.transpose(
                mix[e // 2, 2 * g + lax.rem(e, 2)].astype(F32)
            ).astype(BF16)
        left = mixt[pl.ds(pl.multiple_of(32 * b, 32), 32)]
        go[e // 2, lax.rem(e, 2)] = nn(left, dbr[...].reshape(1024, 1024)).astype(BF16)
        return carry

    lax.fori_loop(0, 8, turn, 0)
    sum_o = SeqSum(p, y_o, z_o)
    sum_o.start(go)
    sum_u.reduce()
    for k in range(1, 8):
        p.landed(got_back[k - 1], dqr.at[lax.rem(s + 8 - k, 8)])

    first_n = p.slots(3)
    zero_row = jnp.zeros((1, 128), F32)

    def heads(t, carry):
        sum_q, sum_k = carry
        g = batch_order(p, t)
        for kk in (0, 1):
            at = 256 * kk
            q, k = pre[g, :, at : at + 128], pre[g, :, at + 128 : at + 256]
            rq = lax.rsqrt(head_mean(q * q) + eps)
            rk = lax.rsqrt(head_mean(k * k) + eps)
            dq = rope_back(dqr[2 * g + kk, :, 0:128].astype(F32), cos[...], sin[...])
            dkv = dqr[2 * g + kk, :, 128:256].astype(F32)
            dk = rope_back(dkv, cos[...], sin[...])
            sum_q = sum_q + jnp.sum(dq * q * rq, axis=0, keepdims=True)
            sum_k = sum_k + jnp.sum(dk * k * rk, axis=0, keepdims=True)
            dq = dq * gain_q[...]
            dk = dk * gain_k[...]
            dq = rq * (dq - q * rq * rq * head_mean(dq * q))
            dk = rk * (dk - k * rk * rk * head_mean(dk * k))
            dpre[g, :, at : at + 128] = dq.astype(BF16)
            dpre[g, :, at + 128 : at + 256] = jnp.where(lanes(dk.shape) < 64, dk, dkv).astype(BF16)
        part = nt(dpre[g], wqkv[...].reshape(1024, 512))
        parts[g] = part.astype(BF16)

        @pl.when(t == 3)
        def _():
            keep[...] = part

        chip_sum_post(p, t, parts, recv, first_n)
        return (sum_q, sum_k)

    sum_q, sum_k = lax.fori_loop(0, 4, heads, (zero_row, zero_row))
    gain_sum[2:3, 0:128] = sum_q
    gain_sum[3:4, 0:128] = sum_k
    chip_sum_across(p, parts, recv, first_n)

    def qkv_rows(c, carry):
        at = pl.multiple_of(128 * c, 128)
        left = norm[:, :, pl.ds(at, 128)].reshape(1024, 128)
        gqkv[c // 2, lax.rem(c, 2)] = tn(left, dpre[...].reshape(1024, 512)).astype(BF16)
        return carry

    lax.fori_loop(0, 8, qkv_rows, 0)
    sum_qkv = SeqSum(p, y_q, z_q)
    sum_qkv.start(gqkv)
    sum_u.relay()
    sum_o.middle()

    dn1 = keep[...] + chip_sum_rest(p, parts, recv, first_n)
    xf = x[...].astype(F32)
    r1 = rms_factor(xf)
    gain_sum[0:1] = jnp.sum(dn1 * xf * r1, axis=0, keepdims=True)
    dx[...] = (dmid[...] + norm_back(dn1 * gain_a[...], xf, r1)).astype(BF16)
    got_gain = [p.post(gain_sum, gain_batch.at[b], (s, lax.rem(b + k, 4))) for k in (1, 2, 3)]
    gain_batch[b] = gain_sum[...]
    sum_qkv.middle()

    rd[...] = sum_d.finish()

    def exchange(total, fin, dst):
        fin[...] = total.astype(BF16)
        got = []
        for k in (1, 2, 3):
            to = lax.rem(b + k, 4)
            rows = pl.ds(pl.multiple_of(32 * to, 32), 32)
            got.append(p.post(fin.at[rows], dst(b), (s, to)))
        dst(b)[...] = fin[pl.ds(pl.multiple_of(32 * b, 32), 32)]
        return got

    def arrive(got, dst):
        for k in (1, 2, 3):
            p.landed(got[k - 1], dst(lax.rem(b + 4 - k, 4)))

    dst_g, dst_u, dst_q = (lambda i: rgu.at[i, 0]), (lambda i: rgu.at[i, 1]), (lambda i: rqkv.at[i])
    got_g = exchange(sum_g.finish(), fin_g, dst_g)
    for k in (1, 2, 3):
        p.landed(got_gain[k - 1], gain_batch.at[lax.rem(b + 4 - k, 4)])
    gain_seq[s] = (gain_batch[0] + gain_batch[1]) + (gain_batch[2] + gain_batch[3])
    got_all = [p.post(gain_seq.at[s], gain_seq.at[s], (lax.rem(s + k, 8), b)) for k in range(1, 8)]
    got_u = exchange(sum_u.finish(), fin_u, dst_u)
    ro[...] = sum_o.finish()
    got_q = exchange(sum_qkv.finish(), fin_q, dst_q)
    for k in range(1, 8):
        p.landed(got_all[k - 1], gain_seq.at[lax.rem(s + 8 - k, 8)])
    total = gain_seq[0]
    for k in range(1, 8):
        total = total + gain_seq[k]
    gains_out[...] = total
    arrive(got_g, dst_g)
    arrive(got_u, dst_u)
    arrive(got_q, dst_q)
    p.drain()


def call(kernel, outs, in_specs, out_specs, scratch, cid, sems=(64, 16)):
    return pl.pallas_call(
        kernel,
        out_shape=[jax.ShapeDtypeStruct(shape, dtype) for shape, dtype in outs],
        in_specs=in_specs,
        out_specs=out_specs,
        scratch_shapes=[pltpu.VMEM(shape, dtype) for shape, dtype in scratch]
        + [
            pltpu.SemaphoreType.DMA((sems[0],)),
            pltpu.SemaphoreType.DMA((sems[0],)),
            pltpu.SemaphoreType.DMA((sems[1],)),
        ],
        compiler_params=pltpu.CompilerParams(
            collective_id=cid, has_side_effects=True, vmem_limit_bytes=60 * 2**20
        ),
    )


def body(
    inputs, lengths, w_query, key_weight, value_weight, w_out, w_gate, w_up, w_down,
    gain_attn, gain_ffn, gain_query, gain_key, cotangent,
):
    x = inputs.reshape(256, 1024)
    dy = cotangent.reshape(256, 1024)
    positions = lax.axis_index("seq") * 256 + jnp.arange(256, dtype=jnp.int32)
    freqs = theta ** (-(jnp.arange(32, dtype=F32) * 2.0) / 64)
    angles = positions.astype(F32)[:, None] * freqs[None, :]
    cosine = jnp.tile(jnp.cos(angles), (1, 4))
    sine = jnp.tile(jnp.sin(angles), (1, 4))
    length = jnp.broadcast_to(lengths[:, None], (8, 128))
    wqkv_in = jnp.concatenate(
        [
            w_query.reshape(32, 4, 2, 128),
            key_weight.reshape(32, 4, 2, 64),
            value_weight.reshape(32, 4, 2, 64),
        ],
        axis=-1,
    )
    wqkv_in = jnp.transpose(wqkv_in.reshape(32, 4, 512), (1, 0, 2))
    wgu_in = jnp.stack([w_gate, w_up]).reshape(2, 32, 8, 4, 144)
    wgu_in = jnp.transpose(wgu_in, (3, 0, 1, 2, 4)).reshape(4, 2, 32, 1152)
    gain_q = jnp.tile(gain_query, 2)[None]
    gain_k = jnp.tile(gain_key, 2)[None]
    gain_a = gain_attn[None]
    gain_f = gain_ffn[None]

    (wgu, wd, wo, wqkv, norm, pre, unit, unit_out, lse, mix, norm_two, middle, dy_all, length_all) = call(
        forward_kernel,
        [
            ((8, 2, 128, 1152), BF16), ((8, 144, 1024), BF16), ((8, 4, 32, 1024), BF16),
            ((8, 128, 512), BF16), ((4, 256, 1024), BF16), ((4, 256, 512), F32),
            ((8, 256, 256), BF16), ((8, 256, 128), BF16), ((8, 8, 512), F32),
            ((4, 8, 256, 128), BF16), ((4, 256, 1024), BF16), ((256, 1024), F32),
            ((4, 256, 1024), BF16), ((4, 8, 128), jnp.int32),
        ],
        [VMEM, ANY, VMEM, VMEM, ANY, ANY, VMEM] + [VMEM] * 6,
        [ANY, ANY] + [VMEM] * 10 + [ANY, VMEM],
        [
            ((4, 256, 1024), BF16), ((8, 256, 256), BF16), ((8, 256, 128), BF16), ((8, 80, 256), BF16),
        ],
        0,
        sems=(128, 16),
    )(x, dy, length, wqkv_in, wgu_in, w_down, w_out, cosine, sine, gain_q, gain_k, gain_a, gain_f)

    output, dn2, ggu, gd, gd_other = call(
        feed_kernel,
        [
            ((256, 1024), BF16), ((256, 1024), F32), ((8, 2, 128, 1152), BF16), ((1152, 1024), BF16),
            ((4, 144, 1024), BF16),
        ],
        [VMEM] * 5,
        [VMEM] * 5,
        [
            ((1024, 1152), BF16), ((1024, 1152), BF16), ((1024, 1152), BF16),
            ((4, 256, 1024), BF16), ((3, 256, 1024), BF16), ((4, 256, 1024), BF16),
            ((3, 256, 1024), BF16), ((256, 1024), F32), ((256, 1024), F32),
        ],
        1,
    )(norm_two, dy_all, wgu, wd, middle)

    dx, rqkv, rgu, rd, ro, gains = call(
        backward_kernel,
        [
            ((256, 1024), BF16), ((4, 32, 512), BF16), ((4, 2, 32, 1152), BF16),
            ((144, 1024), F32), ((32, 1024), F32), ((8, 1024), F32),
        ],
        [VMEM] * 22,
        [VMEM] * 6,
        [
            ((256, 1024), F32), ((4, 2, 256, 128), BF16), ((8, 256, 128), BF16), ((8, 256, 128), BF16),
            ((4, 256, 1024), BF16), ((8, 256, 128), BF16), ((8, 64, 256), BF16), ((8, 128, 512), BF16),
            ((8, 128, 512), BF16), ((8, 512, 128), BF16), ((8, 512, 128), BF16), ((8, 8, 512), F32),
            ((8, 256, 128), F32), ((8, 256, 128), F32), ((8, 256, 256), BF16), ((8, 256, 256), BF16),
            ((4, 256, 512), BF16), ((4, 256, 1024), BF16), ((3, 256, 1024), BF16), ((256, 1024), F32),
            ((4, 2, 128, 512), BF16), ((4, 2, 32, 1024), BF16), ((128, 1024), BF16),
            ((4, 144, 1024), BF16), ((2, 144, 1024), BF16), ((2, 144, 1024), BF16),
            ((4, 128, 1152), BF16), ((2, 128, 1152), BF16), ((2, 128, 1152), BF16),
            ((4, 128, 1152), BF16), ((2, 128, 1152), BF16), ((2, 128, 1152), BF16),
            ((4, 128, 512), BF16), ((3, 128, 512), BF16), ((4, 32, 1024), BF16), ((3, 32, 1024), BF16),
            ((128, 1152), BF16), ((128, 1152), BF16), ((128, 512), BF16),
            ((8, 1024), F32), ((4, 8, 1024), F32), ((8, 8, 1024), F32),
        ],
        2,
        sems=(96, 16),
    )(
        dn2, middle, x, dy, wo, mix, unit, unit_out, lse, length_all, pre, norm, wqkv,
        cosine, sine, gain_q, gain_k, gain_a, gain_f,
        ggu.reshape(4, 2, 2, 128, 1152), gd.reshape(4, 2, 144, 1024), gd_other,
    )

    rows = jnp.transpose(rqkv, (1, 0, 2)).reshape(32, 8, 256).astype(F32)
    grad_query = rows[:, :, 0:128].reshape(32, 1024)
    grad_key = rows[:, :, 128:192].reshape(32, 512)
    grad_value = rows[:, :, 192:256].reshape(32, 512)
    wide = jnp.transpose(rgu.reshape(4, 2, 32, 8, 144), (1, 2, 3, 0, 4)).reshape(2, 32, 4608).astype(F32)
    return (
        output.reshape(256, 1, 1024),
        dx.reshape(256, 1, 1024),
        grad_query,
        grad_key,
        grad_value,
        ro,
        wide[0],
        wide[1],
        rd,
        gains[0],
        gains[1],
        gains[2, 0:64] + gains[2, 64:128],
        gains[3, 0:64],
    )


def rotary_tables(positions, width):
    half = width // 2
    freqs = theta ** (-(jnp.arange(half, dtype=jnp.float32) * 2.0) / width)
    angles = positions.astype(jnp.float32)[:, None] * freqs[None, :]
    cosine = jnp.concatenate([jnp.cos(angles), jnp.cos(angles)], axis=-1)
    sine = jnp.concatenate([jnp.sin(angles), jnp.sin(angles)], axis=-1)
    return (cosine, sine)


def rotate(v, cosine, sine):
    half = v.shape[-1] // 2
    turned = jnp.concatenate([-v[..., half:], v[..., :half]], axis=-1)
    return v * cosine + turned * sine


def rotate_back(grad, cosine, sine):
    half = grad.shape[-1] // 2
    moved = grad * sine
    return grad * cosine + jnp.concatenate([moved[..., half:], -moved[..., :half]], axis=-1)


def product(left, right):
    return jnp.dot(left, right, preferred_element_type=jnp.float32)


def left_product(left, right):
    return jnp.einsum("rd,rn->dn", left, right, preferred_element_type=jnp.float32)


def right_product(left, right):
    return jnp.einsum("rn,dn->rd", left, right, preferred_element_type=jnp.float32)


def rounded(v):
    return v.astype(jnp.bfloat16)


def split_rows(term, seq_size, batch_size):
    return term.reshape(
        seq_size, batch_size, term.shape[0] // (seq_size * batch_size), term.shape[1]
    )


def fold_sources(piece):
    return jnp.sum(piece, axis=1).reshape(-1, piece.shape[-1])


def general_body(
    inputs,
    lengths,
    w_query,
    key_weight,
    value_weight,
    w_out,
    w_gate,
    w_up,
    w_down,
    gain_attn,
    gain_ffn,
    gain_query,
    gain_key,
    cotangent,
):
    slice_len, seq_count, width = inputs.shape
    rows = slice_len * seq_count
    head_dim = gain_query.shape[0]
    kv_width = key_weight.shape[1]
    kv_heads = kv_width // head_dim
    q_heads = w_query.shape[1] // head_dim
    sequence_group = q_heads // kv_heads
    scale = head_dim ** (-0.5)
    cycle_size = lax.axis_size("seq")
    batch_size = lax.axis_size("batch")
    positions = lax.axis_index("seq") * slice_len + jnp.arange(slice_len, dtype=jnp.int32)
    cosine, sine = rotary_tables(positions, head_dim)
    cosine = cosine[:, None, None, :]
    sine = sine[:, None, None, :]
    shards = (w_query, key_weight, value_weight, w_out, w_gate, w_up, w_down)
    wq, key_matrix, value_matrix, wo, wg, wu, wd = (
        lax.all_gather(shards[0], ("seq", "batch"), axis=0, tiled=True),
        lax.all_gather(shards[1], ("seq", "batch"), axis=0, tiled=True),
        lax.all_gather(shards[2], ("seq", "batch"), axis=0, tiled=True),
        lax.all_gather(shards[3], ("seq", "batch"), axis=0, tiled=True),
        lax.all_gather(shards[4], ("seq", "batch"), axis=0, tiled=True),
        lax.all_gather(shards[5], ("seq", "batch"), axis=0, tiled=True),
        lax.all_gather(shards[6], ("seq", "batch"), axis=0, tiled=True),
    )
    stream = inputs.reshape(rows, width).astype(jnp.float32)
    factor_one = rms_factor(stream)
    normalized_input = rounded(stream * factor_one * gain_attn)
    query_pre = product(normalized_input, wq).reshape(slice_len, seq_count, q_heads, head_dim)
    key_before_rotation = product(normalized_input, key_matrix).reshape(
        slice_len, seq_count, kv_heads, head_dim
    )
    value_b = rounded(product(normalized_input, value_matrix)).reshape(
        slice_len, seq_count, kv_width
    )
    factor_q = rms_factor(query_pre)
    factor_k = rms_factor(key_before_rotation)
    query_b = rounded(rotate(query_pre * factor_q * gain_query, cosine, sine))
    key_b = rounded(rotate(key_before_rotation * factor_k * gain_key, cosine, sine)).reshape(
        slice_len, seq_count, kv_width
    )
    query_five = query_b.reshape(slice_len, seq_count, kv_heads, sequence_group, head_dim)

    def scores_of(keys, start):
        count = keys.shape[0]
        raw = (
            jnp.einsum(
                "tsgrd,csgd->sgrtc",
                query_five,
                keys.reshape(count, seq_count, kv_heads, head_dim),
                preferred_element_type=jnp.float32,
            )
            * scale
        )
        key_pos = start + jnp.arange(count, dtype=jnp.int32)
        causal = key_pos[None, :] <= positions[:, None]
        inside = key_pos[None, :] < lengths[:, None]
        valid = causal[None, :, :] & inside[:, None, :]
        return (raw, valid[:, None, None, :, :])

    state_shape = (seq_count, kv_heads, sequence_group, slice_len)
    shard_ids = jnp.arange(cycle_size, dtype=jnp.int32)
    top = jnp.full(state_shape, -1e30, jnp.float32)
    keys = lax.all_gather(key_b, "seq", axis=0, tiled=True)
    value_rows = lax.all_gather(value_b, "seq", axis=0, tiled=True)
    count = keys.shape[0]
    raw, valid = scores_of(keys, jnp.int32(0))
    masked = jnp.where(valid, raw, -jnp.inf)
    new_top = jnp.maximum(top, jnp.max(masked, axis=-1))
    probs = jnp.exp(masked - new_top[..., None])
    total = jnp.sum(probs, axis=-1)
    acc = jnp.einsum(
        "sgrtc,csgd->sgrtd",
        rounded(probs),
        value_rows.reshape(count, seq_count, kv_heads, head_dim),
        preferred_element_type=jnp.float32,
    )
    state = (new_top, total, acc)
    top, total, acc = state
    attn_out = acc / total[..., None]
    log_total = top + jnp.log(total)
    mixed_b = rounded(jnp.transpose(attn_out, (3, 0, 1, 2, 4)).reshape(rows, q_heads * head_dim))
    middle = stream + product(mixed_b, wo)
    factor_two = rms_factor(middle)
    normed_two = rounded(middle * factor_two * gain_ffn)
    gate = product(normed_two, wg)
    up_part = product(normed_two, wu)
    sigma = jax.nn.sigmoid(gate)
    swish = gate * sigma
    hidden_b = rounded(swish * up_part)
    result = middle + product(hidden_b, wd)
    output = rounded(result).reshape(slice_len, seq_count, width)
    wq, key_matrix, value_matrix, wo, wg, wu, wd = (
        lax.all_gather(shards[0], ("seq", "batch"), axis=0, tiled=True),
        lax.all_gather(shards[1], ("seq", "batch"), axis=0, tiled=True),
        lax.all_gather(shards[2], ("seq", "batch"), axis=0, tiled=True),
        lax.all_gather(shards[3], ("seq", "batch"), axis=0, tiled=True),
        lax.all_gather(shards[4], ("seq", "batch"), axis=0, tiled=True),
        lax.all_gather(shards[5], ("seq", "batch"), axis=0, tiled=True),
        lax.all_gather(shards[6], ("seq", "batch"), axis=0, tiled=True),
    )
    grad_res = cotangent.reshape(rows, width).astype(jnp.float32)
    grad_ffo = rounded(grad_res)
    grad_wd = left_product(hidden_b, grad_ffo)
    grad_hidden = right_product(grad_ffo, wd)
    grad_gate = rounded(grad_hidden * up_part * sigma * (1.0 + gate * (1.0 - sigma)))
    grad_up = rounded(grad_hidden * swish)
    grad_wg = left_product(normed_two, grad_gate)
    grad_wu = left_product(normed_two, grad_up)
    grad_normed_two = right_product(grad_gate, wg) + right_product(grad_up, wu)
    grad_gain_ffn = jnp.sum(grad_normed_two * middle * factor_two, axis=0)
    grad_middle = grad_res + norm_back(grad_normed_two * gain_ffn, middle, factor_two)
    grad_branch = rounded(grad_middle)
    grad_wo = left_product(mixed_b, grad_branch)
    grad_mixed = rounded(right_product(grad_branch, wo))
    grad_five = grad_mixed.reshape(slice_len, seq_count, kv_heads, sequence_group, head_dim)
    delta = jnp.sum(
        jnp.transpose(grad_five, (1, 2, 3, 0, 4)).astype(jnp.float32) * attn_out, axis=-1
    )
    gathered = (
        lax.all_gather(key_b, "seq", axis=0, tiled=True),
        lax.all_gather(value_b, "seq", axis=0, tiled=True),
    )

    def back_step(grad_query, item):
        index, keys, value_rows = item
        raw, valid = scores_of(keys, index * slice_len)
        probs = jnp.where(valid, jnp.exp(raw - log_total[..., None]), 0.0)
        key_four = keys.reshape(slice_len, seq_count, kv_heads, head_dim)
        value_four = value_rows.reshape(slice_len, seq_count, kv_heads, head_dim)
        grad_probs = jnp.einsum(
            "tsgrd,csgd->sgrtc", grad_five, value_four, preferred_element_type=jnp.float32
        )
        grad_score = rounded(probs * (grad_probs - delta[..., None]))
        grad_query = (
            grad_query
            + jnp.einsum(
                "sgrtc,csgd->tsgrd", grad_score, key_four, preferred_element_type=jnp.float32
            )
            * scale
        )
        key_term = (
            jnp.einsum(
                "sgrtc,tsgrd->csgd", grad_score, query_five, preferred_element_type=jnp.float32
            )
            * scale
        )
        value_term = jnp.einsum(
            "sgrtc,tsgrd->csgd", rounded(probs), grad_five, preferred_element_type=jnp.float32
        )
        return (
            grad_query,
            (
                key_term.reshape(slice_len, seq_count, kv_width),
                value_term.reshape(slice_len, seq_count, kv_width),
            ),
        )

    items = (
        shard_ids,
        gathered[0].reshape(cycle_size, slice_len, seq_count, kv_width),
        gathered[1].reshape(cycle_size, slice_len, seq_count, kv_width),
    )
    grad_query, terms = lax.scan(
        back_step,
        jnp.zeros((slice_len, seq_count, kv_heads, sequence_group, head_dim), jnp.float32),
        items,
    )
    key_terms = terms[0].reshape(cycle_size * slice_len, seq_count, kv_width)
    value_terms = terms[1].reshape(cycle_size * slice_len, seq_count, kv_width)
    grad_key, grad_value = (
        lax.psum_scatter(
            key_terms.astype(jnp.bfloat16), "seq", scatter_dimension=0, tiled=True
        ).astype(jnp.float32),
        lax.psum_scatter(
            value_terms.astype(jnp.bfloat16), "seq", scatter_dimension=0, tiled=True
        ).astype(jnp.float32),
    )
    grad_qr = (
        rounded(grad_query).astype(jnp.float32).reshape(slice_len, seq_count, q_heads, head_dim)
    )
    grad_qn = rotate_back(grad_qr, cosine, sine)
    grad_gain_query = jnp.sum(grad_qn * query_pre * factor_q, axis=(0, 1, 2))
    grad_qp = rounded(
        norm_back(grad_qn * gain_query, query_pre, factor_q).reshape(rows, q_heads * head_dim)
    )
    grad_kr = (
        rounded(grad_key).astype(jnp.float32).reshape(slice_len, seq_count, kv_heads, head_dim)
    )
    grad_kn = rotate_back(grad_kr, cosine, sine)
    grad_gain_key = jnp.sum(grad_kn * key_before_rotation * factor_k, axis=(0, 1, 2))
    grad_kp = rounded(
        norm_back(grad_kn * gain_key, key_before_rotation, factor_k).reshape(rows, kv_width)
    )
    grad_vp = rounded(grad_value).reshape(rows, kv_width)
    grad_wq = left_product(normalized_input, grad_qp)
    grad_wk = left_product(normalized_input, grad_kp)
    grad_wv = left_product(normalized_input, grad_vp)
    grad_normed = (
        right_product(grad_qp, wq)
        + right_product(grad_kp, key_matrix)
        + right_product(grad_vp, value_matrix)
    )
    grad_gain_attn = jnp.sum(grad_normed * stream * factor_one, axis=0)
    grad_stream = grad_middle + norm_back(grad_normed * gain_attn, stream, factor_one)
    spread = (
        lax.all_to_all(
            split_rows(grad_wq, cycle_size, batch_size).astype(jnp.bfloat16),
            "batch",
            split_axis=1,
            concat_axis=1,
            tiled=True,
        ).astype(jnp.float32),
        lax.all_to_all(
            split_rows(grad_wk, cycle_size, batch_size).astype(jnp.bfloat16),
            "batch",
            split_axis=1,
            concat_axis=1,
            tiled=True,
        ).astype(jnp.float32),
        lax.all_to_all(
            split_rows(grad_wv, cycle_size, batch_size).astype(jnp.bfloat16),
            "batch",
            split_axis=1,
            concat_axis=1,
            tiled=True,
        ).astype(jnp.float32),
        lax.all_to_all(
            split_rows(grad_wo, cycle_size, batch_size).astype(jnp.bfloat16),
            "batch",
            split_axis=1,
            concat_axis=1,
            tiled=True,
        ).astype(jnp.float32),
        lax.all_to_all(
            split_rows(grad_wg, cycle_size, batch_size).astype(jnp.bfloat16),
            "batch",
            split_axis=1,
            concat_axis=1,
            tiled=True,
        ).astype(jnp.float32),
        lax.all_to_all(
            split_rows(grad_wu, cycle_size, batch_size).astype(jnp.bfloat16),
            "batch",
            split_axis=1,
            concat_axis=1,
            tiled=True,
        ).astype(jnp.float32),
        lax.all_to_all(
            split_rows(grad_wd, cycle_size, batch_size).astype(jnp.bfloat16),
            "batch",
            split_axis=1,
            concat_axis=1,
            tiled=True,
        ).astype(jnp.float32),
    )
    partial_sums = [fold_sources(piece) for piece in spread]
    summed = (
        lax.psum_scatter(
            partial_sums[0].astype(jnp.bfloat16), "seq", scatter_dimension=0, tiled=True
        ).astype(jnp.float32),
        lax.psum_scatter(
            partial_sums[1].astype(jnp.bfloat16), "seq", scatter_dimension=0, tiled=True
        ).astype(jnp.float32),
        lax.psum_scatter(
            partial_sums[2].astype(jnp.bfloat16), "seq", scatter_dimension=0, tiled=True
        ).astype(jnp.float32),
        lax.psum_scatter(
            partial_sums[3].astype(jnp.bfloat16), "seq", scatter_dimension=0, tiled=True
        ).astype(jnp.float32),
        lax.psum_scatter(
            partial_sums[4].astype(jnp.bfloat16), "seq", scatter_dimension=0, tiled=True
        ).astype(jnp.float32),
        lax.psum_scatter(
            partial_sums[5].astype(jnp.bfloat16), "seq", scatter_dimension=0, tiled=True
        ).astype(jnp.float32),
        lax.psum_scatter(
            partial_sums[6].astype(jnp.bfloat16), "seq", scatter_dimension=0, tiled=True
        ).astype(jnp.float32),
    )
    gains = lax.psum(
        (grad_gain_attn, grad_gain_ffn, grad_gain_query, grad_gain_key), ("seq", "batch")
    )
    grad_inputs = rounded(grad_stream).reshape(slice_len, seq_count, width)
    return (
        output,
        grad_inputs,
        summed[0],
        summed[1],
        summed[2],
        summed[3],
        summed[4],
        summed[5],
        summed[6],
        gains[0],
        gains[1],
        gains[2],
        gains[3],
    )


def solution(mesh):
    sharded = P(("seq", "batch"), None)
    stream = P("seq", "batch", None)
    in_specs = (stream, P("batch")) + (sharded,) * 7 + (P(),) * 4 + (stream,)
    out_specs = (stream, stream) + (sharded,) * 7 + (P(),) * 4
    grouped = mesh.shape["seq"] == 8 and mesh.shape["batch"] == 4
    step = body if grouped else general_body
    return jax.shard_map(step, mesh=mesh, in_specs=in_specs, out_specs=out_specs, check_vma=False)
```

```python
import functools

import jax
import jax.numpy as jnp
import numpy as np
from jax import lax
from jax.experimental import pallas as pl
from jax.experimental.pallas import tpu as pltpu
from jax.sharding import PartitionSpec as P

MESH = pl.DeviceIdType.MESH
F32 = jnp.float32
BF16 = jnp.bfloat16
eps = 1e-05
theta = 1000000.0
VMEM = pl.BlockSpec(memory_space=pltpu.VMEM)
ANY = pl.BlockSpec(memory_space=pl.ANY)
SMEM = pl.BlockSpec(memory_space=pltpu.SMEM)


def nn(left, right):
    return lax.dot_general(left, right, (((1,), (0,)), ((), ())), preferred_element_type=F32)


def nt(left, right):
    return lax.dot_general(left, right, (((1,), (1,)), ((), ())), preferred_element_type=F32)


def tn(left, right):
    return lax.dot_general(left, right, (((0,), (0,)), ((), ())), preferred_element_type=F32)


def rms_factor(v):
    return lax.rsqrt(jnp.mean(v * v, axis=-1, keepdims=True) + eps)


def norm_back(grad, value, factor):
    return factor * (
        grad - value * factor * factor * jnp.mean(grad * value, axis=-1, keepdims=True)
    )


def lanes(shape):
    return lax.broadcasted_iota(jnp.int32, shape, len(shape) - 1)


def rows_of(shape):
    return lax.broadcasted_iota(jnp.int32, shape, len(shape) - 2)


def head_mean(v):
    first = lanes(v.shape) < 64
    low = jnp.sum(jnp.where(first, v, 0.0), axis=-1, keepdims=True)
    high = jnp.sum(jnp.where(first, 0.0, v), axis=-1, keepdims=True)
    return jnp.where(first, low, high) * (1.0 / 64.0)


def rope(u, cosine, sine):
    early = lax.rem(lanes(u.shape), 64) < 32
    turned = jnp.where(early, -pltpu.roll(u, 96, 1), pltpu.roll(u, 32, 1))
    return u * cosine + turned * sine


def rope_back(u, cosine, sine):
    early = lax.rem(lanes(u.shape), 64) < 32
    w = u * sine
    return u * cosine + jnp.where(early, pltpu.roll(w, 96, 1), -pltpu.roll(w, 32, 1))


class Place:
    def __init__(self, send_sem, recv_sem, local_sem):
        self.s = lax.axis_index("seq")
        self.b = lax.axis_index("batch")
        self.z = self.s // 2
        self.y = lax.rem(self.s, 2)
        self.core = self.b + 1 - 2 * lax.rem(self.b, 2)
        self.across = lax.rem(self.b + 2, 4)
        self.far = 3 - self.b
        self.flip = 2 * self.z + 1 - self.y
        self.inner = jnp.logical_or(self.z == 1, self.z == 2)
        self.pair = self.z + 1 - 2 * lax.rem(self.z, 2)
        self.there = jnp.where(self.z < 2, 2, 1)
        self.beyond = jnp.where(self.z < 2, 3, 0)
        self.send_sem, self.recv_sem, self.local_sem = send_sem, recv_sem, local_sem
        self.used = 0
        self.used_local = 0
        self.sent = []

    def up(self, k):
        return lax.rem(self.z + k, 4)

    def down(self, k):
        return lax.rem(self.z + 4 - k, 4)

    def greet(self):
        self.hello()
        self.meet()

    def hello(self):
        barrier = pltpu.get_barrier_semaphore()
        for k in (1, 2, 3):
            pl.semaphore_signal(
                barrier, inc=1, device_id=(self.s, lax.rem(self.b + k, 4)), device_id_type=MESH
            )
        for k in range(1, 8):
            pl.semaphore_signal(
                barrier, inc=1, device_id=(lax.rem(self.s + k, 8), self.b), device_id_type=MESH
            )

    def meet(self):
        pl.semaphore_wait(pltpu.get_barrier_semaphore(), 10)

    def slots(self, count):
        first = self.used
        self.used += count
        return first

    def copy(self, src, dst, device, out, into=None):
        return pltpu.make_async_remote_copy(
            src_ref=src,
            dst_ref=dst,
            send_sem=self.send_sem.at[out],
            recv_sem=self.recv_sem.at[out if into is None else into],
            device_id=device,
            device_id_type=MESH,
        )

    def post(self, src, dst, device):
        index = self.slots(1)
        made = self.copy(src, dst, device, index)
        made.start()
        self.sent.append(made)
        return index

    def landed(self, index, ref):
        self.copy(ref, ref, (self.s, self.core), index).wait_recv()

    def local(self, src, dst):
        index = self.used_local
        self.used_local += 1
        made = pltpu.make_async_copy(src, dst, self.local_sem.at[index])
        made.start()
        return made

    def drain(self):
        for made in self.sent:
            made.wait_send()
        self.sent = []


class Spread:
    def __init__(self, p, slot):
        self.p, self.slot = p, slot
        self.first = p.slots(8)
        self.from_z = (p.pair, p.there, p.beyond)

    def send(self, s, device, out, into):
        self.p.copy(self.slot(s), self.slot(s), device, self.first + out, self.first + into).start()

    def start(self):
        p = self.p
        self.send(p.s, (2 * p.pair + p.y, p.b), 0, 0)
        self.send(p.s, (2 * p.there + p.y, p.b), 1, jnp.where(p.inner, 1, 2))
        self.send(p.s, (p.flip, p.b), 4, 3)

    def land(self, j):
        p = self.p
        s = 2 * self.from_z[j] + p.y
        p.landed(self.first + j, self.slot(s))
        if j > 0:

            @pl.when(p.inner)
            def _():
                self.send(s, (2 * p.pair + p.y, p.b), 1 + j, j)

        self.send(s, (p.flip, p.b), 5 + j, 4 + j)

    def land_inner(self):
        @pl.when(self.p.inner)
        def _():
            self.land(1)
            self.land(2)

    def land_end(self):
        @pl.when(jnp.logical_not(self.p.inner))
        def _():
            self.land(1)
            self.land(2)

    def finish(self):
        p = self.p
        p.landed(self.first + 3, self.slot(p.flip))
        for j in range(3):
            p.landed(self.first + 4 + j, self.slot(2 * self.from_z[j] + 1 - p.y))

    def drain(self):
        p = self.p

        def sent(out):
            p.copy(self.slot(p.s), self.slot(p.s), (p.flip, p.b), self.first + out).wait_send()

        for out in (0, 1, 4, 5, 6, 7):
            sent(out)

        @pl.when(p.inner)
        def _():
            sent(2)
            sent(3)


def heads_of(whole, kk):
    return whole[:, 256 * kk : 256 * kk + 128], whole[:, 256 * kk + 128 : 256 * kk + 256]


def pack_projections(w_query, key_weight, value_weight, out):
    for c in range(4):
        k = key_weight[:, 128 * c : 128 * c + 128].astype(F32)
        v = value_weight[:, 128 * c : 128 * c + 128].astype(F32)
        first = lanes(k.shape) < 64
        pairs = (
            jnp.where(first, k, pltpu.roll(v, 64, 1)),
            jnp.where(first, pltpu.roll(k, 64, 1), v),
        )
        for kk in (0, 1):
            h = 2 * c + kk
            out[c, :, 256 * kk : 256 * kk + 128] = w_query[:, 128 * h : 128 * h + 128]
            out[c, :, 256 * kk + 128 : 256 * kk + 256] = pairs[kk].astype(BF16)


def pack_hidden(source, out, which):
    wide = source[...].astype(F32)
    for c in range(4):
        pieces = [wide[:, 144 * (4 * i + c) : 144 * (4 * i + c) + 144] for i in range(8)]
        out[c, which] = jnp.concatenate(pieces, axis=1).astype(BF16)


def twice(v):
    return jnp.concatenate([v[...], v[...]], axis=1)


def near_first(p, t):
    return jnp.where(t == 0, p.b, jnp.where(t == 1, p.core, jnp.where(t == 2, p.across, p.far)))


def forward_kernel(
    x, dy, lengths, w_query, key_weight, value_weight, w_out, w_gate, w_up, w_down,
    cos_table, sin_table, gain_query, gain_key, gain_a, gain_f,
    output, dn2, ggu_out, gd_mine, gd_other, wo_out, wqkv_out, norm_out, unit_out_, lse_out, attn_out, mix_out,
    middle, length_all,
    xa, norm, wqkv, wo, pack, unit, unit_out, lse, kv, vt, mix, norm_two, dy_all, wgu, wd, gd,
    hid, dgate, dup, parts_n, recv_n, parts_o, recv_o, keep_n, keep_o,
    qkv_send, gu_send, length, cos, sin,
    send_sem, recv_sem, local_sem,
):
    p = Place(send_sem, recv_sem, local_sem)
    s, b, z, y = p.s, p.b, p.z, p.y
    my_rows = pl.ds(pl.multiple_of(32 * b, 32), 32)
    my_positions = pl.ds(pl.multiple_of(256 * s, 256), 256)
    p.hello()
    own_d = p.local(w_down, wd.at[s])
    own_x = p.local(x, xa.at[b])
    own_wo = p.local(w_out, wo.at[s, b])
    own_dy = p.local(dy, dy_all.at[b])
    own_tables = [p.local(cos_table.at[my_positions], cos), p.local(sin_table.at[my_positions], sin)]
    pack_projections(w_query, key_weight, value_weight, qkv_send)
    length[...] = jnp.broadcast_to(lengths[0], (8, 128)).astype(jnp.int32)
    own_qkv = p.local(qkv_send.at[b], wqkv.at[s, my_rows])
    length_all[b] = length[...]
    p.meet()

    got_qkv, got_len = [], []
    for k in (1, 2, 3):
        to = lax.rem(b + k, 4)
        got_qkv.append(p.post(qkv_send.at[to], wqkv.at[s, my_rows], (s, to)))
    x_across = p.post(x, xa.at[b], (s, p.across))
    x_core = p.post(x, xa.at[b], (s, p.core))
    for k in (1, 2, 3):
        to = lax.rem(b + k, 4)
        got_len.append(p.post(length, length_all.at[b], (s, to)))
    spread_d = Spread(p, lambda i: wd.at[i])
    spread_g = Spread(p, lambda i: wgu.at[i, 0])
    spread_u = Spread(p, lambda i: wgu.at[i, 1])
    own_d.wait()
    spread_d.start()
    own_x.wait()

    def normalize(g):
        xg = xa[g].astype(F32)
        norm[g] = (xg * rms_factor(xg) * gain_a[...]).astype(BF16)

    normalize(b)
    own_qkv.wait()
    for k in (1, 2, 3):
        p.landed(got_qkv[k - 1], wqkv.at[s, my_rows])
    z_qkv = [p.post(wqkv.at[s], wqkv.at[s], (2 * p.up(k) + y, b)) for k in (1, 2, 3)]
    y_qkv = [p.post(wqkv.at[s], wqkv.at[s], (p.flip, b))]
    pack_hidden(w_gate, gu_send, 0)
    pack_hidden(w_up, gu_send, 1)
    own_gu = p.local(gu_send.at[b], wgu.at[s, :, my_rows])
    got_gu = []
    for k in (1, 2, 3):
        to = lax.rem(b + k, 4)
        got_gu.append(p.post(gu_send.at[to], wgu.at[s, :, my_rows], (s, to)))
    for k in (1, 2, 3):
        slot = 2 * p.down(k) + y
        p.landed(z_qkv[k - 1], wqkv.at[slot])
        y_qkv.append(p.post(wqkv.at[slot], wqkv.at[slot], (p.flip, b)))
    p.landed(x_core, xa.at[p.core])
    normalize(p.core)
    p.landed(x_across, xa.at[p.across])
    x_far = p.post(xa.at[p.across], xa.at[p.across], (s, p.core))
    for made in own_tables:
        made.wait()
    p.landed(y_qkv[0], wqkv.at[p.flip])
    for k in (1, 2, 3):
        p.landed(y_qkv[k], wqkv.at[2 * p.down(k) + 1 - y])
    kept = [p.local(wqkv, wqkv_out)]
    gain_q, gain_k = twice(gain_query), twice(gain_key)

    first_unit = p.slots(8)

    def each_piece(t, kk, act):
        to = 2 * near_first(p, t) + kk

        @pl.when(to != s)
        def _():
            act(p.copy(pack.at[to], unit.at[s], (to, b), first_unit + 2 * t + kk, first_unit + s))

    def project(t, carry):
        g = near_first(p, t)

        @pl.when(t == 3)
        def _():
            p.landed(x_far, xa.at[p.far])

        @pl.when(t >= 2)
        def _():
            normalize(g)

        whole = nn(norm[g], wqkv[...].reshape(1024, 512))
        for kk in (0, 1):
            q, kvp = heads_of(whole, kk)
            qn = q * lax.rsqrt(head_mean(q * q) + eps) * gain_q
            kn = kvp * lax.rsqrt(head_mean(kvp * kvp) + eps) * gain_k
            qr = rope(qn, cos[...], sin[...]) * 0.125
            kr = rope(kn, cos[...], sin[...])
            pack[2 * g + kk, :, 0:128] = qr.astype(BF16)
            pack[2 * g + kk, :, 128:256] = jnp.where(lanes(kr.shape) < 64, kr, kvp).astype(BF16)
            each_piece(t, kk, lambda made: made.start())

        @pl.when(t == 2)
        def _():
            spread_d.land(0)
            spread_d.land_inner()

        return carry

    lax.fori_loop(0, 4, project, 0)
    own_unit = p.local(pack.at[s], unit.at[s])
    kept.append(p.local(norm, norm_out))
    own_wo.wait()
    z_wo = [p.post(wo.at[s, b], wo.at[s, b], (2 * p.up(k) + y, b)) for k in (1, 2, 3)]
    y_wo = [p.post(wo.at[s, b], wo.at[s, b], (p.flip, b))]
    spread_d.land_end()
    own_dy.wait()
    dy_across = p.post(dy, dy_all.at[b], (s, p.across))
    dy_core = p.post(dy, dy_all.at[b], (s, p.core))
    for k in (1, 2, 3):
        p.landed(got_len[k - 1], length_all.at[lax.rem(b + 4 - k, 4)])

    for k in range(1, 8):
        src = lax.rem(s + k, 8)
        p.landed(first_unit + src, unit.at[src])
    own_unit.wait()
    kept.append(p.local(unit, unit_out_))
    own_gu.wait()
    for k in (1, 2, 3):
        p.landed(got_gu[k - 1], wgu.at[s, :, my_rows])
    spread_g.start()
    spread_u.send(s, (p.flip, b), 4, 3)
    for k in (1, 2, 3):
        slot = 2 * p.down(k) + y
        p.landed(z_wo[k - 1], wo.at[slot, b])
        y_wo.append(p.post(wo.at[slot, b], wo.at[slot, b], (p.flip, b)))

    def prepare(j, carry):
        live = j * 256 + rows_of((256, 128)) < length_all[z][0:1, :]
        masked = jnp.where(live, unit[j, :, 128:256].astype(F32), 0.0)
        kv[j] = masked.astype(BF16)
        vt[j, 0:64] = jnp.transpose(masked)[64:128].astype(BF16)
        alive = j * 256 + lanes((16, 256)) < length_all[z][0:1, 0:1]
        vt[j, 64:80] = jnp.where(alive, 1.0, 0.0).astype(BF16)
        return carry

    lax.fori_loop(0, 8, prepare, 0)
    p.landed(dy_across, dy_all.at[p.across])
    dy_far = p.post(dy_all.at[p.across], dy_all.at[p.across], (s, p.core))
    p.landed(y_wo[0], wo.at[p.flip, b])
    for k in (1, 2, 3):
        p.landed(y_wo[k], wo.at[2 * p.down(k) + 1 - y, b])
    wo_across = p.post(wo.at[:, b], wo.at[:, b], (s, p.across))
    wo_core = p.post(wo.at[:, b], wo.at[:, b], (s, p.core))
    first_mix, first_across, first_core = p.slots(8), p.slots(8), p.slots(8)

    def mix_send(src, t):
        p.copy(mix.at[b, src], mix.at[b, src], (s, p.across), first_across + t).start()
        p.copy(mix.at[b, src], mix.at[b, src], (s, p.core), first_core + t).start()

    def mix_arrived(t):
        src = lax.rem(s + 7 - t, 8)
        p.landed(first_mix + t, mix.at[b, src])
        mix_send(src, t)

    def attend(t, carry):
        i = lax.rem(s + 1 + t, 8)
        qt = jnp.transpose(unit[i, :, 0:128].astype(F32)).astype(BF16)
        both = jnp.concatenate([qt[0:64], qt[64:128]], axis=1)
        right = jnp.concatenate([both, jnp.zeros((64, 512), BF16)], axis=0)

        def block(j, acc):
            return acc + nn(vt[j], jnp.exp(nn(kv[j], right)).astype(BF16))

        acc = lax.fori_loop(0, i, block, jnp.zeros((80, 512), F32))
        causal = rows_of((256, 512)) <= lax.rem(lanes((256, 512)), 256)
        edge = jnp.where(causal, jnp.exp(nn(kv[i], right)), 0.0).astype(BF16)
        acc = acc + nn(vt[i], edge)
        total = acc[64:65]
        out = acc[0:64] / total
        out = jnp.concatenate([out[:, 0:256], out[:, 256:512]], axis=0)
        unit_out[i] = jnp.transpose(out).astype(BF16)
        lse[i] = jnp.broadcast_to(jnp.log(total), (8, 512))

        @pl.when(t < 7)
        def _():
            p.copy(unit_out.at[i], mix.at[b, s], (i, b), first_mix + t).start()

        @pl.when(t == 3)
        def _():
            spread_g.land(0)
            spread_g.land_inner()
            spread_u.send(s, (2 * p.pair + y, b), 0, 0)
            spread_u.send(s, (2 * p.there + y, b), 1, jnp.where(p.inner, 1, 2))

        @pl.when(t == 6)
        def _():
            spread_g.land_end()

        @pl.when(t >= 4)
        def _():
            mix_arrived(t - 4)

        return carry

    lax.fori_loop(0, 8, attend, 0)
    own_mix = p.local(unit_out.at[s], mix.at[b, s])
    kept.append(p.local(unit_out, attn_out))
    kept.append(p.local(lse, lse_out))
    own_mix.wait()
    mix_send(s, 7)
    for t in range(4, 7):
        mix_arrived(t)
    spread_u.land(0)
    spread_u.land_inner()
    p.landed(wo_across, wo.at[:, p.across])
    wo_far = p.post(wo.at[:, p.across], wo.at[:, p.across], (s, p.core))
    for t in range(8):
        p.landed(first_across + t, mix.at[p.across, lax.rem(s + 7 - t, 8)])
    mix_far = p.post(mix.at[p.across], mix.at[p.across], (s, p.core))
    for t in range(8):
        p.landed(first_core + t, mix.at[p.core, lax.rem(s + 7 - t, 8)])
    p.landed(wo_core, wo.at[:, p.core])
    p.landed(wo_far, wo.at[:, p.far])
    kept.append(p.local(wo, wo_out))
    spread_u.land_end()
    p.landed(mix_far, mix.at[p.far])
    kept.append(p.local(mix, mix_out))

    def project_out(g, carry):
        mixed = jnp.concatenate([mix[c, 2 * g + kk] for c in range(4) for kk in (0, 1)], axis=1)
        mid = xa[g].astype(F32) + nn(mixed, wo[...].reshape(1024, 1024))
        norm_two[g] = (mid * rms_factor(mid) * gain_f[...]).astype(BF16)

        @pl.when(g == b)
        def _():
            middle[...] = mid

        return carry

    lax.fori_loop(0, 4, project_out, 0)
    p.landed(dy_core, dy_all.at[p.core])
    p.landed(dy_far, dy_all.at[p.far])
    for spread in (spread_d, spread_g, spread_u):
        spread.finish()

    first_n, first_o = p.slots(3), p.slots(3)

    def gated(t, carry):
        g = batch_order(p, t)
        rows = pl.ds(pl.multiple_of(g * 256, 256), 256)
        n2 = norm_two[g]
        gate = nn(n2, wgu[:, 0].reshape(1024, 1152))
        up = nn(n2, wgu[:, 1].reshape(1024, 1152))
        dh = nt(dy_all[g], wd[...].reshape(1152, 1024))
        sg = 1.0 / (1.0 + jnp.exp(-gate))
        swish = gate * sg
        hid[rows] = (swish * up).astype(BF16)
        dg = (dh * up * sg * (1.0 + gate * (1.0 - sg))).astype(BF16)
        du = (dh * swish).astype(BF16)
        dgate[rows] = dg
        dup[rows] = du
        part = nt(dg, wgu[:, 0].reshape(1024, 1152)) + nt(du, wgu[:, 1].reshape(1024, 1152))
        parts_n[g] = part.astype(BF16)

        @pl.when(t == 3)
        def _():
            keep_n[...] = part

        chip_sum_post(p, t, parts_n, recv_n, first_n)
        return carry

    lax.fori_loop(0, 4, gated, 0)
    chip_sum_across(p, parts_n, recv_n, first_n)

    def down_rows(c, carry):
        at = pl.multiple_of(128 * c, 128)
        gd[pl.ds(at, 128)] = tn(hid[:, pl.ds(at, 128)], dy_all[...].reshape(1024, 1024)).astype(BF16)
        return carry

    lax.fori_loop(0, 9, down_rows, 0)
    sent_d = []
    for i in range(4):
        other = pl.ds(pl.multiple_of(144 * (2 * i + 1 - y), 16), 144)
        mine = pl.ds(pl.multiple_of(144 * (2 * i + y), 16), 144)
        sent_d.append(p.post(gd.at[other], gd_other.at[i], (p.flip, b)))
        kept.append(p.local(gd.at[mine], gd_mine.at[i]))

    def down(t, carry):
        g = batch_order(p, t)
        part = nn(hid[pl.ds(pl.multiple_of(g * 256, 256), 256)], wd[...].reshape(1152, 1024))
        parts_o[g] = part.astype(BF16)

        @pl.when(t == 3)
        def _():
            keep_o[...] = part

        chip_sum_post(p, t, parts_o, recv_o, first_o)
        return carry

    lax.fori_loop(0, 4, down, 0)
    chip_sum_across(p, parts_o, recv_o, first_o)
    for spread in (spread_d, spread_g, spread_u):
        spread.drain()

    def gate_rows(c, carry):
        at = pl.multiple_of(128 * c, 128)
        left = norm_two[:, :, pl.ds(at, 128)].reshape(1024, 128)
        wgu[c, 0] = tn(left, dgate[...]).astype(BF16)
        wgu[c, 1] = tn(left, dup[...]).astype(BF16)
        return carry

    lax.fori_loop(0, 8, gate_rows, 0)
    kept.append(p.local(wgu, ggu_out))
    dn2[...] = keep_n[...] + chip_sum_rest(p, parts_n, recv_n, first_n)
    total = keep_o[...] + chip_sum_rest(p, parts_o, recv_o, first_o)
    output[...] = (middle[...] + total).astype(BF16)
    for i in range(4):
        p.landed(sent_d[i], gd_other.at[i])
    for t in range(8):
        if t < 7:
            p.copy(unit_out.at[s], mix.at[b, s], (p.flip, b), first_mix + t).wait_send()
        p.copy(mix.at[b, s], mix.at[b, s], (s, p.across), first_across + t).wait_send()
        p.copy(mix.at[b, s], mix.at[b, s], (s, p.core), first_core + t).wait_send()
    for t in range(4):
        for kk in (0, 1):
            each_piece(t, kk, lambda made: made.wait_send())
    for made in kept:
        made.wait()
    p.drain()


def chip_sum_post(p, t, parts, recv, first):
    @pl.when(t == 0)
    def _():
        p.copy(parts.at[p.far], recv.at[0], (p.s, p.core), first).start()

    @pl.when(t == 1)
    def _():
        p.copy(parts.at[p.core], recv.at[1], (p.s, p.core), first + 1).start()


def chip_sum_across(p, parts, recv, first):
    p.copy(recv.at[0], recv.at[0], (p.s, p.core), first).wait_recv()
    parts[p.across] = (parts[p.across].astype(F32) + recv[0].astype(F32)).astype(BF16)
    p.copy(parts.at[p.across], recv.at[2], (p.s, p.across), first + 2).start()


def chip_sum_rest(p, parts, recv, first):
    p.copy(recv.at[1], recv.at[1], (p.s, p.core), first + 1).wait_recv()
    p.copy(recv.at[2], recv.at[2], (p.s, p.core), first + 2).wait_recv()
    for k in range(3):
        p.copy(parts.at[p.b], recv.at[k], (p.s, p.core), first + k).wait_send()
    return recv[1].astype(F32) + recv[2].astype(F32)


def batch_order(p, t):
    return jnp.where(t == 0, p.far, jnp.where(t == 1, p.core, jnp.where(t == 2, p.across, p.b)))


class SeqTree:
    def __init__(self, p, mine, y_recv, relayed, z_recv, sums=None):
        self.p, self.mine, self.y_recv, self.relayed, self.z_recv = p, mine, y_recv, relayed, z_recv
        self.sums = y_recv if sums is None else sums
        self.first = p.slots(6)
        self.started = False

    def start(self, source):
        p = self.p
        self.started = True
        p.copy(source, self.y_recv, (p.flip, p.b), self.first + 4).start()

    def send(self, i, dst, z, out, into):
        p = self.p
        p.copy(self.sums.at[i], dst, (2 * z + p.y, p.b), self.first + out, self.first + into).start()

    def reduce(self):
        p = self.p
        if self.started:
            p.landed(self.first + 4, self.y_recv)

        def add(i):
            self.sums[i] = (self.y_recv[i].astype(F32) + self.mine[i].astype(F32)).astype(BF16)

        add(p.there)
        add(p.beyond)

        @pl.when(jnp.logical_not(p.inner))
        def _():
            self.send(p.there, self.relayed.at[0], p.pair, 1, 1)
            self.send(p.beyond, self.relayed.at[1], p.pair, 2, 2)

        add(p.pair)
        self.send(p.pair, self.z_recv.at[0], p.pair, 0, 0)

    def relay(self):
        p = self.p

        @pl.when(p.inner)
        def _():
            for k, i in ((0, p.there), (1, p.beyond)):
                p.landed(self.first + 1 + k, self.relayed.at[k])
                self.sums[i] = (self.sums[i].astype(F32) + self.relayed[k].astype(F32)).astype(BF16)
                self.send(i, self.z_recv.at[1], i, 1 + k, 3)

    def finish(self):
        p = self.p
        total = self.y_recv[p.z].astype(F32) + self.mine[p.z].astype(F32)
        p.landed(self.first, self.z_recv.at[0])
        total = total + self.z_recv[0].astype(F32)
        p.landed(self.first + 3, self.z_recv.at[1])
        for out in range(3):
            p.copy(self.z_recv.at[0], self.z_recv.at[0], (p.flip, p.b), self.first + out).wait_send()
        if self.started:
            p.copy(self.y_recv, self.y_recv, (p.flip, p.b), self.first + 4).wait_send()
        return total + self.z_recv[1].astype(F32)


class SeqSum:
    def __init__(self, p, y_recv, z_recv):
        self.p, self.y_recv, self.z_recv = p, y_recv, z_recv

    def start(self, source, mine=None):
        p = self.p
        self.index = p.post(source.at[:, 1 - p.y], self.y_recv, (p.flip, p.b))
        self.load = None
        if mine is None:
            self.mine = lambda i: source.at[i, p.y]
        else:
            self.load = p.local(source.at[:, p.y], mine)
            self.mine = lambda i: mine.at[i]

    def middle(self):
        p = self.p
        if self.load is not None:
            self.load.wait()
        p.landed(self.index, self.y_recv)
        self.far = []
        for k in (1, 2, 3):
            i = p.up(k)
            self.y_recv[i] = (self.y_recv[i].astype(F32) + self.mine(i)[...].astype(F32)).astype(BF16)
            self.far.append(p.post(self.y_recv.at[i], self.z_recv.at[k - 1], (2 * i + p.y, p.b)))

    def finish(self):
        p = self.p
        total = self.y_recv[p.z].astype(F32) + self.mine(p.z)[...].astype(F32)
        for k in (1, 2, 3):
            p.landed(self.far[k - 1], self.z_recv.at[k - 1])
            total = total + self.z_recv[k - 1].astype(F32)
        return total


def backward_kernel(
    dn2, middle, x, dy, wo_in, mix_in, unit_in, attn_in, lse_in, length_all, norm_in, wqkv_in,
    cos_table, sin_table, gain_query, gain_key, gain_a, gain_f, ggu, gd, y_d,
    dx, rqkv, rgu, rd, ro, gains_out,
    wo, mix, unit, unit_out, lse, norm, wqkv, cos, sin, m_g, m_u,
    dmid, dox, doq, dou, dbr, kv, kt, delta, dk2, dv2, back, dqr,
    dpre, parts, recv, keep, gqkv, go, mixt,
    s_d, t_d, z_d, y_g, t_g, z_g, y_u, t_u, z_u, y_q, z_q, y_o, z_o, fin_g, fin_u, fin_q,
    gain_sum, gain_batch, gain_seq,
    send_sem, recv_sem, local_sem,
):
    p = Place(send_sem, recv_sem, local_sem)
    s, b, z, y = p.s, p.b, p.z, p.y
    p.hello()
    my_positions = pl.ds(pl.multiple_of(256 * s, 256), 256)
    load_wo = p.local(wo_in, wo)
    load_unit = p.local(unit_in, unit)
    load_more = [p.local(attn_in, unit_out), p.local(lse_in, lse)]
    load_g = p.local(ggu.at[:, y, 0], m_g)
    load_u = p.local(ggu.at[:, y, 1], m_u)
    load_mix = p.local(mix_in, mix)
    load_last = [
        p.local(norm_in, norm), p.local(wqkv_in, wqkv),
        p.local(cos_table.at[my_positions], cos), p.local(sin_table.at[my_positions], sin),
    ]
    p.meet()
    sum_d = SeqTree(p, gd, y_d, t_d, z_d, s_d)
    sum_g = SeqTree(p, m_g, y_g, t_g, z_g)
    sum_u = SeqTree(p, m_u, y_u, t_u, z_u)
    sum_g.start(ggu.at[:, 1 - y, 0])
    sum_d.reduce()

    mid = middle[...]
    r2 = rms_factor(mid)
    grad_two = dn2[...]
    gain_sum[...] = jnp.zeros((8, 1024), F32)
    gain_sum[1:2] = jnp.sum(grad_two * mid * r2, axis=0, keepdims=True)
    dm = dy[...].astype(F32) + norm_back(grad_two * gain_f[...], mid, r2)
    dmid[...] = dm
    dbr[b] = dm.astype(BF16)
    load_wo.wait()
    for c in range(4):
        for kk in (0, 1):
            h = 2 * c + kk
            dox[c, kk] = nt(dbr[b], wo[h].reshape(128, 1024)).astype(BF16)
    got_do = []
    for k in (1, 2, 3):
        to = lax.rem(b + k, 4)
        got_do.append(p.post(dox.at[to], doq.at[pl.ds(2 * b, 2)], (s, to)))
    doq[pl.ds(2 * b, 2)] = dox[b]
    dbr_across = p.post(dbr.at[b], dbr.at[b], (s, p.across))
    dbr_core = p.post(dbr.at[b], dbr.at[b], (s, p.core))
    for k in (1, 2, 3):
        p.landed(got_do[k - 1], doq.at[pl.ds(2 * lax.rem(b + 4 - k, 4), 2)])
    got_unit = []
    for k in range(1, 8):
        to = lax.rem(s + k, 8)
        got_unit.append(p.post(doq.at[to], dou.at[s], (to, b)))
    dou[s] = doq[s]
    load_unit.wait()

    def prepare(i, carry):
        live = i * 256 + rows_of((256, 128)) < length_all[z][0:1, :]
        masked = jnp.where(live, unit[i, :, 128:256].astype(F32), 0.0)
        kv[i] = masked.astype(BF16)
        kt[i] = jnp.transpose(masked)[0:64].astype(BF16)
        dk2[i] = jnp.zeros((256, 128), F32)
        dv2[i] = jnp.zeros((256, 128), F32)
        return carry

    lax.fori_loop(0, 8, prepare, 0)
    sum_d.relay()
    p.landed(dbr_across, dbr.at[p.across])
    dbr_far = p.post(dbr.at[p.across], dbr.at[p.across], (s, p.core))
    for k in range(1, 8):
        p.landed(got_unit[k - 1], dou.at[lax.rem(s + 8 - k, 8)])

    for made in load_more:
        made.wait()

    def queries(t, carry):
        i = 7 - t
        q, do = unit[i, :, 0:128].astype(F32), dou[i].astype(F32)
        qt, dot = jnp.transpose(q).astype(BF16), jnp.transpose(do)
        first = lanes(q.shape) < 64
        blank = jnp.zeros((64, 512), BF16)
        qr = jnp.concatenate([jnp.concatenate([qt[0:64], qt[64:128]], axis=1), blank], axis=0)
        dr = jnp.concatenate([dot[0:64], dot[64:128]], axis=1).astype(BF16)
        dr = jnp.concatenate([blank, dr], axis=0)
        ql = jnp.concatenate([jnp.where(first, q, 0.0), jnp.where(first, 0.0, q)], axis=0).astype(BF16)
        dl = jnp.concatenate([jnp.where(first, do, 0.0), jnp.where(first, 0.0, do)], axis=0).astype(BF16)
        both = dot * jnp.transpose(unit_out[i].astype(F32))
        low = jnp.sum(both[0:64], axis=0, keepdims=True)
        high = jnp.sum(both[64:128], axis=0, keepdims=True)
        shift = jnp.concatenate([low, high], axis=1)
        log_total = lse[i][0:1]

        def block(j, probs):
            ds = (probs * (nn(kv[j], dr) - shift)).astype(BF16)
            dv2[j] += nn(probs.astype(BF16), dl)
            dk2[j] += nn(ds, ql)
            return nn(kt[j], ds)

        def step(j, acc):
            return acc + block(j, jnp.exp(nn(kv[j], qr) - log_total))

        acc = lax.fori_loop(0, i, step, jnp.zeros((64, 512), F32))
        causal = rows_of((256, 512)) <= lax.rem(lanes((256, 512)), 256)
        acc = acc + block(i, jnp.where(causal, jnp.exp(nn(kv[i], qr) - log_total), 0.0))
        dq = jnp.concatenate([acc[:, 0:256], acc[:, 256:512]], axis=0) * 0.125
        back[i, :, 0:128] = jnp.transpose(dq).astype(BF16)
        live = i * 256 + rows_of((256, 128)) < length_all[z][0:1, :]
        dk, dv = dk2[i], dv2[i]
        dk = dk + pltpu.roll(dk, 64, 1)
        dv = dv + pltpu.roll(dv, 64, 1)
        dkv = jnp.where(lanes((256, 128)) < 64, dk, dv)
        back[i, :, 128:256] = jnp.where(live, dkv, 0.0).astype(BF16)
        return carry

    lax.fori_loop(0, 1, queries, 0)
    load_g.wait()
    sum_g.reduce()
    sum_u.start(ggu.at[:, 1 - y, 1])
    lax.fori_loop(1, 4, queries, 0)
    sum_g.relay()
    lax.fori_loop(4, 8, queries, 0)
    got_back = []
    for k in range(1, 8):
        to = lax.rem(s + k, 8)
        got_back.append(p.post(back.at[to], dqr.at[s], (to, b)))
    dqr[s] = back[s]

    p.landed(dbr_core, dbr.at[p.core])
    p.landed(dbr_far, dbr.at[p.far])

    load_mix.wait()

    def turn(e, carry):
        for g in range(4):
            mixt[:, 256 * g : 256 * g + 256] = jnp.transpose(
                mix[e // 2, 2 * g + lax.rem(e, 2)].astype(F32)
            ).astype(BF16)
        left = mixt[pl.ds(pl.multiple_of(32 * b, 32), 32)]
        go[e // 2, lax.rem(e, 2)] = nn(left, dbr[...].reshape(1024, 1024)).astype(BF16)
        return carry

    lax.fori_loop(0, 8, turn, 0)
    sum_o = SeqSum(p, y_o, z_o)
    sum_o.start(go)
    load_u.wait()
    sum_u.reduce()
    for made in load_last:
        made.wait()
    gain_q, gain_k = twice(gain_query), twice(gain_key)
    for k in range(1, 8):
        p.landed(got_back[k - 1], dqr.at[lax.rem(s + 8 - k, 8)])

    first_n = p.slots(3)
    zero_row = jnp.zeros((1, 128), F32)

    def heads(t, carry):
        sum_q, sum_k = carry
        g = batch_order(p, t)
        whole = nn(norm[g], wqkv[...].reshape(1024, 512))
        for kk in (0, 1):
            at = 256 * kk
            q, k = heads_of(whole, kk)
            rq = lax.rsqrt(head_mean(q * q) + eps)
            rk = lax.rsqrt(head_mean(k * k) + eps)
            dq = rope_back(dqr[2 * g + kk, :, 0:128].astype(F32), cos[...], sin[...])
            dkv = dqr[2 * g + kk, :, 128:256].astype(F32)
            dk = rope_back(dkv, cos[...], sin[...])
            sum_q = sum_q + jnp.sum(dq * q * rq, axis=0, keepdims=True)
            sum_k = sum_k + jnp.sum(dk * k * rk, axis=0, keepdims=True)
            dq = dq * gain_q
            dk = dk * gain_k
            dq = rq * (dq - q * rq * rq * head_mean(dq * q))
            dk = rk * (dk - k * rk * rk * head_mean(dk * k))
            dpre[g, :, at : at + 128] = dq.astype(BF16)
            dpre[g, :, at + 128 : at + 256] = jnp.where(lanes(dk.shape) < 64, dk, dkv).astype(BF16)
        part = nt(dpre[g], wqkv[...].reshape(1024, 512))
        parts[g] = part.astype(BF16)

        @pl.when(t == 3)
        def _():
            keep[...] = part

        chip_sum_post(p, t, parts, recv, first_n)
        return (sum_q, sum_k)

    sum_q, sum_k = lax.fori_loop(0, 4, heads, (zero_row, zero_row))
    gain_sum[2:3, 0:128] = sum_q
    gain_sum[3:4, 0:128] = sum_k
    chip_sum_across(p, parts, recv, first_n)

    def qkv_rows(c, carry):
        at = pl.multiple_of(128 * c, 128)
        left = norm[:, :, pl.ds(at, 128)].reshape(1024, 128)
        gqkv[c // 2, lax.rem(c, 2)] = tn(left, dpre[...].reshape(1024, 512)).astype(BF16)
        return carry

    lax.fori_loop(0, 8, qkv_rows, 0)
    sum_qkv = SeqSum(p, y_q, z_q)
    sum_qkv.start(gqkv)
    sum_u.relay()
    sum_o.middle()

    dn1 = keep[...] + chip_sum_rest(p, parts, recv, first_n)
    xf = x[...].astype(F32)
    r1 = rms_factor(xf)
    gain_sum[0:1] = jnp.sum(dn1 * xf * r1, axis=0, keepdims=True)
    dx[...] = (dmid[...] + norm_back(dn1 * gain_a[...], xf, r1)).astype(BF16)
    got_gain = [p.post(gain_sum, gain_batch.at[b], (s, lax.rem(b + k, 4))) for k in (1, 2, 3)]
    gain_batch[b] = gain_sum[...]
    sum_qkv.middle()

    rd[...] = sum_d.finish()

    def exchange(total, fin, dst):
        fin[...] = total.astype(BF16)
        got = []
        for k in (1, 2, 3):
            to = lax.rem(b + k, 4)
            rows = pl.ds(pl.multiple_of(32 * to, 32), 32)
            got.append(p.post(fin.at[rows], dst(b), (s, to)))
        dst(b)[...] = fin[pl.ds(pl.multiple_of(32 * b, 32), 32)]
        return got

    def arrive(got, dst):
        for k in (1, 2, 3):
            p.landed(got[k - 1], dst(lax.rem(b + 4 - k, 4)))

    dst_g, dst_u, dst_q = (lambda i: rgu.at[i, 0]), (lambda i: rgu.at[i, 1]), (lambda i: rqkv.at[i])
    got_g = exchange(sum_g.finish(), fin_g, dst_g)
    for k in (1, 2, 3):
        p.landed(got_gain[k - 1], gain_batch.at[lax.rem(b + 4 - k, 4)])
    gain_seq[s] = (gain_batch[0] + gain_batch[1]) + (gain_batch[2] + gain_batch[3])
    got_all = [p.post(gain_seq.at[s], gain_seq.at[s], (lax.rem(s + k, 8), b)) for k in range(1, 8)]
    got_u = exchange(sum_u.finish(), fin_u, dst_u)
    ro[...] = sum_o.finish()
    got_q = exchange(sum_qkv.finish(), fin_q, dst_q)
    for k in range(1, 8):
        p.landed(got_all[k - 1], gain_seq.at[lax.rem(s + 8 - k, 8)])
    total = gain_seq[0]
    for k in range(1, 8):
        total = total + gain_seq[k]
    gains_out[...] = total
    arrive(got_g, dst_g)
    arrive(got_u, dst_u)
    arrive(got_q, dst_q)
    p.drain()


def finish_kernel(
    output, dx, rqkv, rgu, rd, ro, gains,
    output_, dx_, grad_query, grad_key, grad_value, grad_out, grad_gate, grad_up, grad_down,
    gain_attn, gain_ffn, gain_query, gain_key,
):
    output_[...] = output[...]
    dx_[...] = dx[...]
    grad_out[...] = ro[...]
    grad_down[...] = rd[...]
    for c in range(4):
        pairs = []
        for kk in (0, 1):
            h = 2 * c + kk
            q, kv = heads_of(rqkv[c].astype(F32), kk)
            grad_query[:, 128 * h : 128 * h + 128] = q
            pairs.append(kv)
        first = lanes(pairs[0].shape) < 64
        grad_key[:, 128 * c : 128 * c + 128] = jnp.where(first, pairs[0], pltpu.roll(pairs[1], 64, 1))
        grad_value[:, 128 * c : 128 * c + 128] = jnp.where(first, pltpu.roll(pairs[0], 64, 1), pairs[1])
    for which, out in ((0, grad_gate), (1, grad_up)):
        wide = [rgu[c, which].astype(F32) for c in range(4)]
        out[...] = jnp.concatenate(
            [wide[c][:, 144 * i : 144 * i + 144] for i in range(8) for c in range(4)], axis=1
        )
    gain_attn[...] = gains[0:1]
    gain_ffn[...] = gains[1:2]
    gain_query[...] = gains[2:3, 0:64] + gains[2:3, 64:128]
    gain_key[...] = gains[3:4, 0:64]


def call(kernel, outs, in_specs, out_specs, scratch, cid, sems):
    return pl.pallas_call(
        kernel,
        out_shape=[jax.ShapeDtypeStruct(shape, dtype) for shape, dtype in outs],
        in_specs=in_specs,
        out_specs=out_specs,
        scratch_shapes=[pltpu.VMEM(shape, dtype) for shape, dtype in scratch]
        + [
            pltpu.SemaphoreType.DMA((sems[0],)),
            pltpu.SemaphoreType.DMA((sems[0],)),
            pltpu.SemaphoreType.DMA((sems[1],)),
        ],
        compiler_params=pltpu.CompilerParams(
            collective_id=cid, has_side_effects=True, vmem_limit_bytes=60 * 2**20
        ),
    )


def body(
    inputs, lengths, w_query, key_weight, value_weight, w_out, w_gate, w_up, w_down,
    gain_attn, gain_ffn, gain_query, gain_key, cotangent,
):
    x = inputs.reshape(256, 1024)
    dy = cotangent.reshape(256, 1024)
    freqs = theta ** (-(np.arange(32, dtype=np.float32) * 2.0) / 64)
    angles = np.arange(2048, dtype=np.float32)[:, None] * freqs.astype(np.float32)[None, :]
    cosine = jnp.asarray(np.tile(np.cos(angles), (1, 4)), F32)
    sine = jnp.asarray(np.tile(np.sin(angles), (1, 4)), F32)
    gains = [g[None] for g in (gain_query, gain_key, gain_attn, gain_ffn)]

    (
        output, dn2, ggu, gd_mine, gd_other, wo, wqkv, norm, unit, lse, unit_out, mix, middle, length_all,
    ) = call(
        forward_kernel,
        [
            ((256, 1024), BF16), ((256, 1024), F32), ((8, 2, 128, 1152), BF16), ((4, 144, 1024), BF16),
            ((4, 144, 1024), BF16), ((8, 4, 32, 1024), BF16), ((8, 128, 512), BF16),
            ((4, 256, 1024), BF16), ((8, 256, 256), BF16), ((8, 8, 512), F32), ((8, 256, 128), BF16),
            ((4, 8, 256, 128), BF16), ((256, 1024), F32), ((4, 8, 128), jnp.int32),
        ],
        [VMEM, VMEM, SMEM] + [VMEM] * 6 + [ANY] * 3 + [VMEM] * 4,
        [VMEM, VMEM, ANY, ANY, VMEM] + [ANY] * 7 + [VMEM] * 2,
        [
            ((4, 256, 1024), BF16), ((4, 256, 1024), BF16), ((8, 128, 512), BF16), ((8, 4, 32, 1024), BF16),
            ((8, 256, 256), BF16), ((8, 256, 256), BF16), ((8, 256, 128), BF16), ((8, 8, 512), F32),
            ((8, 256, 128), BF16), ((8, 80, 256), BF16), ((4, 8, 256, 128), BF16), ((4, 256, 1024), BF16),
            ((4, 256, 1024), BF16), ((8, 2, 128, 1152), BF16), ((8, 144, 1024), BF16), ((1152, 1024), BF16),
            ((1024, 1152), BF16), ((1024, 1152), BF16), ((1024, 1152), BF16),
            ((4, 256, 1024), BF16), ((3, 256, 1024), BF16), ((4, 256, 1024), BF16),
            ((3, 256, 1024), BF16), ((256, 1024), F32), ((256, 1024), F32),
            ((4, 32, 512), BF16), ((4, 2, 32, 1152), BF16), ((8, 128), jnp.int32),
            ((256, 128), F32), ((256, 128), F32),
        ],
        0,
        (128, 32),
    )(x, dy, lengths, w_query, key_weight, value_weight, w_out, w_gate, w_up, w_down, cosine, sine, *gains)

    raw = call(
        backward_kernel,
        [
            ((256, 1024), BF16), ((4, 32, 512), BF16), ((4, 2, 32, 1152), BF16),
            ((144, 1024), F32), ((32, 1024), F32), ((8, 1024), F32),
        ],
        [VMEM] * 4 + [ANY] * 5 + [VMEM] + [ANY] * 4 + [VMEM] * 4 + [ANY, VMEM, VMEM],
        [VMEM] * 6,
        [
            ((8, 4, 32, 1024), BF16), ((4, 8, 256, 128), BF16), ((8, 256, 256), BF16), ((8, 256, 128), BF16),
            ((8, 8, 512), F32), ((4, 256, 1024), BF16), ((8, 128, 512), BF16), ((256, 128), F32),
            ((256, 128), F32), ((4, 128, 1152), BF16), ((4, 128, 1152), BF16),
            ((256, 1024), F32), ((4, 2, 256, 128), BF16), ((8, 256, 128), BF16), ((8, 256, 128), BF16),
            ((4, 256, 1024), BF16), ((8, 256, 128), BF16), ((8, 64, 256), BF16), ((8, 8, 512), F32),
            ((8, 256, 128), F32), ((8, 256, 128), F32), ((8, 256, 256), BF16), ((8, 256, 256), BF16),
            ((4, 256, 512), BF16), ((4, 256, 1024), BF16), ((3, 256, 1024), BF16), ((256, 1024), F32),
            ((4, 2, 128, 512), BF16), ((4, 2, 32, 1024), BF16), ((128, 1024), BF16),
            ((4, 144, 1024), BF16), ((2, 144, 1024), BF16), ((2, 144, 1024), BF16),
            ((4, 128, 1152), BF16), ((2, 128, 1152), BF16), ((2, 128, 1152), BF16),
            ((4, 128, 1152), BF16), ((2, 128, 1152), BF16), ((2, 128, 1152), BF16),
            ((4, 128, 512), BF16), ((3, 128, 512), BF16), ((4, 32, 1024), BF16), ((3, 32, 1024), BF16),
            ((128, 1152), BF16), ((128, 1152), BF16), ((128, 512), BF16),
            ((8, 1024), F32), ((4, 8, 1024), F32), ((8, 8, 1024), F32),
        ],
        1,
        (96, 32),
    )(
        dn2, middle, x, dy, wo, mix, unit, unit_out, lse, length_all, norm, wqkv,
        cosine, sine, *gains, ggu.reshape(4, 2, 2, 128, 1152), gd_mine, gd_other,
    )
    done = pl.pallas_call(
        finish_kernel,
        out_shape=[
            jax.ShapeDtypeStruct(shape, dtype)
            for shape, dtype in (
                ((256, 1024), BF16), ((256, 1024), BF16), ((32, 1024), F32), ((32, 512), F32),
                ((32, 512), F32), ((32, 1024), F32), ((32, 4608), F32), ((32, 4608), F32),
                ((144, 1024), F32), ((1, 1024), F32), ((1, 1024), F32), ((1, 64), F32), ((1, 64), F32),
            )
        ],
        in_specs=[VMEM] * 7,
        out_specs=[VMEM] * 13,
    )(output, *raw)
    return (
        done[0].reshape(256, 1, 1024), done[1].reshape(256, 1, 1024), *done[2:9], *[g[0] for g in done[9:]],
    )


def rotary_tables(positions, width):
    half = width // 2
    freqs = theta ** (-(jnp.arange(half, dtype=jnp.float32) * 2.0) / width)
    angles = positions.astype(jnp.float32)[:, None] * freqs[None, :]
    cosine = jnp.concatenate([jnp.cos(angles), jnp.cos(angles)], axis=-1)
    sine = jnp.concatenate([jnp.sin(angles), jnp.sin(angles)], axis=-1)
    return (cosine, sine)


def rotate(v, cosine, sine):
    half = v.shape[-1] // 2
    turned = jnp.concatenate([-v[..., half:], v[..., :half]], axis=-1)
    return v * cosine + turned * sine


def rotate_back(grad, cosine, sine):
    half = grad.shape[-1] // 2
    moved = grad * sine
    return grad * cosine + jnp.concatenate([moved[..., half:], -moved[..., :half]], axis=-1)


def product(left, right):
    return jnp.dot(left, right, preferred_element_type=jnp.float32)


def left_product(left, right):
    return jnp.einsum("rd,rn->dn", left, right, preferred_element_type=jnp.float32)


def right_product(left, right):
    return jnp.einsum("rn,dn->rd", left, right, preferred_element_type=jnp.float32)


def rounded(v):
    return v.astype(jnp.bfloat16)


def split_rows(term, seq_size, batch_size):
    return term.reshape(
        seq_size, batch_size, term.shape[0] // (seq_size * batch_size), term.shape[1]
    )


def fold_sources(piece):
    return jnp.sum(piece, axis=1).reshape(-1, piece.shape[-1])


def general_body(
    inputs,
    lengths,
    w_query,
    key_weight,
    value_weight,
    w_out,
    w_gate,
    w_up,
    w_down,
    gain_attn,
    gain_ffn,
    gain_query,
    gain_key,
    cotangent,
):
    slice_len, seq_count, width = inputs.shape
    rows = slice_len * seq_count
    head_dim = gain_query.shape[0]
    kv_width = key_weight.shape[1]
    kv_heads = kv_width // head_dim
    q_heads = w_query.shape[1] // head_dim
    sequence_group = q_heads // kv_heads
    scale = head_dim ** (-0.5)
    cycle_size = lax.axis_size("seq")
    batch_size = lax.axis_size("batch")
    positions = lax.axis_index("seq") * slice_len + jnp.arange(slice_len, dtype=jnp.int32)
    cosine, sine = rotary_tables(positions, head_dim)
    cosine = cosine[:, None, None, :]
    sine = sine[:, None, None, :]
    shards = (w_query, key_weight, value_weight, w_out, w_gate, w_up, w_down)
    wq, key_matrix, value_matrix, wo, wg, wu, wd = (
        lax.all_gather(shards[0], ("seq", "batch"), axis=0, tiled=True),
        lax.all_gather(shards[1], ("seq", "batch"), axis=0, tiled=True),
        lax.all_gather(shards[2], ("seq", "batch"), axis=0, tiled=True),
        lax.all_gather(shards[3], ("seq", "batch"), axis=0, tiled=True),
        lax.all_gather(shards[4], ("seq", "batch"), axis=0, tiled=True),
        lax.all_gather(shards[5], ("seq", "batch"), axis=0, tiled=True),
        lax.all_gather(shards[6], ("seq", "batch"), axis=0, tiled=True),
    )
    stream = inputs.reshape(rows, width).astype(jnp.float32)
    factor_one = rms_factor(stream)
    normalized_input = rounded(stream * factor_one * gain_attn)
    query_pre = product(normalized_input, wq).reshape(slice_len, seq_count, q_heads, head_dim)
    key_before_rotation = product(normalized_input, key_matrix).reshape(
        slice_len, seq_count, kv_heads, head_dim
    )
    value_b = rounded(product(normalized_input, value_matrix)).reshape(
        slice_len, seq_count, kv_width
    )
    factor_q = rms_factor(query_pre)
    factor_k = rms_factor(key_before_rotation)
    query_b = rounded(rotate(query_pre * factor_q * gain_query, cosine, sine))
    key_b = rounded(rotate(key_before_rotation * factor_k * gain_key, cosine, sine)).reshape(
        slice_len, seq_count, kv_width
    )
    query_five = query_b.reshape(slice_len, seq_count, kv_heads, sequence_group, head_dim)

    def scores_of(keys, start):
        count = keys.shape[0]
        raw = (
            jnp.einsum(
                "tsgrd,csgd->sgrtc",
                query_five,
                keys.reshape(count, seq_count, kv_heads, head_dim),
                preferred_element_type=jnp.float32,
            )
            * scale
        )
        key_pos = start + jnp.arange(count, dtype=jnp.int32)
        causal = key_pos[None, :] <= positions[:, None]
        inside = key_pos[None, :] < lengths[:, None]
        valid = causal[None, :, :] & inside[:, None, :]
        return (raw, valid[:, None, None, :, :])

    state_shape = (seq_count, kv_heads, sequence_group, slice_len)
    shard_ids = jnp.arange(cycle_size, dtype=jnp.int32)
    top = jnp.full(state_shape, -1e30, jnp.float32)
    keys = lax.all_gather(key_b, "seq", axis=0, tiled=True)
    value_rows = lax.all_gather(value_b, "seq", axis=0, tiled=True)
    count = keys.shape[0]
    raw, valid = scores_of(keys, jnp.int32(0))
    masked = jnp.where(valid, raw, -jnp.inf)
    new_top = jnp.maximum(top, jnp.max(masked, axis=-1))
    probs = jnp.exp(masked - new_top[..., None])
    total = jnp.sum(probs, axis=-1)
    acc = jnp.einsum(
        "sgrtc,csgd->sgrtd",
        rounded(probs),
        value_rows.reshape(count, seq_count, kv_heads, head_dim),
        preferred_element_type=jnp.float32,
    )
    state = (new_top, total, acc)
    top, total, acc = state
    attn_out = acc / total[..., None]
    log_total = top + jnp.log(total)
    mixed_b = rounded(jnp.transpose(attn_out, (3, 0, 1, 2, 4)).reshape(rows, q_heads * head_dim))
    middle = stream + product(mixed_b, wo)
    factor_two = rms_factor(middle)
    normed_two = rounded(middle * factor_two * gain_ffn)
    gate = product(normed_two, wg)
    up_part = product(normed_two, wu)
    sigma = jax.nn.sigmoid(gate)
    swish = gate * sigma
    hidden_b = rounded(swish * up_part)
    result = middle + product(hidden_b, wd)
    output = rounded(result).reshape(slice_len, seq_count, width)
    wq, key_matrix, value_matrix, wo, wg, wu, wd = (
        lax.all_gather(shards[0], ("seq", "batch"), axis=0, tiled=True),
        lax.all_gather(shards[1], ("seq", "batch"), axis=0, tiled=True),
        lax.all_gather(shards[2], ("seq", "batch"), axis=0, tiled=True),
        lax.all_gather(shards[3], ("seq", "batch"), axis=0, tiled=True),
        lax.all_gather(shards[4], ("seq", "batch"), axis=0, tiled=True),
        lax.all_gather(shards[5], ("seq", "batch"), axis=0, tiled=True),
        lax.all_gather(shards[6], ("seq", "batch"), axis=0, tiled=True),
    )
    grad_res = cotangent.reshape(rows, width).astype(jnp.float32)
    grad_ffo = rounded(grad_res)
    grad_wd = left_product(hidden_b, grad_ffo)
    grad_hidden = right_product(grad_ffo, wd)
    grad_gate = rounded(grad_hidden * up_part * sigma * (1.0 + gate * (1.0 - sigma)))
    grad_up = rounded(grad_hidden * swish)
    grad_wg = left_product(normed_two, grad_gate)
    grad_wu = left_product(normed_two, grad_up)
    grad_normed_two = right_product(grad_gate, wg) + right_product(grad_up, wu)
    grad_gain_ffn = jnp.sum(grad_normed_two * middle * factor_two, axis=0)
    grad_middle = grad_res + norm_back(grad_normed_two * gain_ffn, middle, factor_two)
    grad_branch = rounded(grad_middle)
    grad_wo = left_product(mixed_b, grad_branch)
    grad_mixed = rounded(right_product(grad_branch, wo))
    grad_five = grad_mixed.reshape(slice_len, seq_count, kv_heads, sequence_group, head_dim)
    delta = jnp.sum(
        jnp.transpose(grad_five, (1, 2, 3, 0, 4)).astype(jnp.float32) * attn_out, axis=-1
    )
    gathered = (
        lax.all_gather(key_b, "seq", axis=0, tiled=True),
        lax.all_gather(value_b, "seq", axis=0, tiled=True),
    )

    def back_step(grad_query, item):
        index, keys, value_rows = item
        raw, valid = scores_of(keys, index * slice_len)
        probs = jnp.where(valid, jnp.exp(raw - log_total[..., None]), 0.0)
        key_four = keys.reshape(slice_len, seq_count, kv_heads, head_dim)
        value_four = value_rows.reshape(slice_len, seq_count, kv_heads, head_dim)
        grad_probs = jnp.einsum(
            "tsgrd,csgd->sgrtc", grad_five, value_four, preferred_element_type=jnp.float32
        )
        grad_score = rounded(probs * (grad_probs - delta[..., None]))
        grad_query = (
            grad_query
            + jnp.einsum(
                "sgrtc,csgd->tsgrd", grad_score, key_four, preferred_element_type=jnp.float32
            )
            * scale
        )
        key_term = (
            jnp.einsum(
                "sgrtc,tsgrd->csgd", grad_score, query_five, preferred_element_type=jnp.float32
            )
            * scale
        )
        value_term = jnp.einsum(
            "sgrtc,tsgrd->csgd", rounded(probs), grad_five, preferred_element_type=jnp.float32
        )
        return (
            grad_query,
            (
                key_term.reshape(slice_len, seq_count, kv_width),
                value_term.reshape(slice_len, seq_count, kv_width),
            ),
        )

    items = (
        shard_ids,
        gathered[0].reshape(cycle_size, slice_len, seq_count, kv_width),
        gathered[1].reshape(cycle_size, slice_len, seq_count, kv_width),
    )
    grad_query, terms = lax.scan(
        back_step,
        jnp.zeros((slice_len, seq_count, kv_heads, sequence_group, head_dim), jnp.float32),
        items,
    )
    key_terms = terms[0].reshape(cycle_size * slice_len, seq_count, kv_width)
    value_terms = terms[1].reshape(cycle_size * slice_len, seq_count, kv_width)
    grad_key, grad_value = (
        lax.psum_scatter(
            key_terms.astype(jnp.bfloat16), "seq", scatter_dimension=0, tiled=True
        ).astype(jnp.float32),
        lax.psum_scatter(
            value_terms.astype(jnp.bfloat16), "seq", scatter_dimension=0, tiled=True
        ).astype(jnp.float32),
    )
    grad_qr = (
        rounded(grad_query).astype(jnp.float32).reshape(slice_len, seq_count, q_heads, head_dim)
    )
    grad_qn = rotate_back(grad_qr, cosine, sine)
    grad_gain_query = jnp.sum(grad_qn * query_pre * factor_q, axis=(0, 1, 2))
    grad_qp = rounded(
        norm_back(grad_qn * gain_query, query_pre, factor_q).reshape(rows, q_heads * head_dim)
    )
    grad_kr = (
        rounded(grad_key).astype(jnp.float32).reshape(slice_len, seq_count, kv_heads, head_dim)
    )
    grad_kn = rotate_back(grad_kr, cosine, sine)
    grad_gain_key = jnp.sum(grad_kn * key_before_rotation * factor_k, axis=(0, 1, 2))
    grad_kp = rounded(
        norm_back(grad_kn * gain_key, key_before_rotation, factor_k).reshape(rows, kv_width)
    )
    grad_vp = rounded(grad_value).reshape(rows, kv_width)
    grad_wq = left_product(normalized_input, grad_qp)
    grad_wk = left_product(normalized_input, grad_kp)
    grad_wv = left_product(normalized_input, grad_vp)
    grad_normed = (
        right_product(grad_qp, wq)
        + right_product(grad_kp, key_matrix)
        + right_product(grad_vp, value_matrix)
    )
    grad_gain_attn = jnp.sum(grad_normed * stream * factor_one, axis=0)
    grad_stream = grad_middle + norm_back(grad_normed * gain_attn, stream, factor_one)
    spread = (
        lax.all_to_all(
            split_rows(grad_wq, cycle_size, batch_size).astype(jnp.bfloat16),
            "batch",
            split_axis=1,
            concat_axis=1,
            tiled=True,
        ).astype(jnp.float32),
        lax.all_to_all(
            split_rows(grad_wk, cycle_size, batch_size).astype(jnp.bfloat16),
            "batch",
            split_axis=1,
            concat_axis=1,
            tiled=True,
        ).astype(jnp.float32),
        lax.all_to_all(
            split_rows(grad_wv, cycle_size, batch_size).astype(jnp.bfloat16),
            "batch",
            split_axis=1,
            concat_axis=1,
            tiled=True,
        ).astype(jnp.float32),
        lax.all_to_all(
            split_rows(grad_wo, cycle_size, batch_size).astype(jnp.bfloat16),
            "batch",
            split_axis=1,
            concat_axis=1,
            tiled=True,
        ).astype(jnp.float32),
        lax.all_to_all(
            split_rows(grad_wg, cycle_size, batch_size).astype(jnp.bfloat16),
            "batch",
            split_axis=1,
            concat_axis=1,
            tiled=True,
        ).astype(jnp.float32),
        lax.all_to_all(
            split_rows(grad_wu, cycle_size, batch_size).astype(jnp.bfloat16),
            "batch",
            split_axis=1,
            concat_axis=1,
            tiled=True,
        ).astype(jnp.float32),
        lax.all_to_all(
            split_rows(grad_wd, cycle_size, batch_size).astype(jnp.bfloat16),
            "batch",
            split_axis=1,
            concat_axis=1,
            tiled=True,
        ).astype(jnp.float32),
    )
    partial_sums = [fold_sources(piece) for piece in spread]
    summed = (
        lax.psum_scatter(
            partial_sums[0].astype(jnp.bfloat16), "seq", scatter_dimension=0, tiled=True
        ).astype(jnp.float32),
        lax.psum_scatter(
            partial_sums[1].astype(jnp.bfloat16), "seq", scatter_dimension=0, tiled=True
        ).astype(jnp.float32),
        lax.psum_scatter(
            partial_sums[2].astype(jnp.bfloat16), "seq", scatter_dimension=0, tiled=True
        ).astype(jnp.float32),
        lax.psum_scatter(
            partial_sums[3].astype(jnp.bfloat16), "seq", scatter_dimension=0, tiled=True
        ).astype(jnp.float32),
        lax.psum_scatter(
            partial_sums[4].astype(jnp.bfloat16), "seq", scatter_dimension=0, tiled=True
        ).astype(jnp.float32),
        lax.psum_scatter(
            partial_sums[5].astype(jnp.bfloat16), "seq", scatter_dimension=0, tiled=True
        ).astype(jnp.float32),
        lax.psum_scatter(
            partial_sums[6].astype(jnp.bfloat16), "seq", scatter_dimension=0, tiled=True
        ).astype(jnp.float32),
    )
    gains = lax.psum(
        (grad_gain_attn, grad_gain_ffn, grad_gain_query, grad_gain_key), ("seq", "batch")
    )
    grad_inputs = rounded(grad_stream).reshape(slice_len, seq_count, width)
    return (
        output,
        grad_inputs,
        summed[0],
        summed[1],
        summed[2],
        summed[3],
        summed[4],
        summed[5],
        summed[6],
        gains[0],
        gains[1],
        gains[2],
        gains[3],
    )


def solution(mesh):
    sharded = P(("seq", "batch"), None)
    stream = P("seq", "batch", None)
    in_specs = (stream, P("batch")) + (sharded,) * 7 + (P(),) * 4 + (stream,)
    out_specs = (stream, stream) + (sharded,) * 7 + (P(),) * 4
    grouped = mesh.shape["seq"] == 8 and mesh.shape["batch"] == 4
    step = body if grouped else general_body
    return jax.shard_map(step, mesh=mesh, in_specs=in_specs, out_specs=out_specs, check_vma=False)
```

```python
import functools

import jax
import jax.numpy as jnp
import numpy as np
from jax import lax
from jax.experimental import pallas as pl
from jax.experimental.pallas import tpu as pltpu
from jax.sharding import PartitionSpec as P

MESH = pl.DeviceIdType.MESH
F32 = jnp.float32
BF16 = jnp.bfloat16
eps = 1e-05
theta = 1000000.0
VMEM = pl.BlockSpec(memory_space=pltpu.VMEM)
ANY = pl.BlockSpec(memory_space=pl.ANY)
SMEM = pl.BlockSpec(memory_space=pltpu.SMEM)


def nn(left, right):
    return lax.dot_general(left, right, (((1,), (0,)), ((), ())), preferred_element_type=F32)


def nt(left, right):
    return lax.dot_general(left, right, (((1,), (1,)), ((), ())), preferred_element_type=F32)


def tn(left, right):
    return lax.dot_general(left, right, (((0,), (0,)), ((), ())), preferred_element_type=F32)


def rms_factor(v):
    return lax.rsqrt(jnp.mean(v * v, axis=-1, keepdims=True) + eps)


def norm_back(grad, value, factor):
    return factor * (
        grad - value * factor * factor * jnp.mean(grad * value, axis=-1, keepdims=True)
    )


def lanes(shape):
    return lax.broadcasted_iota(jnp.int32, shape, len(shape) - 1)


def rows_of(shape):
    return lax.broadcasted_iota(jnp.int32, shape, len(shape) - 2)


def head_mean(v):
    first = lanes(v.shape) < 64
    low = jnp.sum(jnp.where(first, v, 0.0), axis=-1, keepdims=True)
    high = jnp.sum(jnp.where(first, 0.0, v), axis=-1, keepdims=True)
    return jnp.where(first, low, high) * (1.0 / 64.0)


def rope(u, cosine, sine):
    early = lax.rem(lanes(u.shape), 64) < 32
    turned = jnp.where(early, -pltpu.roll(u, 96, 1), pltpu.roll(u, 32, 1))
    return u * cosine + turned * sine


def rope_back(u, cosine, sine):
    early = lax.rem(lanes(u.shape), 64) < 32
    w = u * sine
    return u * cosine + jnp.where(early, pltpu.roll(w, 96, 1), -pltpu.roll(w, 32, 1))


class Place:
    def __init__(self, send_sem, recv_sem, local_sem):
        self.s = lax.axis_index("seq")
        self.b = lax.axis_index("batch")
        self.z = self.s // 2
        self.y = lax.rem(self.s, 2)
        self.core = self.b + 1 - 2 * lax.rem(self.b, 2)
        self.across = lax.rem(self.b + 2, 4)
        self.far = 3 - self.b
        self.flip = 2 * self.z + 1 - self.y
        self.inner = jnp.logical_or(self.z == 1, self.z == 2)
        self.pair = self.z + 1 - 2 * lax.rem(self.z, 2)
        self.there = jnp.where(self.z < 2, 2, 1)
        self.beyond = jnp.where(self.z < 2, 3, 0)
        self.send_sem, self.recv_sem, self.local_sem = send_sem, recv_sem, local_sem
        self.used = 0
        self.used_local = 0
        self.sent = []

    def up(self, k):
        return lax.rem(self.z + k, 4)

    def down(self, k):
        return lax.rem(self.z + 4 - k, 4)

    def greet(self):
        self.hello()
        self.meet()

    def hello(self):
        barrier = pltpu.get_barrier_semaphore()
        for k in (1, 2, 3):
            pl.semaphore_signal(
                barrier, inc=1, device_id=(self.s, lax.rem(self.b + k, 4)), device_id_type=MESH
            )
        for k in range(1, 8):
            pl.semaphore_signal(
                barrier, inc=1, device_id=(lax.rem(self.s + k, 8), self.b), device_id_type=MESH
            )

    def meet(self):
        pl.semaphore_wait(pltpu.get_barrier_semaphore(), 10)

    def slots(self, count):
        first = self.used
        self.used += count
        return first

    def copy(self, src, dst, device, out, into=None):
        return pltpu.make_async_remote_copy(
            src_ref=src,
            dst_ref=dst,
            send_sem=self.send_sem.at[out],
            recv_sem=self.recv_sem.at[out if into is None else into],
            device_id=device,
            device_id_type=MESH,
        )

    def post(self, src, dst, device):
        index = self.slots(1)
        made = self.copy(src, dst, device, index)
        made.start()
        self.sent.append(made)
        return index

    def landed(self, index, ref):
        self.copy(ref, ref, (self.s, self.core), index).wait_recv()

    def local(self, src, dst):
        index = self.used_local
        self.used_local += 1
        made = pltpu.make_async_copy(src, dst, self.local_sem.at[index])
        made.start()
        return made

    def drain(self):
        for made in self.sent:
            made.wait_send()
        self.sent = []


class Spread:
    def __init__(self, p, slot):
        self.p, self.slot = p, slot
        self.first = p.slots(8)
        self.from_z = (p.pair, p.there, p.beyond)

    def send(self, s, device, out, into):
        self.p.copy(self.slot(s), self.slot(s), device, self.first + out, self.first + into).start()

    def start(self):
        p = self.p
        self.send(p.s, (2 * p.pair + p.y, p.b), 0, 0)
        self.send(p.s, (2 * p.there + p.y, p.b), 1, jnp.where(p.inner, 1, 2))
        self.send(p.s, (p.flip, p.b), 4, 3)

    def land(self, j):
        p = self.p
        s = 2 * self.from_z[j] + p.y
        p.landed(self.first + j, self.slot(s))
        if j > 0:

            @pl.when(p.inner)
            def _():
                self.send(s, (2 * p.pair + p.y, p.b), 1 + j, j)

        self.send(s, (p.flip, p.b), 5 + j, 4 + j)

    def land_inner(self):
        @pl.when(self.p.inner)
        def _():
            self.land(1)
            self.land(2)

    def land_end(self):
        @pl.when(jnp.logical_not(self.p.inner))
        def _():
            self.land(1)
            self.land(2)

    def finish(self):
        p = self.p
        p.landed(self.first + 3, self.slot(p.flip))
        for j in range(3):
            p.landed(self.first + 4 + j, self.slot(2 * self.from_z[j] + 1 - p.y))

    def drain(self):
        p = self.p

        def sent(out):
            p.copy(self.slot(p.s), self.slot(p.s), (p.flip, p.b), self.first + out).wait_send()

        for out in (0, 1, 4, 5, 6, 7):
            sent(out)

        @pl.when(p.inner)
        def _():
            sent(2)
            sent(3)


def heads_of(whole, kk):
    return whole[:, 256 * kk : 256 * kk + 128], whole[:, 256 * kk + 128 : 256 * kk + 256]


def pack_projections(w_query, key_weight, value_weight, out):
    for c in range(4):
        k = key_weight[:, 128 * c : 128 * c + 128].astype(F32)
        v = value_weight[:, 128 * c : 128 * c + 128].astype(F32)
        first = lanes(k.shape) < 64
        pairs = (
            jnp.where(first, k, pltpu.roll(v, 64, 1)),
            jnp.where(first, pltpu.roll(k, 64, 1), v),
        )
        for kk in (0, 1):
            h = 2 * c + kk
            out[c, :, 256 * kk : 256 * kk + 128] = w_query[:, 128 * h : 128 * h + 128]
            out[c, :, 256 * kk + 128 : 256 * kk + 256] = pairs[kk].astype(BF16)


def pack_hidden(source, out, which):
    wide = source[...].astype(F32)
    for c in range(4):
        pieces = [wide[:, 144 * (4 * i + c) : 144 * (4 * i + c) + 144] for i in range(8)]
        out[c, which] = jnp.concatenate(pieces, axis=1).astype(BF16)


def twice(v):
    return jnp.concatenate([v[...], v[...]], axis=1)


def near_first(p, t):
    return jnp.where(t == 0, p.b, jnp.where(t == 1, p.core, jnp.where(t == 2, p.across, p.far)))


def block_kernel(
    x, dy, lengths, w_query, key_weight, value_weight, w_out, w_gate, w_up, w_down,
    cos_table, sin_table, gain_query, gain_key, gain_a, gain_f,
    output, dx, rqkv, rgu, rd, ro, gains_out, norm_park,
    xa, norm, wqkv, wo, pack, unit, unit_out, lse, kv, mix, dy_all, wgu, wd, gd,
    hid, dgate, dup, dk_sum, dv_sum, parts, recv, recv_o, keep, result, middle,
    qkv_send, gu_send, length, cos, sin, length_all,
    dou, delta,
    y_d, t_d, z_d, y_g, t_g, z_g, y_u, t_u, z_u, y_q, z_q, y_o, z_o,
    gain_sum, gain_batch, gain_seq,
    send_sem, recv_sem, local_sem,
):
    p = Place(send_sem, recv_sem, local_sem)
    s, b, z, y = p.s, p.b, p.z, p.y
    my_rows = pl.ds(pl.multiple_of(32 * b, 32), 32)
    my_positions = pl.ds(pl.multiple_of(256 * s, 256), 256)
    p.hello()
    own_d = p.local(w_down, wd.at[s])
    own_x = p.local(x, xa.at[b])
    own_wo = p.local(w_out, wo.at[s, b])
    own_dy = p.local(dy, dy_all.at[b])
    own_tables = [p.local(cos_table.at[my_positions], cos), p.local(sin_table.at[my_positions], sin)]
    pack_projections(w_query, key_weight, value_weight, qkv_send)
    length[...] = jnp.broadcast_to(lengths[0], (8, 128)).astype(jnp.int32)
    own_qkv = p.local(qkv_send.at[b], wqkv.at[s, my_rows])
    length_all[b] = length[...]
    pack_hidden(w_gate, gu_send, 0)
    pack_hidden(w_up, gu_send, 1)
    p.meet()

    got_qkv, got_len = [], []
    for k in (1, 2, 3):
        to = lax.rem(b + k, 4)
        got_qkv.append(p.post(qkv_send.at[to], wqkv.at[s, my_rows], (s, to)))
    own_x.wait()
    x_across = p.post(xa.at[b], xa.at[b], (s, p.across))
    x_core = p.post(xa.at[b], xa.at[b], (s, p.core))
    for k in (1, 2, 3):
        to = lax.rem(b + k, 4)
        got_len.append(p.post(length, length_all.at[b], (s, to)))
    spread_d = Spread(p, lambda i: wd.at[i])
    spread_g = Spread(p, lambda i: wgu.at[i, 0])
    spread_u = Spread(p, lambda i: wgu.at[i, 1])

    def normalize(g):
        xg = xa[g].astype(F32)
        norm[g] = (xg * rms_factor(xg) * gain_a[...]).astype(BF16)

    normalize(b)
    own_qkv.wait()
    for k in (1, 2, 3):
        p.landed(got_qkv[k - 1], wqkv.at[s, my_rows])
    z_qkv = [p.post(wqkv.at[s], wqkv.at[s], (2 * p.up(k) + y, b)) for k in (1, 2, 3)]
    y_qkv = [p.post(wqkv.at[s], wqkv.at[s], (p.flip, b))]
    own_gu = p.local(gu_send.at[b], wgu.at[s, :, my_rows])
    got_gu = []
    for k in (1, 2, 3):
        to = lax.rem(b + k, 4)
        got_gu.append(p.post(gu_send.at[to], wgu.at[s, :, my_rows], (s, to)))
    for k in (1, 2, 3):
        slot = 2 * p.down(k) + y
        p.landed(z_qkv[k - 1], wqkv.at[slot])
        y_qkv.append(p.post(wqkv.at[slot], wqkv.at[slot], (p.flip, b)))
    own_d.wait()
    spread_d.start()
    own_wo.wait()
    z_wo = [p.post(wo.at[s, b], wo.at[s, b], (2 * p.up(k) + y, b)) for k in (1, 2, 3)]
    y_wo = [p.post(wo.at[s, b], wo.at[s, b], (p.flip, b))]
    p.landed(x_core, xa.at[p.core])
    normalize(p.core)
    p.landed(x_across, xa.at[p.across])
    x_far = p.post(xa.at[p.across], xa.at[p.across], (s, p.core))
    for made in own_tables:
        made.wait()
    p.landed(y_qkv[0], wqkv.at[p.flip])
    for k in (1, 2, 3):
        p.landed(y_qkv[k], wqkv.at[2 * p.down(k) + 1 - y])
    gain_q, gain_k = twice(gain_query), twice(gain_key)

    first_unit = p.slots(8)

    def each_piece(t, kk, act):
        to = 2 * near_first(p, t) + kk

        @pl.when(to != s)
        def _():
            act(p.copy(pack.at[to], unit.at[s], (to, b), first_unit + 2 * t + kk, first_unit + s))

    def project(t, carry):
        g = near_first(p, t)

        @pl.when(t == 3)
        def _():
            p.landed(x_far, xa.at[p.far])

        @pl.when(t >= 2)
        def _():
            normalize(g)

        whole = nn(norm[g], wqkv[...].reshape(1024, 512))
        for kk in (0, 1):
            q, kvp = heads_of(whole, kk)
            qn = q * lax.rsqrt(head_mean(q * q) + eps) * gain_q
            kn = kvp * lax.rsqrt(head_mean(kvp * kvp) + eps) * gain_k
            qr = rope(qn, cos[...], sin[...]) * 0.125
            kr = rope(kn, cos[...], sin[...])
            pack[2 * g + kk, :, 0:128] = qr.astype(BF16)
            pack[2 * g + kk, :, 128:256] = jnp.where(lanes(kr.shape) < 64, kr, kvp).astype(BF16)
            each_piece(t, kk, lambda made: made.start())

        return carry

    lax.fori_loop(0, 4, project, 0)
    own_unit = p.local(pack.at[s], unit.at[s])
    parked = p.local(norm, norm_park)
    for k in (1, 2, 3):
        slot = 2 * p.down(k) + y
        p.landed(z_wo[k - 1], wo.at[slot, b])
        y_wo.append(p.post(wo.at[slot, b], wo.at[slot, b], (p.flip, b)))
    spread_d.land(0)
    spread_d.land_inner()
    own_dy.wait()
    dy_across = p.post(dy_all.at[b], dy_all.at[b], (s, p.across))
    dy_core = p.post(dy_all.at[b], dy_all.at[b], (s, p.core))
    for k in (1, 2, 3):
        p.landed(got_len[k - 1], length_all.at[lax.rem(b + 4 - k, 4)])

    for k in range(1, 8):
        src = lax.rem(s + k, 8)
        p.landed(first_unit + src, unit.at[src])
    own_unit.wait()
    own_gu.wait()
    for k in (1, 2, 3):
        p.landed(got_gu[k - 1], wgu.at[s, :, my_rows])
    spread_g.start()
    spread_u.send(s, (p.flip, b), 4, 3)
    p.landed(y_wo[0], wo.at[p.flip, b])
    for k in (1, 2, 3):
        p.landed(y_wo[k], wo.at[2 * p.down(k) + 1 - y, b])
    wo_across = p.post(wo.at[:, b], wo.at[:, b], (s, p.across))
    wo_core = p.post(wo.at[:, b], wo.at[:, b], (s, p.core))
    spread_d.land_end()

    def values(j):
        return dup.at[j // 2, lax.rem(j, 2), 0:80, 0:256]

    def prepare(j, carry):
        live = j * 256 + rows_of((256, 128)) < length_all[z][0:1, :]
        masked = jnp.where(live, unit[j, :, 128:256].astype(F32), 0.0)
        kv[j] = masked.astype(BF16)
        turned = jnp.transpose(masked)[64:128].astype(BF16)
        alive = j * 256 + lanes((16, 256)) < length_all[z][0:1, 0:1]
        counted = jnp.where(alive, 1.0, 0.0).astype(BF16)
        values(j)[...] = jnp.concatenate([turned, counted], axis=0)
        return carry

    lax.fori_loop(0, 8, prepare, 0)
    p.landed(dy_across, dy_all.at[p.across])
    dy_far = p.post(dy_all.at[p.across], dy_all.at[p.across], (s, p.core))
    first_mix, first_across, first_core = p.slots(8), p.slots(8), p.slots(8)

    def mix_send(src, t):
        p.copy(mix.at[b, src], mix.at[b, src], (s, p.across), first_across + t).start()
        p.copy(mix.at[b, src], mix.at[b, src], (s, p.core), first_core + t).start()

    def mix_arrived(t):
        src = lax.rem(s + 7 - t, 8)
        p.landed(first_mix + t, mix.at[b, src])
        mix_send(src, t)

    def attend(t, carry):
        i = lax.rem(s + 1 + t, 8)
        qt = jnp.transpose(unit[i, :, 0:128].astype(F32)).astype(BF16)
        both = jnp.concatenate([qt[0:64], qt[64:128]], axis=1)
        right = jnp.concatenate([both, jnp.zeros((64, 512), BF16)], axis=0)

        def block(j, acc):
            return acc + nn(values(j)[...], jnp.exp(nn(kv[j], right)).astype(BF16))

        acc = lax.fori_loop(0, i, block, jnp.zeros((80, 512), F32))
        causal = rows_of((256, 512)) <= lax.rem(lanes((256, 512)), 256)
        edge = jnp.where(causal, jnp.exp(nn(kv[i], right)), 0.0).astype(BF16)
        acc = acc + nn(values(i)[...], edge)
        total = acc[64:65]
        out = acc[0:64] / total
        out = jnp.concatenate([out[:, 0:256], out[:, 256:512]], axis=0)
        unit_out[i] = jnp.transpose(out).astype(BF16)
        lse[i] = jnp.broadcast_to(jnp.log(total), (8, 512))

        @pl.when(t < 7)
        def _():
            p.copy(unit_out.at[i], mix.at[b, s], (i, b), first_mix + t).start()

        @pl.when(t == 2)
        def _():
            spread_u.send(s, (2 * p.pair + y, b), 0, 0)
            spread_u.send(s, (2 * p.there + y, b), 1, jnp.where(p.inner, 1, 2))

        @pl.when(t == 5)
        def _():
            spread_g.land(0)
            spread_g.land_inner()

        @pl.when(t >= 4)
        def _():
            mix_arrived(t - 4)

        return carry

    lax.fori_loop(0, 8, attend, 0)
    own_mix = p.local(unit_out.at[s], mix.at[b, s])
    own_mix.wait()
    mix_send(s, 7)
    for t in range(4, 7):
        mix_arrived(t)
    spread_g.land_end()
    spread_u.land(0)
    spread_u.land_inner()
    p.landed(dy_core, dy_all.at[p.core])
    p.landed(dy_far, dy_all.at[p.far])
    spread_d.finish()

    def hidden_back(g, carry):
        rows = pl.ds(pl.multiple_of(g * 256, 256), 256)
        dgate[g] = nt(dy_all[g], wd[...].reshape(1152, 1024)).astype(BF16).reshape(2, 128, 1152)
        return carry

    lax.fori_loop(0, 4, hidden_back, 0)
    p.landed(wo_across, wo.at[:, p.across])
    wo_far = p.post(wo.at[:, p.across], wo.at[:, p.across], (s, p.core))
    for t in range(8):
        p.landed(first_across + t, mix.at[p.across, lax.rem(s + 7 - t, 8)])
    mix_far = p.post(mix.at[p.across], mix.at[p.across], (s, p.core))
    for t in range(8):
        p.landed(first_core + t, mix.at[p.core, lax.rem(s + 7 - t, 8)])
    p.landed(wo_core, wo.at[:, p.core])
    p.landed(wo_far, wo.at[:, p.far])
    spread_u.land_end()
    p.landed(mix_far, mix.at[p.far])

    parked.wait()

    def project_out(g, carry):
        mixed = jnp.concatenate([mix[c, 2 * g + kk] for c in range(4) for kk in (0, 1)], axis=1)
        mid = xa[g].astype(F32) + nn(mixed, wo[...].reshape(1024, 1024))
        norm[g] = (mid * rms_factor(mid) * gain_f[...]).astype(BF16)

        @pl.when(g == b)
        def _():
            middle[...] = mid

        return carry

    lax.fori_loop(0, 4, project_out, 0)

    for t in range(8):
        if t < 7:
            p.copy(unit_out.at[s], mix.at[b, s], (p.flip, b), first_mix + t).wait_send()
        p.copy(mix.at[b, s], mix.at[b, s], (s, p.across), first_across + t).wait_send()
        p.copy(mix.at[b, s], mix.at[b, s], (s, p.core), first_core + t).wait_send()
    for t in range(4):
        for kk in (0, 1):
            each_piece(t, kk, lambda made: made.wait_send())
    p.drain()

    def turn(e, carry):
        for g in range(4):
            hid[0:128, 256 * g : 256 * g + 256] = jnp.transpose(
                mix[e // 2, 2 * g + lax.rem(e, 2)].astype(F32)
            ).astype(BF16)
        gu_send[e // 2, lax.rem(e, 2), :, 0:1024] = hid[my_rows, 0:1024]
        return carry

    lax.fori_loop(0, 8, turn, 0)
    spread_g.finish()

    def gate_of(g, carry):
        rows = pl.ds(pl.multiple_of(g * 256, 256), 256)
        hid[rows] = nn(norm[g], wgu[:, 0].reshape(1024, 1152)).astype(BF16)
        return carry

    lax.fori_loop(0, 4, gate_of, 0)
    spread_u.finish()
    first_n = p.slots(3)

    def gated(t, carry):
        g = batch_order(p, t)
        rows = pl.ds(pl.multiple_of(g * 256, 256), 256)
        gate = hid[rows].astype(F32)
        up = nn(norm[g], wgu[:, 1].reshape(1024, 1152))
        dh = dgate[g].reshape(256, 1152).astype(F32)
        sg = 1.0 / (1.0 + jnp.exp(-gate))
        swish = gate * sg
        hid[rows] = (swish * up).astype(BF16)
        dg = (dh * up * sg * (1.0 + gate * (1.0 - sg))).astype(BF16)
        du = (dh * swish).astype(BF16)
        dgate[g] = dg.reshape(2, 128, 1152)
        dup[g] = du.reshape(2, 128, 1152)
        part = nt(dg, wgu[:, 0].reshape(1024, 1152)) + nt(du, wgu[:, 1].reshape(1024, 1152))
        parts[g] = part.astype(BF16)

        @pl.when(t == 3)
        def _():
            keep[...] = part

        chip_sum_post(p, t, parts, recv, first_n)
        return carry

    lax.fori_loop(0, 4, gated, 0)
    chip_sum_across(p, parts, recv, first_n)

    def down_rows(c, carry):
        at = pl.multiple_of(128 * c, 128)
        gd[pl.ds(at, 128)] = tn(hid[:, pl.ds(at, 128)], dy_all[...].reshape(1024, 1024)).astype(BF16)
        return carry

    lax.fori_loop(0, 9, down_rows, 0)
    sum_d = SeqTree(
        p, lambda i: gd.at[pl.ds(pl.multiple_of(144 * i, 16), 144)], y_d, t_d, z_d
    )
    sum_g = SeqTree(p, lambda i: wgu.at[i, 0], y_g, t_g, z_g)
    sum_u = SeqTree(p, lambda i: wgu.at[i, 1], y_u, t_u, z_u)
    sum_d.start()

    for spread in (spread_d, spread_g, spread_u):
        spread.drain()

    def gate_rows(c, carry):
        at = pl.multiple_of(128 * c, 128)
        side = norm[:, :, pl.ds(at, 128)].reshape(1024, 128)
        wgu[c, 0] = tn(side, dgate[...].reshape(1024, 1152)).astype(BF16)
        wgu[c, 1] = tn(side, dup[...].reshape(1024, 1152)).astype(BF16)
        return carry

    lax.fori_loop(0, 8, gate_rows, 0)
    load_norm = p.local(norm_park, norm)

    mid = middle[...]
    r2 = rms_factor(mid)
    grad_two = keep[...] + chip_sum_rest(p, parts, recv, first_n)
    gain_sum[...] = jnp.zeros((8, 1024), F32)
    gain_sum[1:2] = jnp.sum(grad_two * mid * r2, axis=0, keepdims=True)
    dm = dy_all[b].astype(F32) + norm_back(grad_two * gain_f[...], mid, r2)
    result[...] = mid
    middle[...] = dm
    xa[b] = dm.astype(BF16)

    first_mixed = p.slots(3)

    def mixed_back(t, carry):
        c = batch_order(p, t)
        place = jnp.where(t == 3, 1, 0)
        for kk in (0, 1):
            mix[place, 2 * c + kk] = nt(xa[b], wo[2 * c + kk].reshape(128, 1024)).astype(BF16)

        @pl.when(t < 3)
        def _():
            p.copy(
                mix.at[0, pl.ds(2 * c, 2)], mix.at[1, pl.ds(2 * b, 2)], (s, c), first_mixed + t
            ).start()

        return carry

    lax.fori_loop(0, 4, mixed_back, 0)
    dbr_across = p.post(xa.at[b], xa.at[b], (s, p.across))
    dbr_core = p.post(xa.at[b], xa.at[b], (s, p.core))
    def down(g, carry):
        part = nn(hid[pl.ds(pl.multiple_of(g * 256, 256), 256)], wd[...].reshape(1152, 1024))
        dy_all[g] = part.astype(BF16)

        @pl.when(g == b)
        def _():
            result[...] = result[...] + part

        return carry

    lax.fori_loop(0, 4, down, 0)

    first_o = p.slots(3)
    chip_sum_post(p, 0, dy_all, recv_o, first_o)
    chip_sum_post(p, 1, dy_all, recv_o, first_o)
    def q_right(i):
        return hid.at[pl.ds(pl.multiple_of(128 * i, 128), 128), 0:512]

    def do_right(i):
        return hid.at[pl.ds(pl.multiple_of(128 * i, 128), 128), 512:1024]

    def tall(i, base):
        half = pl.ds(2 * lax.rem(i, 2), 2)
        return dgate.at[half, :, :, pl.ds(pl.multiple_of(base + 128 * (i // 2), 128), 128)]

    def q_left(i):
        return tall(i, 0)

    def do_left(i):
        return tall(i, 512)

    def dk2(i):
        return dk_sum.at[i]

    def dv2(i):
        return dv_sum.at[i]

    def dq2(i):
        rows = pl.ds(pl.multiple_of(64 * lax.rem(i, 4), 64), 64)
        return keep.at[rows, pl.ds(pl.multiple_of(512 * (i // 4), 512), 512)]

    def keys_turned(i):
        return dup.at[i // 2, lax.rem(i, 2), 0:64, 0:256]

    def prepare_back(i, carry):
        keys_turned(i)[...] = jnp.transpose(kv[i].astype(F32))[0:64].astype(BF16)
        q = unit[i, :, 0:128].astype(F32)
        qt = jnp.transpose(q).astype(BF16)
        both = jnp.concatenate([qt[0:64], qt[64:128]], axis=1)
        q_right(i)[...] = jnp.concatenate([both, jnp.zeros((64, 512), BF16)], axis=0)
        first = lanes(q.shape) < 64
        both = jnp.concatenate([jnp.where(first, q, 0.0), jnp.where(first, 0.0, q)], axis=0)
        q_left(i)[...] = both.astype(BF16).reshape(2, 2, 128, 128)
        dq2(i)[...] = jnp.zeros((64, 512), F32)
        dk2(i)[...] = jnp.zeros((256, 128), F32)
        dv2(i)[...] = jnp.zeros((256, 128), F32)
        return carry

    lax.fori_loop(0, 8, prepare_back, 0)
    first_do = p.slots(8)

    def grad_piece(t, kk, act):
        to = 2 * near_first(p, t) + kk

        @pl.when(to != s)
        def _():
            act(p.copy(mix.at[1, to], dou.at[s], (to, b), first_do + 2 * t + kk, first_do + s))

    for t, index in ((0, None), (1, 1), (2, 2), (3, 0)):
        if index is not None:
            p.landed(first_mixed + index, mix.at[1, pl.ds(2 * near_first(p, t), 2)])
        for kk in (0, 1):
            grad_piece(t, kk, lambda made: made.start())
    dou[s] = mix[1, s]

    chip_sum_across(p, dy_all, recv_o, first_o)
    sum_d.reduce()
    sum_g.start()
    for k in range(1, 8):
        src = lax.rem(s + k, 8)
        p.landed(first_do + src, dou.at[src])

    def prepare_grad(i, carry):
        do = dou[i].astype(F32)
        dot = jnp.transpose(do)
        right = jnp.concatenate([dot[0:64], dot[64:128]], axis=1).astype(BF16)
        do_right(i)[...] = jnp.concatenate([jnp.zeros((64, 512), BF16), right], axis=0)
        first = lanes(do.shape) < 64
        tall_do = jnp.concatenate([jnp.where(first, do, 0.0), jnp.where(first, 0.0, do)], axis=0)
        do_left(i)[...] = tall_do.astype(BF16).reshape(2, 2, 128, 128)
        both = dot * jnp.transpose(unit_out[i].astype(F32))
        low = jnp.sum(both[0:64], axis=0, keepdims=True)
        high = jnp.sum(both[64:128], axis=0, keepdims=True)
        delta[i] = jnp.broadcast_to(jnp.concatenate([low, high], axis=1), (8, 512))
        return carry

    lax.fori_loop(0, 8, prepare_grad, 0)

    def meet(i, j, probs):
        ds = (probs * (nn(kv[j], do_right(i)[...]) - delta[i][0:1])).astype(BF16)
        dv2(j)[...] += nn(probs.astype(BF16), do_left(i)[...].reshape(512, 128))
        dk2(j)[...] += nn(ds, q_left(i)[...].reshape(512, 128))
        dq2(i)[...] += nn(keys_turned(j)[...], ds)

    first_back = p.slots(8)

    def blocks(t, carry):
        c = lax.rem(s + 1 + t, 8)
        causal = rows_of((256, 512)) <= lax.rem(lanes((256, 512)), 256)
        meet(c, c, jnp.where(causal, jnp.exp(nn(kv[c], q_right(c)[...]) - lse[c][0:1]), 0.0))

        def other(u, inner_carry):
            o = lax.rem(s + 1 + u, 8)
            i, j = jnp.maximum(c, o), jnp.minimum(c, o)
            meet(i, j, jnp.exp(nn(kv[j], q_right(i)[...]) - lse[i][0:1]))
            return inner_carry

        lax.fori_loop(t + 1, 8, other, 0)
        acc = dq2(c)[...]
        dq = jnp.concatenate([acc[:, 0:256], acc[:, 256:512]], axis=0) * 0.125
        pack[c, :, 0:128] = jnp.transpose(dq).astype(BF16)
        live = c * 256 + rows_of((256, 128)) < length_all[z][0:1, :]
        dk, dv = dk2(c)[...], dv2(c)[...]
        dk = dk + pltpu.roll(dk, 64, 1)
        dv = dv + pltpu.roll(dv, 64, 1)
        dkv = jnp.where(lanes((256, 128)) < 64, dk, dv)
        pack[c, :, 128:256] = jnp.where(live, dkv, 0.0).astype(BF16)

        @pl.when(t < 7)
        def _():
            p.copy(pack.at[c], unit.at[s], (c, b), first_back + t).start()

        @pl.when(t == 0)
        def _():
            p.landed(dbr_across, xa.at[p.across])
            p.copy(xa.at[p.across], xa.at[p.across], (s, p.core), dbr_far).start()

        @pl.when(t == 4)
        def _():
            sum_d.relay()

        return carry

    dbr_far = p.slots(1)
    lax.fori_loop(0, 8, blocks, 0)
    unit[s] = pack[s]

    p.landed(dbr_core, xa.at[p.core])
    p.landed(dbr_far, xa.at[p.far])
    out_rows = nn(gu_send[:, :, :, 0:1024].reshape(256, 1024), xa[...].reshape(1024, 1024)).astype(BF16)
    for e in range(8):
        dgate[e // 2, e % 2, 0:32, 0:1024] = out_rows[32 * e : 32 * e + 32]
    sum_o = SeqSum(p, y_o, z_o)
    sum_o.start(dgate.at[:, :, 0:32, 0:1024])
    load_x = p.local(x, xa.at[p.far])
    sum_g.reduce()
    sum_u.start()
    load_norm.wait()

    first_n = p.slots(3)
    zero_row = jnp.zeros((1, 128), F32)

    def heads(t, carry):
        sum_q, sum_k = carry
        unit_of = lax.rem(s + 7 - t, 8)

        @pl.when(t < 7)
        def _():
            p.landed(first_back + t, unit.at[unit_of])

        g = unit_of // 2
        at = pl.multiple_of(256 * lax.rem(unit_of, 2), 256)
        whole = nn(norm[g], wqkv[:, :, pl.ds(at, 256)].reshape(1024, 256))
        q, k = heads_of(whole, 0)
        rq = lax.rsqrt(head_mean(q * q) + eps)
        rk = lax.rsqrt(head_mean(k * k) + eps)
        dq = rope_back(unit[unit_of, :, 0:128].astype(F32), cos[...], sin[...])
        dkv = unit[unit_of, :, 128:256].astype(F32)
        dk = rope_back(dkv, cos[...], sin[...])
        sum_q = sum_q + jnp.sum(dq * q * rq, axis=0, keepdims=True)
        sum_k = sum_k + jnp.sum(dk * k * rk, axis=0, keepdims=True)
        dq = dq * gain_q
        dk = dk * gain_k
        dq = rq * (dq - q * rq * rq * head_mean(dq * q))
        dk = rk * (dk - k * rk * rk * head_mean(dk * k))
        dup[g, :, :, pl.ds(at, 128)] = dq.astype(BF16).reshape(2, 128, 128)
        dkv = jnp.where(lanes(dk.shape) < 64, dk, dkv).astype(BF16)
        dup[g, :, :, pl.ds(pl.multiple_of(at + 128, 128), 128)] = dkv.reshape(2, 128, 128)
        return (sum_q, sum_k)

    sum_q, sum_k = lax.fori_loop(0, 8, heads, (zero_row, zero_row))

    gain_sum[2:3, 0:128] = sum_q
    gain_sum[3:4, 0:128] = sum_k
    def qkv_rows(c, carry):
        at = pl.multiple_of(128 * c, 128)
        side = norm[:, :, pl.ds(at, 128)].reshape(1024, 128)
        dup[c // 2, lax.rem(c, 2), :, 512:1024] = tn(side, dup[:, :, :, 0:512].reshape(1024, 512)).astype(BF16)
        return carry

    lax.fori_loop(0, 8, qkv_rows, 0)
    sum_qkv = SeqSum(p, y_q, z_q)
    sum_qkv.start(dup.at[:, :, :, pl.ds(512, 512)])
    sum_g.relay()

    def stream_back(t, carry):
        g = batch_order(p, t)
        part = nt(dup[g, :, :, 0:512].reshape(256, 512), wqkv[...].reshape(1024, 512))
        parts[g] = part.astype(BF16)

        @pl.when(t == 3)
        def _():
            keep[...] = part

        chip_sum_post(p, t, parts, recv, first_n)
        return carry

    lax.fori_loop(0, 4, stream_back, 0)
    chip_sum_across(p, parts, recv, first_n)
    sum_o.middle()
    sum_u.reduce()
    xa[p.core] = (result[...] + chip_sum_rest(p, dy_all, recv_o, first_o)).astype(BF16)
    leave = [p.local(xa.at[p.core], output)]
    sum_qkv.middle()

    dn1 = keep[...] + chip_sum_rest(p, parts, recv, first_n)
    load_x.wait()
    xf = xa[p.far].astype(F32)
    r1 = rms_factor(xf)
    gain_sum[0:1] = jnp.sum(dn1 * xf * r1, axis=0, keepdims=True)
    xa[p.far] = (middle[...] + norm_back(dn1 * gain_a[...], xf, r1)).astype(BF16)
    leave.append(p.local(xa.at[p.far], dx))
    got_gain = [p.post(gain_sum, gain_batch.at[b], (s, lax.rem(b + k, 4))) for k in (1, 2, 3)]
    gain_batch[b] = gain_sum[...]
    sum_u.relay()

    rd[...] = sum_d.finish()

    def exchange(total, own, dst):
        for c in range(4):
            own(c)[...] = total[32 * c : 32 * c + 32].astype(BF16)
        got = []
        for k in (1, 2, 3):
            to = lax.rem(b + k, 4)
            got.append(p.post(own(to), dst(b), (s, to)))
        dst(b)[...] = own(b)[...]
        return got

    def arrive(got, dst):
        for k in (1, 2, 3):
            p.landed(got[k - 1], dst(lax.rem(b + 4 - k, 4)))

    dst_g, dst_u, dst_q = (lambda i: rgu.at[i, 0]), (lambda i: rgu.at[i, 1]), (lambda i: rqkv.at[i])
    got_g = exchange(sum_g.finish(), lambda c: gu_send.at[c, 0], dst_g)
    for k in (1, 2, 3):
        p.landed(got_gain[k - 1], gain_batch.at[lax.rem(b + 4 - k, 4)])
    gain_seq[s] = (gain_batch[0] + gain_batch[1]) + (gain_batch[2] + gain_batch[3])
    got_all = [p.post(gain_seq.at[s], gain_seq.at[s], (lax.rem(s + k, 8), b)) for k in range(1, 8)]
    got_u = exchange(sum_u.finish(), lambda c: gu_send.at[c, 1], dst_u)
    ro[...] = sum_o.finish()
    got_q = exchange(sum_qkv.finish(), lambda c: qkv_send.at[c], dst_q)
    for k in range(1, 8):
        p.landed(got_all[k - 1], gain_seq.at[lax.rem(s + 8 - k, 8)])
    total = gain_seq[0]
    for k in range(1, 8):
        total = total + gain_seq[k]
    gains_out[...] = total
    arrive(got_g, dst_g)
    arrive(got_u, dst_u)
    arrive(got_q, dst_q)
    for t in range(4):
        for kk in (0, 1):
            grad_piece(t, kk, lambda made: made.wait_send())
    for t in range(7):
        p.copy(pack.at[s], unit.at[s], (p.flip, b), first_back + t).wait_send()
    for made in leave:
        made.wait()
    p.copy(xa.at[b], xa.at[b], (s, p.core), dbr_far).wait_send()
    for t in range(3):
        p.copy(mix.at[0, 0:2], mix.at[0, 0:2], (s, p.core), first_mixed + t).wait_send()
    p.drain()


def chip_sum_post(p, t, parts, recv, first):
    @pl.when(jnp.equal(t, 0))
    def _():
        p.copy(parts.at[p.far], recv.at[0], (p.s, p.core), first).start()

    @pl.when(jnp.equal(t, 1))
    def _():
        p.copy(parts.at[p.core], recv.at[1], (p.s, p.core), first + 1).start()


def chip_sum_across(p, parts, recv, first):
    p.copy(recv.at[0], recv.at[0], (p.s, p.core), first).wait_recv()
    parts[p.across] = (parts[p.across].astype(F32) + recv[0].astype(F32)).astype(BF16)
    p.copy(parts.at[p.across], recv.at[2], (p.s, p.across), first + 2).start()


def chip_sum_rest(p, parts, recv, first):
    p.copy(recv.at[1], recv.at[1], (p.s, p.core), first + 1).wait_recv()
    p.copy(recv.at[2], recv.at[2], (p.s, p.core), first + 2).wait_recv()
    for k in range(3):
        p.copy(parts.at[p.b], recv.at[k], (p.s, p.core), first + k).wait_send()
    return recv[1].astype(F32) + recv[2].astype(F32)


def batch_order(p, t):
    return jnp.where(t == 0, p.far, jnp.where(t == 1, p.core, jnp.where(t == 2, p.across, p.b)))


class SeqTree:
    def __init__(self, p, slot, y_recv, relayed, z_recv):
        self.p, self.slot, self.y_recv, self.relayed, self.z_recv = p, slot, y_recv, relayed, z_recv
        self.first = p.slots(8)

    def mine(self, i):
        return self.slot(2 * i + self.p.y)[...].astype(F32)

    def start(self):
        p = self.p
        for i in range(4):
            p.copy(
                self.slot(2 * i + 1 - p.y), self.y_recv.at[i], (p.flip, p.b), self.first + 4 + i
            ).start()

    def send(self, i, dst, z, out, into):
        p = self.p
        p.copy(self.y_recv.at[i], dst, (2 * z + p.y, p.b), self.first + out, self.first + into).start()

    def reduce(self):
        p = self.p
        for i in range(4):
            p.landed(self.first + 4 + i, self.y_recv.at[i])

        def add(i):
            self.y_recv[i] = (self.y_recv[i].astype(F32) + self.mine(i)).astype(BF16)

        add(p.there)
        add(p.beyond)

        @pl.when(jnp.logical_not(p.inner))
        def _():
            self.send(p.there, self.relayed.at[0], p.pair, 1, 1)
            self.send(p.beyond, self.relayed.at[1], p.pair, 2, 2)

        add(p.pair)
        self.send(p.pair, self.z_recv.at[0], p.pair, 0, 0)

    def relay(self):
        p = self.p

        @pl.when(p.inner)
        def _():
            for k, i in ((0, p.there), (1, p.beyond)):
                p.landed(self.first + 1 + k, self.relayed.at[k])
                self.y_recv[i] = (self.y_recv[i].astype(F32) + self.relayed[k].astype(F32)).astype(BF16)
                self.send(i, self.z_recv.at[1], i, 1 + k, 3)

    def finish(self):
        p = self.p
        total = self.y_recv[p.z].astype(F32) + self.mine(p.z)
        p.landed(self.first, self.z_recv.at[0])
        total = total + self.z_recv[0].astype(F32)
        p.landed(self.first + 3, self.z_recv.at[1])
        for out in range(3):
            p.copy(self.z_recv.at[0], self.z_recv.at[0], (p.flip, p.b), self.first + out).wait_send()
        for i in range(4):
            p.copy(self.y_recv.at[i], self.y_recv.at[i], (p.flip, p.b), self.first + 4 + i).wait_send()
        return total + self.z_recv[1].astype(F32)


class SeqSum:
    def __init__(self, p, y_recv, z_recv):
        self.p, self.y_recv, self.z_recv = p, y_recv, z_recv

    def start(self, source, mine=None):
        p = self.p
        self.index = p.post(source.at[:, 1 - p.y], self.y_recv, (p.flip, p.b))
        self.load = None
        if mine is None:
            self.mine = lambda i: source.at[i, p.y]
        else:
            self.load = p.local(source.at[:, p.y], mine)
            self.mine = lambda i: mine.at[i]

    def middle(self):
        p = self.p
        if self.load is not None:
            self.load.wait()
        p.landed(self.index, self.y_recv)
        self.far = []
        for k in (1, 2, 3):
            i = p.up(k)
            self.y_recv[i] = (self.y_recv[i].astype(F32) + self.mine(i)[...].astype(F32)).astype(BF16)
            self.far.append(p.post(self.y_recv.at[i], self.z_recv.at[k - 1], (2 * i + p.y, p.b)))

    def finish(self):
        p = self.p
        total = self.y_recv[p.z].astype(F32) + self.mine(p.z)[...].astype(F32)
        for k in (1, 2, 3):
            p.landed(self.far[k - 1], self.z_recv.at[k - 1])
            total = total + self.z_recv[k - 1].astype(F32)
        return total


def finish_kernel(
    output, dx, rqkv, rgu, rd, ro, gains,
    output_, dx_, grad_query, grad_key, grad_value, grad_out, grad_gate, grad_up, grad_down,
    gain_attn, gain_ffn, gain_query, gain_key,
):
    output_[...] = output[...]
    dx_[...] = dx[...]
    grad_out[...] = ro[...]
    grad_down[...] = rd[...]
    for c in range(4):
        pairs = []
        for kk in (0, 1):
            h = 2 * c + kk
            q, kv = heads_of(rqkv[c].astype(F32), kk)
            grad_query[:, 128 * h : 128 * h + 128] = q
            pairs.append(kv)
        first = lanes(pairs[0].shape) < 64
        grad_key[:, 128 * c : 128 * c + 128] = jnp.where(first, pairs[0], pltpu.roll(pairs[1], 64, 1))
        grad_value[:, 128 * c : 128 * c + 128] = jnp.where(first, pltpu.roll(pairs[0], 64, 1), pairs[1])
    for which, out in ((0, grad_gate), (1, grad_up)):
        wide = [rgu[c, which].astype(F32) for c in range(4)]
        out[...] = jnp.concatenate(
            [wide[c][:, 144 * i : 144 * i + 144] for i in range(8) for c in range(4)], axis=1
        )
    gain_attn[...] = gains[0:1]
    gain_ffn[...] = gains[1:2]
    gain_query[...] = gains[2:3, 0:64] + gains[2:3, 64:128]
    gain_key[...] = gains[3:4, 0:64]


def call(kernel, outs, in_specs, out_specs, scratch, cid, sems):
    return pl.pallas_call(
        kernel,
        out_shape=[jax.ShapeDtypeStruct(shape, dtype) for shape, dtype in outs],
        in_specs=in_specs,
        out_specs=out_specs,
        scratch_shapes=[pltpu.VMEM(shape, dtype) for shape, dtype in scratch]
        + [
            pltpu.SemaphoreType.DMA((sems[0],)),
            pltpu.SemaphoreType.DMA((sems[0],)),
            pltpu.SemaphoreType.DMA((sems[1],)),
        ],
        compiler_params=pltpu.CompilerParams(
            collective_id=cid, has_side_effects=True, vmem_limit_bytes=64 * 2**20
        ),
    )


def body(
    inputs, lengths, w_query, key_weight, value_weight, w_out, w_gate, w_up, w_down,
    gain_attn, gain_ffn, gain_query, gain_key, cotangent,
):
    x = inputs.reshape(256, 1024)
    dy = cotangent.reshape(256, 1024)
    freqs = theta ** (-(np.arange(32, dtype=np.float32) * 2.0) / 64)
    angles = np.arange(2048, dtype=np.float32)[:, None] * freqs.astype(np.float32)[None, :]
    cosine = jnp.asarray(np.tile(np.cos(angles), (1, 4)), F32)
    sine = jnp.asarray(np.tile(np.sin(angles), (1, 4)), F32)
    gains = [g[None] for g in (gain_query, gain_key, gain_attn, gain_ffn)]

    raw = call(
        block_kernel,
        [
            ((256, 1024), BF16), ((256, 1024), BF16), ((4, 32, 512), BF16), ((4, 2, 32, 1152), BF16),
            ((144, 1024), F32), ((32, 1024), F32), ((8, 1024), F32), ((4, 256, 1024), BF16),
        ],
        [ANY, ANY, SMEM] + [VMEM] * 6 + [ANY] * 3 + [VMEM] * 4,
        [ANY] * 2 + [VMEM] * 5 + [ANY],
        [
            ((4, 256, 1024), BF16), ((4, 256, 1024), BF16), ((8, 128, 512), BF16), ((8, 4, 32, 1024), BF16),
            ((8, 256, 256), BF16), ((8, 256, 256), BF16), ((8, 256, 128), BF16), ((8, 8, 512), F32),
            ((8, 256, 128), BF16), ((4, 8, 256, 128), BF16),
            ((4, 256, 1024), BF16), ((8, 2, 128, 1152), BF16), ((8, 144, 1024), BF16), ((1152, 1024), BF16),
            ((1024, 1152), BF16), ((4, 2, 128, 1152), BF16), ((4, 2, 128, 1152), BF16),
            ((8, 256, 128), F32), ((8, 256, 128), F32),
            ((4, 256, 1024), BF16), ((3, 256, 1024), BF16), ((3, 256, 1024), BF16),
            ((256, 1024), F32), ((256, 1024), F32), ((256, 1024), F32),
            ((4, 32, 512), BF16), ((4, 2, 32, 1152), BF16), ((8, 128), jnp.int32),
            ((256, 128), F32), ((256, 128), F32), ((4, 8, 128), jnp.int32),
            ((8, 256, 128), BF16), ((8, 8, 512), F32),
            ((4, 144, 1024), BF16), ((2, 144, 1024), BF16), ((2, 144, 1024), BF16),
            ((4, 128, 1152), BF16), ((2, 128, 1152), BF16), ((2, 128, 1152), BF16),
            ((4, 128, 1152), BF16), ((2, 128, 1152), BF16), ((2, 128, 1152), BF16),
            ((4, 128, 512), BF16), ((3, 128, 512), BF16), ((4, 32, 1024), BF16), ((3, 32, 1024), BF16),
            ((8, 1024), F32), ((4, 8, 1024), F32), ((8, 8, 1024), F32),
        ],
        0,
        (256, 32),
    )(x, dy, lengths, w_query, key_weight, value_weight, w_out, w_gate, w_up, w_down, cosine, sine, *gains)
    done = pl.pallas_call(
        finish_kernel,
        out_shape=[
            jax.ShapeDtypeStruct(shape, dtype)
            for shape, dtype in (
                ((256, 1024), BF16), ((256, 1024), BF16), ((32, 1024), F32), ((32, 512), F32),
                ((32, 512), F32), ((32, 1024), F32), ((32, 4608), F32), ((32, 4608), F32),
                ((144, 1024), F32), ((1, 1024), F32), ((1, 1024), F32), ((1, 64), F32), ((1, 64), F32),
            )
        ],
        in_specs=[VMEM] * 7,
        out_specs=[VMEM] * 13,
    )(*raw[:7])
    return (
        done[0].reshape(256, 1, 1024), done[1].reshape(256, 1, 1024), *done[2:9], *[g[0] for g in done[9:]],
    )


def rotary_tables(positions, width):
    half = width // 2
    freqs = theta ** (-(jnp.arange(half, dtype=jnp.float32) * 2.0) / width)
    angles = positions.astype(jnp.float32)[:, None] * freqs[None, :]
    cosine = jnp.concatenate([jnp.cos(angles), jnp.cos(angles)], axis=-1)
    sine = jnp.concatenate([jnp.sin(angles), jnp.sin(angles)], axis=-1)
    return (cosine, sine)


def rotate(v, cosine, sine):
    half = v.shape[-1] // 2
    turned = jnp.concatenate([-v[..., half:], v[..., :half]], axis=-1)
    return v * cosine + turned * sine


def rotate_back(grad, cosine, sine):
    half = grad.shape[-1] // 2
    moved = grad * sine
    return grad * cosine + jnp.concatenate([moved[..., half:], -moved[..., :half]], axis=-1)


def product(left, right):
    return jnp.dot(left, right, preferred_element_type=jnp.float32)


def left_product(left, right):
    return jnp.einsum("rd,rn->dn", left, right, preferred_element_type=jnp.float32)


def right_product(left, right):
    return jnp.einsum("rn,dn->rd", left, right, preferred_element_type=jnp.float32)


def rounded(v):
    return v.astype(jnp.bfloat16)


def split_rows(term, seq_size, batch_size):
    return term.reshape(
        seq_size, batch_size, term.shape[0] // (seq_size * batch_size), term.shape[1]
    )


def fold_sources(piece):
    return jnp.sum(piece, axis=1).reshape(-1, piece.shape[-1])


def general_body(
    inputs,
    lengths,
    w_query,
    key_weight,
    value_weight,
    w_out,
    w_gate,
    w_up,
    w_down,
    gain_attn,
    gain_ffn,
    gain_query,
    gain_key,
    cotangent,
):
    slice_len, seq_count, width = inputs.shape
    rows = slice_len * seq_count
    head_dim = gain_query.shape[0]
    kv_width = key_weight.shape[1]
    kv_heads = kv_width // head_dim
    q_heads = w_query.shape[1] // head_dim
    sequence_group = q_heads // kv_heads
    scale = head_dim ** (-0.5)
    cycle_size = lax.axis_size("seq")
    batch_size = lax.axis_size("batch")
    positions = lax.axis_index("seq") * slice_len + jnp.arange(slice_len, dtype=jnp.int32)
    cosine, sine = rotary_tables(positions, head_dim)
    cosine = cosine[:, None, None, :]
    sine = sine[:, None, None, :]
    shards = (w_query, key_weight, value_weight, w_out, w_gate, w_up, w_down)
    wq, key_matrix, value_matrix, wo, wg, wu, wd = (
        lax.all_gather(shards[0], ("seq", "batch"), axis=0, tiled=True),
        lax.all_gather(shards[1], ("seq", "batch"), axis=0, tiled=True),
        lax.all_gather(shards[2], ("seq", "batch"), axis=0, tiled=True),
        lax.all_gather(shards[3], ("seq", "batch"), axis=0, tiled=True),
        lax.all_gather(shards[4], ("seq", "batch"), axis=0, tiled=True),
        lax.all_gather(shards[5], ("seq", "batch"), axis=0, tiled=True),
        lax.all_gather(shards[6], ("seq", "batch"), axis=0, tiled=True),
    )
    stream = inputs.reshape(rows, width).astype(jnp.float32)
    factor_one = rms_factor(stream)
    normalized_input = rounded(stream * factor_one * gain_attn)
    query_pre = product(normalized_input, wq).reshape(slice_len, seq_count, q_heads, head_dim)
    key_before_rotation = product(normalized_input, key_matrix).reshape(
        slice_len, seq_count, kv_heads, head_dim
    )
    value_b = rounded(product(normalized_input, value_matrix)).reshape(
        slice_len, seq_count, kv_width
    )
    factor_q = rms_factor(query_pre)
    factor_k = rms_factor(key_before_rotation)
    query_b = rounded(rotate(query_pre * factor_q * gain_query, cosine, sine))
    key_b = rounded(rotate(key_before_rotation * factor_k * gain_key, cosine, sine)).reshape(
        slice_len, seq_count, kv_width
    )
    query_five = query_b.reshape(slice_len, seq_count, kv_heads, sequence_group, head_dim)

    def scores_of(keys, start):
        count = keys.shape[0]
        raw = (
            jnp.einsum(
                "tsgrd,csgd->sgrtc",
                query_five,
                keys.reshape(count, seq_count, kv_heads, head_dim),
                preferred_element_type=jnp.float32,
            )
            * scale
        )
        key_pos = start + jnp.arange(count, dtype=jnp.int32)
        causal = key_pos[None, :] <= positions[:, None]
        inside = key_pos[None, :] < lengths[:, None]
        valid = causal[None, :, :] & inside[:, None, :]
        return (raw, valid[:, None, None, :, :])

    state_shape = (seq_count, kv_heads, sequence_group, slice_len)
    shard_ids = jnp.arange(cycle_size, dtype=jnp.int32)
    top = jnp.full(state_shape, -1e30, jnp.float32)
    keys = lax.all_gather(key_b, "seq", axis=0, tiled=True)
    value_rows = lax.all_gather(value_b, "seq", axis=0, tiled=True)
    count = keys.shape[0]
    raw, valid = scores_of(keys, jnp.int32(0))
    masked = jnp.where(valid, raw, -jnp.inf)
    new_top = jnp.maximum(top, jnp.max(masked, axis=-1))
    probs = jnp.exp(masked - new_top[..., None])
    total = jnp.sum(probs, axis=-1)
    acc = jnp.einsum(
        "sgrtc,csgd->sgrtd",
        rounded(probs),
        value_rows.reshape(count, seq_count, kv_heads, head_dim),
        preferred_element_type=jnp.float32,
    )
    state = (new_top, total, acc)
    top, total, acc = state
    attn_out = acc / total[..., None]
    log_total = top + jnp.log(total)
    mixed_b = rounded(jnp.transpose(attn_out, (3, 0, 1, 2, 4)).reshape(rows, q_heads * head_dim))
    middle = stream + product(mixed_b, wo)
    factor_two = rms_factor(middle)
    normed_two = rounded(middle * factor_two * gain_ffn)
    gate = product(normed_two, wg)
    up_part = product(normed_two, wu)
    sigma = jax.nn.sigmoid(gate)
    swish = gate * sigma
    hidden_b = rounded(swish * up_part)
    result = middle + product(hidden_b, wd)
    output = rounded(result).reshape(slice_len, seq_count, width)
    wq, key_matrix, value_matrix, wo, wg, wu, wd = (
        lax.all_gather(shards[0], ("seq", "batch"), axis=0, tiled=True),
        lax.all_gather(shards[1], ("seq", "batch"), axis=0, tiled=True),
        lax.all_gather(shards[2], ("seq", "batch"), axis=0, tiled=True),
        lax.all_gather(shards[3], ("seq", "batch"), axis=0, tiled=True),
        lax.all_gather(shards[4], ("seq", "batch"), axis=0, tiled=True),
        lax.all_gather(shards[5], ("seq", "batch"), axis=0, tiled=True),
        lax.all_gather(shards[6], ("seq", "batch"), axis=0, tiled=True),
    )
    grad_res = cotangent.reshape(rows, width).astype(jnp.float32)
    grad_ffo = rounded(grad_res)
    grad_wd = left_product(hidden_b, grad_ffo)
    grad_hidden = right_product(grad_ffo, wd)
    grad_gate = rounded(grad_hidden * up_part * sigma * (1.0 + gate * (1.0 - sigma)))
    grad_up = rounded(grad_hidden * swish)
    grad_wg = left_product(normed_two, grad_gate)
    grad_wu = left_product(normed_two, grad_up)
    grad_normed_two = right_product(grad_gate, wg) + right_product(grad_up, wu)
    grad_gain_ffn = jnp.sum(grad_normed_two * middle * factor_two, axis=0)
    grad_middle = grad_res + norm_back(grad_normed_two * gain_ffn, middle, factor_two)
    grad_branch = rounded(grad_middle)
    grad_wo = left_product(mixed_b, grad_branch)
    grad_mixed = rounded(right_product(grad_branch, wo))
    grad_five = grad_mixed.reshape(slice_len, seq_count, kv_heads, sequence_group, head_dim)
    delta = jnp.sum(
        jnp.transpose(grad_five, (1, 2, 3, 0, 4)).astype(jnp.float32) * attn_out, axis=-1
    )
    gathered = (
        lax.all_gather(key_b, "seq", axis=0, tiled=True),
        lax.all_gather(value_b, "seq", axis=0, tiled=True),
    )

    def back_step(grad_query, item):
        index, keys, value_rows = item
        raw, valid = scores_of(keys, index * slice_len)
        probs = jnp.where(valid, jnp.exp(raw - log_total[..., None]), 0.0)
        key_four = keys.reshape(slice_len, seq_count, kv_heads, head_dim)
        value_four = value_rows.reshape(slice_len, seq_count, kv_heads, head_dim)
        grad_probs = jnp.einsum(
            "tsgrd,csgd->sgrtc", grad_five, value_four, preferred_element_type=jnp.float32
        )
        grad_score = rounded(probs * (grad_probs - delta[..., None]))
        grad_query = (
            grad_query
            + jnp.einsum(
                "sgrtc,csgd->tsgrd", grad_score, key_four, preferred_element_type=jnp.float32
            )
            * scale
        )
        key_term = (
            jnp.einsum(
                "sgrtc,tsgrd->csgd", grad_score, query_five, preferred_element_type=jnp.float32
            )
            * scale
        )
        value_term = jnp.einsum(
            "sgrtc,tsgrd->csgd", rounded(probs), grad_five, preferred_element_type=jnp.float32
        )
        return (
            grad_query,
            (
                key_term.reshape(slice_len, seq_count, kv_width),
                value_term.reshape(slice_len, seq_count, kv_width),
            ),
        )

    items = (
        shard_ids,
        gathered[0].reshape(cycle_size, slice_len, seq_count, kv_width),
        gathered[1].reshape(cycle_size, slice_len, seq_count, kv_width),
    )
    grad_query, terms = lax.scan(
        back_step,
        jnp.zeros((slice_len, seq_count, kv_heads, sequence_group, head_dim), jnp.float32),
        items,
    )
    key_terms = terms[0].reshape(cycle_size * slice_len, seq_count, kv_width)
    value_terms = terms[1].reshape(cycle_size * slice_len, seq_count, kv_width)
    grad_key, grad_value = (
        lax.psum_scatter(
            key_terms.astype(jnp.bfloat16), "seq", scatter_dimension=0, tiled=True
        ).astype(jnp.float32),
        lax.psum_scatter(
            value_terms.astype(jnp.bfloat16), "seq", scatter_dimension=0, tiled=True
        ).astype(jnp.float32),
    )
    grad_qr = (
        rounded(grad_query).astype(jnp.float32).reshape(slice_len, seq_count, q_heads, head_dim)
    )
    grad_qn = rotate_back(grad_qr, cosine, sine)
    grad_gain_query = jnp.sum(grad_qn * query_pre * factor_q, axis=(0, 1, 2))
    grad_qp = rounded(
        norm_back(grad_qn * gain_query, query_pre, factor_q).reshape(rows, q_heads * head_dim)
    )
    grad_kr = (
        rounded(grad_key).astype(jnp.float32).reshape(slice_len, seq_count, kv_heads, head_dim)
    )
    grad_kn = rotate_back(grad_kr, cosine, sine)
    grad_gain_key = jnp.sum(grad_kn * key_before_rotation * factor_k, axis=(0, 1, 2))
    grad_kp = rounded(
        norm_back(grad_kn * gain_key, key_before_rotation, factor_k).reshape(rows, kv_width)
    )
    grad_vp = rounded(grad_value).reshape(rows, kv_width)
    grad_wq = left_product(normalized_input, grad_qp)
    grad_wk = left_product(normalized_input, grad_kp)
    grad_wv = left_product(normalized_input, grad_vp)
    grad_normed = (
        right_product(grad_qp, wq)
        + right_product(grad_kp, key_matrix)
        + right_product(grad_vp, value_matrix)
    )
    grad_gain_attn = jnp.sum(grad_normed * stream * factor_one, axis=0)
    grad_stream = grad_middle + norm_back(grad_normed * gain_attn, stream, factor_one)
    spread = (
        lax.all_to_all(
            split_rows(grad_wq, cycle_size, batch_size).astype(jnp.bfloat16),
            "batch",
            split_axis=1,
            concat_axis=1,
            tiled=True,
        ).astype(jnp.float32),
        lax.all_to_all(
            split_rows(grad_wk, cycle_size, batch_size).astype(jnp.bfloat16),
            "batch",
            split_axis=1,
            concat_axis=1,
            tiled=True,
        ).astype(jnp.float32),
        lax.all_to_all(
            split_rows(grad_wv, cycle_size, batch_size).astype(jnp.bfloat16),
            "batch",
            split_axis=1,
            concat_axis=1,
            tiled=True,
        ).astype(jnp.float32),
        lax.all_to_all(
            split_rows(grad_wo, cycle_size, batch_size).astype(jnp.bfloat16),
            "batch",
            split_axis=1,
            concat_axis=1,
            tiled=True,
        ).astype(jnp.float32),
        lax.all_to_all(
            split_rows(grad_wg, cycle_size, batch_size).astype(jnp.bfloat16),
            "batch",
            split_axis=1,
            concat_axis=1,
            tiled=True,
        ).astype(jnp.float32),
        lax.all_to_all(
            split_rows(grad_wu, cycle_size, batch_size).astype(jnp.bfloat16),
            "batch",
            split_axis=1,
            concat_axis=1,
            tiled=True,
        ).astype(jnp.float32),
        lax.all_to_all(
            split_rows(grad_wd, cycle_size, batch_size).astype(jnp.bfloat16),
            "batch",
            split_axis=1,
            concat_axis=1,
            tiled=True,
        ).astype(jnp.float32),
    )
    partial_sums = [fold_sources(piece) for piece in spread]
    summed = (
        lax.psum_scatter(
            partial_sums[0].astype(jnp.bfloat16), "seq", scatter_dimension=0, tiled=True
        ).astype(jnp.float32),
        lax.psum_scatter(
            partial_sums[1].astype(jnp.bfloat16), "seq", scatter_dimension=0, tiled=True
        ).astype(jnp.float32),
        lax.psum_scatter(
            partial_sums[2].astype(jnp.bfloat16), "seq", scatter_dimension=0, tiled=True
        ).astype(jnp.float32),
        lax.psum_scatter(
            partial_sums[3].astype(jnp.bfloat16), "seq", scatter_dimension=0, tiled=True
        ).astype(jnp.float32),
        lax.psum_scatter(
            partial_sums[4].astype(jnp.bfloat16), "seq", scatter_dimension=0, tiled=True
        ).astype(jnp.float32),
        lax.psum_scatter(
            partial_sums[5].astype(jnp.bfloat16), "seq", scatter_dimension=0, tiled=True
        ).astype(jnp.float32),
        lax.psum_scatter(
            partial_sums[6].astype(jnp.bfloat16), "seq", scatter_dimension=0, tiled=True
        ).astype(jnp.float32),
    )
    gains = lax.psum(
        (grad_gain_attn, grad_gain_ffn, grad_gain_query, grad_gain_key), ("seq", "batch")
    )
    grad_inputs = rounded(grad_stream).reshape(slice_len, seq_count, width)
    return (
        output,
        grad_inputs,
        summed[0],
        summed[1],
        summed[2],
        summed[3],
        summed[4],
        summed[5],
        summed[6],
        gains[0],
        gains[1],
        gains[2],
        gains[3],
    )


def solution(mesh):
    sharded = P(("seq", "batch"), None)
    stream = P("seq", "batch", None)
    in_specs = (stream, P("batch")) + (sharded,) * 7 + (P(),) * 4 + (stream,)
    out_specs = (stream, stream) + (sharded,) * 7 + (P(),) * 4
    grouped = mesh.shape["seq"] == 8 and mesh.shape["batch"] == 4
    step = body if grouped else general_body
    return jax.shard_map(step, mesh=mesh, in_specs=in_specs, out_specs=out_specs, check_vma=False)
```

```python
import functools

import jax
import jax.numpy as jnp
import numpy as np
from jax import lax
from jax.experimental import pallas as pl
from jax.experimental.pallas import tpu as pltpu
from jax.sharding import PartitionSpec as P

MESH = pl.DeviceIdType.MESH
F32 = jnp.float32
BF16 = jnp.bfloat16
eps = 1e-05
theta = 1000000.0
VMEM = pl.BlockSpec(memory_space=pltpu.VMEM)
ANY = pl.BlockSpec(memory_space=pl.ANY)
SMEM = pl.BlockSpec(memory_space=pltpu.SMEM)


def nn(left, right):
    return lax.dot_general(left, right, (((1,), (0,)), ((), ())), preferred_element_type=F32)


def nt(left, right):
    return lax.dot_general(left, right, (((1,), (1,)), ((), ())), preferred_element_type=F32)


def tn(left, right):
    return lax.dot_general(left, right, (((0,), (0,)), ((), ())), preferred_element_type=F32)


def rms_factor(v):
    return lax.rsqrt(jnp.mean(v * v, axis=-1, keepdims=True) + eps)


def norm_back(grad, value, factor):
    return factor * (
        grad - value * factor * factor * jnp.mean(grad * value, axis=-1, keepdims=True)
    )


def lanes(shape):
    return lax.broadcasted_iota(jnp.int32, shape, len(shape) - 1)


def rows_of(shape):
    return lax.broadcasted_iota(jnp.int32, shape, len(shape) - 2)


def head_mean(v):
    first = lanes(v.shape) < 64
    low = jnp.sum(jnp.where(first, v, 0.0), axis=-1, keepdims=True)
    high = jnp.sum(jnp.where(first, 0.0, v), axis=-1, keepdims=True)
    return jnp.where(first, low, high) * (1.0 / 64.0)


def rope(u, cosine, sine):
    early = lax.rem(lanes(u.shape), 64) < 32
    turned = jnp.where(early, -pltpu.roll(u, 96, 1), pltpu.roll(u, 32, 1))
    return u * cosine + turned * sine


def rope_back(u, cosine, sine):
    early = lax.rem(lanes(u.shape), 64) < 32
    w = u * sine
    return u * cosine + jnp.where(early, pltpu.roll(w, 96, 1), -pltpu.roll(w, 32, 1))


class Place:
    def __init__(self, send_sem, recv_sem, local_sem):
        self.s = lax.axis_index("seq")
        self.b = lax.axis_index("batch")
        self.z = self.s // 2
        self.y = lax.rem(self.s, 2)
        self.core = self.b + 1 - 2 * lax.rem(self.b, 2)
        self.across = lax.rem(self.b + 2, 4)
        self.far = 3 - self.b
        self.flip = 2 * self.z + 1 - self.y
        self.inner = jnp.logical_or(self.z == 1, self.z == 2)
        self.pair = self.z + 1 - 2 * lax.rem(self.z, 2)
        self.there = jnp.where(self.z < 2, 2, 1)
        self.beyond = jnp.where(self.z < 2, 3, 0)
        self.send_sem, self.recv_sem, self.local_sem = send_sem, recv_sem, local_sem
        self.used = 0
        self.used_local = 0
        self.sent = []

    def up(self, k):
        return lax.rem(self.z + k, 4)

    def down(self, k):
        return lax.rem(self.z + 4 - k, 4)

    def greet(self):
        self.hello()
        self.meet()

    def hello(self):
        barrier = pltpu.get_barrier_semaphore()
        for k in (1, 2, 3):
            pl.semaphore_signal(
                barrier, inc=1, device_id=(self.s, lax.rem(self.b + k, 4)), device_id_type=MESH
            )
        for k in range(1, 8):
            pl.semaphore_signal(
                barrier, inc=1, device_id=(lax.rem(self.s + k, 8), self.b), device_id_type=MESH
            )

    def meet(self):
        pl.semaphore_wait(pltpu.get_barrier_semaphore(), 10)

    def slots(self, count):
        first = self.used
        self.used += count
        return first

    def copy(self, src, dst, device, out, into=None):
        return pltpu.make_async_remote_copy(
            src_ref=src,
            dst_ref=dst,
            send_sem=self.send_sem.at[out],
            recv_sem=self.recv_sem.at[out if into is None else into],
            device_id=device,
            device_id_type=MESH,
        )

    def post(self, src, dst, device):
        index = self.slots(1)
        made = self.copy(src, dst, device, index)
        made.start()
        self.sent.append(made)
        return index

    def landed(self, index, ref):
        self.copy(ref, ref, (self.s, self.core), index).wait_recv()

    def local(self, src, dst):
        index = self.used_local
        self.used_local += 1
        made = pltpu.make_async_copy(src, dst, self.local_sem.at[index])
        made.start()
        return made

    def drain(self):
        for made in self.sent:
            made.wait_send()
        self.sent = []


class Spread:
    def __init__(self, p, slot):
        self.p, self.slot = p, slot
        self.first = p.slots(8)
        self.from_z = (p.pair, p.there, p.beyond)

    def send(self, s, device, out, into):
        self.p.copy(self.slot(s), self.slot(s), device, self.first + out, self.first + into).start()

    def start_z(self):
        p = self.p
        self.send(p.s, (2 * p.pair + p.y, p.b), 0, 0)
        self.send(p.s, (2 * p.there + p.y, p.b), 1, jnp.where(p.inner, 1, 2))

    def start_y(self):
        p = self.p
        self.send(p.s, (p.flip, p.b), 4, 3)

    def start(self):
        self.start_z()
        self.start_y()

    def land(self, j):
        p = self.p
        s = 2 * self.from_z[j] + p.y
        p.landed(self.first + j, self.slot(s))
        if j > 0:

            @pl.when(p.inner)
            def _():
                self.send(s, (2 * p.pair + p.y, p.b), 1 + j, j)

        self.send(s, (p.flip, p.b), 5 + j, 4 + j)

    def land_inner(self):
        @pl.when(self.p.inner)
        def _():
            self.land(1)
            self.land(2)

    def land_end(self):
        @pl.when(jnp.logical_not(self.p.inner))
        def _():
            self.land(1)
            self.land(2)

    def finish(self):
        p = self.p
        p.landed(self.first + 3, self.slot(p.flip))
        for j in range(3):
            p.landed(self.first + 4 + j, self.slot(2 * self.from_z[j] + 1 - p.y))

    def drain(self):
        p = self.p

        def sent(out):
            p.copy(self.slot(p.s), self.slot(p.s), (p.flip, p.b), self.first + out).wait_send()

        for out in (0, 1, 4, 5, 6, 7):
            sent(out)

        @pl.when(p.inner)
        def _():
            sent(2)
            sent(3)


def heads_of(whole, kk):
    return whole[:, 256 * kk : 256 * kk + 128], whole[:, 256 * kk + 128 : 256 * kk + 256]


def pack_projections(w_query, key_weight, value_weight, out):
    for c in range(4):
        k = key_weight[:, 128 * c : 128 * c + 128].astype(F32)
        v = value_weight[:, 128 * c : 128 * c + 128].astype(F32)
        first = lanes(k.shape) < 64
        pairs = (
            jnp.where(first, k, pltpu.roll(v, 64, 1)),
            jnp.where(first, pltpu.roll(k, 64, 1), v),
        )
        for kk in (0, 1):
            h = 2 * c + kk
            out[c, :, 256 * kk : 256 * kk + 128] = w_query[:, 128 * h : 128 * h + 128]
            out[c, :, 256 * kk + 128 : 256 * kk + 256] = pairs[kk].astype(BF16)


def pack_hidden(source, out, which):
    wide = source[...].astype(F32)
    for c in range(4):
        pieces = [wide[:, 144 * (4 * i + c) : 144 * (4 * i + c) + 144] for i in range(8)]
        out[c, which] = jnp.concatenate(pieces, axis=1).astype(BF16)


def twice(v):
    return jnp.concatenate([v[...], v[...]], axis=1)


def near_first(p, t):
    return jnp.where(t == 0, p.b, jnp.where(t == 1, p.core, jnp.where(t == 2, p.across, p.far)))


def block_kernel(
    x, dy, lengths, w_query, key_weight, value_weight, w_out, w_gate, w_up, w_down,
    cos_table, sin_table, gain_query, gain_key, gain_a, gain_f,
    output, dx, rqkv, rgu, rd, ro, gains_out, norm_park,
    xa, norm, wqkv, wo, pack, unit, unit_out, lse, kv, mix, dy_all, wgu, wd, gd,
    hid, dgate, dup, dk_sum, dv_sum, parts, recv, recv_o, keep, result, middle,
    qkv_send, gu_send, length, cos, sin, length_all,
    dou, delta,
    y_d, t_d, z_d, y_g, t_g, z_g, y_u, t_u, z_u, y_q, z_q, y_o, z_o,
    gain_sum, gain_batch, gain_seq,
    send_sem, recv_sem, local_sem,
):
    p = Place(send_sem, recv_sem, local_sem)
    s, b, z, y = p.s, p.b, p.z, p.y
    my_rows = pl.ds(pl.multiple_of(32 * b, 32), 32)
    my_positions = pl.ds(pl.multiple_of(256 * s, 256), 256)
    p.hello()
    own_d = p.local(w_down, wd.at[s])
    own_x = p.local(x, xa.at[b])
    own_wo = p.local(w_out, wo.at[s, b])
    own_dy = p.local(dy, dy_all.at[b])
    own_tables = [p.local(cos_table.at[my_positions], cos), p.local(sin_table.at[my_positions], sin)]
    pack_projections(w_query, key_weight, value_weight, qkv_send)
    length[...] = jnp.broadcast_to(lengths[0], (8, 128)).astype(jnp.int32)
    own_qkv = p.local(qkv_send.at[b], wqkv.at[s, my_rows])
    length_all[b] = length[...]
    pack_hidden(w_gate, gu_send, 0)
    pack_hidden(w_up, gu_send, 1)
    p.meet()

    got_qkv, got_len = [], []
    for k in (1, 2, 3):
        to = lax.rem(b + k, 4)
        got_qkv.append(p.post(qkv_send.at[to], wqkv.at[s, my_rows], (s, to)))
    own_x.wait()
    x_across = p.post(xa.at[b], xa.at[b], (s, p.across))
    x_core = p.post(xa.at[b], xa.at[b], (s, p.core))
    for k in (1, 2, 3):
        to = lax.rem(b + k, 4)
        got_len.append(p.post(length, length_all.at[b], (s, to)))
    spread_d = Spread(p, lambda i: wd.at[i])
    spread_g = Spread(p, lambda i: wgu.at[i, 0])
    spread_u = Spread(p, lambda i: wgu.at[i, 1])
    own_d.wait()
    spread_d.start_y()

    def normalize(g):
        xg = xa[g].astype(F32)
        norm[g] = (xg * rms_factor(xg) * gain_a[...]).astype(BF16)

    normalize(b)
    own_qkv.wait()
    for k in (1, 2, 3):
        p.landed(got_qkv[k - 1], wqkv.at[s, my_rows])
    z_qkv = [p.post(wqkv.at[s], wqkv.at[s], (2 * p.up(k) + y, b)) for k in (1, 2, 3)]
    y_qkv = [p.post(wqkv.at[s], wqkv.at[s], (p.flip, b))]
    own_gu = p.local(gu_send.at[b], wgu.at[s, :, my_rows])
    got_gu = []
    for k in (1, 2, 3):
        to = lax.rem(b + k, 4)
        got_gu.append(p.post(gu_send.at[to], wgu.at[s, :, my_rows], (s, to)))
    for k in (1, 2, 3):
        slot = 2 * p.down(k) + y
        p.landed(z_qkv[k - 1], wqkv.at[slot])
        y_qkv.append(p.post(wqkv.at[slot], wqkv.at[slot], (p.flip, b)))
    spread_d.start_z()
    own_wo.wait()
    z_wo = [p.post(wo.at[s, b], wo.at[s, b], (2 * p.up(k) + y, b)) for k in (1, 2, 3)]
    y_wo = [p.post(wo.at[s, b], wo.at[s, b], (p.flip, b))]
    p.landed(x_core, xa.at[p.core])
    normalize(p.core)
    p.landed(x_across, xa.at[p.across])
    x_far = p.post(xa.at[p.across], xa.at[p.across], (s, p.core))
    for made in own_tables:
        made.wait()
    p.landed(y_qkv[0], wqkv.at[p.flip])
    for k in (1, 2, 3):
        p.landed(y_qkv[k], wqkv.at[2 * p.down(k) + 1 - y])
    gain_q, gain_k = twice(gain_query), twice(gain_key)
    own_gu.wait()
    for k in (1, 2, 3):
        p.landed(got_gu[k - 1], wgu.at[s, :, my_rows])
    spread_g.start_y()
    spread_u.start_y()

    first_unit = p.slots(8)

    def each_piece(t, kk, act):
        to = 2 * near_first(p, t) + kk

        @pl.when(to != s)
        def _():
            act(p.copy(pack.at[to], unit.at[s], (to, b), first_unit + 2 * t + kk, first_unit + s))

    def project(t, carry):
        g = near_first(p, t)

        @pl.when(t == 3)
        def _():
            p.landed(x_far, xa.at[p.far])

        @pl.when(t >= 2)
        def _():
            normalize(g)

        whole = nn(norm[g], wqkv[...].reshape(1024, 512))
        for kk in (0, 1):
            q, kvp = heads_of(whole, kk)
            qn = q * lax.rsqrt(head_mean(q * q) + eps) * gain_q
            kn = kvp * lax.rsqrt(head_mean(kvp * kvp) + eps) * gain_k
            qr = rope(qn, cos[...], sin[...]) * 0.125
            kr = rope(kn, cos[...], sin[...])
            pack[2 * g + kk, :, 0:128] = qr.astype(BF16)
            pack[2 * g + kk, :, 128:256] = jnp.where(lanes(kr.shape) < 64, kr, kvp).astype(BF16)
            each_piece(t, kk, lambda made: made.start())

        return carry

    lax.fori_loop(0, 4, project, 0)
    own_unit = p.local(pack.at[s], unit.at[s])
    parked = p.local(norm, norm_park)
    for k in (1, 2, 3):
        slot = 2 * p.down(k) + y
        p.landed(z_wo[k - 1], wo.at[slot, b])
        y_wo.append(p.post(wo.at[slot, b], wo.at[slot, b], (p.flip, b)))
    spread_d.land(0)
    spread_d.land_inner()
    own_dy.wait()
    dy_across = p.post(dy_all.at[b], dy_all.at[b], (s, p.across))
    dy_core = p.post(dy_all.at[b], dy_all.at[b], (s, p.core))
    for k in (1, 2, 3):
        p.landed(got_len[k - 1], length_all.at[lax.rem(b + 4 - k, 4)])

    for k in range(1, 8):
        src = lax.rem(s + k, 8)
        p.landed(first_unit + src, unit.at[src])
    own_unit.wait()
    spread_g.start_z()
    p.landed(y_wo[0], wo.at[p.flip, b])
    for k in (1, 2, 3):
        p.landed(y_wo[k], wo.at[2 * p.down(k) + 1 - y, b])
    wo_across = p.post(wo.at[:, b], wo.at[:, b], (s, p.across))
    wo_core = p.post(wo.at[:, b], wo.at[:, b], (s, p.core))

    def values(j):
        return dup.at[j // 2, lax.rem(j, 2), 0:80, 0:256]

    def prepare(j, carry):
        live = j * 256 + rows_of((256, 128)) < length_all[z][0:1, :]
        masked = jnp.where(live, unit[j, :, 128:256].astype(F32), 0.0)
        kv[j] = masked.astype(BF16)
        turned = jnp.transpose(masked)[64:128].astype(BF16)
        alive = j * 256 + lanes((16, 256)) < length_all[z][0:1, 0:1]
        counted = jnp.where(alive, 1.0, 0.0).astype(BF16)
        values(j)[...] = jnp.concatenate([turned, counted], axis=0)
        return carry

    lax.fori_loop(0, 8, prepare, 0)
    p.landed(dy_across, dy_all.at[p.across])
    dy_far = p.post(dy_all.at[p.across], dy_all.at[p.across], (s, p.core))
    first_mix, first_across, first_core = p.slots(8), p.slots(8), p.slots(8)

    def mix_send(src, t):
        p.copy(mix.at[b, src], mix.at[b, src], (s, p.across), first_across + t).start()
        p.copy(mix.at[b, src], mix.at[b, src], (s, p.core), first_core + t).start()

    def mix_arrived(t):
        src = lax.rem(s + 7 - t, 8)
        p.landed(first_mix + t, mix.at[b, src])
        mix_send(src, t)

    def attend(t, carry):
        i = lax.rem(s + 1 + t, 8)
        qt = jnp.transpose(unit[i, :, 0:128].astype(F32)).astype(BF16)
        both = jnp.concatenate([qt[0:64], qt[64:128]], axis=1)
        right = jnp.concatenate([both, jnp.zeros((64, 512), BF16)], axis=0)

        def block(j, acc):
            return acc + nn(values(j)[...], jnp.exp(nn(kv[j], right)).astype(BF16))

        acc = lax.fori_loop(0, i, block, jnp.zeros((80, 512), F32))
        causal = rows_of((256, 512)) <= lax.rem(lanes((256, 512)), 256)
        edge = jnp.where(causal, jnp.exp(nn(kv[i], right)), 0.0).astype(BF16)
        acc = acc + nn(values(i)[...], edge)
        total = acc[64:65]
        out = acc[0:64] / total
        out = jnp.concatenate([out[:, 0:256], out[:, 256:512]], axis=0)
        unit_out[i] = jnp.transpose(out).astype(BF16)
        lse[i] = jnp.broadcast_to(jnp.log(total), (8, 512))

        @pl.when(t < 7)
        def _():
            p.copy(unit_out.at[i], mix.at[b, s], (i, b), first_mix + t).start()

        @pl.when(t == 3)
        def _():
            spread_d.land_end()

        @pl.when(t == 7)
        def _():
            spread_g.land(0)
            spread_g.land_inner()

        @pl.when(t >= 4)
        def _():
            mix_arrived(t - 4)

        return carry

    lax.fori_loop(0, 8, attend, 0)
    spread_u.start_z()
    own_mix = p.local(unit_out.at[s], mix.at[b, s])
    own_mix.wait()
    mix_send(s, 7)
    for t in range(4, 7):
        mix_arrived(t)
    spread_g.land_end()
    p.landed(dy_core, dy_all.at[p.core])
    p.landed(dy_far, dy_all.at[p.far])
    spread_d.finish()

    def hidden_back(g, carry):
        rows = pl.ds(pl.multiple_of(g * 256, 256), 256)
        dgate[g] = nt(dy_all[g], wd[...].reshape(1152, 1024)).astype(BF16).reshape(2, 128, 1152)
        return carry

    lax.fori_loop(0, 4, hidden_back, 0)
    p.landed(wo_across, wo.at[:, p.across])
    wo_far = p.post(wo.at[:, p.across], wo.at[:, p.across], (s, p.core))
    for t in range(8):
        p.landed(first_across + t, mix.at[p.across, lax.rem(s + 7 - t, 8)])
    mix_far = p.post(mix.at[p.across], mix.at[p.across], (s, p.core))
    for t in range(8):
        p.landed(first_core + t, mix.at[p.core, lax.rem(s + 7 - t, 8)])
    p.landed(wo_core, wo.at[:, p.core])
    p.landed(wo_far, wo.at[:, p.far])
    spread_u.land(0)
    spread_u.land_inner()
    p.landed(mix_far, mix.at[p.far])

    parked.wait()

    def project_out(g, carry):
        mixed = jnp.concatenate([mix[c, 2 * g + kk] for c in range(4) for kk in (0, 1)], axis=1)
        mid = xa[g].astype(F32) + nn(mixed, wo[...].reshape(1024, 1024))
        norm[g] = (mid * rms_factor(mid) * gain_f[...]).astype(BF16)

        @pl.when(g == b)
        def _():
            middle[...] = mid

        return carry

    lax.fori_loop(0, 4, project_out, 0)

    for t in range(8):
        if t < 7:
            p.copy(unit_out.at[s], mix.at[b, s], (p.flip, b), first_mix + t).wait_send()
        p.copy(mix.at[b, s], mix.at[b, s], (s, p.across), first_across + t).wait_send()
        p.copy(mix.at[b, s], mix.at[b, s], (s, p.core), first_core + t).wait_send()
    for t in range(4):
        for kk in (0, 1):
            each_piece(t, kk, lambda made: made.wait_send())
    p.drain()

    def turn(e, carry):
        for g in range(4):
            hid[0:128, 256 * g : 256 * g + 256] = jnp.transpose(
                mix[e // 2, 2 * g + lax.rem(e, 2)].astype(F32)
            ).astype(BF16)
        gu_send[e // 2, lax.rem(e, 2), :, 0:1024] = hid[my_rows, 0:1024]
        return carry

    lax.fori_loop(0, 8, turn, 0)
    spread_u.land_end()
    spread_g.finish()

    def gate_of(g, carry):
        rows = pl.ds(pl.multiple_of(g * 256, 256), 256)
        hid[rows] = nn(norm[g], wgu[:, 0].reshape(1024, 1152)).astype(BF16)
        return carry

    lax.fori_loop(0, 4, gate_of, 0)
    spread_u.finish()
    first_n = p.slots(3)

    def gated(g, carry):
        rows = pl.ds(pl.multiple_of(g * 256, 256), 256)
        gate = hid[rows].astype(F32)
        up = nn(norm[g], wgu[:, 1].reshape(1024, 1152))
        dh = dgate[g].reshape(256, 1152).astype(F32)
        sg = 1.0 / (1.0 + jnp.exp(-gate))
        swish = gate * sg
        hid[rows] = (swish * up).astype(BF16)
        dgate[g] = (dh * up * sg * (1.0 + gate * (1.0 - sg))).astype(BF16).reshape(2, 128, 1152)
        dup[g] = (dh * swish).astype(BF16).reshape(2, 128, 1152)
        return carry

    lax.fori_loop(0, 4, gated, 0)

    def down_rows(c, carry, at=None):
        rows = pl.multiple_of(128 * c, 128)
        gd[pl.ds(rows, 128), at] = tn(
            hid[:, pl.ds(rows, 128)], dy_all[:, :, at].reshape(1024, 512)
        ).astype(BF16)
        return carry

    halves = (pl.ds(0, 512), pl.ds(512, 512))
    sum_d, more_d = [
        SeqTree(
            p,
            functools.partial(lambda at, i: gd.at[pl.ds(pl.multiple_of(144 * i, 16), 144), at], at),
            y_d.at[:, :, at], t_d.at[:, :, at], z_d.at[:, :, at],
        )
        for at in halves
    ]
    lax.fori_loop(0, 9, functools.partial(down_rows, at=halves[0]), 0)
    sum_d.start()

    def narrowed(t, carry):
        g = batch_order(p, t)
        part = nt(dgate[g].reshape(256, 1152), wgu[:, 0].reshape(1024, 1152)) + nt(
            dup[g].reshape(256, 1152), wgu[:, 1].reshape(1024, 1152)
        )
        parts[g] = part.astype(BF16)

        @pl.when(t == 3)
        def _():
            keep[...] = part

        chip_sum_post(p, t, parts, recv, first_n)
        return carry

    lax.fori_loop(0, 4, narrowed, 0)
    chip_sum_across(p, parts, recv, first_n)
    lax.fori_loop(0, 9, functools.partial(down_rows, at=halves[1]), 0)
    more_d.start()
    parts_of = (pl.ds(0, 640), pl.ds(640, 512))

    def tree(which, at, y_recv, relayed, z_recv):
        return SeqTree(
            p, lambda i: wgu.at[i, which, :, at], y_recv.at[:, :, at], relayed.at[:, :, at], z_recv.at[:, :, at]
        )

    sum_g, more_g = [tree(0, at, y_g, t_g, z_g) for at in parts_of]
    sum_u, more_u = [tree(1, at, y_u, t_u, z_u) for at in parts_of]

    for spread in (spread_d, spread_g, spread_u):
        spread.drain()

    def gate_rows(c, carry):
        at = pl.multiple_of(128 * c, 128)
        side = norm[:, :, pl.ds(at, 128)].reshape(1024, 128)
        wgu[c, 0] = tn(side, dgate[...].reshape(1024, 1152)).astype(BF16)
        wgu[c, 1] = tn(side, dup[...].reshape(1024, 1152)).astype(BF16)
        return carry

    lax.fori_loop(0, 8, gate_rows, 0)
    load_norm = p.local(norm_park, norm)

    mid = middle[...]
    r2 = rms_factor(mid)
    grad_two = keep[...] + chip_sum_rest(p, parts, recv, first_n)
    gain_sum[...] = jnp.zeros((8, 1024), F32)
    gain_sum[1:2] = jnp.sum(grad_two * mid * r2, axis=0, keepdims=True)
    dm = dy_all[b].astype(F32) + norm_back(grad_two * gain_f[...], mid, r2)
    result[...] = mid
    middle[...] = dm
    xa[b] = dm.astype(BF16)

    first_mixed = p.slots(3)

    def mixed_back(t, carry):
        c = batch_order(p, t)
        place = jnp.where(t == 3, 1, 0)
        for kk in (0, 1):
            mix[place, 2 * c + kk] = nt(xa[b], wo[2 * c + kk].reshape(128, 1024)).astype(BF16)

        @pl.when(t < 3)
        def _():
            p.copy(
                mix.at[0, pl.ds(2 * c, 2)], mix.at[1, pl.ds(2 * b, 2)], (s, c), first_mixed + t
            ).start()

        return carry

    lax.fori_loop(0, 4, mixed_back, 0)
    dbr_across = p.post(xa.at[b], xa.at[b], (s, p.across))
    dbr_core = p.post(xa.at[b], xa.at[b], (s, p.core))
    def down(g, carry):
        part = nn(hid[pl.ds(pl.multiple_of(g * 256, 256), 256)], wd[...].reshape(1152, 1024))
        dy_all[g] = part.astype(BF16)

        @pl.when(g == b)
        def _():
            result[...] = result[...] + part

        return carry

    lax.fori_loop(0, 4, down, 0)

    first_o = p.slots(3)
    chip_sum_post(p, 0, dy_all, recv_o, first_o)
    chip_sum_post(p, 1, dy_all, recv_o, first_o)
    def q_right(i):
        return hid.at[pl.ds(pl.multiple_of(128 * i, 128), 128), 0:512]

    def do_right(i):
        return hid.at[pl.ds(pl.multiple_of(128 * i, 128), 128), 512:1024]

    def tall(i, base):
        half = pl.ds(2 * lax.rem(i, 2), 2)
        return dgate.at[half, :, :, pl.ds(pl.multiple_of(base + 128 * (i // 2), 128), 128)]

    def q_left(i):
        return tall(i, 0)

    def do_left(i):
        return tall(i, 512)

    def dk2(i):
        return dk_sum.at[i]

    def dv2(i):
        return dv_sum.at[i]

    def dq2(i):
        rows = pl.ds(pl.multiple_of(64 * lax.rem(i, 4), 64), 64)
        return keep.at[rows, pl.ds(pl.multiple_of(512 * (i // 4), 512), 512)]

    def keys_turned(i):
        return dup.at[i // 2, lax.rem(i, 2), 0:64, 0:256]

    def prepare_back(i, carry):
        keys_turned(i)[...] = jnp.transpose(kv[i].astype(F32))[0:64].astype(BF16)
        q = unit[i, :, 0:128].astype(F32)
        qt = jnp.transpose(q).astype(BF16)
        both = jnp.concatenate([qt[0:64], qt[64:128]], axis=1)
        q_right(i)[...] = jnp.concatenate([both, jnp.zeros((64, 512), BF16)], axis=0)
        first = lanes(q.shape) < 64
        both = jnp.concatenate([jnp.where(first, q, 0.0), jnp.where(first, 0.0, q)], axis=0)
        q_left(i)[...] = both.astype(BF16).reshape(2, 2, 128, 128)
        dq2(i)[...] = jnp.zeros((64, 512), F32)
        dk2(i)[...] = jnp.zeros((256, 128), F32)
        dv2(i)[...] = jnp.zeros((256, 128), F32)
        return carry

    lax.fori_loop(0, 8, prepare_back, 0)
    first_do = p.slots(8)

    def grad_piece(t, kk, act):
        to = 2 * near_first(p, t) + kk

        @pl.when(to != s)
        def _():
            act(p.copy(mix.at[1, to], dou.at[s], (to, b), first_do + 2 * t + kk, first_do + s))

    for t, index in ((0, None), (1, 1), (2, 2), (3, 0)):
        if index is not None:
            p.landed(first_mixed + index, mix.at[1, pl.ds(2 * near_first(p, t), 2)])
        for kk in (0, 1):
            grad_piece(t, kk, lambda made: made.start())
    sum_g.start()
    sum_d.reduce()
    dou[s] = mix[1, s]

    chip_sum_across(p, dy_all, recv_o, first_o)
    for k in range(1, 8):
        src = lax.rem(s + k, 8)
        p.landed(first_do + src, dou.at[src])

    def prepare_grad(i, carry):
        do = dou[i].astype(F32)
        dot = jnp.transpose(do)
        right = jnp.concatenate([dot[0:64], dot[64:128]], axis=1).astype(BF16)
        do_right(i)[...] = jnp.concatenate([jnp.zeros((64, 512), BF16), right], axis=0)
        first = lanes(do.shape) < 64
        tall_do = jnp.concatenate([jnp.where(first, do, 0.0), jnp.where(first, 0.0, do)], axis=0)
        do_left(i)[...] = tall_do.astype(BF16).reshape(2, 2, 128, 128)
        both = dot * jnp.transpose(unit_out[i].astype(F32))
        low = jnp.sum(both[0:64], axis=0, keepdims=True)
        high = jnp.sum(both[64:128], axis=0, keepdims=True)
        delta[i] = jnp.broadcast_to(jnp.concatenate([low, high], axis=1), (8, 512))
        return carry

    lax.fori_loop(0, 8, prepare_grad, 0)

    def meet(i, j, probs):
        ds = (probs * (nn(kv[j], do_right(i)[...]) - delta[i][0:1])).astype(BF16)
        dv2(j)[...] += nn(probs.astype(BF16), do_left(i)[...].reshape(512, 128))
        dk2(j)[...] += nn(ds, q_left(i)[...].reshape(512, 128))
        dq2(i)[...] += nn(keys_turned(j)[...], ds)

    first_back = p.slots(8)

    def blocks(t, carry):
        c = lax.rem(s + 1 + t, 8)
        causal = rows_of((256, 512)) <= lax.rem(lanes((256, 512)), 256)
        meet(c, c, jnp.where(causal, jnp.exp(nn(kv[c], q_right(c)[...]) - lse[c][0:1]), 0.0))

        def other(u, inner_carry):
            o = lax.rem(s + 1 + u, 8)
            i, j = jnp.maximum(c, o), jnp.minimum(c, o)
            meet(i, j, jnp.exp(nn(kv[j], q_right(i)[...]) - lse[i][0:1]))
            return inner_carry

        lax.fori_loop(t + 1, 8, other, 0)
        acc = dq2(c)[...]
        dq = jnp.concatenate([acc[:, 0:256], acc[:, 256:512]], axis=0) * 0.125
        pack[c, :, 0:128] = jnp.transpose(dq).astype(BF16)
        live = c * 256 + rows_of((256, 128)) < length_all[z][0:1, :]
        dk, dv = dk2(c)[...], dv2(c)[...]
        dk = dk + pltpu.roll(dk, 64, 1)
        dv = dv + pltpu.roll(dv, 64, 1)
        dkv = jnp.where(lanes((256, 128)) < 64, dk, dv)
        pack[c, :, 128:256] = jnp.where(live, dkv, 0.0).astype(BF16)

        @pl.when(t < 7)
        def _():
            p.copy(pack.at[c], unit.at[s], (c, b), first_back + t).start()

        @pl.when(t == 0)
        def _():
            p.landed(dbr_across, xa.at[p.across])
            p.copy(xa.at[p.across], xa.at[p.across], (s, p.core), dbr_far).start()

        @pl.when(t == 1)
        def _():
            sum_d.relay()

        @pl.when(t == 2)
        def _():
            more_g.start()
            more_d.reduce()

        return carry

    dbr_far = p.slots(1)
    lax.fori_loop(0, 8, blocks, 0)
    sum_u.start()
    sum_g.reduce()
    more_d.relay()
    unit[s] = pack[s]

    p.landed(dbr_core, xa.at[p.core])
    p.landed(dbr_far, xa.at[p.far])
    out_rows = nn(gu_send[:, :, :, 0:1024].reshape(256, 1024), xa[...].reshape(1024, 1024)).astype(BF16)
    for e in range(8):
        dgate[e // 2, e % 2, 0:32, 0:1024] = out_rows[32 * e : 32 * e + 32]
    sum_o = SeqSum(p, y_o, z_o)
    sum_o.start(dgate.at[:, :, 0:32, 0:1024])
    load_x = p.local(x, xa.at[p.far])
    load_norm.wait()

    first_n = p.slots(3)
    zero_row = jnp.zeros((1, 128), F32)

    def heads(t, carry):
        sum_q, sum_k = carry
        unit_of = lax.rem(s + 7 - t, 8)

        @pl.when(t < 7)
        def _():
            p.landed(first_back + t, unit.at[unit_of])

        g = unit_of // 2
        at = pl.multiple_of(256 * lax.rem(unit_of, 2), 256)
        whole = nn(norm[g], wqkv[:, :, pl.ds(at, 256)].reshape(1024, 256))
        q, k = heads_of(whole, 0)
        rq = lax.rsqrt(head_mean(q * q) + eps)
        rk = lax.rsqrt(head_mean(k * k) + eps)
        dq = rope_back(unit[unit_of, :, 0:128].astype(F32), cos[...], sin[...])
        dkv = unit[unit_of, :, 128:256].astype(F32)
        dk = rope_back(dkv, cos[...], sin[...])
        sum_q = sum_q + jnp.sum(dq * q * rq, axis=0, keepdims=True)
        sum_k = sum_k + jnp.sum(dk * k * rk, axis=0, keepdims=True)
        dq = dq * gain_q
        dk = dk * gain_k
        dq = rq * (dq - q * rq * rq * head_mean(dq * q))
        dk = rk * (dk - k * rk * rk * head_mean(dk * k))
        dup[g, :, :, pl.ds(at, 128)] = dq.astype(BF16).reshape(2, 128, 128)
        dkv = jnp.where(lanes(dk.shape) < 64, dk, dkv).astype(BF16)
        dup[g, :, :, pl.ds(pl.multiple_of(at + 128, 128), 128)] = dkv.reshape(2, 128, 128)
        return (sum_q, sum_k)

    sum_q, sum_k = lax.fori_loop(0, 8, heads, (zero_row, zero_row))
    sum_g.relay()
    more_g.reduce()

    gain_sum[2:3, 0:128] = sum_q
    gain_sum[3:4, 0:128] = sum_k
    def qkv_rows(c, carry):
        at = pl.multiple_of(128 * c, 128)
        side = norm[:, :, pl.ds(at, 128)].reshape(1024, 128)
        dup[c // 2, lax.rem(c, 2), :, 512:1024] = tn(side, dup[:, :, :, 0:512].reshape(1024, 512)).astype(BF16)
        return carry

    lax.fori_loop(0, 8, qkv_rows, 0)
    sum_qkv = SeqSum(p, y_q, z_q)
    sum_qkv.start(dup.at[:, :, :, pl.ds(512, 512)])
    more_u.start()

    def stream_back(t, carry):
        g = batch_order(p, t)
        part = nt(dup[g, :, :, 0:512].reshape(256, 512), wqkv[...].reshape(1024, 512))
        parts[g] = part.astype(BF16)

        @pl.when(t == 3)
        def _():
            keep[...] = part

        chip_sum_post(p, t, parts, recv, first_n)
        return carry

    lax.fori_loop(0, 4, stream_back, 0)
    chip_sum_across(p, parts, recv, first_n)
    sum_o.middle()
    sum_u.reduce()
    more_g.relay()
    xa[p.core] = (result[...] + chip_sum_rest(p, dy_all, recv_o, first_o)).astype(BF16)
    leave = [p.local(xa.at[p.core], output)]
    sum_qkv.middle()

    dn1 = keep[...] + chip_sum_rest(p, parts, recv, first_n)
    load_x.wait()
    xf = xa[p.far].astype(F32)
    r1 = rms_factor(xf)
    gain_sum[0:1] = jnp.sum(dn1 * xf * r1, axis=0, keepdims=True)
    xa[p.far] = (middle[...] + norm_back(dn1 * gain_a[...], xf, r1)).astype(BF16)
    leave.append(p.local(xa.at[p.far], dx))
    got_gain = [p.post(gain_sum, gain_batch.at[b], (s, lax.rem(b + k, 4))) for k in (1, 2, 3)]
    gain_batch[b] = gain_sum[...]
    sum_u.relay()
    for at, half in zip(halves, (sum_d, more_d)):
        rd[:, at] = half.finish()

    def exchange(total, own, dst):
        for c in range(4):
            own(c)[...] = total[32 * c : 32 * c + 32].astype(BF16)
        got = []
        for k in (1, 2, 3):
            to = lax.rem(b + k, 4)
            got.append(p.post(own(to), dst(b), (s, to)))
        dst(b)[...] = own(b)[...]
        return got

    def arrive(got, dst):
        for k in (1, 2, 3):
            p.landed(got[k - 1], dst(lax.rem(b + 4 - k, 4)))

    finished = []

    def hand_over(total, which, at):
        dst = lambda i: rgu.at[i, which, :, at]
        finished.append((exchange(total, lambda c: gu_send.at[c, which, :, at], dst), dst))

    hand_over(sum_g.finish(), 0, parts_of[0])
    for k in (1, 2, 3):
        p.landed(got_gain[k - 1], gain_batch.at[lax.rem(b + 4 - k, 4)])
    gain_seq[s] = (gain_batch[0] + gain_batch[1]) + (gain_batch[2] + gain_batch[3])
    got_all = [p.post(gain_seq.at[s], gain_seq.at[s], (lax.rem(s + k, 8), b)) for k in range(1, 8)]
    more_u.reduce()
    hand_over(more_g.finish(), 0, parts_of[1])
    ro[...] = sum_o.finish()
    dst_q = lambda i: rqkv.at[i]
    finished.append((exchange(sum_qkv.finish(), lambda c: qkv_send.at[c], dst_q), dst_q))
    hand_over(sum_u.finish(), 1, parts_of[0])
    for k in range(1, 8):
        p.landed(got_all[k - 1], gain_seq.at[lax.rem(s + 8 - k, 8)])
    total = gain_seq[0]
    for k in range(1, 8):
        total = total + gain_seq[k]
    gains_out[...] = total
    more_u.relay()
    hand_over(more_u.finish(), 1, parts_of[1])
    for got, dst in finished:
        arrive(got, dst)
    for t in range(4):
        for kk in (0, 1):
            grad_piece(t, kk, lambda made: made.wait_send())
    for t in range(7):
        p.copy(pack.at[s], unit.at[s], (p.flip, b), first_back + t).wait_send()
    for made in leave:
        made.wait()
    p.copy(xa.at[b], xa.at[b], (s, p.core), dbr_far).wait_send()
    for t in range(3):
        p.copy(mix.at[0, 0:2], mix.at[0, 0:2], (s, p.core), first_mixed + t).wait_send()
    p.drain()


def chip_sum_post(p, t, parts, recv, first):
    @pl.when(jnp.equal(t, 0))
    def _():
        p.copy(parts.at[p.far], recv.at[0], (p.s, p.core), first).start()

    @pl.when(jnp.equal(t, 1))
    def _():
        p.copy(parts.at[p.core], recv.at[1], (p.s, p.core), first + 1).start()


def chip_sum_across(p, parts, recv, first):
    p.copy(recv.at[0], recv.at[0], (p.s, p.core), first).wait_recv()
    parts[p.across] = (parts[p.across].astype(F32) + recv[0].astype(F32)).astype(BF16)
    p.copy(parts.at[p.across], recv.at[2], (p.s, p.across), first + 2).start()


def chip_sum_rest(p, parts, recv, first):
    p.copy(recv.at[1], recv.at[1], (p.s, p.core), first + 1).wait_recv()
    p.copy(recv.at[2], recv.at[2], (p.s, p.core), first + 2).wait_recv()
    for k in range(3):
        p.copy(parts.at[p.b], recv.at[k], (p.s, p.core), first + k).wait_send()
    return recv[1].astype(F32) + recv[2].astype(F32)


def batch_order(p, t):
    return jnp.where(t == 0, p.far, jnp.where(t == 1, p.core, jnp.where(t == 2, p.across, p.b)))


class SeqTree:
    def __init__(self, p, slot, y_recv, relayed, z_recv):
        self.p, self.slot, self.y_recv, self.relayed, self.z_recv = p, slot, y_recv, relayed, z_recv
        self.first = p.slots(8)

    def mine(self, i):
        return self.slot(2 * i + self.p.y)[...].astype(F32)

    def start(self, pieces=(0, 1, 2, 3)):
        p = self.p
        for i in pieces:
            p.copy(
                self.slot(2 * i + 1 - p.y), self.y_recv.at[i], (p.flip, p.b), self.first + 4 + i
            ).start()

    def send(self, i, dst, z, out, into):
        p = self.p
        p.copy(self.y_recv.at[i], dst, (2 * z + p.y, p.b), self.first + out, self.first + into).start()

    def load(self, i):
        return self.y_recv.at[i][...].astype(F32)

    def reduce(self):
        p = self.p
        for i in range(4):
            p.landed(self.first + 4 + i, self.y_recv.at[i])

        def add(i):
            self.y_recv.at[i][...] = (self.load(i) + self.mine(i)).astype(BF16)

        add(p.there)
        add(p.beyond)

        @pl.when(jnp.logical_not(p.inner))
        def _():
            self.send(p.there, self.relayed.at[0], p.pair, 1, 1)
            self.send(p.beyond, self.relayed.at[1], p.pair, 2, 2)

        add(p.pair)
        self.send(p.pair, self.z_recv.at[0], p.pair, 0, 0)

    def relay(self):
        p = self.p

        @pl.when(p.inner)
        def _():
            for k, i in ((0, p.there), (1, p.beyond)):
                p.landed(self.first + 1 + k, self.relayed.at[k])
                self.y_recv.at[i][...] = (self.load(i) + self.relayed.at[k][...].astype(F32)).astype(BF16)
                self.send(i, self.z_recv.at[1], i, 1 + k, 3)

    def finish(self):
        p = self.p
        total = self.load(p.z) + self.mine(p.z)
        p.landed(self.first, self.z_recv.at[0])
        total = total + self.z_recv.at[0][...].astype(F32)
        p.landed(self.first + 3, self.z_recv.at[1])
        for out in range(3):
            p.copy(self.z_recv.at[0], self.z_recv.at[0], (p.flip, p.b), self.first + out).wait_send()
        for i in range(4):
            p.copy(self.y_recv.at[i], self.y_recv.at[i], (p.flip, p.b), self.first + 4 + i).wait_send()
        return total + self.z_recv.at[1][...].astype(F32)


class SeqSum:
    def __init__(self, p, y_recv, z_recv):
        self.p, self.y_recv, self.z_recv = p, y_recv, z_recv

    def start(self, source, mine=None):
        p = self.p
        self.index = p.post(source.at[:, 1 - p.y], self.y_recv, (p.flip, p.b))
        self.load = None
        if mine is None:
            self.mine = lambda i: source.at[i, p.y]
        else:
            self.load = p.local(source.at[:, p.y], mine)
            self.mine = lambda i: mine.at[i]

    def middle(self):
        p = self.p
        if self.load is not None:
            self.load.wait()
        p.landed(self.index, self.y_recv)
        self.far = []
        for k in (1, 2, 3):
            i = p.up(k)
            self.y_recv[i] = (self.y_recv[i].astype(F32) + self.mine(i)[...].astype(F32)).astype(BF16)
            self.far.append(p.post(self.y_recv.at[i], self.z_recv.at[k - 1], (2 * i + p.y, p.b)))

    def finish(self):
        p = self.p
        total = self.y_recv[p.z].astype(F32) + self.mine(p.z)[...].astype(F32)
        for k in (1, 2, 3):
            p.landed(self.far[k - 1], self.z_recv.at[k - 1])
            total = total + self.z_recv[k - 1].astype(F32)
        return total


def finish_kernel(
    output, dx, rqkv, rgu, rd, ro, gains,
    output_, dx_, grad_query, grad_key, grad_value, grad_out, grad_gate, grad_up, grad_down,
    gain_attn, gain_ffn, gain_query, gain_key,
):
    output_[...] = output[...]
    dx_[...] = dx[...]
    grad_out[...] = ro[...]
    grad_down[...] = rd[...]
    for c in range(4):
        pairs = []
        for kk in (0, 1):
            h = 2 * c + kk
            q, kv = heads_of(rqkv[c].astype(F32), kk)
            grad_query[:, 128 * h : 128 * h + 128] = q
            pairs.append(kv)
        first = lanes(pairs[0].shape) < 64
        grad_key[:, 128 * c : 128 * c + 128] = jnp.where(first, pairs[0], pltpu.roll(pairs[1], 64, 1))
        grad_value[:, 128 * c : 128 * c + 128] = jnp.where(first, pltpu.roll(pairs[0], 64, 1), pairs[1])
    for which, out in ((0, grad_gate), (1, grad_up)):
        wide = [rgu[c, which].astype(F32) for c in range(4)]
        out[...] = jnp.concatenate(
            [wide[c][:, 144 * i : 144 * i + 144] for i in range(8) for c in range(4)], axis=1
        )
    gain_attn[...] = gains[0:1]
    gain_ffn[...] = gains[1:2]
    gain_query[...] = gains[2:3, 0:64] + gains[2:3, 64:128]
    gain_key[...] = gains[3:4, 0:64]


def call(kernel, outs, in_specs, out_specs, scratch, cid, sems):
    return pl.pallas_call(
        kernel,
        out_shape=[jax.ShapeDtypeStruct(shape, dtype) for shape, dtype in outs],
        in_specs=in_specs,
        out_specs=out_specs,
        scratch_shapes=[pltpu.VMEM(shape, dtype) for shape, dtype in scratch]
        + [
            pltpu.SemaphoreType.DMA((sems[0],)),
            pltpu.SemaphoreType.DMA((sems[0],)),
            pltpu.SemaphoreType.DMA((sems[1],)),
        ],
        compiler_params=pltpu.CompilerParams(
            collective_id=cid, has_side_effects=True, vmem_limit_bytes=64 * 2**20
        ),
    )


def body(
    inputs, lengths, w_query, key_weight, value_weight, w_out, w_gate, w_up, w_down,
    gain_attn, gain_ffn, gain_query, gain_key, cotangent,
):
    x = inputs.reshape(256, 1024)
    dy = cotangent.reshape(256, 1024)
    freqs = theta ** (-(np.arange(32, dtype=np.float32) * 2.0) / 64)
    angles = np.arange(2048, dtype=np.float32)[:, None] * freqs.astype(np.float32)[None, :]
    cosine = jnp.asarray(np.tile(np.cos(angles), (1, 4)), F32)
    sine = jnp.asarray(np.tile(np.sin(angles), (1, 4)), F32)
    gains = [g[None] for g in (gain_query, gain_key, gain_attn, gain_ffn)]

    raw = call(
        block_kernel,
        [
            ((256, 1024), BF16), ((256, 1024), BF16), ((4, 32, 512), BF16), ((4, 2, 32, 1152), BF16),
            ((144, 1024), F32), ((32, 1024), F32), ((8, 1024), F32), ((4, 256, 1024), BF16),
        ],
        [ANY, ANY, SMEM] + [VMEM] * 6 + [ANY] * 3 + [VMEM] * 4,
        [ANY] * 2 + [VMEM] * 5 + [ANY],
        [
            ((4, 256, 1024), BF16), ((4, 256, 1024), BF16), ((8, 128, 512), BF16), ((8, 4, 32, 1024), BF16),
            ((8, 256, 256), BF16), ((8, 256, 256), BF16), ((8, 256, 128), BF16), ((8, 8, 512), F32),
            ((8, 256, 128), BF16), ((4, 8, 256, 128), BF16),
            ((4, 256, 1024), BF16), ((8, 2, 128, 1152), BF16), ((8, 144, 1024), BF16), ((1152, 1024), BF16),
            ((1024, 1152), BF16), ((4, 2, 128, 1152), BF16), ((4, 2, 128, 1152), BF16),
            ((8, 256, 128), F32), ((8, 256, 128), F32),
            ((4, 256, 1024), BF16), ((3, 256, 1024), BF16), ((3, 256, 1024), BF16),
            ((256, 1024), F32), ((256, 1024), F32), ((256, 1024), F32),
            ((4, 32, 512), BF16), ((4, 2, 32, 1152), BF16), ((8, 128), jnp.int32),
            ((256, 128), F32), ((256, 128), F32), ((4, 8, 128), jnp.int32),
            ((8, 256, 128), BF16), ((8, 8, 512), F32),
            ((4, 144, 1024), BF16), ((2, 144, 1024), BF16), ((2, 144, 1024), BF16),
            ((4, 128, 1152), BF16), ((2, 128, 1152), BF16), ((2, 128, 1152), BF16),
            ((4, 128, 1152), BF16), ((2, 128, 1152), BF16), ((2, 128, 1152), BF16),
            ((4, 128, 512), BF16), ((3, 128, 512), BF16), ((4, 32, 1024), BF16), ((3, 32, 1024), BF16),
            ((8, 1024), F32), ((4, 8, 1024), F32), ((8, 8, 1024), F32),
        ],
        0,
        (256, 32),
    )(x, dy, lengths, w_query, key_weight, value_weight, w_out, w_gate, w_up, w_down, cosine, sine, *gains)
    done = pl.pallas_call(
        finish_kernel,
        out_shape=[
            jax.ShapeDtypeStruct(shape, dtype)
            for shape, dtype in (
                ((256, 1024), BF16), ((256, 1024), BF16), ((32, 1024), F32), ((32, 512), F32),
                ((32, 512), F32), ((32, 1024), F32), ((32, 4608), F32), ((32, 4608), F32),
                ((144, 1024), F32), ((1, 1024), F32), ((1, 1024), F32), ((1, 64), F32), ((1, 64), F32),
            )
        ],
        in_specs=[VMEM] * 7,
        out_specs=[VMEM] * 13,
    )(*raw[:7])
    return (
        done[0].reshape(256, 1, 1024), done[1].reshape(256, 1, 1024), *done[2:9], *[g[0] for g in done[9:]],
    )


def rotary_tables(positions, width):
    half = width // 2
    freqs = theta ** (-(jnp.arange(half, dtype=jnp.float32) * 2.0) / width)
    angles = positions.astype(jnp.float32)[:, None] * freqs[None, :]
    cosine = jnp.concatenate([jnp.cos(angles), jnp.cos(angles)], axis=-1)
    sine = jnp.concatenate([jnp.sin(angles), jnp.sin(angles)], axis=-1)
    return (cosine, sine)


def rotate(v, cosine, sine):
    half = v.shape[-1] // 2
    turned = jnp.concatenate([-v[..., half:], v[..., :half]], axis=-1)
    return v * cosine + turned * sine


def rotate_back(grad, cosine, sine):
    half = grad.shape[-1] // 2
    moved = grad * sine
    return grad * cosine + jnp.concatenate([moved[..., half:], -moved[..., :half]], axis=-1)


def product(left, right):
    return jnp.dot(left, right, preferred_element_type=jnp.float32)


def left_product(left, right):
    return jnp.einsum("rd,rn->dn", left, right, preferred_element_type=jnp.float32)


def right_product(left, right):
    return jnp.einsum("rn,dn->rd", left, right, preferred_element_type=jnp.float32)


def rounded(v):
    return v.astype(jnp.bfloat16)


def split_rows(term, seq_size, batch_size):
    return term.reshape(
        seq_size, batch_size, term.shape[0] // (seq_size * batch_size), term.shape[1]
    )


def fold_sources(piece):
    return jnp.sum(piece, axis=1).reshape(-1, piece.shape[-1])


def general_body(
    inputs,
    lengths,
    w_query,
    key_weight,
    value_weight,
    w_out,
    w_gate,
    w_up,
    w_down,
    gain_attn,
    gain_ffn,
    gain_query,
    gain_key,
    cotangent,
):
    slice_len, seq_count, width = inputs.shape
    rows = slice_len * seq_count
    head_dim = gain_query.shape[0]
    kv_width = key_weight.shape[1]
    kv_heads = kv_width // head_dim
    q_heads = w_query.shape[1] // head_dim
    sequence_group = q_heads // kv_heads
    scale = head_dim ** (-0.5)
    cycle_size = lax.axis_size("seq")
    batch_size = lax.axis_size("batch")
    positions = lax.axis_index("seq") * slice_len + jnp.arange(slice_len, dtype=jnp.int32)
    cosine, sine = rotary_tables(positions, head_dim)
    cosine = cosine[:, None, None, :]
    sine = sine[:, None, None, :]
    shards = (w_query, key_weight, value_weight, w_out, w_gate, w_up, w_down)
    wq, key_matrix, value_matrix, wo, wg, wu, wd = (
        lax.all_gather(shards[0], ("seq", "batch"), axis=0, tiled=True),
        lax.all_gather(shards[1], ("seq", "batch"), axis=0, tiled=True),
        lax.all_gather(shards[2], ("seq", "batch"), axis=0, tiled=True),
        lax.all_gather(shards[3], ("seq", "batch"), axis=0, tiled=True),
        lax.all_gather(shards[4], ("seq", "batch"), axis=0, tiled=True),
        lax.all_gather(shards[5], ("seq", "batch"), axis=0, tiled=True),
        lax.all_gather(shards[6], ("seq", "batch"), axis=0, tiled=True),
    )
    stream = inputs.reshape(rows, width).astype(jnp.float32)
    factor_one = rms_factor(stream)
    normalized_input = rounded(stream * factor_one * gain_attn)
    query_pre = product(normalized_input, wq).reshape(slice_len, seq_count, q_heads, head_dim)
    key_before_rotation = product(normalized_input, key_matrix).reshape(
        slice_len, seq_count, kv_heads, head_dim
    )
    value_b = rounded(product(normalized_input, value_matrix)).reshape(
        slice_len, seq_count, kv_width
    )
    factor_q = rms_factor(query_pre)
    factor_k = rms_factor(key_before_rotation)
    query_b = rounded(rotate(query_pre * factor_q * gain_query, cosine, sine))
    key_b = rounded(rotate(key_before_rotation * factor_k * gain_key, cosine, sine)).reshape(
        slice_len, seq_count, kv_width
    )
    query_five = query_b.reshape(slice_len, seq_count, kv_heads, sequence_group, head_dim)

    def scores_of(keys, start):
        count = keys.shape[0]
        raw = (
            jnp.einsum(
                "tsgrd,csgd->sgrtc",
                query_five,
                keys.reshape(count, seq_count, kv_heads, head_dim),
                preferred_element_type=jnp.float32,
            )
            * scale
        )
        key_pos = start + jnp.arange(count, dtype=jnp.int32)
        causal = key_pos[None, :] <= positions[:, None]
        inside = key_pos[None, :] < lengths[:, None]
        valid = causal[None, :, :] & inside[:, None, :]
        return (raw, valid[:, None, None, :, :])

    state_shape = (seq_count, kv_heads, sequence_group, slice_len)
    shard_ids = jnp.arange(cycle_size, dtype=jnp.int32)
    top = jnp.full(state_shape, -1e30, jnp.float32)
    keys = lax.all_gather(key_b, "seq", axis=0, tiled=True)
    value_rows = lax.all_gather(value_b, "seq", axis=0, tiled=True)
    count = keys.shape[0]
    raw, valid = scores_of(keys, jnp.int32(0))
    masked = jnp.where(valid, raw, -jnp.inf)
    new_top = jnp.maximum(top, jnp.max(masked, axis=-1))
    probs = jnp.exp(masked - new_top[..., None])
    total = jnp.sum(probs, axis=-1)
    acc = jnp.einsum(
        "sgrtc,csgd->sgrtd",
        rounded(probs),
        value_rows.reshape(count, seq_count, kv_heads, head_dim),
        preferred_element_type=jnp.float32,
    )
    state = (new_top, total, acc)
    top, total, acc = state
    attn_out = acc / total[..., None]
    log_total = top + jnp.log(total)
    mixed_b = rounded(jnp.transpose(attn_out, (3, 0, 1, 2, 4)).reshape(rows, q_heads * head_dim))
    middle = stream + product(mixed_b, wo)
    factor_two = rms_factor(middle)
    normed_two = rounded(middle * factor_two * gain_ffn)
    gate = product(normed_two, wg)
    up_part = product(normed_two, wu)
    sigma = jax.nn.sigmoid(gate)
    swish = gate * sigma
    hidden_b = rounded(swish * up_part)
    result = middle + product(hidden_b, wd)
    output = rounded(result).reshape(slice_len, seq_count, width)
    wq, key_matrix, value_matrix, wo, wg, wu, wd = (
        lax.all_gather(shards[0], ("seq", "batch"), axis=0, tiled=True),
        lax.all_gather(shards[1], ("seq", "batch"), axis=0, tiled=True),
        lax.all_gather(shards[2], ("seq", "batch"), axis=0, tiled=True),
        lax.all_gather(shards[3], ("seq", "batch"), axis=0, tiled=True),
        lax.all_gather(shards[4], ("seq", "batch"), axis=0, tiled=True),
        lax.all_gather(shards[5], ("seq", "batch"), axis=0, tiled=True),
        lax.all_gather(shards[6], ("seq", "batch"), axis=0, tiled=True),
    )
    grad_res = cotangent.reshape(rows, width).astype(jnp.float32)
    grad_ffo = rounded(grad_res)
    grad_wd = left_product(hidden_b, grad_ffo)
    grad_hidden = right_product(grad_ffo, wd)
    grad_gate = rounded(grad_hidden * up_part * sigma * (1.0 + gate * (1.0 - sigma)))
    grad_up = rounded(grad_hidden * swish)
    grad_wg = left_product(normed_two, grad_gate)
    grad_wu = left_product(normed_two, grad_up)
    grad_normed_two = right_product(grad_gate, wg) + right_product(grad_up, wu)
    grad_gain_ffn = jnp.sum(grad_normed_two * middle * factor_two, axis=0)
    grad_middle = grad_res + norm_back(grad_normed_two * gain_ffn, middle, factor_two)
    grad_branch = rounded(grad_middle)
    grad_wo = left_product(mixed_b, grad_branch)
    grad_mixed = rounded(right_product(grad_branch, wo))
    grad_five = grad_mixed.reshape(slice_len, seq_count, kv_heads, sequence_group, head_dim)
    delta = jnp.sum(
        jnp.transpose(grad_five, (1, 2, 3, 0, 4)).astype(jnp.float32) * attn_out, axis=-1
    )
    gathered = (
        lax.all_gather(key_b, "seq", axis=0, tiled=True),
        lax.all_gather(value_b, "seq", axis=0, tiled=True),
    )

    def back_step(grad_query, item):
        index, keys, value_rows = item
        raw, valid = scores_of(keys, index * slice_len)
        probs = jnp.where(valid, jnp.exp(raw - log_total[..., None]), 0.0)
        key_four = keys.reshape(slice_len, seq_count, kv_heads, head_dim)
        value_four = value_rows.reshape(slice_len, seq_count, kv_heads, head_dim)
        grad_probs = jnp.einsum(
            "tsgrd,csgd->sgrtc", grad_five, value_four, preferred_element_type=jnp.float32
        )
        grad_score = rounded(probs * (grad_probs - delta[..., None]))
        grad_query = (
            grad_query
            + jnp.einsum(
                "sgrtc,csgd->tsgrd", grad_score, key_four, preferred_element_type=jnp.float32
            )
            * scale
        )
        key_term = (
            jnp.einsum(
                "sgrtc,tsgrd->csgd", grad_score, query_five, preferred_element_type=jnp.float32
            )
            * scale
        )
        value_term = jnp.einsum(
            "sgrtc,tsgrd->csgd", rounded(probs), grad_five, preferred_element_type=jnp.float32
        )
        return (
            grad_query,
            (
                key_term.reshape(slice_len, seq_count, kv_width),
                value_term.reshape(slice_len, seq_count, kv_width),
            ),
        )

    items = (
        shard_ids,
        gathered[0].reshape(cycle_size, slice_len, seq_count, kv_width),
        gathered[1].reshape(cycle_size, slice_len, seq_count, kv_width),
    )
    grad_query, terms = lax.scan(
        back_step,
        jnp.zeros((slice_len, seq_count, kv_heads, sequence_group, head_dim), jnp.float32),
        items,
    )
    key_terms = terms[0].reshape(cycle_size * slice_len, seq_count, kv_width)
    value_terms = terms[1].reshape(cycle_size * slice_len, seq_count, kv_width)
    grad_key, grad_value = (
        lax.psum_scatter(
            key_terms.astype(jnp.bfloat16), "seq", scatter_dimension=0, tiled=True
        ).astype(jnp.float32),
        lax.psum_scatter(
            value_terms.astype(jnp.bfloat16), "seq", scatter_dimension=0, tiled=True
        ).astype(jnp.float32),
    )
    grad_qr = (
        rounded(grad_query).astype(jnp.float32).reshape(slice_len, seq_count, q_heads, head_dim)
    )
    grad_qn = rotate_back(grad_qr, cosine, sine)
    grad_gain_query = jnp.sum(grad_qn * query_pre * factor_q, axis=(0, 1, 2))
    grad_qp = rounded(
        norm_back(grad_qn * gain_query, query_pre, factor_q).reshape(rows, q_heads * head_dim)
    )
    grad_kr = (
        rounded(grad_key).astype(jnp.float32).reshape(slice_len, seq_count, kv_heads, head_dim)
    )
    grad_kn = rotate_back(grad_kr, cosine, sine)
    grad_gain_key = jnp.sum(grad_kn * key_before_rotation * factor_k, axis=(0, 1, 2))
    grad_kp = rounded(
        norm_back(grad_kn * gain_key, key_before_rotation, factor_k).reshape(rows, kv_width)
    )
    grad_vp = rounded(grad_value).reshape(rows, kv_width)
    grad_wq = left_product(normalized_input, grad_qp)
    grad_wk = left_product(normalized_input, grad_kp)
    grad_wv = left_product(normalized_input, grad_vp)
    grad_normed = (
        right_product(grad_qp, wq)
        + right_product(grad_kp, key_matrix)
        + right_product(grad_vp, value_matrix)
    )
    grad_gain_attn = jnp.sum(grad_normed * stream * factor_one, axis=0)
    grad_stream = grad_middle + norm_back(grad_normed * gain_attn, stream, factor_one)
    spread = (
        lax.all_to_all(
            split_rows(grad_wq, cycle_size, batch_size).astype(jnp.bfloat16),
            "batch",
            split_axis=1,
            concat_axis=1,
            tiled=True,
        ).astype(jnp.float32),
        lax.all_to_all(
            split_rows(grad_wk, cycle_size, batch_size).astype(jnp.bfloat16),
            "batch",
            split_axis=1,
            concat_axis=1,
            tiled=True,
        ).astype(jnp.float32),
        lax.all_to_all(
            split_rows(grad_wv, cycle_size, batch_size).astype(jnp.bfloat16),
            "batch",
            split_axis=1,
            concat_axis=1,
            tiled=True,
        ).astype(jnp.float32),
        lax.all_to_all(
            split_rows(grad_wo, cycle_size, batch_size).astype(jnp.bfloat16),
            "batch",
            split_axis=1,
            concat_axis=1,
            tiled=True,
        ).astype(jnp.float32),
        lax.all_to_all(
            split_rows(grad_wg, cycle_size, batch_size).astype(jnp.bfloat16),
            "batch",
            split_axis=1,
            concat_axis=1,
            tiled=True,
        ).astype(jnp.float32),
        lax.all_to_all(
            split_rows(grad_wu, cycle_size, batch_size).astype(jnp.bfloat16),
            "batch",
            split_axis=1,
            concat_axis=1,
            tiled=True,
        ).astype(jnp.float32),
        lax.all_to_all(
            split_rows(grad_wd, cycle_size, batch_size).astype(jnp.bfloat16),
            "batch",
            split_axis=1,
            concat_axis=1,
            tiled=True,
        ).astype(jnp.float32),
    )
    partial_sums = [fold_sources(piece) for piece in spread]
    summed = (
        lax.psum_scatter(
            partial_sums[0].astype(jnp.bfloat16), "seq", scatter_dimension=0, tiled=True
        ).astype(jnp.float32),
        lax.psum_scatter(
            partial_sums[1].astype(jnp.bfloat16), "seq", scatter_dimension=0, tiled=True
        ).astype(jnp.float32),
        lax.psum_scatter(
            partial_sums[2].astype(jnp.bfloat16), "seq", scatter_dimension=0, tiled=True
        ).astype(jnp.float32),
        lax.psum_scatter(
            partial_sums[3].astype(jnp.bfloat16), "seq", scatter_dimension=0, tiled=True
        ).astype(jnp.float32),
        lax.psum_scatter(
            partial_sums[4].astype(jnp.bfloat16), "seq", scatter_dimension=0, tiled=True
        ).astype(jnp.float32),
        lax.psum_scatter(
            partial_sums[5].astype(jnp.bfloat16), "seq", scatter_dimension=0, tiled=True
        ).astype(jnp.float32),
        lax.psum_scatter(
            partial_sums[6].astype(jnp.bfloat16), "seq", scatter_dimension=0, tiled=True
        ).astype(jnp.float32),
    )
    gains = lax.psum(
        (grad_gain_attn, grad_gain_ffn, grad_gain_query, grad_gain_key), ("seq", "batch")
    )
    grad_inputs = rounded(grad_stream).reshape(slice_len, seq_count, width)
    return (
        output,
        grad_inputs,
        summed[0],
        summed[1],
        summed[2],
        summed[3],
        summed[4],
        summed[5],
        summed[6],
        gains[0],
        gains[1],
        gains[2],
        gains[3],
    )


def solution(mesh):
    sharded = P(("seq", "batch"), None)
    stream = P("seq", "batch", None)
    in_specs = (stream, P("batch")) + (sharded,) * 7 + (P(),) * 4 + (stream,)
    out_specs = (stream, stream) + (sharded,) * 7 + (P(),) * 4
    grouped = mesh.shape["seq"] == 8 and mesh.shape["batch"] == 4
    step = body if grouped else general_body
    return jax.shard_map(step, mesh=mesh, in_specs=in_specs, out_specs=out_specs, check_vma=False)
```

```python
import functools

import jax
import jax.numpy as jnp
import numpy as np
from jax import lax
from jax.experimental import pallas as pl
from jax.experimental.pallas import tpu as pltpu
from jax.sharding import PartitionSpec as P

MESH = pl.DeviceIdType.MESH
F32 = jnp.float32
BF16 = jnp.bfloat16
eps = 1e-05
theta = 1000000.0
VMEM = pl.BlockSpec(memory_space=pltpu.VMEM)
ANY = pl.BlockSpec(memory_space=pl.ANY)
SMEM = pl.BlockSpec(memory_space=pltpu.SMEM)


def nn(left, right):
    return lax.dot_general(left, right, (((1,), (0,)), ((), ())), preferred_element_type=F32)


def nt(left, right):
    return lax.dot_general(left, right, (((1,), (1,)), ((), ())), preferred_element_type=F32)


def tn(left, right):
    return lax.dot_general(left, right, (((0,), (0,)), ((), ())), preferred_element_type=F32)


def rms_factor(v):
    return lax.rsqrt(jnp.mean(v * v, axis=-1, keepdims=True) + eps)


def norm_back(grad, value, factor):
    return factor * (
        grad - value * factor * factor * jnp.mean(grad * value, axis=-1, keepdims=True)
    )


def lanes(shape):
    return lax.broadcasted_iota(jnp.int32, shape, len(shape) - 1)


def rows_of(shape):
    return lax.broadcasted_iota(jnp.int32, shape, len(shape) - 2)


def head_mean(v):
    first = lanes(v.shape) < 64
    low = jnp.sum(jnp.where(first, v, 0.0), axis=-1, keepdims=True)
    high = jnp.sum(jnp.where(first, 0.0, v), axis=-1, keepdims=True)
    return jnp.where(first, low, high) * (1.0 / 64.0)


def rope(u, cosine, sine):
    early = lax.rem(lanes(u.shape), 64) < 32
    turned = jnp.where(early, -pltpu.roll(u, 96, 1), pltpu.roll(u, 32, 1))
    return u * cosine + turned * sine


def rope_back(u, cosine, sine):
    early = lax.rem(lanes(u.shape), 64) < 32
    w = u * sine
    return u * cosine + jnp.where(early, pltpu.roll(w, 96, 1), -pltpu.roll(w, 32, 1))


class Place:
    def __init__(self, send_sem, recv_sem, local_sem):
        self.s = lax.axis_index("seq")
        self.b = lax.axis_index("batch")
        self.z = self.s // 2
        self.y = lax.rem(self.s, 2)
        self.core = self.b + 1 - 2 * lax.rem(self.b, 2)
        self.across = lax.rem(self.b + 2, 4)
        self.far = 3 - self.b
        self.flip = 2 * self.z + 1 - self.y
        self.inner = jnp.logical_or(self.z == 1, self.z == 2)
        self.pair = self.z + 1 - 2 * lax.rem(self.z, 2)
        self.there = jnp.where(self.z < 2, 2, 1)
        self.beyond = jnp.where(self.z < 2, 3, 0)
        self.send_sem, self.recv_sem, self.local_sem = send_sem, recv_sem, local_sem
        self.used = 0
        self.used_local = 0
        self.sent = []

    def up(self, k):
        return lax.rem(self.z + k, 4)

    def down(self, k):
        return lax.rem(self.z + 4 - k, 4)

    def greet(self):
        self.hello()
        self.meet()

    def hello(self):
        barrier = pltpu.get_barrier_semaphore()
        for k in (1, 2, 3):
            pl.semaphore_signal(
                barrier, inc=1, device_id=(self.s, lax.rem(self.b + k, 4)), device_id_type=MESH
            )
        for k in range(1, 8):
            pl.semaphore_signal(
                barrier, inc=1, device_id=(lax.rem(self.s + k, 8), self.b), device_id_type=MESH
            )

    def meet(self):
        pl.semaphore_wait(pltpu.get_barrier_semaphore(), 10)

    def slots(self, count):
        first = self.used
        self.used += count
        return first

    def copy(self, src, dst, device, out, into=None):
        return pltpu.make_async_remote_copy(
            src_ref=src,
            dst_ref=dst,
            send_sem=self.send_sem.at[out],
            recv_sem=self.recv_sem.at[out if into is None else into],
            device_id=device,
            device_id_type=MESH,
        )

    def post(self, src, dst, device):
        index = self.slots(1)
        made = self.copy(src, dst, device, index)
        made.start()
        self.sent.append(made)
        return index

    def landed(self, index, ref):
        self.copy(ref, ref, (self.s, self.core), index).wait_recv()

    def local(self, src, dst):
        index = self.used_local
        self.used_local += 1
        made = pltpu.make_async_copy(src, dst, self.local_sem.at[index])
        made.start()
        return made

    def drain(self):
        for made in self.sent:
            made.wait_send()
        self.sent = []


class Spread:
    def __init__(self, p, slot):
        self.p, self.slot = p, slot
        self.first = p.slots(8)
        self.from_z = (p.pair, p.there, p.beyond)

    def send(self, s, device, out, into):
        self.p.copy(self.slot(s), self.slot(s), device, self.first + out, self.first + into).start()

    def start_z(self):
        p = self.p
        self.send(p.s, (2 * p.pair + p.y, p.b), 0, 0)
        self.send(p.s, (2 * p.there + p.y, p.b), 1, jnp.where(p.inner, 1, 2))

    def start_y(self):
        p = self.p
        self.send(p.s, (p.flip, p.b), 4, 3)

    def start(self):
        self.start_z()
        self.start_y()

    def land(self, j):
        p = self.p
        s = 2 * self.from_z[j] + p.y
        p.landed(self.first + j, self.slot(s))
        if j > 0:

            @pl.when(p.inner)
            def _():
                self.send(s, (2 * p.pair + p.y, p.b), 1 + j, j)

        self.send(s, (p.flip, p.b), 5 + j, 4 + j)

    def land_inner(self):
        @pl.when(self.p.inner)
        def _():
            self.land(1)
            self.land(2)

    def land_end(self):
        @pl.when(jnp.logical_not(self.p.inner))
        def _():
            self.land(1)
            self.land(2)

    def finish(self):
        p = self.p
        p.landed(self.first + 3, self.slot(p.flip))
        for j in range(3):
            p.landed(self.first + 4 + j, self.slot(2 * self.from_z[j] + 1 - p.y))

    def drain(self):
        p = self.p

        def sent(out):
            p.copy(self.slot(p.s), self.slot(p.s), (p.flip, p.b), self.first + out).wait_send()

        for out in (0, 1, 4, 5, 6, 7):
            sent(out)

        @pl.when(p.inner)
        def _():
            sent(2)
            sent(3)


def heads_of(whole, kk):
    return whole[:, 256 * kk : 256 * kk + 128], whole[:, 256 * kk + 128 : 256 * kk + 256]


def pack_projections(w_query, key_weight, value_weight, out):
    for c in range(4):
        k = key_weight[:, 128 * c : 128 * c + 128].astype(F32)
        v = value_weight[:, 128 * c : 128 * c + 128].astype(F32)
        first = lanes(k.shape) < 64
        pairs = (
            jnp.where(first, k, pltpu.roll(v, 64, 1)),
            jnp.where(first, pltpu.roll(k, 64, 1), v),
        )
        for kk in (0, 1):
            h = 2 * c + kk
            out[c, :, 256 * kk : 256 * kk + 128] = w_query[:, 128 * h : 128 * h + 128]
            out[c, :, 256 * kk + 128 : 256 * kk + 256] = pairs[kk].astype(BF16)


def pack_hidden(source, out, which):
    wide = source[...].astype(F32)
    for c in range(4):
        pieces = [wide[:, 144 * (4 * i + c) : 144 * (4 * i + c) + 144] for i in range(8)]
        out[c, which] = jnp.concatenate(pieces, axis=1).astype(BF16)


def twice(v):
    return jnp.concatenate([v[...], v[...]], axis=1)


def near_first(p, t):
    return jnp.where(t == 0, p.b, jnp.where(t == 1, p.core, jnp.where(t == 2, p.across, p.far)))


def block_kernel(
    x, dy, lengths, w_query, key_weight, value_weight, w_out, w_gate, w_up, w_down,
    cos_table, sin_table, gain_query, gain_key, gain_a, gain_f,
    output, dx, rqkv, rgu, rd, ro, gains_out, norm_park,
    xa, norm, wqkv, wo, pack, unit, unit_out, lse, kv, mix, dy_all, wgu, wd, gd,
    hid, dgate, dup, dk_sum, dv_sum, parts, recv, recv_o, keep, result, middle,
    qkv_send, gu_send, length, cos, sin, length_all,
    dou, delta,
    y_d, t_d, z_d, y_g, t_g, z_g, y_u, t_u, z_u, y_q, z_q, y_o, z_o,
    gain_sum, gain_batch, gain_seq,
    send_sem, recv_sem, local_sem,
):
    p = Place(send_sem, recv_sem, local_sem)
    s, b, z, y = p.s, p.b, p.z, p.y
    my_rows = pl.ds(pl.multiple_of(32 * b, 32), 32)
    my_positions = pl.ds(pl.multiple_of(256 * s, 256), 256)
    p.hello()
    own_d = p.local(w_down, wd.at[s])
    own_x = p.local(x, xa.at[b])
    own_wo = p.local(w_out, wo.at[s, b])
    own_dy = p.local(dy, dy_all.at[b])
    own_tables = [p.local(cos_table.at[my_positions], cos), p.local(sin_table.at[my_positions], sin)]
    pack_projections(w_query, key_weight, value_weight, qkv_send)
    length[...] = jnp.broadcast_to(lengths[0], (8, 128)).astype(jnp.int32)
    own_qkv = p.local(qkv_send.at[b], wqkv.at[s, my_rows])
    length_all[b] = length[...]
    pack_hidden(w_gate, gu_send, 0)
    pack_hidden(w_up, gu_send, 1)
    p.meet()

    got_qkv, got_len = [], []
    for k in (1, 2, 3):
        to = lax.rem(b + k, 4)
        got_qkv.append(p.post(qkv_send.at[to], wqkv.at[s, my_rows], (s, to)))
    own_x.wait()
    x_across = p.post(xa.at[b], xa.at[b], (s, p.across))
    x_core = p.post(xa.at[b], xa.at[b], (s, p.core))
    for k in (1, 2, 3):
        to = lax.rem(b + k, 4)
        got_len.append(p.post(length, length_all.at[b], (s, to)))
    spread_d = Spread(p, lambda i: wd.at[i])
    spread_g = Spread(p, lambda i: wgu.at[i, 0])
    spread_u = Spread(p, lambda i: wgu.at[i, 1])
    own_d.wait()
    spread_d.start_y()

    def normalize(g):
        xg = xa[g].astype(F32)
        norm[g] = (xg * rms_factor(xg) * gain_a[...]).astype(BF16)

    normalize(b)
    own_qkv.wait()
    for k in (1, 2, 3):
        p.landed(got_qkv[k - 1], wqkv.at[s, my_rows])
    z_qkv = [p.post(wqkv.at[s], wqkv.at[s], (2 * p.up(k) + y, b)) for k in (1, 2, 3)]
    y_qkv = [p.post(wqkv.at[s], wqkv.at[s], (p.flip, b))]
    own_gu = p.local(gu_send.at[b], wgu.at[s, :, my_rows])
    got_gu = []
    for k in (1, 2, 3):
        to = lax.rem(b + k, 4)
        got_gu.append(p.post(gu_send.at[to], wgu.at[s, :, my_rows], (s, to)))
    for k in (1, 2, 3):
        slot = 2 * p.down(k) + y
        p.landed(z_qkv[k - 1], wqkv.at[slot])
        y_qkv.append(p.post(wqkv.at[slot], wqkv.at[slot], (p.flip, b)))
    spread_d.start_z()
    own_wo.wait()
    z_wo = [p.post(wo.at[s, b], wo.at[s, b], (2 * p.up(k) + y, b)) for k in (1, 2, 3)]
    y_wo = [p.post(wo.at[s, b], wo.at[s, b], (p.flip, b))]
    p.landed(x_core, xa.at[p.core])
    normalize(p.core)
    p.landed(x_across, xa.at[p.across])
    x_far = p.post(xa.at[p.across], xa.at[p.across], (s, p.core))
    for made in own_tables:
        made.wait()
    p.landed(y_qkv[0], wqkv.at[p.flip])
    for k in (1, 2, 3):
        p.landed(y_qkv[k], wqkv.at[2 * p.down(k) + 1 - y])
    gain_q, gain_k = twice(gain_query), twice(gain_key)
    own_gu.wait()
    for k in (1, 2, 3):
        p.landed(got_gu[k - 1], wgu.at[s, :, my_rows])
    spread_g.start_y()
    spread_u.start_y()

    first_unit = p.slots(8)

    def each_piece(t, kk, act):
        to = 2 * near_first(p, t) + kk

        @pl.when(to != s)
        def _():
            act(p.copy(pack.at[to], unit.at[s], (to, b), first_unit + 2 * t + kk, first_unit + s))

    def project(t, carry):
        g = near_first(p, t)

        @pl.when(t == 3)
        def _():
            p.landed(x_far, xa.at[p.far])

        @pl.when(t >= 2)
        def _():
            normalize(g)

        whole = nn(norm[g], wqkv[...].reshape(1024, 512))
        for kk in (0, 1):
            q, kvp = heads_of(whole, kk)
            qn = q * lax.rsqrt(head_mean(q * q) + eps) * gain_q
            kn = kvp * lax.rsqrt(head_mean(kvp * kvp) + eps) * gain_k
            qr = rope(qn, cos[...], sin[...]) * 0.125
            kr = rope(kn, cos[...], sin[...])
            pack[2 * g + kk, :, 0:128] = qr.astype(BF16)
            pack[2 * g + kk, :, 128:256] = jnp.where(lanes(kr.shape) < 64, kr, kvp).astype(BF16)
            each_piece(t, kk, lambda made: made.start())

        return carry

    lax.fori_loop(0, 4, project, 0)
    own_unit = p.local(pack.at[s], unit.at[s])
    parked = p.local(norm, norm_park)
    for k in (1, 2, 3):
        slot = 2 * p.down(k) + y
        p.landed(z_wo[k - 1], wo.at[slot, b])
        y_wo.append(p.post(wo.at[slot, b], wo.at[slot, b], (p.flip, b)))
    spread_d.land(0)
    spread_d.land_inner()
    own_dy.wait()
    dy_across = p.post(dy_all.at[b], dy_all.at[b], (s, p.across))
    dy_core = p.post(dy_all.at[b], dy_all.at[b], (s, p.core))
    for k in (1, 2, 3):
        p.landed(got_len[k - 1], length_all.at[lax.rem(b + 4 - k, 4)])

    spread_g.start_z()
    for k in range(1, 8):
        src = lax.rem(s + k, 8)
        p.landed(first_unit + src, unit.at[src])
    own_unit.wait()
    p.landed(y_wo[0], wo.at[p.flip, b])
    for k in (1, 2, 3):
        p.landed(y_wo[k], wo.at[2 * p.down(k) + 1 - y, b])
    wo_across = p.post(wo.at[:, b], wo.at[:, b], (s, p.across))
    wo_core = p.post(wo.at[:, b], wo.at[:, b], (s, p.core))

    def values(j):
        return dup.at[j // 2, lax.rem(j, 2), 0:80, 0:256]

    def prepare(j, carry):
        live = j * 256 + rows_of((256, 128)) < length_all[z][0:1, :]
        masked = jnp.where(live, unit[j, :, 128:256].astype(F32), 0.0)
        kv[j] = masked.astype(BF16)
        turned = jnp.transpose(masked)[64:128].astype(BF16)
        alive = j * 256 + lanes((16, 256)) < length_all[z][0:1, 0:1]
        counted = jnp.where(alive, 1.0, 0.0).astype(BF16)
        values(j)[...] = jnp.concatenate([turned, counted], axis=0)
        return carry

    lax.fori_loop(0, 8, prepare, 0)
    p.landed(dy_across, dy_all.at[p.across])
    dy_far = p.post(dy_all.at[p.across], dy_all.at[p.across], (s, p.core))
    first_mix, first_across, first_core = p.slots(8), p.slots(8), p.slots(8)

    def mix_send(src, t):
        p.copy(mix.at[b, src], mix.at[b, src], (s, p.across), first_across + t).start()
        p.copy(mix.at[b, src], mix.at[b, src], (s, p.core), first_core + t).start()

    def mix_arrived(t):
        src = lax.rem(s + 7 - t, 8)
        p.landed(first_mix + t, mix.at[b, src])
        mix_send(src, t)

    def attend(t, carry):
        i = lax.rem(s + 1 + t, 8)
        qt = jnp.transpose(unit[i, :, 0:128].astype(F32)).astype(BF16)
        both = jnp.concatenate([qt[0:64], qt[64:128]], axis=1)
        right = jnp.concatenate([both, jnp.zeros((64, 512), BF16)], axis=0)

        def block(j, acc):
            return acc + nn(values(j)[...], jnp.exp(nn(kv[j], right)).astype(BF16))

        acc = lax.fori_loop(0, i, block, jnp.zeros((80, 512), F32))
        causal = rows_of((256, 512)) <= lax.rem(lanes((256, 512)), 256)
        edge = jnp.where(causal, jnp.exp(nn(kv[i], right)), 0.0).astype(BF16)
        acc = acc + nn(values(i)[...], edge)
        total = acc[64:65]
        out = acc[0:64] / total
        out = jnp.concatenate([out[:, 0:256], out[:, 256:512]], axis=0)
        unit_out[i] = jnp.transpose(out).astype(BF16)
        lse[i] = jnp.broadcast_to(jnp.log(total), (8, 512))

        @pl.when(t < 7)
        def _():
            p.copy(unit_out.at[i], mix.at[b, s], (i, b), first_mix + t).start()

        @pl.when(t == 1)
        def _():
            spread_d.land_end()

        @pl.when(t == 6)
        def _():
            spread_g.land(0)
            spread_g.land_inner()
            spread_u.start_z()

        @pl.when(t >= 4)
        def _():
            mix_arrived(t - 4)

        return carry

    lax.fori_loop(0, 8, attend, 0)
    own_mix = p.local(unit_out.at[s], mix.at[b, s])
    own_mix.wait()
    mix_send(s, 7)
    for t in range(4, 7):
        mix_arrived(t)
    spread_g.land_end()
    p.landed(dy_core, dy_all.at[p.core])
    p.landed(dy_far, dy_all.at[p.far])
    spread_d.finish()

    def hidden_back(g, carry):
        rows = pl.ds(pl.multiple_of(g * 256, 256), 256)
        dgate[g] = nt(dy_all[g], wd[...].reshape(1152, 1024)).astype(BF16).reshape(2, 128, 1152)
        return carry

    lax.fori_loop(0, 4, hidden_back, 0)
    p.landed(wo_across, wo.at[:, p.across])
    wo_far = p.post(wo.at[:, p.across], wo.at[:, p.across], (s, p.core))
    for t in range(8):
        p.landed(first_across + t, mix.at[p.across, lax.rem(s + 7 - t, 8)])
    mix_far = p.post(mix.at[p.across], mix.at[p.across], (s, p.core))
    for t in range(8):
        p.landed(first_core + t, mix.at[p.core, lax.rem(s + 7 - t, 8)])
    p.landed(wo_core, wo.at[:, p.core])
    p.landed(wo_far, wo.at[:, p.far])
    spread_u.land(0)
    spread_u.land_inner()
    p.landed(mix_far, mix.at[p.far])

    parked.wait()

    def project_out(g, carry):
        mixed = jnp.concatenate([mix[c, 2 * g + kk] for c in range(4) for kk in (0, 1)], axis=1)
        mid = xa[g].astype(F32) + nn(mixed, wo[...].reshape(1024, 1024))
        norm[g] = (mid * rms_factor(mid) * gain_f[...]).astype(BF16)

        @pl.when(g == b)
        def _():
            middle[...] = mid

        return carry

    lax.fori_loop(0, 4, project_out, 0)

    for t in range(8):
        if t < 7:
            p.copy(unit_out.at[s], mix.at[b, s], (p.flip, b), first_mix + t).wait_send()
        p.copy(mix.at[b, s], mix.at[b, s], (s, p.across), first_across + t).wait_send()
        p.copy(mix.at[b, s], mix.at[b, s], (s, p.core), first_core + t).wait_send()
    for t in range(4):
        for kk in (0, 1):
            each_piece(t, kk, lambda made: made.wait_send())
    p.drain()

    def turn(e, carry):
        for g in range(4):
            hid[0:128, 256 * g : 256 * g + 256] = jnp.transpose(
                mix[e // 2, 2 * g + lax.rem(e, 2)].astype(F32)
            ).astype(BF16)
        gu_send[e // 2, lax.rem(e, 2), :, 0:1024] = hid[my_rows, 0:1024]
        return carry

    lax.fori_loop(0, 8, turn, 0)
    spread_u.land_end()
    spread_g.finish()

    def gate_of(g, carry):
        rows = pl.ds(pl.multiple_of(g * 256, 256), 256)
        hid[rows] = nn(norm[g], wgu[:, 0].reshape(1024, 1152)).astype(BF16)
        return carry

    lax.fori_loop(0, 4, gate_of, 0)
    spread_u.finish()
    first_n = p.slots(3)

    def gated(g, carry):
        rows = pl.ds(pl.multiple_of(g * 256, 256), 256)
        gate = hid[rows].astype(F32)
        up = nn(norm[g], wgu[:, 1].reshape(1024, 1152))
        dh = dgate[g].reshape(256, 1152).astype(F32)
        sg = 1.0 / (1.0 + jnp.exp(-gate))
        swish = gate * sg
        hid[rows] = (swish * up).astype(BF16)
        dgate[g] = (dh * up * sg * (1.0 + gate * (1.0 - sg))).astype(BF16).reshape(2, 128, 1152)
        dup[g] = (dh * swish).astype(BF16).reshape(2, 128, 1152)
        return carry

    lax.fori_loop(0, 4, gated, 0)

    def down_rows(c, carry, at=None):
        rows = pl.multiple_of(128 * c, 128)
        gd[pl.ds(rows, 128), at] = tn(
            hid[:, pl.ds(rows, 128)], dy_all[:, :, at].reshape(1024, 512)
        ).astype(BF16)
        return carry

    halves = (pl.ds(0, 512), pl.ds(512, 512))
    sum_d, more_d = [
        SeqTree(
            p,
            functools.partial(lambda at, i: gd.at[pl.ds(pl.multiple_of(144 * i, 16), 144), at], at),
            y_d.at[:, :, at], t_d.at[:, :, at], z_d.at[:, :, at],
        )
        for at in halves
    ]
    lax.fori_loop(0, 9, functools.partial(down_rows, at=halves[0]), 0)
    sum_d.start()

    def narrowed(t, carry):
        g = batch_order(p, t)
        part = nt(dgate[g].reshape(256, 1152), wgu[:, 0].reshape(1024, 1152)) + nt(
            dup[g].reshape(256, 1152), wgu[:, 1].reshape(1024, 1152)
        )
        parts[g] = part.astype(BF16)

        @pl.when(t == 3)
        def _():
            keep[...] = part

        chip_sum_post(p, t, parts, recv, first_n)
        return carry

    lax.fori_loop(0, 4, narrowed, 0)
    chip_sum_across(p, parts, recv, first_n)
    lax.fori_loop(0, 9, functools.partial(down_rows, at=halves[1]), 0)
    more_d.start()
    parts_of = (pl.ds(0, 640), pl.ds(640, 512))

    def tree(which, at, y_recv, relayed, z_recv):
        return SeqTree(
            p, lambda i: wgu.at[i, which, :, at], y_recv.at[:, :, at], relayed.at[:, :, at], z_recv.at[:, :, at]
        )

    sum_g, more_g = [tree(0, at, y_g, t_g, z_g) for at in parts_of]
    sum_u, more_u = [tree(1, at, y_u, t_u, z_u) for at in parts_of]

    for spread in (spread_d, spread_g, spread_u):
        spread.drain()

    def gate_rows(c, carry):
        at = pl.multiple_of(128 * c, 128)
        side = norm[:, :, pl.ds(at, 128)].reshape(1024, 128)
        wgu[c, 0] = tn(side, dgate[...].reshape(1024, 1152)).astype(BF16)
        wgu[c, 1] = tn(side, dup[...].reshape(1024, 1152)).astype(BF16)
        return carry

    lax.fori_loop(0, 8, gate_rows, 0)
    load_norm = p.local(norm_park, norm)

    mid = middle[...]
    r2 = rms_factor(mid)
    grad_two = keep[...] + chip_sum_rest(p, parts, recv, first_n)
    gain_sum[...] = jnp.zeros((8, 1024), F32)
    gain_sum[1:2] = jnp.sum(grad_two * mid * r2, axis=0, keepdims=True)
    dm = dy_all[b].astype(F32) + norm_back(grad_two * gain_f[...], mid, r2)
    result[...] = mid
    middle[...] = dm
    xa[b] = dm.astype(BF16)

    first_mixed = p.slots(3)

    def mixed_back(t, carry):
        c = batch_order(p, t)
        place = jnp.where(t == 3, 1, 0)
        for kk in (0, 1):
            mix[place, 2 * c + kk] = nt(xa[b], wo[2 * c + kk].reshape(128, 1024)).astype(BF16)

        @pl.when(t < 3)
        def _():
            p.copy(
                mix.at[0, pl.ds(2 * c, 2)], mix.at[1, pl.ds(2 * b, 2)], (s, c), first_mixed + t
            ).start()

        return carry

    lax.fori_loop(0, 4, mixed_back, 0)
    dbr_across = p.post(xa.at[b], xa.at[b], (s, p.across))
    dbr_core = p.post(xa.at[b], xa.at[b], (s, p.core))
    def down(g, carry):
        part = nn(hid[pl.ds(pl.multiple_of(g * 256, 256), 256)], wd[...].reshape(1152, 1024))
        dy_all[g] = part.astype(BF16)

        @pl.when(g == b)
        def _():
            result[...] = result[...] + part

        return carry

    lax.fori_loop(0, 4, down, 0)

    first_o = p.slots(3)
    chip_sum_post(p, 0, dy_all, recv_o, first_o)
    chip_sum_post(p, 1, dy_all, recv_o, first_o)
    def q_right(i):
        return hid.at[pl.ds(pl.multiple_of(128 * i, 128), 128), 0:512]

    def do_right(i):
        return hid.at[pl.ds(pl.multiple_of(128 * i, 128), 128), 512:1024]

    def tall(i, base):
        half = pl.ds(2 * lax.rem(i, 2), 2)
        return dgate.at[half, :, :, pl.ds(pl.multiple_of(base + 128 * (i // 2), 128), 128)]

    def q_left(i):
        return tall(i, 0)

    def do_left(i):
        return tall(i, 512)

    def dk2(i):
        return dk_sum.at[i]

    def dv2(i):
        return dv_sum.at[i]

    def dq2(i):
        rows = pl.ds(pl.multiple_of(64 * lax.rem(i, 4), 64), 64)
        return keep.at[rows, pl.ds(pl.multiple_of(512 * (i // 4), 512), 512)]

    def keys_turned(i):
        return dup.at[i // 2, lax.rem(i, 2), 0:64, 0:256]

    def prepare_back(i, carry):
        keys_turned(i)[...] = jnp.transpose(kv[i].astype(F32))[0:64].astype(BF16)
        q = unit[i, :, 0:128].astype(F32)
        qt = jnp.transpose(q).astype(BF16)
        both = jnp.concatenate([qt[0:64], qt[64:128]], axis=1)
        q_right(i)[...] = jnp.concatenate([both, jnp.zeros((64, 512), BF16)], axis=0)
        first = lanes(q.shape) < 64
        both = jnp.concatenate([jnp.where(first, q, 0.0), jnp.where(first, 0.0, q)], axis=0)
        q_left(i)[...] = both.astype(BF16).reshape(2, 2, 128, 128)
        dq2(i)[...] = jnp.zeros((64, 512), F32)
        dk2(i)[...] = jnp.zeros((256, 128), F32)
        dv2(i)[...] = jnp.zeros((256, 128), F32)
        return carry

    lax.fori_loop(0, 8, prepare_back, 0)
    first_do = p.slots(8)

    def grad_piece(t, kk, act):
        to = 2 * near_first(p, t) + kk

        @pl.when(to != s)
        def _():
            act(p.copy(mix.at[1, to], dou.at[s], (to, b), first_do + 2 * t + kk, first_do + s))

    for t, index in ((0, None), (1, 1), (2, 2), (3, 0)):
        if index is not None:
            p.landed(first_mixed + index, mix.at[1, pl.ds(2 * near_first(p, t), 2)])
        for kk in (0, 1):
            grad_piece(t, kk, lambda made: made.start())
    sum_g.start()
    sum_d.reduce()
    dou[s] = mix[1, s]

    chip_sum_across(p, dy_all, recv_o, first_o)
    for k in range(1, 8):
        src = lax.rem(s + k, 8)
        p.landed(first_do + src, dou.at[src])

    def prepare_grad(i, carry):
        do = dou[i].astype(F32)
        dot = jnp.transpose(do)
        right = jnp.concatenate([dot[0:64], dot[64:128]], axis=1).astype(BF16)
        do_right(i)[...] = jnp.concatenate([jnp.zeros((64, 512), BF16), right], axis=0)
        first = lanes(do.shape) < 64
        tall_do = jnp.concatenate([jnp.where(first, do, 0.0), jnp.where(first, 0.0, do)], axis=0)
        do_left(i)[...] = tall_do.astype(BF16).reshape(2, 2, 128, 128)
        both = dot * jnp.transpose(unit_out[i].astype(F32))
        low = jnp.sum(both[0:64], axis=0, keepdims=True)
        high = jnp.sum(both[64:128], axis=0, keepdims=True)
        delta[i] = jnp.broadcast_to(jnp.concatenate([low, high], axis=1), (8, 512))
        return carry

    lax.fori_loop(0, 8, prepare_grad, 0)

    def meet(i, j, probs):
        ds = (probs * (nn(kv[j], do_right(i)[...]) - delta[i][0:1])).astype(BF16)
        dv2(j)[...] += nn(probs.astype(BF16), do_left(i)[...].reshape(512, 128))
        dk2(j)[...] += nn(ds, q_left(i)[...].reshape(512, 128))
        dq2(i)[...] += nn(keys_turned(j)[...], ds)

    first_back = p.slots(8)

    def blocks(t, carry):
        c = lax.rem(s + 1 + t, 8)
        causal = rows_of((256, 512)) <= lax.rem(lanes((256, 512)), 256)
        meet(c, c, jnp.where(causal, jnp.exp(nn(kv[c], q_right(c)[...]) - lse[c][0:1]), 0.0))

        def other(u, inner_carry):
            o = lax.rem(s + 1 + u, 8)
            i, j = jnp.maximum(c, o), jnp.minimum(c, o)
            meet(i, j, jnp.exp(nn(kv[j], q_right(i)[...]) - lse[i][0:1]))
            return inner_carry

        lax.fori_loop(t + 1, 8, other, 0)
        acc = dq2(c)[...]
        dq = jnp.concatenate([acc[:, 0:256], acc[:, 256:512]], axis=0) * 0.125
        pack[c, :, 0:128] = jnp.transpose(dq).astype(BF16)
        live = c * 256 + rows_of((256, 128)) < length_all[z][0:1, :]
        dk, dv = dk2(c)[...], dv2(c)[...]
        dk = dk + pltpu.roll(dk, 64, 1)
        dv = dv + pltpu.roll(dv, 64, 1)
        dkv = jnp.where(lanes((256, 128)) < 64, dk, dv)
        pack[c, :, 128:256] = jnp.where(live, dkv, 0.0).astype(BF16)

        @pl.when(t < 7)
        def _():
            p.copy(pack.at[c], unit.at[s], (c, b), first_back + t).start()

        @pl.when(t == 0)
        def _():
            p.landed(dbr_across, xa.at[p.across])
            p.copy(xa.at[p.across], xa.at[p.across], (s, p.core), dbr_far).start()

        @pl.when(t == 1)
        def _():
            sum_d.relay()

        @pl.when(t == 2)
        def _():
            more_g.start()
            more_d.reduce()

        return carry

    dbr_far = p.slots(1)
    lax.fori_loop(0, 8, blocks, 0)
    sum_u.start()
    sum_g.reduce()
    more_d.relay()
    unit[s] = pack[s]

    p.landed(dbr_core, xa.at[p.core])
    p.landed(dbr_far, xa.at[p.far])
    out_rows = nn(gu_send[:, :, :, 0:1024].reshape(256, 1024), xa[...].reshape(1024, 1024)).astype(BF16)
    for e in range(8):
        dgate[e // 2, e % 2, 0:32, 0:1024] = out_rows[32 * e : 32 * e + 32]
    sum_o = SeqSum(p, y_o, z_o)
    sum_o.start(dgate.at[:, :, 0:32, 0:1024])
    load_x = p.local(x, xa.at[p.far])
    load_norm.wait()

    first_n = p.slots(3)
    zero_row = jnp.zeros((1, 128), F32)

    def heads(t, carry):
        sum_q, sum_k = carry
        unit_of = lax.rem(s + 7 - t, 8)

        @pl.when(t < 7)
        def _():
            p.landed(first_back + t, unit.at[unit_of])

        g = unit_of // 2
        at = pl.multiple_of(256 * lax.rem(unit_of, 2), 256)
        whole = nn(norm[g], wqkv[:, :, pl.ds(at, 256)].reshape(1024, 256))
        q, k = heads_of(whole, 0)
        rq = lax.rsqrt(head_mean(q * q) + eps)
        rk = lax.rsqrt(head_mean(k * k) + eps)
        dq = rope_back(unit[unit_of, :, 0:128].astype(F32), cos[...], sin[...])
        dkv = unit[unit_of, :, 128:256].astype(F32)
        dk = rope_back(dkv, cos[...], sin[...])
        sum_q = sum_q + jnp.sum(dq * q * rq, axis=0, keepdims=True)
        sum_k = sum_k + jnp.sum(dk * k * rk, axis=0, keepdims=True)
        dq = dq * gain_q
        dk = dk * gain_k
        dq = rq * (dq - q * rq * rq * head_mean(dq * q))
        dk = rk * (dk - k * rk * rk * head_mean(dk * k))
        dup[g, :, :, pl.ds(at, 128)] = dq.astype(BF16).reshape(2, 128, 128)
        dkv = jnp.where(lanes(dk.shape) < 64, dk, dkv).astype(BF16)
        dup[g, :, :, pl.ds(pl.multiple_of(at + 128, 128), 128)] = dkv.reshape(2, 128, 128)
        return (sum_q, sum_k)

    sum_q, sum_k = lax.fori_loop(0, 8, heads, (zero_row, zero_row))
    sum_g.relay()
    more_g.reduce()

    gain_sum[2:3, 0:128] = sum_q
    gain_sum[3:4, 0:128] = sum_k
    def qkv_rows(c, carry):
        at = pl.multiple_of(128 * c, 128)
        side = norm[:, :, pl.ds(at, 128)].reshape(1024, 128)
        dup[c // 2, lax.rem(c, 2), :, 512:1024] = tn(side, dup[:, :, :, 0:512].reshape(1024, 512)).astype(BF16)
        return carry

    lax.fori_loop(0, 8, qkv_rows, 0)
    sum_qkv = SeqSum(p, y_q, z_q)
    sum_qkv.start(dup.at[:, :, :, pl.ds(512, 512)])
    more_u.start()

    def stream_back(t, carry):
        g = batch_order(p, t)
        part = nt(dup[g, :, :, 0:512].reshape(256, 512), wqkv[...].reshape(1024, 512))
        parts[g] = part.astype(BF16)

        @pl.when(t == 3)
        def _():
            keep[...] = part

        chip_sum_post(p, t, parts, recv, first_n)
        return carry

    lax.fori_loop(0, 4, stream_back, 0)
    chip_sum_across(p, parts, recv, first_n)
    sum_o.middle()
    sum_u.reduce()
    more_g.relay()
    xa[p.core] = (result[...] + chip_sum_rest(p, dy_all, recv_o, first_o)).astype(BF16)
    leave = [p.local(xa.at[p.core], output)]
    sum_qkv.middle()

    dn1 = keep[...] + chip_sum_rest(p, parts, recv, first_n)
    load_x.wait()
    xf = xa[p.far].astype(F32)
    r1 = rms_factor(xf)
    gain_sum[0:1] = jnp.sum(dn1 * xf * r1, axis=0, keepdims=True)
    xa[p.far] = (middle[...] + norm_back(dn1 * gain_a[...], xf, r1)).astype(BF16)
    leave.append(p.local(xa.at[p.far], dx))
    got_gain = [p.post(gain_sum, gain_batch.at[b], (s, lax.rem(b + k, 4))) for k in (1, 2, 3)]
    gain_batch[b] = gain_sum[...]
    sum_u.relay()
    for at, half in zip(halves, (sum_d, more_d)):
        rd[:, at] = half.finish()

    def exchange(total, own, dst):
        for c in range(4):
            own(c)[...] = total[32 * c : 32 * c + 32].astype(BF16)
        got = []
        for k in (1, 2, 3):
            to = lax.rem(b + k, 4)
            got.append(p.post(own(to), dst(b), (s, to)))
        dst(b)[...] = own(b)[...]
        return got

    def arrive(got, dst):
        for k in (1, 2, 3):
            p.landed(got[k - 1], dst(lax.rem(b + 4 - k, 4)))

    finished = []

    def hand_over(total, which, at):
        dst = lambda i: rgu.at[i, which, :, at]
        finished.append((exchange(total, lambda c: gu_send.at[c, which, :, at], dst), dst))

    hand_over(sum_g.finish(), 0, parts_of[0])
    for k in (1, 2, 3):
        p.landed(got_gain[k - 1], gain_batch.at[lax.rem(b + 4 - k, 4)])
    gain_seq[s] = (gain_batch[0] + gain_batch[1]) + (gain_batch[2] + gain_batch[3])
    got_all = [p.post(gain_seq.at[s], gain_seq.at[s], (lax.rem(s + k, 8), b)) for k in range(1, 8)]
    more_u.reduce()
    hand_over(more_g.finish(), 0, parts_of[1])
    ro[...] = sum_o.finish()
    dst_q = lambda i: rqkv.at[i]
    finished.append((exchange(sum_qkv.finish(), lambda c: qkv_send.at[c], dst_q), dst_q))
    hand_over(sum_u.finish(), 1, parts_of[0])
    for k in range(1, 8):
        p.landed(got_all[k - 1], gain_seq.at[lax.rem(s + 8 - k, 8)])
    total = gain_seq[0]
    for k in range(1, 8):
        total = total + gain_seq[k]
    gains_out[...] = total
    more_u.relay()
    hand_over(more_u.finish(), 1, parts_of[1])
    for got, dst in finished:
        arrive(got, dst)
    for t in range(4):
        for kk in (0, 1):
            grad_piece(t, kk, lambda made: made.wait_send())
    for t in range(7):
        p.copy(pack.at[s], unit.at[s], (p.flip, b), first_back + t).wait_send()
    for made in leave:
        made.wait()
    p.copy(xa.at[b], xa.at[b], (s, p.core), dbr_far).wait_send()
    for t in range(3):
        p.copy(mix.at[0, 0:2], mix.at[0, 0:2], (s, p.core), first_mixed + t).wait_send()
    p.drain()


def chip_sum_post(p, t, parts, recv, first):
    @pl.when(jnp.equal(t, 0))
    def _():
        p.copy(parts.at[p.far], recv.at[0], (p.s, p.core), first).start()

    @pl.when(jnp.equal(t, 1))
    def _():
        p.copy(parts.at[p.core], recv.at[1], (p.s, p.core), first + 1).start()


def chip_sum_across(p, parts, recv, first):
    p.copy(recv.at[0], recv.at[0], (p.s, p.core), first).wait_recv()
    parts[p.across] = (parts[p.across].astype(F32) + recv[0].astype(F32)).astype(BF16)
    p.copy(parts.at[p.across], recv.at[2], (p.s, p.across), first + 2).start()


def chip_sum_rest(p, parts, recv, first):
    p.copy(recv.at[1], recv.at[1], (p.s, p.core), first + 1).wait_recv()
    p.copy(recv.at[2], recv.at[2], (p.s, p.core), first + 2).wait_recv()
    for k in range(3):
        p.copy(parts.at[p.b], recv.at[k], (p.s, p.core), first + k).wait_send()
    return recv[1].astype(F32) + recv[2].astype(F32)


def batch_order(p, t):
    return jnp.where(t == 0, p.far, jnp.where(t == 1, p.core, jnp.where(t == 2, p.across, p.b)))


class SeqTree:
    def __init__(self, p, slot, y_recv, relayed, z_recv):
        self.p, self.slot, self.y_recv, self.relayed, self.z_recv = p, slot, y_recv, relayed, z_recv
        self.first = p.slots(8)

    def mine(self, i):
        return self.slot(2 * i + self.p.y)[...].astype(F32)

    def start(self, pieces=(0, 1, 2, 3)):
        p = self.p
        for i in pieces:
            p.copy(
                self.slot(2 * i + 1 - p.y), self.y_recv.at[i], (p.flip, p.b), self.first + 4 + i
            ).start()

    def send(self, i, dst, z, out, into):
        p = self.p
        p.copy(self.y_recv.at[i], dst, (2 * z + p.y, p.b), self.first + out, self.first + into).start()

    def load(self, i):
        return self.y_recv.at[i][...].astype(F32)

    def reduce(self):
        p = self.p
        for i in range(4):
            p.landed(self.first + 4 + i, self.y_recv.at[i])

        def add(i):
            self.y_recv.at[i][...] = (self.load(i) + self.mine(i)).astype(BF16)

        add(p.there)
        add(p.beyond)

        @pl.when(jnp.logical_not(p.inner))
        def _():
            self.send(p.there, self.relayed.at[0], p.pair, 1, 1)
            self.send(p.beyond, self.relayed.at[1], p.pair, 2, 2)

        add(p.pair)
        self.send(p.pair, self.z_recv.at[0], p.pair, 0, 0)

    def relay(self):
        p = self.p

        @pl.when(p.inner)
        def _():
            for k, i in ((0, p.there), (1, p.beyond)):
                p.landed(self.first + 1 + k, self.relayed.at[k])
                self.y_recv.at[i][...] = (self.load(i) + self.relayed.at[k][...].astype(F32)).astype(BF16)
                self.send(i, self.z_recv.at[1], i, 1 + k, 3)

    def finish(self):
        p = self.p
        total = self.load(p.z) + self.mine(p.z)
        p.landed(self.first, self.z_recv.at[0])
        total = total + self.z_recv.at[0][...].astype(F32)
        p.landed(self.first + 3, self.z_recv.at[1])
        for out in range(3):
            p.copy(self.z_recv.at[0], self.z_recv.at[0], (p.flip, p.b), self.first + out).wait_send()
        for i in range(4):
            p.copy(self.y_recv.at[i], self.y_recv.at[i], (p.flip, p.b), self.first + 4 + i).wait_send()
        return total + self.z_recv.at[1][...].astype(F32)


class SeqSum:
    def __init__(self, p, y_recv, z_recv):
        self.p, self.y_recv, self.z_recv = p, y_recv, z_recv

    def start(self, source, mine=None):
        p = self.p
        self.index = p.post(source.at[:, 1 - p.y], self.y_recv, (p.flip, p.b))
        self.load = None
        if mine is None:
            self.mine = lambda i: source.at[i, p.y]
        else:
            self.load = p.local(source.at[:, p.y], mine)
            self.mine = lambda i: mine.at[i]

    def middle(self):
        p = self.p
        if self.load is not None:
            self.load.wait()
        p.landed(self.index, self.y_recv)
        self.far = []
        for k in (1, 2, 3):
            i = p.up(k)
            self.y_recv[i] = (self.y_recv[i].astype(F32) + self.mine(i)[...].astype(F32)).astype(BF16)
            self.far.append(p.post(self.y_recv.at[i], self.z_recv.at[k - 1], (2 * i + p.y, p.b)))

    def finish(self):
        p = self.p
        total = self.y_recv[p.z].astype(F32) + self.mine(p.z)[...].astype(F32)
        for k in (1, 2, 3):
            p.landed(self.far[k - 1], self.z_recv.at[k - 1])
            total = total + self.z_recv[k - 1].astype(F32)
        return total


def finish_kernel(
    output, dx, rqkv, rgu, rd, ro, gains,
    output_, dx_, grad_query, grad_key, grad_value, grad_out, grad_gate, grad_up, grad_down,
    gain_attn, gain_ffn, gain_query, gain_key,
):
    output_[...] = output[...]
    dx_[...] = dx[...]
    grad_out[...] = ro[...]
    grad_down[...] = rd[...]
    for c in range(4):
        pairs = []
        for kk in (0, 1):
            h = 2 * c + kk
            q, kv = heads_of(rqkv[c].astype(F32), kk)
            grad_query[:, 128 * h : 128 * h + 128] = q
            pairs.append(kv)
        first = lanes(pairs[0].shape) < 64
        grad_key[:, 128 * c : 128 * c + 128] = jnp.where(first, pairs[0], pltpu.roll(pairs[1], 64, 1))
        grad_value[:, 128 * c : 128 * c + 128] = jnp.where(first, pltpu.roll(pairs[0], 64, 1), pairs[1])
    for which, out in ((0, grad_gate), (1, grad_up)):
        wide = [rgu[c, which].astype(F32) for c in range(4)]
        out[...] = jnp.concatenate(
            [wide[c][:, 144 * i : 144 * i + 144] for i in range(8) for c in range(4)], axis=1
        )
    gain_attn[...] = gains[0:1]
    gain_ffn[...] = gains[1:2]
    gain_query[...] = gains[2:3, 0:64] + gains[2:3, 64:128]
    gain_key[...] = gains[3:4, 0:64]


def call(kernel, outs, in_specs, out_specs, scratch, cid, sems):
    return pl.pallas_call(
        kernel,
        out_shape=[jax.ShapeDtypeStruct(shape, dtype) for shape, dtype in outs],
        in_specs=in_specs,
        out_specs=out_specs,
        scratch_shapes=[pltpu.VMEM(shape, dtype) for shape, dtype in scratch]
        + [
            pltpu.SemaphoreType.DMA((sems[0],)),
            pltpu.SemaphoreType.DMA((sems[0],)),
            pltpu.SemaphoreType.DMA((sems[1],)),
        ],
        compiler_params=pltpu.CompilerParams(
            collective_id=cid, has_side_effects=True, vmem_limit_bytes=64 * 2**20
        ),
    )


def body(
    inputs, lengths, w_query, key_weight, value_weight, w_out, w_gate, w_up, w_down,
    gain_attn, gain_ffn, gain_query, gain_key, cotangent,
):
    x = inputs.reshape(256, 1024)
    dy = cotangent.reshape(256, 1024)
    freqs = theta ** (-(np.arange(32, dtype=np.float32) * 2.0) / 64)
    angles = np.arange(2048, dtype=np.float32)[:, None] * freqs.astype(np.float32)[None, :]
    cosine = jnp.asarray(np.tile(np.cos(angles), (1, 4)), F32)
    sine = jnp.asarray(np.tile(np.sin(angles), (1, 4)), F32)
    gains = [g[None] for g in (gain_query, gain_key, gain_attn, gain_ffn)]

    raw = call(
        block_kernel,
        [
            ((256, 1024), BF16), ((256, 1024), BF16), ((4, 32, 512), BF16), ((4, 2, 32, 1152), BF16),
            ((144, 1024), F32), ((32, 1024), F32), ((8, 1024), F32), ((4, 256, 1024), BF16),
        ],
        [ANY, ANY, SMEM] + [VMEM] * 6 + [ANY] * 3 + [VMEM] * 4,
        [ANY] * 2 + [VMEM] * 5 + [ANY],
        [
            ((4, 256, 1024), BF16), ((4, 256, 1024), BF16), ((8, 128, 512), BF16), ((8, 4, 32, 1024), BF16),
            ((8, 256, 256), BF16), ((8, 256, 256), BF16), ((8, 256, 128), BF16), ((8, 8, 512), F32),
            ((8, 256, 128), BF16), ((4, 8, 256, 128), BF16),
            ((4, 256, 1024), BF16), ((8, 2, 128, 1152), BF16), ((8, 144, 1024), BF16), ((1152, 1024), BF16),
            ((1024, 1152), BF16), ((4, 2, 128, 1152), BF16), ((4, 2, 128, 1152), BF16),
            ((8, 256, 128), F32), ((8, 256, 128), F32),
            ((4, 256, 1024), BF16), ((3, 256, 1024), BF16), ((3, 256, 1024), BF16),
            ((256, 1024), F32), ((256, 1024), F32), ((256, 1024), F32),
            ((4, 32, 512), BF16), ((4, 2, 32, 1152), BF16), ((8, 128), jnp.int32),
            ((256, 128), F32), ((256, 128), F32), ((4, 8, 128), jnp.int32),
            ((8, 256, 128), BF16), ((8, 8, 512), F32),
            ((4, 144, 1024), BF16), ((2, 144, 1024), BF16), ((2, 144, 1024), BF16),
            ((4, 128, 1152), BF16), ((2, 128, 1152), BF16), ((2, 128, 1152), BF16),
            ((4, 128, 1152), BF16), ((2, 128, 1152), BF16), ((2, 128, 1152), BF16),
            ((4, 128, 512), BF16), ((3, 128, 512), BF16), ((4, 32, 1024), BF16), ((3, 32, 1024), BF16),
            ((8, 1024), F32), ((4, 8, 1024), F32), ((8, 8, 1024), F32),
        ],
        0,
        (256, 32),
    )(x, dy, lengths, w_query, key_weight, value_weight, w_out, w_gate, w_up, w_down, cosine, sine, *gains)
    done = pl.pallas_call(
        finish_kernel,
        out_shape=[
            jax.ShapeDtypeStruct(shape, dtype)
            for shape, dtype in (
                ((256, 1024), BF16), ((256, 1024), BF16), ((32, 1024), F32), ((32, 512), F32),
                ((32, 512), F32), ((32, 1024), F32), ((32, 4608), F32), ((32, 4608), F32),
                ((144, 1024), F32), ((1, 1024), F32), ((1, 1024), F32), ((1, 64), F32), ((1, 64), F32),
            )
        ],
        in_specs=[VMEM] * 7,
        out_specs=[VMEM] * 13,
    )(*raw[:7])
    return (
        done[0].reshape(256, 1, 1024), done[1].reshape(256, 1, 1024), *done[2:9], *[g[0] for g in done[9:]],
    )


def rotary_tables(positions, width):
    half = width // 2
    freqs = theta ** (-(jnp.arange(half, dtype=jnp.float32) * 2.0) / width)
    angles = positions.astype(jnp.float32)[:, None] * freqs[None, :]
    cosine = jnp.concatenate([jnp.cos(angles), jnp.cos(angles)], axis=-1)
    sine = jnp.concatenate([jnp.sin(angles), jnp.sin(angles)], axis=-1)
    return (cosine, sine)


def rotate(v, cosine, sine):
    half = v.shape[-1] // 2
    turned = jnp.concatenate([-v[..., half:], v[..., :half]], axis=-1)
    return v * cosine + turned * sine


def rotate_back(grad, cosine, sine):
    half = grad.shape[-1] // 2
    moved = grad * sine
    return grad * cosine + jnp.concatenate([moved[..., half:], -moved[..., :half]], axis=-1)


def product(left, right):
    return jnp.dot(left, right, preferred_element_type=jnp.float32)


def left_product(left, right):
    return jnp.einsum("rd,rn->dn", left, right, preferred_element_type=jnp.float32)


def right_product(left, right):
    return jnp.einsum("rn,dn->rd", left, right, preferred_element_type=jnp.float32)


def rounded(v):
    return v.astype(jnp.bfloat16)


def split_rows(term, seq_size, batch_size):
    return term.reshape(
        seq_size, batch_size, term.shape[0] // (seq_size * batch_size), term.shape[1]
    )


def fold_sources(piece):
    return jnp.sum(piece, axis=1).reshape(-1, piece.shape[-1])


def general_body(
    inputs,
    lengths,
    w_query,
    key_weight,
    value_weight,
    w_out,
    w_gate,
    w_up,
    w_down,
    gain_attn,
    gain_ffn,
    gain_query,
    gain_key,
    cotangent,
):
    slice_len, seq_count, width = inputs.shape
    rows = slice_len * seq_count
    head_dim = gain_query.shape[0]
    kv_width = key_weight.shape[1]
    kv_heads = kv_width // head_dim
    q_heads = w_query.shape[1] // head_dim
    sequence_group = q_heads // kv_heads
    scale = head_dim ** (-0.5)
    cycle_size = lax.axis_size("seq")
    batch_size = lax.axis_size("batch")
    positions = lax.axis_index("seq") * slice_len + jnp.arange(slice_len, dtype=jnp.int32)
    cosine, sine = rotary_tables(positions, head_dim)
    cosine = cosine[:, None, None, :]
    sine = sine[:, None, None, :]
    shards = (w_query, key_weight, value_weight, w_out, w_gate, w_up, w_down)
    wq, key_matrix, value_matrix, wo, wg, wu, wd = (
        lax.all_gather(shards[0], ("seq", "batch"), axis=0, tiled=True),
        lax.all_gather(shards[1], ("seq", "batch"), axis=0, tiled=True),
        lax.all_gather(shards[2], ("seq", "batch"), axis=0, tiled=True),
        lax.all_gather(shards[3], ("seq", "batch"), axis=0, tiled=True),
        lax.all_gather(shards[4], ("seq", "batch"), axis=0, tiled=True),
        lax.all_gather(shards[5], ("seq", "batch"), axis=0, tiled=True),
        lax.all_gather(shards[6], ("seq", "batch"), axis=0, tiled=True),
    )
    stream = inputs.reshape(rows, width).astype(jnp.float32)
    factor_one = rms_factor(stream)
    normalized_input = rounded(stream * factor_one * gain_attn)
    query_pre = product(normalized_input, wq).reshape(slice_len, seq_count, q_heads, head_dim)
    key_before_rotation = product(normalized_input, key_matrix).reshape(
        slice_len, seq_count, kv_heads, head_dim
    )
    value_b = rounded(product(normalized_input, value_matrix)).reshape(
        slice_len, seq_count, kv_width
    )
    factor_q = rms_factor(query_pre)
    factor_k = rms_factor(key_before_rotation)
    query_b = rounded(rotate(query_pre * factor_q * gain_query, cosine, sine))
    key_b = rounded(rotate(key_before_rotation * factor_k * gain_key, cosine, sine)).reshape(
        slice_len, seq_count, kv_width
    )
    query_five = query_b.reshape(slice_len, seq_count, kv_heads, sequence_group, head_dim)

    def scores_of(keys, start):
        count = keys.shape[0]
        raw = (
            jnp.einsum(
                "tsgrd,csgd->sgrtc",
                query_five,
                keys.reshape(count, seq_count, kv_heads, head_dim),
                preferred_element_type=jnp.float32,
            )
            * scale
        )
        key_pos = start + jnp.arange(count, dtype=jnp.int32)
        causal = key_pos[None, :] <= positions[:, None]
        inside = key_pos[None, :] < lengths[:, None]
        valid = causal[None, :, :] & inside[:, None, :]
        return (raw, valid[:, None, None, :, :])

    state_shape = (seq_count, kv_heads, sequence_group, slice_len)
    shard_ids = jnp.arange(cycle_size, dtype=jnp.int32)
    top = jnp.full(state_shape, -1e30, jnp.float32)
    keys = lax.all_gather(key_b, "seq", axis=0, tiled=True)
    value_rows = lax.all_gather(value_b, "seq", axis=0, tiled=True)
    count = keys.shape[0]
    raw, valid = scores_of(keys, jnp.int32(0))
    masked = jnp.where(valid, raw, -jnp.inf)
    new_top = jnp.maximum(top, jnp.max(masked, axis=-1))
    probs = jnp.exp(masked - new_top[..., None])
    total = jnp.sum(probs, axis=-1)
    acc = jnp.einsum(
        "sgrtc,csgd->sgrtd",
        rounded(probs),
        value_rows.reshape(count, seq_count, kv_heads, head_dim),
        preferred_element_type=jnp.float32,
    )
    state = (new_top, total, acc)
    top, total, acc = state
    attn_out = acc / total[..., None]
    log_total = top + jnp.log(total)
    mixed_b = rounded(jnp.transpose(attn_out, (3, 0, 1, 2, 4)).reshape(rows, q_heads * head_dim))
    middle = stream + product(mixed_b, wo)
    factor_two = rms_factor(middle)
    normed_two = rounded(middle * factor_two * gain_ffn)
    gate = product(normed_two, wg)
    up_part = product(normed_two, wu)
    sigma = jax.nn.sigmoid(gate)
    swish = gate * sigma
    hidden_b = rounded(swish * up_part)
    result = middle + product(hidden_b, wd)
    output = rounded(result).reshape(slice_len, seq_count, width)
    wq, key_matrix, value_matrix, wo, wg, wu, wd = (
        lax.all_gather(shards[0], ("seq", "batch"), axis=0, tiled=True),
        lax.all_gather(shards[1], ("seq", "batch"), axis=0, tiled=True),
        lax.all_gather(shards[2], ("seq", "batch"), axis=0, tiled=True),
        lax.all_gather(shards[3], ("seq", "batch"), axis=0, tiled=True),
        lax.all_gather(shards[4], ("seq", "batch"), axis=0, tiled=True),
        lax.all_gather(shards[5], ("seq", "batch"), axis=0, tiled=True),
        lax.all_gather(shards[6], ("seq", "batch"), axis=0, tiled=True),
    )
    grad_res = cotangent.reshape(rows, width).astype(jnp.float32)
    grad_ffo = rounded(grad_res)
    grad_wd = left_product(hidden_b, grad_ffo)
    grad_hidden = right_product(grad_ffo, wd)
    grad_gate = rounded(grad_hidden * up_part * sigma * (1.0 + gate * (1.0 - sigma)))
    grad_up = rounded(grad_hidden * swish)
    grad_wg = left_product(normed_two, grad_gate)
    grad_wu = left_product(normed_two, grad_up)
    grad_normed_two = right_product(grad_gate, wg) + right_product(grad_up, wu)
    grad_gain_ffn = jnp.sum(grad_normed_two * middle * factor_two, axis=0)
    grad_middle = grad_res + norm_back(grad_normed_two * gain_ffn, middle, factor_two)
    grad_branch = rounded(grad_middle)
    grad_wo = left_product(mixed_b, grad_branch)
    grad_mixed = rounded(right_product(grad_branch, wo))
    grad_five = grad_mixed.reshape(slice_len, seq_count, kv_heads, sequence_group, head_dim)
    delta = jnp.sum(
        jnp.transpose(grad_five, (1, 2, 3, 0, 4)).astype(jnp.float32) * attn_out, axis=-1
    )
    gathered = (
        lax.all_gather(key_b, "seq", axis=0, tiled=True),
        lax.all_gather(value_b, "seq", axis=0, tiled=True),
    )

    def back_step(grad_query, item):
        index, keys, value_rows = item
        raw, valid = scores_of(keys, index * slice_len)
        probs = jnp.where(valid, jnp.exp(raw - log_total[..., None]), 0.0)
        key_four = keys.reshape(slice_len, seq_count, kv_heads, head_dim)
        value_four = value_rows.reshape(slice_len, seq_count, kv_heads, head_dim)
        grad_probs = jnp.einsum(
            "tsgrd,csgd->sgrtc", grad_five, value_four, preferred_element_type=jnp.float32
        )
        grad_score = rounded(probs * (grad_probs - delta[..., None]))
        grad_query = (
            grad_query
            + jnp.einsum(
                "sgrtc,csgd->tsgrd", grad_score, key_four, preferred_element_type=jnp.float32
            )
            * scale
        )
        key_term = (
            jnp.einsum(
                "sgrtc,tsgrd->csgd", grad_score, query_five, preferred_element_type=jnp.float32
            )
            * scale
        )
        value_term = jnp.einsum(
            "sgrtc,tsgrd->csgd", rounded(probs), grad_five, preferred_element_type=jnp.float32
        )
        return (
            grad_query,
            (
                key_term.reshape(slice_len, seq_count, kv_width),
                value_term.reshape(slice_len, seq_count, kv_width),
            ),
        )

    items = (
        shard_ids,
        gathered[0].reshape(cycle_size, slice_len, seq_count, kv_width),
        gathered[1].reshape(cycle_size, slice_len, seq_count, kv_width),
    )
    grad_query, terms = lax.scan(
        back_step,
        jnp.zeros((slice_len, seq_count, kv_heads, sequence_group, head_dim), jnp.float32),
        items,
    )
    key_terms = terms[0].reshape(cycle_size * slice_len, seq_count, kv_width)
    value_terms = terms[1].reshape(cycle_size * slice_len, seq_count, kv_width)
    grad_key, grad_value = (
        lax.psum_scatter(
            key_terms.astype(jnp.bfloat16), "seq", scatter_dimension=0, tiled=True
        ).astype(jnp.float32),
        lax.psum_scatter(
            value_terms.astype(jnp.bfloat16), "seq", scatter_dimension=0, tiled=True
        ).astype(jnp.float32),
    )
    grad_qr = (
        rounded(grad_query).astype(jnp.float32).reshape(slice_len, seq_count, q_heads, head_dim)
    )
    grad_qn = rotate_back(grad_qr, cosine, sine)
    grad_gain_query = jnp.sum(grad_qn * query_pre * factor_q, axis=(0, 1, 2))
    grad_qp = rounded(
        norm_back(grad_qn * gain_query, query_pre, factor_q).reshape(rows, q_heads * head_dim)
    )
    grad_kr = (
        rounded(grad_key).astype(jnp.float32).reshape(slice_len, seq_count, kv_heads, head_dim)
    )
    grad_kn = rotate_back(grad_kr, cosine, sine)
    grad_gain_key = jnp.sum(grad_kn * key_before_rotation * factor_k, axis=(0, 1, 2))
    grad_kp = rounded(
        norm_back(grad_kn * gain_key, key_before_rotation, factor_k).reshape(rows, kv_width)
    )
    grad_vp = rounded(grad_value).reshape(rows, kv_width)
    grad_wq = left_product(normalized_input, grad_qp)
    grad_wk = left_product(normalized_input, grad_kp)
    grad_wv = left_product(normalized_input, grad_vp)
    grad_normed = (
        right_product(grad_qp, wq)
        + right_product(grad_kp, key_matrix)
        + right_product(grad_vp, value_matrix)
    )
    grad_gain_attn = jnp.sum(grad_normed * stream * factor_one, axis=0)
    grad_stream = grad_middle + norm_back(grad_normed * gain_attn, stream, factor_one)
    spread = (
        lax.all_to_all(
            split_rows(grad_wq, cycle_size, batch_size).astype(jnp.bfloat16),
            "batch",
            split_axis=1,
            concat_axis=1,
            tiled=True,
        ).astype(jnp.float32),
        lax.all_to_all(
            split_rows(grad_wk, cycle_size, batch_size).astype(jnp.bfloat16),
            "batch",
            split_axis=1,
            concat_axis=1,
            tiled=True,
        ).astype(jnp.float32),
        lax.all_to_all(
            split_rows(grad_wv, cycle_size, batch_size).astype(jnp.bfloat16),
            "batch",
            split_axis=1,
            concat_axis=1,
            tiled=True,
        ).astype(jnp.float32),
        lax.all_to_all(
            split_rows(grad_wo, cycle_size, batch_size).astype(jnp.bfloat16),
            "batch",
            split_axis=1,
            concat_axis=1,
            tiled=True,
        ).astype(jnp.float32),
        lax.all_to_all(
            split_rows(grad_wg, cycle_size, batch_size).astype(jnp.bfloat16),
            "batch",
            split_axis=1,
            concat_axis=1,
            tiled=True,
        ).astype(jnp.float32),
        lax.all_to_all(
            split_rows(grad_wu, cycle_size, batch_size).astype(jnp.bfloat16),
            "batch",
            split_axis=1,
            concat_axis=1,
            tiled=True,
        ).astype(jnp.float32),
        lax.all_to_all(
            split_rows(grad_wd, cycle_size, batch_size).astype(jnp.bfloat16),
            "batch",
            split_axis=1,
            concat_axis=1,
            tiled=True,
        ).astype(jnp.float32),
    )
    partial_sums = [fold_sources(piece) for piece in spread]
    summed = (
        lax.psum_scatter(
            partial_sums[0].astype(jnp.bfloat16), "seq", scatter_dimension=0, tiled=True
        ).astype(jnp.float32),
        lax.psum_scatter(
            partial_sums[1].astype(jnp.bfloat16), "seq", scatter_dimension=0, tiled=True
        ).astype(jnp.float32),
        lax.psum_scatter(
            partial_sums[2].astype(jnp.bfloat16), "seq", scatter_dimension=0, tiled=True
        ).astype(jnp.float32),
        lax.psum_scatter(
            partial_sums[3].astype(jnp.bfloat16), "seq", scatter_dimension=0, tiled=True
        ).astype(jnp.float32),
        lax.psum_scatter(
            partial_sums[4].astype(jnp.bfloat16), "seq", scatter_dimension=0, tiled=True
        ).astype(jnp.float32),
        lax.psum_scatter(
            partial_sums[5].astype(jnp.bfloat16), "seq", scatter_dimension=0, tiled=True
        ).astype(jnp.float32),
        lax.psum_scatter(
            partial_sums[6].astype(jnp.bfloat16), "seq", scatter_dimension=0, tiled=True
        ).astype(jnp.float32),
    )
    gains = lax.psum(
        (grad_gain_attn, grad_gain_ffn, grad_gain_query, grad_gain_key), ("seq", "batch")
    )
    grad_inputs = rounded(grad_stream).reshape(slice_len, seq_count, width)
    return (
        output,
        grad_inputs,
        summed[0],
        summed[1],
        summed[2],
        summed[3],
        summed[4],
        summed[5],
        summed[6],
        gains[0],
        gains[1],
        gains[2],
        gains[3],
    )


def solution(mesh):
    sharded = P(("seq", "batch"), None)
    stream = P("seq", "batch", None)
    in_specs = (stream, P("batch")) + (sharded,) * 7 + (P(),) * 4 + (stream,)
    out_specs = (stream, stream) + (sharded,) * 7 + (P(),) * 4
    grouped = mesh.shape["seq"] == 8 and mesh.shape["batch"] == 4
    step = body if grouped else general_body
    return jax.shard_map(step, mesh=mesh, in_specs=in_specs, out_specs=out_specs, check_vma=False)
```

```python
import functools

import jax
import jax.numpy as jnp
import numpy as np
from jax import lax
from jax.experimental import pallas as pl
from jax.experimental.pallas import tpu as pltpu
from jax.sharding import PartitionSpec as P

MESH = pl.DeviceIdType.MESH
F32 = jnp.float32
BF16 = jnp.bfloat16
eps = 1e-05
theta = 1000000.0
VMEM = pl.BlockSpec(memory_space=pltpu.VMEM)
ANY = pl.BlockSpec(memory_space=pl.ANY)
SMEM = pl.BlockSpec(memory_space=pltpu.SMEM)


def nn(left, right):
    return lax.dot_general(left, right, (((1,), (0,)), ((), ())), preferred_element_type=F32)


def nt(left, right):
    return lax.dot_general(left, right, (((1,), (1,)), ((), ())), preferred_element_type=F32)


def tn(left, right):
    return lax.dot_general(left, right, (((0,), (0,)), ((), ())), preferred_element_type=F32)


def rms_factor(v):
    return lax.rsqrt(jnp.mean(v * v, axis=-1, keepdims=True) + eps)


def norm_back(grad, value, factor):
    return factor * (
        grad - value * factor * factor * jnp.mean(grad * value, axis=-1, keepdims=True)
    )


def lanes(shape):
    return lax.broadcasted_iota(jnp.int32, shape, len(shape) - 1)


def rows_of(shape):
    return lax.broadcasted_iota(jnp.int32, shape, len(shape) - 2)


def head_mean(v):
    first = lanes(v.shape) < 64
    low = jnp.sum(jnp.where(first, v, 0.0), axis=-1, keepdims=True)
    high = jnp.sum(jnp.where(first, 0.0, v), axis=-1, keepdims=True)
    return jnp.where(first, low, high) * (1.0 / 64.0)


def rope(u, cosine, sine):
    early = lax.rem(lanes(u.shape), 64) < 32
    turned = jnp.where(early, -pltpu.roll(u, 96, 1), pltpu.roll(u, 32, 1))
    return u * cosine + turned * sine


def rope_back(u, cosine, sine):
    early = lax.rem(lanes(u.shape), 64) < 32
    w = u * sine
    return u * cosine + jnp.where(early, pltpu.roll(w, 96, 1), -pltpu.roll(w, 32, 1))


class Place:
    def __init__(self, send_sem, recv_sem, local_sem):
        self.s = lax.axis_index("seq")
        self.b = lax.axis_index("batch")
        self.z = self.s // 2
        self.y = lax.rem(self.s, 2)
        self.core = self.b + 1 - 2 * lax.rem(self.b, 2)
        self.across = lax.rem(self.b + 2, 4)
        self.far = 3 - self.b
        self.flip = 2 * self.z + 1 - self.y
        self.inner = jnp.logical_or(self.z == 1, self.z == 2)
        self.pair = self.z + 1 - 2 * lax.rem(self.z, 2)
        self.there = jnp.where(self.z < 2, 2, 1)
        self.beyond = jnp.where(self.z < 2, 3, 0)
        self.send_sem, self.recv_sem, self.local_sem = send_sem, recv_sem, local_sem
        self.used = 0
        self.used_local = 0
        self.sent = []

    def up(self, k):
        return lax.rem(self.z + k, 4)

    def down(self, k):
        return lax.rem(self.z + 4 - k, 4)

    def greet(self):
        self.hello()
        self.meet()

    def hello(self):
        barrier = pltpu.get_barrier_semaphore()
        for k in (1, 2, 3):
            pl.semaphore_signal(
                barrier, inc=1, device_id=(self.s, lax.rem(self.b + k, 4)), device_id_type=MESH
            )
        for k in range(1, 8):
            pl.semaphore_signal(
                barrier, inc=1, device_id=(lax.rem(self.s + k, 8), self.b), device_id_type=MESH
            )

    def meet(self):
        pl.semaphore_wait(pltpu.get_barrier_semaphore(), 10)

    def slots(self, count):
        first = self.used
        self.used += count
        return first

    def copy(self, src, dst, device, out, into=None):
        return pltpu.make_async_remote_copy(
            src_ref=src,
            dst_ref=dst,
            send_sem=self.send_sem.at[out],
            recv_sem=self.recv_sem.at[out if into is None else into],
            device_id=device,
            device_id_type=MESH,
        )

    def post(self, src, dst, device):
        index = self.slots(1)
        made = self.copy(src, dst, device, index)
        made.start()
        self.sent.append(made)
        return index

    def landed(self, index, ref):
        self.copy(ref, ref, (self.s, self.core), index).wait_recv()

    def local(self, src, dst):
        index = self.used_local
        self.used_local += 1
        made = pltpu.make_async_copy(src, dst, self.local_sem.at[index])
        made.start()
        return made

    def drain(self):
        for made in self.sent:
            made.wait_send()
        self.sent = []


class Spread:
    def __init__(self, p, slot):
        self.p, self.slot = p, slot
        self.first = p.slots(8)
        self.from_z = (p.pair, p.there, p.beyond)

    def send(self, s, device, out, into):
        self.p.copy(self.slot(s), self.slot(s), device, self.first + out, self.first + into).start()

    def start_z(self):
        p = self.p
        self.send(p.s, (2 * p.pair + p.y, p.b), 0, 0)
        self.send(p.s, (2 * p.there + p.y, p.b), 1, jnp.where(p.inner, 1, 2))

    def start_y(self):
        p = self.p
        self.send(p.s, (p.flip, p.b), 4, 3)

    def start(self):
        self.start_z()
        self.start_y()

    def land(self, j):
        p = self.p
        s = 2 * self.from_z[j] + p.y
        p.landed(self.first + j, self.slot(s))
        if j > 0:

            @pl.when(p.inner)
            def _():
                self.send(s, (2 * p.pair + p.y, p.b), 1 + j, j)

        self.send(s, (p.flip, p.b), 5 + j, 4 + j)

    def land_inner(self):
        @pl.when(self.p.inner)
        def _():
            self.land(1)
            self.land(2)

    def land_end(self):
        @pl.when(jnp.logical_not(self.p.inner))
        def _():
            self.land(1)
            self.land(2)

    def finish(self):
        p = self.p
        p.landed(self.first + 3, self.slot(p.flip))
        for j in range(3):
            p.landed(self.first + 4 + j, self.slot(2 * self.from_z[j] + 1 - p.y))

    def drain(self):
        p = self.p

        def sent(out):
            p.copy(self.slot(p.s), self.slot(p.s), (p.flip, p.b), self.first + out).wait_send()

        for out in (0, 1, 4, 5, 6, 7):
            sent(out)

        @pl.when(p.inner)
        def _():
            sent(2)
            sent(3)


def heads_of(whole, kk):
    return whole[:, 256 * kk : 256 * kk + 128], whole[:, 256 * kk + 128 : 256 * kk + 256]


def pack_projections(w_query, key_weight, value_weight, out):
    for c in range(4):
        k = key_weight[:, 128 * c : 128 * c + 128].astype(F32)
        v = value_weight[:, 128 * c : 128 * c + 128].astype(F32)
        first = lanes(k.shape) < 64
        pairs = (
            jnp.where(first, k, pltpu.roll(v, 64, 1)),
            jnp.where(first, pltpu.roll(k, 64, 1), v),
        )
        for kk in (0, 1):
            h = 2 * c + kk
            out[c, :, 256 * kk : 256 * kk + 128] = w_query[:, 128 * h : 128 * h + 128]
            out[c, :, 256 * kk + 128 : 256 * kk + 256] = pairs[kk].astype(BF16)


def pack_hidden(source, out, which):
    wide = source[...].astype(F32)
    for c in range(4):
        pieces = [wide[:, 144 * (4 * i + c) : 144 * (4 * i + c) + 144] for i in range(8)]
        out[c, which] = jnp.concatenate(pieces, axis=1).astype(BF16)


def twice(v):
    return jnp.concatenate([v[...], v[...]], axis=1)


def near_first(p, t):
    return jnp.where(t == 0, p.b, jnp.where(t == 1, p.core, jnp.where(t == 2, p.across, p.far)))


def block_kernel(
    x, dy, lengths, w_query, key_weight, value_weight, w_out, w_gate, w_up, w_down,
    cos_table, sin_table, gain_query, gain_key, gain_a, gain_f,
    output, dx, rqkv, rgu, rd, ro, gains_out, norm_park,
    xa, norm, wqkv, wo, pack, unit, unit_out, lse, kv, mix, dy_all, wgu, wd, gd,
    hid, dgate, dup, dk_sum, dv_sum, parts, recv, recv_o, keep, result, middle,
    qkv_send, gu_send, length, cos, sin, length_all,
    dou, delta,
    y_d, t_d, z_d, y_g, t_g, z_g, y_u, t_u, z_u, y_q, z_q, y_o, z_o,
    gain_sum, gain_batch, gain_seq,
    send_sem, recv_sem, local_sem,
):
    p = Place(send_sem, recv_sem, local_sem)
    s, b, z, y = p.s, p.b, p.z, p.y
    my_rows = pl.ds(pl.multiple_of(32 * b, 32), 32)
    my_positions = pl.ds(pl.multiple_of(256 * s, 256), 256)
    p.hello()
    own_d = p.local(w_down, wd.at[s])
    own_x = p.local(x, xa.at[b])
    own_wo = p.local(w_out, wo.at[s, b])
    own_dy = p.local(dy, dy_all.at[b])
    own_tables = [p.local(cos_table.at[my_positions], cos), p.local(sin_table.at[my_positions], sin)]
    pack_projections(w_query, key_weight, value_weight, qkv_send)
    length[...] = jnp.broadcast_to(lengths[0], (8, 128)).astype(jnp.int32)
    own_qkv = p.local(qkv_send.at[b], wqkv.at[s, my_rows])
    length_all[b] = length[...]
    pack_hidden(w_gate, gu_send, 0)
    pack_hidden(w_up, gu_send, 1)
    p.meet()

    got_qkv, got_len = [], []
    for k in (1, 2, 3):
        to = lax.rem(b + k, 4)
        got_qkv.append(p.post(qkv_send.at[to], wqkv.at[s, my_rows], (s, to)))
    own_x.wait()
    x_across = p.post(xa.at[b], xa.at[b], (s, p.across))
    x_core = p.post(xa.at[b], xa.at[b], (s, p.core))
    for k in (1, 2, 3):
        to = lax.rem(b + k, 4)
        got_len.append(p.post(length, length_all.at[b], (s, to)))
    spread_d = Spread(p, lambda i: wd.at[i])
    spread_g = Spread(p, lambda i: wgu.at[i, 0])
    spread_u = Spread(p, lambda i: wgu.at[i, 1])
    own_d.wait()
    spread_d.start_y()

    def normalize(g):
        xg = xa[g].astype(F32)
        norm[g] = (xg * rms_factor(xg) * gain_a[...]).astype(BF16)

    normalize(b)
    own_qkv.wait()
    for k in (1, 2, 3):
        p.landed(got_qkv[k - 1], wqkv.at[s, my_rows])
    z_qkv = [p.post(wqkv.at[s], wqkv.at[s], (2 * p.up(k) + y, b)) for k in (1, 2, 3)]
    y_qkv = [p.post(wqkv.at[s], wqkv.at[s], (p.flip, b))]
    own_gu = p.local(gu_send.at[b], wgu.at[s, :, my_rows])
    got_gu = []
    for k in (1, 2, 3):
        to = lax.rem(b + k, 4)
        got_gu.append(p.post(gu_send.at[to], wgu.at[s, :, my_rows], (s, to)))
    for k in (1, 2, 3):
        slot = 2 * p.down(k) + y
        p.landed(z_qkv[k - 1], wqkv.at[slot])
        y_qkv.append(p.post(wqkv.at[slot], wqkv.at[slot], (p.flip, b)))
    spread_d.start_z()
    own_wo.wait()
    z_wo = [p.post(wo.at[s, b], wo.at[s, b], (2 * p.up(k) + y, b)) for k in (1, 2, 3)]
    y_wo = [p.post(wo.at[s, b], wo.at[s, b], (p.flip, b))]
    p.landed(x_core, xa.at[p.core])
    normalize(p.core)
    p.landed(x_across, xa.at[p.across])
    x_far = p.post(xa.at[p.across], xa.at[p.across], (s, p.core))
    for made in own_tables:
        made.wait()
    p.landed(y_qkv[0], wqkv.at[p.flip])
    for k in (1, 2, 3):
        p.landed(y_qkv[k], wqkv.at[2 * p.down(k) + 1 - y])
    gain_q, gain_k = twice(gain_query), twice(gain_key)
    own_gu.wait()
    for k in (1, 2, 3):
        p.landed(got_gu[k - 1], wgu.at[s, :, my_rows])
    spread_g.start_y()
    spread_u.start_y()

    first_unit = p.slots(8)

    def each_piece(t, kk, act):
        to = 2 * near_first(p, t) + kk

        @pl.when(to != s)
        def _():
            act(p.copy(pack.at[to], unit.at[s], (to, b), first_unit + 2 * t + kk, first_unit + s))

    def project(t, carry):
        g = near_first(p, t)

        @pl.when(t == 3)
        def _():
            p.landed(x_far, xa.at[p.far])

        @pl.when(t >= 2)
        def _():
            normalize(g)

        whole = nn(norm[g], wqkv[...].reshape(1024, 512))
        for kk in (0, 1):
            q, kvp = heads_of(whole, kk)
            qn = q * lax.rsqrt(head_mean(q * q) + eps) * gain_q
            kn = kvp * lax.rsqrt(head_mean(kvp * kvp) + eps) * gain_k
            qr = rope(qn, cos[...], sin[...]) * 0.125
            kr = rope(kn, cos[...], sin[...])
            pack[2 * g + kk, :, 0:128] = qr.astype(BF16)
            pack[2 * g + kk, :, 128:256] = jnp.where(lanes(kr.shape) < 64, kr, kvp).astype(BF16)
            each_piece(t, kk, lambda made: made.start())

        return carry

    lax.fori_loop(0, 4, project, 0)
    own_unit = p.local(pack.at[s], unit.at[s])
    parked = p.local(norm, norm_park)
    for k in (1, 2, 3):
        slot = 2 * p.down(k) + y
        p.landed(z_wo[k - 1], wo.at[slot, b])
        y_wo.append(p.post(wo.at[slot, b], wo.at[slot, b], (p.flip, b)))
    spread_d.land(0)
    spread_d.land_inner()
    own_dy.wait()
    dy_across = p.post(dy_all.at[b], dy_all.at[b], (s, p.across))
    dy_core = p.post(dy_all.at[b], dy_all.at[b], (s, p.core))
    for k in (1, 2, 3):
        p.landed(got_len[k - 1], length_all.at[lax.rem(b + 4 - k, 4)])

    spread_g.start_z()
    for k in range(1, 8):
        src = lax.rem(s + k, 8)
        p.landed(first_unit + src, unit.at[src])
    own_unit.wait()
    p.landed(y_wo[0], wo.at[p.flip, b])
    for k in (1, 2, 3):
        p.landed(y_wo[k], wo.at[2 * p.down(k) + 1 - y, b])
    wo_across = p.post(wo.at[:, b], wo.at[:, b], (s, p.across))
    wo_core = p.post(wo.at[:, b], wo.at[:, b], (s, p.core))

    def values(j):
        return dup.at[j // 2, lax.rem(j, 2), 0:80, 0:256]

    def prepare(j, carry):
        live = j * 256 + rows_of((256, 128)) < length_all[z][0:1, :]
        masked = jnp.where(live, unit[j, :, 128:256].astype(F32), 0.0)
        kv[j] = masked.astype(BF16)
        turned = jnp.transpose(masked)[64:128].astype(BF16)
        alive = j * 256 + lanes((16, 256)) < length_all[z][0:1, 0:1]
        counted = jnp.where(alive, 1.0, 0.0).astype(BF16)
        values(j)[...] = jnp.concatenate([turned, counted], axis=0)
        return carry

    lax.fori_loop(0, 8, prepare, 0)
    p.landed(dy_across, dy_all.at[p.across])
    dy_far = p.post(dy_all.at[p.across], dy_all.at[p.across], (s, p.core))
    first_mix, first_across, first_core = p.slots(8), p.slots(8), p.slots(8)

    def mix_send(src, t):
        p.copy(mix.at[b, src], mix.at[b, src], (s, p.across), first_across + t).start()
        p.copy(mix.at[b, src], mix.at[b, src], (s, p.core), first_core + t).start()

    def mix_arrived(t):
        src = lax.rem(s + 7 - t, 8)
        p.landed(first_mix + t, mix.at[b, src])
        mix_send(src, t)

    def attend(t, carry):
        i = lax.rem(s + 1 + t, 8)
        qt = jnp.transpose(unit[i, :, 0:128].astype(F32)).astype(BF16)
        both = jnp.concatenate([qt[0:64], qt[64:128]], axis=1)
        right = jnp.concatenate([both, jnp.zeros((64, 512), BF16)], axis=0)

        def block(j, acc):
            return acc + nn(values(j)[...], jnp.exp(nn(kv[j], right)).astype(BF16))

        acc = lax.fori_loop(0, i, block, jnp.zeros((80, 512), F32))
        causal = rows_of((256, 512)) <= lax.rem(lanes((256, 512)), 256)
        edge = jnp.where(causal, jnp.exp(nn(kv[i], right)), 0.0).astype(BF16)
        acc = acc + nn(values(i)[...], edge)
        total = acc[64:65]
        out = acc[0:64] / total
        out = jnp.concatenate([out[:, 0:256], out[:, 256:512]], axis=0)
        unit_out[i] = jnp.transpose(out).astype(BF16)
        lse[i] = jnp.broadcast_to(jnp.log(total), (8, 512))

        @pl.when(t < 7)
        def _():
            p.copy(unit_out.at[i], mix.at[b, s], (i, b), first_mix + t).start()

        @pl.when(t == 1)
        def _():
            spread_d.land_end()

        @pl.when(t == 6)
        def _():
            spread_g.land(0)
            spread_g.land_inner()
            spread_u.start_z()

        @pl.when(t >= 4)
        def _():
            mix_arrived(t - 4)

        return carry

    lax.fori_loop(0, 8, attend, 0)
    own_mix = p.local(unit_out.at[s], mix.at[b, s])
    own_mix.wait()
    mix_send(s, 7)
    for t in range(4, 7):
        mix_arrived(t)
    spread_g.land_end()
    p.landed(dy_core, dy_all.at[p.core])
    p.landed(dy_far, dy_all.at[p.far])
    spread_d.finish()

    def hidden_back(g, carry):
        rows = pl.ds(pl.multiple_of(g * 256, 256), 256)
        dgate[g] = nt(dy_all[g], wd[...].reshape(1152, 1024)).astype(BF16).reshape(2, 128, 1152)
        return carry

    lax.fori_loop(0, 4, hidden_back, 0)
    p.landed(wo_across, wo.at[:, p.across])
    wo_far = p.post(wo.at[:, p.across], wo.at[:, p.across], (s, p.core))
    for t in range(8):
        p.landed(first_across + t, mix.at[p.across, lax.rem(s + 7 - t, 8)])
    mix_far = p.post(mix.at[p.across], mix.at[p.across], (s, p.core))
    for t in range(8):
        p.landed(first_core + t, mix.at[p.core, lax.rem(s + 7 - t, 8)])
    p.landed(wo_core, wo.at[:, p.core])
    p.landed(wo_far, wo.at[:, p.far])
    spread_u.land(0)
    spread_u.land_inner()
    p.landed(mix_far, mix.at[p.far])

    parked.wait()

    def project_out(g, carry):
        mixed = jnp.concatenate([mix[c, 2 * g + kk] for c in range(4) for kk in (0, 1)], axis=1)
        mid = xa[g].astype(F32) + nn(mixed, wo[...].reshape(1024, 1024))
        norm[g] = (mid * rms_factor(mid) * gain_f[...]).astype(BF16)

        @pl.when(g == b)
        def _():
            middle[...] = mid

        return carry

    lax.fori_loop(0, 4, project_out, 0)

    for t in range(8):
        if t < 7:
            p.copy(unit_out.at[s], mix.at[b, s], (p.flip, b), first_mix + t).wait_send()
        p.copy(mix.at[b, s], mix.at[b, s], (s, p.across), first_across + t).wait_send()
        p.copy(mix.at[b, s], mix.at[b, s], (s, p.core), first_core + t).wait_send()
    for t in range(4):
        for kk in (0, 1):
            each_piece(t, kk, lambda made: made.wait_send())
    p.drain()

    def turn(e, carry):
        for g in range(4):
            hid[0:128, 256 * g : 256 * g + 256] = jnp.transpose(
                mix[e // 2, 2 * g + lax.rem(e, 2)].astype(F32)
            ).astype(BF16)
        gu_send[e // 2, lax.rem(e, 2), :, 0:1024] = hid[my_rows, 0:1024]
        return carry

    lax.fori_loop(0, 8, turn, 0)
    spread_u.land_end()
    spread_g.finish()

    def gate_of(g, carry):
        rows = pl.ds(pl.multiple_of(g * 256, 256), 256)
        hid[rows] = nn(norm[g], wgu[:, 0].reshape(1024, 1152)).astype(BF16)
        return carry

    lax.fori_loop(0, 4, gate_of, 0)
    spread_u.finish()
    first_n = p.slots(3)

    def gated(g, carry):
        rows = pl.ds(pl.multiple_of(g * 256, 256), 256)
        gate = hid[rows].astype(F32)
        up = nn(norm[g], wgu[:, 1].reshape(1024, 1152))
        dh = dgate[g].reshape(256, 1152).astype(F32)
        sg = 1.0 / (1.0 + jnp.exp(-gate))
        swish = gate * sg
        hid[rows] = (swish * up).astype(BF16)
        dgate[g] = (dh * up * sg * (1.0 + gate * (1.0 - sg))).astype(BF16).reshape(2, 128, 1152)
        dup[g] = (dh * swish).astype(BF16).reshape(2, 128, 1152)
        return carry

    lax.fori_loop(0, 4, gated, 0)

    def down_rows(c, carry, at=None):
        rows = pl.multiple_of(128 * c, 128)
        gd[pl.ds(rows, 128), at] = tn(
            hid[:, pl.ds(rows, 128)], dy_all[:, :, at].reshape(1024, 512)
        ).astype(BF16)
        return carry

    halves = (pl.ds(0, 512), pl.ds(512, 512))
    sum_d, more_d = [
        SeqTree(
            p,
            functools.partial(lambda at, i: gd.at[pl.ds(pl.multiple_of(144 * i, 16), 144), at], at),
            y_d.at[:, :, at], t_d.at[:, :, at], z_d.at[:, :, at],
        )
        for at in halves
    ]
    lax.fori_loop(0, 9, functools.partial(down_rows, at=halves[0]), 0)
    sum_d.start()

    def narrowed(t, carry):
        g = batch_order(p, t)
        part = nt(dgate[g].reshape(256, 1152), wgu[:, 0].reshape(1024, 1152)) + nt(
            dup[g].reshape(256, 1152), wgu[:, 1].reshape(1024, 1152)
        )
        parts[g] = part.astype(BF16)

        @pl.when(t == 3)
        def _():
            keep[...] = part

        chip_sum_post(p, t, parts, recv, first_n)
        return carry

    lax.fori_loop(0, 4, narrowed, 0)
    chip_sum_across(p, parts, recv, first_n)
    lax.fori_loop(0, 9, functools.partial(down_rows, at=halves[1]), 0)
    more_d.start()
    parts_of = (pl.ds(0, 640), pl.ds(640, 512))

    def tree(which, at, y_recv, relayed, z_recv):
        return SeqTree(
            p, lambda i: wgu.at[i, which, :, at], y_recv.at[:, :, at], relayed.at[:, :, at], z_recv.at[:, :, at]
        )

    sum_g, more_g = [tree(0, at, y_g, t_g, z_g) for at in parts_of]
    sum_u, more_u = [tree(1, at, y_u, t_u, z_u) for at in parts_of]

    for spread in (spread_d, spread_g, spread_u):
        spread.drain()

    def gate_rows(c, carry):
        at = pl.multiple_of(128 * c, 128)
        side = norm[:, :, pl.ds(at, 128)].reshape(1024, 128)
        wgu[c, 0] = tn(side, dgate[...].reshape(1024, 1152)).astype(BF16)
        wgu[c, 1] = tn(side, dup[...].reshape(1024, 1152)).astype(BF16)
        return carry

    lax.fori_loop(0, 8, gate_rows, 0)
    load_norm = p.local(norm_park, norm)

    mid = middle[...]
    r2 = rms_factor(mid)
    grad_two = keep[...] + chip_sum_rest(p, parts, recv, first_n)
    gain_sum[...] = jnp.zeros((8, 1024), F32)
    gain_sum[1:2] = jnp.sum(grad_two * mid * r2, axis=0, keepdims=True)
    dm = dy_all[b].astype(F32) + norm_back(grad_two * gain_f[...], mid, r2)
    result[...] = mid
    middle[...] = dm
    xa[b] = dm.astype(BF16)

    first_mixed = p.slots(3)

    def mixed_back(t, carry):
        c = batch_order(p, t)
        place = jnp.where(t == 3, 1, 0)
        for kk in (0, 1):
            mix[place, 2 * c + kk] = nt(xa[b], wo[2 * c + kk].reshape(128, 1024)).astype(BF16)

        @pl.when(t < 3)
        def _():
            p.copy(
                mix.at[0, pl.ds(2 * c, 2)], mix.at[1, pl.ds(2 * b, 2)], (s, c), first_mixed + t
            ).start()

        return carry

    lax.fori_loop(0, 4, mixed_back, 0)
    dbr_across = p.post(xa.at[b], xa.at[b], (s, p.across))
    dbr_core = p.post(xa.at[b], xa.at[b], (s, p.core))
    def down(g, carry):
        part = nn(hid[pl.ds(pl.multiple_of(g * 256, 256), 256)], wd[...].reshape(1152, 1024))
        dy_all[g] = part.astype(BF16)

        @pl.when(g == b)
        def _():
            result[...] = result[...] + part

        return carry

    lax.fori_loop(0, 4, down, 0)

    first_o = p.slots(3)
    chip_sum_post(p, 0, dy_all, recv_o, first_o)
    chip_sum_post(p, 1, dy_all, recv_o, first_o)
    def q_right(i):
        return hid.at[pl.ds(pl.multiple_of(128 * i, 128), 128), 0:512]

    def do_right(i):
        return hid.at[pl.ds(pl.multiple_of(128 * i, 128), 128), 512:1024]

    def tall(i, base):
        half = pl.ds(2 * lax.rem(i, 2), 2)
        return dgate.at[half, :, :, pl.ds(pl.multiple_of(base + 128 * (i // 2), 128), 128)]

    def q_left(i):
        return tall(i, 0)

    def do_left(i):
        return tall(i, 512)

    def dk2(i):
        return dk_sum.at[i]

    def dv2(i):
        return dv_sum.at[i]

    def dq2(i):
        rows = pl.ds(pl.multiple_of(64 * lax.rem(i, 4), 64), 64)
        return keep.at[rows, pl.ds(pl.multiple_of(512 * (i // 4), 512), 512)]

    def keys_turned(i):
        return dup.at[i // 2, lax.rem(i, 2), 0:64, 0:256]

    def prepare_back(i, carry):
        keys_turned(i)[...] = jnp.transpose(kv[i].astype(F32))[0:64].astype(BF16)
        q = unit[i, :, 0:128].astype(F32)
        qt = jnp.transpose(q).astype(BF16)
        both = jnp.concatenate([qt[0:64], qt[64:128]], axis=1)
        q_right(i)[...] = jnp.concatenate([both, jnp.zeros((64, 512), BF16)], axis=0)
        first = lanes(q.shape) < 64
        both = jnp.concatenate([jnp.where(first, q, 0.0), jnp.where(first, 0.0, q)], axis=0)
        q_left(i)[...] = both.astype(BF16).reshape(2, 2, 128, 128)
        dq2(i)[...] = jnp.zeros((64, 512), F32)
        dk2(i)[...] = jnp.zeros((256, 128), F32)
        dv2(i)[...] = jnp.zeros((256, 128), F32)
        return carry

    lax.fori_loop(0, 8, prepare_back, 0)
    first_do = p.slots(8)

    def grad_piece(t, kk, act):
        to = 2 * near_first(p, t) + kk

        @pl.when(to != s)
        def _():
            act(p.copy(mix.at[1, to], dou.at[s], (to, b), first_do + 2 * t + kk, first_do + s))

    for t, index in ((0, None), (1, 1), (2, 2), (3, 0)):
        if index is not None:
            p.landed(first_mixed + index, mix.at[1, pl.ds(2 * near_first(p, t), 2)])
        for kk in (0, 1):
            grad_piece(t, kk, lambda made: made.start())
    sum_g.start()
    sum_d.reduce()
    dou[s] = mix[1, s]

    chip_sum_across(p, dy_all, recv_o, first_o)
    for k in range(1, 8):
        src = lax.rem(s + k, 8)
        p.landed(first_do + src, dou.at[src])

    def prepare_grad(i, carry):
        do = dou[i].astype(F32)
        dot = jnp.transpose(do)
        right = jnp.concatenate([dot[0:64], dot[64:128]], axis=1).astype(BF16)
        do_right(i)[...] = jnp.concatenate([jnp.zeros((64, 512), BF16), right], axis=0)
        first = lanes(do.shape) < 64
        tall_do = jnp.concatenate([jnp.where(first, do, 0.0), jnp.where(first, 0.0, do)], axis=0)
        do_left(i)[...] = tall_do.astype(BF16).reshape(2, 2, 128, 128)
        both = dot * jnp.transpose(unit_out[i].astype(F32))
        low = jnp.sum(both[0:64], axis=0, keepdims=True)
        high = jnp.sum(both[64:128], axis=0, keepdims=True)
        delta[i] = jnp.broadcast_to(jnp.concatenate([low, high], axis=1), (8, 512))
        return carry

    lax.fori_loop(0, 8, prepare_grad, 0)

    def meet(i, j, probs):
        ds = (probs * (nn(kv[j], do_right(i)[...]) - delta[i][0:1])).astype(BF16)
        dv2(j)[...] += nn(probs.astype(BF16), do_left(i)[...].reshape(512, 128))
        dk2(j)[...] += nn(ds, q_left(i)[...].reshape(512, 128))
        dq2(i)[...] += nn(keys_turned(j)[...], ds)

    first_back = p.slots(8)

    def blocks(t, carry):
        c = lax.rem(s + 1 + t, 8)
        causal = rows_of((256, 512)) <= lax.rem(lanes((256, 512)), 256)
        meet(c, c, jnp.where(causal, jnp.exp(nn(kv[c], q_right(c)[...]) - lse[c][0:1]), 0.0))

        def other(u, inner_carry):
            o = lax.rem(s + 1 + u, 8)
            i, j = jnp.maximum(c, o), jnp.minimum(c, o)
            meet(i, j, jnp.exp(nn(kv[j], q_right(i)[...]) - lse[i][0:1]))
            return inner_carry

        lax.fori_loop(t + 1, 8, other, 0)
        acc = dq2(c)[...]
        dq = jnp.concatenate([acc[:, 0:256], acc[:, 256:512]], axis=0) * 0.125
        pack[c, :, 0:128] = jnp.transpose(dq).astype(BF16)
        live = c * 256 + rows_of((256, 128)) < length_all[z][0:1, :]
        dk, dv = dk2(c)[...], dv2(c)[...]
        dk = dk + pltpu.roll(dk, 64, 1)
        dv = dv + pltpu.roll(dv, 64, 1)
        dkv = jnp.where(lanes((256, 128)) < 64, dk, dv)
        pack[c, :, 128:256] = jnp.where(live, dkv, 0.0).astype(BF16)

        @pl.when(t < 7)
        def _():
            p.copy(pack.at[c], unit.at[s], (c, b), first_back + t).start()

        @pl.when(t == 0)
        def _():
            p.landed(dbr_across, xa.at[p.across])
            p.copy(xa.at[p.across], xa.at[p.across], (s, p.core), dbr_far).start()

        @pl.when(t == 1)
        def _():
            sum_d.relay()

        @pl.when(t == 2)
        def _():
            more_g.start()
            more_d.reduce()

        return carry

    dbr_far = p.slots(1)
    lax.fori_loop(0, 8, blocks, 0)
    sum_u.start()
    sum_g.reduce()
    more_d.relay()
    unit[s] = pack[s]

    p.landed(dbr_core, xa.at[p.core])
    p.landed(dbr_far, xa.at[p.far])
    out_rows = nn(gu_send[:, :, :, 0:1024].reshape(256, 1024), xa[...].reshape(1024, 1024)).astype(BF16)
    for e in range(8):
        dgate[e // 2, e % 2, 0:32, 0:1024] = out_rows[32 * e : 32 * e + 32]
    sum_o = SeqSum(p, y_o, z_o)
    sum_o.start(dgate.at[:, :, 0:32, 0:1024])
    load_x = p.local(x, xa.at[p.far])
    load_norm.wait()

    first_n = p.slots(3)
    zero_row = jnp.zeros((1, 128), F32)

    def heads(t, carry):
        sum_q, sum_k = carry
        unit_of = lax.rem(s + 7 - t, 8)

        @pl.when(t < 7)
        def _():
            p.landed(first_back + t, unit.at[unit_of])

        g = unit_of // 2
        at = pl.multiple_of(256 * lax.rem(unit_of, 2), 256)
        whole = nn(norm[g], wqkv[:, :, pl.ds(at, 256)].reshape(1024, 256))
        q, k = heads_of(whole, 0)
        rq = lax.rsqrt(head_mean(q * q) + eps)
        rk = lax.rsqrt(head_mean(k * k) + eps)
        dq = rope_back(unit[unit_of, :, 0:128].astype(F32), cos[...], sin[...])
        dkv = unit[unit_of, :, 128:256].astype(F32)
        dk = rope_back(dkv, cos[...], sin[...])
        sum_q = sum_q + jnp.sum(dq * q * rq, axis=0, keepdims=True)
        sum_k = sum_k + jnp.sum(dk * k * rk, axis=0, keepdims=True)
        dq = dq * gain_q
        dk = dk * gain_k
        dq = rq * (dq - q * rq * rq * head_mean(dq * q))
        dk = rk * (dk - k * rk * rk * head_mean(dk * k))
        dup[g, :, :, pl.ds(at, 128)] = dq.astype(BF16).reshape(2, 128, 128)
        dkv = jnp.where(lanes(dk.shape) < 64, dk, dkv).astype(BF16)
        dup[g, :, :, pl.ds(pl.multiple_of(at + 128, 128), 128)] = dkv.reshape(2, 128, 128)
        return (sum_q, sum_k)

    sum_q, sum_k = lax.fori_loop(0, 8, heads, (zero_row, zero_row))
    sum_g.relay()
    more_g.reduce()

    gain_sum[2:3, 0:128] = sum_q
    gain_sum[3:4, 0:128] = sum_k
    def qkv_rows(c, carry):
        at = pl.multiple_of(128 * c, 128)
        side = norm[:, :, pl.ds(at, 128)].reshape(1024, 128)
        dup[c // 2, lax.rem(c, 2), :, 512:1024] = tn(side, dup[:, :, :, 0:512].reshape(1024, 512)).astype(BF16)
        return carry

    lax.fori_loop(0, 8, qkv_rows, 0)
    sum_qkv = SeqSum(p, y_q, z_q)
    sum_qkv.start(dup.at[:, :, :, pl.ds(512, 512)])
    def stream_back(t, carry):
        g = batch_order(p, t)
        part = nt(dup[g, :, :, 0:512].reshape(256, 512), wqkv[...].reshape(1024, 512))
        parts[g] = part.astype(BF16)

        @pl.when(t == 3)
        def _():
            keep[...] = part

        chip_sum_post(p, t, parts, recv, first_n)
        return carry

    lax.fori_loop(0, 4, stream_back, 0)
    more_u.start()
    chip_sum_across(p, parts, recv, first_n)
    sum_u.reduce()
    sum_o.middle()
    more_g.relay()
    xa[p.core] = (result[...] + chip_sum_rest(p, dy_all, recv_o, first_o)).astype(BF16)
    leave = [p.local(xa.at[p.core], output)]
    sum_qkv.middle()
    sum_u.relay()

    dn1 = keep[...] + chip_sum_rest(p, parts, recv, first_n)
    load_x.wait()
    xf = xa[p.far].astype(F32)
    r1 = rms_factor(xf)
    gain_sum[0:1] = jnp.sum(dn1 * xf * r1, axis=0, keepdims=True)
    xa[p.far] = (middle[...] + norm_back(dn1 * gain_a[...], xf, r1)).astype(BF16)
    leave.append(p.local(xa.at[p.far], dx))
    got_gain = [p.post(gain_sum, gain_batch.at[b], (s, lax.rem(b + k, 4))) for k in (1, 2, 3)]
    gain_batch[b] = gain_sum[...]
    for at, half in zip(halves, (sum_d, more_d)):
        rd[:, at] = half.finish()

    def exchange(total, own, dst):
        for c in range(4):
            own(c)[...] = total[32 * c : 32 * c + 32].astype(BF16)
        got = []
        for k in (1, 2, 3):
            to = lax.rem(b + k, 4)
            got.append(p.post(own(to), dst(b), (s, to)))
        dst(b)[...] = own(b)[...]
        return got

    def arrive(got, dst):
        for k in (1, 2, 3):
            p.landed(got[k - 1], dst(lax.rem(b + 4 - k, 4)))

    finished = []

    def hand_over(total, which, at):
        dst = lambda i: rgu.at[i, which, :, at]
        finished.append((exchange(total, lambda c: gu_send.at[c, which, :, at], dst), dst))

    hand_over(sum_g.finish(), 0, parts_of[0])
    for k in (1, 2, 3):
        p.landed(got_gain[k - 1], gain_batch.at[lax.rem(b + 4 - k, 4)])
    gain_seq[s] = (gain_batch[0] + gain_batch[1]) + (gain_batch[2] + gain_batch[3])
    got_all = [p.post(gain_seq.at[s], gain_seq.at[s], (lax.rem(s + k, 8), b)) for k in range(1, 8)]
    more_u.reduce()
    hand_over(more_g.finish(), 0, parts_of[1])
    ro[...] = sum_o.finish()
    dst_q = lambda i: rqkv.at[i]
    finished.append((exchange(sum_qkv.finish(), lambda c: qkv_send.at[c], dst_q), dst_q))
    hand_over(sum_u.finish(), 1, parts_of[0])
    for k in range(1, 8):
        p.landed(got_all[k - 1], gain_seq.at[lax.rem(s + 8 - k, 8)])
    total = gain_seq[0]
    for k in range(1, 8):
        total = total + gain_seq[k]
    gains_out[...] = total
    more_u.relay()
    hand_over(more_u.finish(), 1, parts_of[1])
    for got, dst in finished:
        arrive(got, dst)
    for t in range(4):
        for kk in (0, 1):
            grad_piece(t, kk, lambda made: made.wait_send())
    for t in range(7):
        p.copy(pack.at[s], unit.at[s], (p.flip, b), first_back + t).wait_send()
    for made in leave:
        made.wait()
    p.copy(xa.at[b], xa.at[b], (s, p.core), dbr_far).wait_send()
    for t in range(3):
        p.copy(mix.at[0, 0:2], mix.at[0, 0:2], (s, p.core), first_mixed + t).wait_send()
    p.drain()


def chip_sum_post(p, t, parts, recv, first):
    @pl.when(jnp.equal(t, 0))
    def _():
        p.copy(parts.at[p.far], recv.at[0], (p.s, p.core), first).start()

    @pl.when(jnp.equal(t, 1))
    def _():
        p.copy(parts.at[p.core], recv.at[1], (p.s, p.core), first + 1).start()


def chip_sum_across(p, parts, recv, first):
    p.copy(recv.at[0], recv.at[0], (p.s, p.core), first).wait_recv()
    parts[p.across] = (parts[p.across].astype(F32) + recv[0].astype(F32)).astype(BF16)
    p.copy(parts.at[p.across], recv.at[2], (p.s, p.across), first + 2).start()


def chip_sum_rest(p, parts, recv, first):
    p.copy(recv.at[1], recv.at[1], (p.s, p.core), first + 1).wait_recv()
    p.copy(recv.at[2], recv.at[2], (p.s, p.core), first + 2).wait_recv()
    for k in range(3):
        p.copy(parts.at[p.b], recv.at[k], (p.s, p.core), first + k).wait_send()
    return recv[1].astype(F32) + recv[2].astype(F32)


def batch_order(p, t):
    return jnp.where(t == 0, p.far, jnp.where(t == 1, p.core, jnp.where(t == 2, p.across, p.b)))


class SeqTree:
    def __init__(self, p, slot, y_recv, relayed, z_recv):
        self.p, self.slot, self.y_recv, self.relayed, self.z_recv = p, slot, y_recv, relayed, z_recv
        self.first = p.slots(8)

    def mine(self, i):
        return self.slot(2 * i + self.p.y)[...].astype(F32)

    def start(self, pieces=(0, 1, 2, 3)):
        p = self.p
        for i in pieces:
            p.copy(
                self.slot(2 * i + 1 - p.y), self.y_recv.at[i], (p.flip, p.b), self.first + 4 + i
            ).start()

    def send(self, i, dst, z, out, into):
        p = self.p
        p.copy(self.y_recv.at[i], dst, (2 * z + p.y, p.b), self.first + out, self.first + into).start()

    def load(self, i):
        return self.y_recv.at[i][...].astype(F32)

    def reduce(self):
        p = self.p
        for i in range(4):
            p.landed(self.first + 4 + i, self.y_recv.at[i])

        def add(i):
            self.y_recv.at[i][...] = (self.load(i) + self.mine(i)).astype(BF16)

        add(p.there)
        add(p.beyond)

        @pl.when(jnp.logical_not(p.inner))
        def _():
            self.send(p.there, self.relayed.at[0], p.pair, 1, 1)
            self.send(p.beyond, self.relayed.at[1], p.pair, 2, 2)

        add(p.pair)
        self.send(p.pair, self.z_recv.at[0], p.pair, 0, 0)

    def relay(self):
        p = self.p

        @pl.when(p.inner)
        def _():
            for k, i in ((0, p.there), (1, p.beyond)):
                p.landed(self.first + 1 + k, self.relayed.at[k])
                self.y_recv.at[i][...] = (self.load(i) + self.relayed.at[k][...].astype(F32)).astype(BF16)
                self.send(i, self.z_recv.at[1], i, 1 + k, 3)

    def finish(self):
        p = self.p
        total = self.load(p.z) + self.mine(p.z)
        p.landed(self.first, self.z_recv.at[0])
        total = total + self.z_recv.at[0][...].astype(F32)
        p.landed(self.first + 3, self.z_recv.at[1])
        for out in range(3):
            p.copy(self.z_recv.at[0], self.z_recv.at[0], (p.flip, p.b), self.first + out).wait_send()
        for i in range(4):
            p.copy(self.y_recv.at[i], self.y_recv.at[i], (p.flip, p.b), self.first + 4 + i).wait_send()
        return total + self.z_recv.at[1][...].astype(F32)


class SeqSum:
    def __init__(self, p, y_recv, z_recv):
        self.p, self.y_recv, self.z_recv = p, y_recv, z_recv

    def start(self, source, mine=None):
        p = self.p
        self.index = p.post(source.at[:, 1 - p.y], self.y_recv, (p.flip, p.b))
        self.load = None
        if mine is None:
            self.mine = lambda i: source.at[i, p.y]
        else:
            self.load = p.local(source.at[:, p.y], mine)
            self.mine = lambda i: mine.at[i]

    def middle(self):
        p = self.p
        if self.load is not None:
            self.load.wait()
        p.landed(self.index, self.y_recv)
        self.far = []
        for k in (1, 2, 3):
            i = p.up(k)
            self.y_recv[i] = (self.y_recv[i].astype(F32) + self.mine(i)[...].astype(F32)).astype(BF16)
            self.far.append(p.post(self.y_recv.at[i], self.z_recv.at[k - 1], (2 * i + p.y, p.b)))

    def finish(self):
        p = self.p
        total = self.y_recv[p.z].astype(F32) + self.mine(p.z)[...].astype(F32)
        for k in (1, 2, 3):
            p.landed(self.far[k - 1], self.z_recv.at[k - 1])
            total = total + self.z_recv[k - 1].astype(F32)
        return total


def finish_kernel(
    output, dx, rqkv, rgu, rd, ro, gains,
    output_, dx_, grad_query, grad_key, grad_value, grad_out, grad_gate, grad_up, grad_down,
    gain_attn, gain_ffn, gain_query, gain_key,
):
    output_[...] = output[...]
    dx_[...] = dx[...]
    grad_out[...] = ro[...]
    grad_down[...] = rd[...]
    for c in range(4):
        pairs = []
        for kk in (0, 1):
            h = 2 * c + kk
            q, kv = heads_of(rqkv[c].astype(F32), kk)
            grad_query[:, 128 * h : 128 * h + 128] = q
            pairs.append(kv)
        first = lanes(pairs[0].shape) < 64
        grad_key[:, 128 * c : 128 * c + 128] = jnp.where(first, pairs[0], pltpu.roll(pairs[1], 64, 1))
        grad_value[:, 128 * c : 128 * c + 128] = jnp.where(first, pltpu.roll(pairs[0], 64, 1), pairs[1])
    for which, out in ((0, grad_gate), (1, grad_up)):
        wide = [rgu[c, which].astype(F32) for c in range(4)]
        out[...] = jnp.concatenate(
            [wide[c][:, 144 * i : 144 * i + 144] for i in range(8) for c in range(4)], axis=1
        )
    gain_attn[...] = gains[0:1]
    gain_ffn[...] = gains[1:2]
    gain_query[...] = gains[2:3, 0:64] + gains[2:3, 64:128]
    gain_key[...] = gains[3:4, 0:64]


def call(kernel, outs, in_specs, out_specs, scratch, cid, sems):
    return pl.pallas_call(
        kernel,
        out_shape=[jax.ShapeDtypeStruct(shape, dtype) for shape, dtype in outs],
        in_specs=in_specs,
        out_specs=out_specs,
        scratch_shapes=[pltpu.VMEM(shape, dtype) for shape, dtype in scratch]
        + [
            pltpu.SemaphoreType.DMA((sems[0],)),
            pltpu.SemaphoreType.DMA((sems[0],)),
            pltpu.SemaphoreType.DMA((sems[1],)),
        ],
        compiler_params=pltpu.CompilerParams(
            collective_id=cid, has_side_effects=True, vmem_limit_bytes=64 * 2**20
        ),
    )


def body(
    inputs, lengths, w_query, key_weight, value_weight, w_out, w_gate, w_up, w_down,
    gain_attn, gain_ffn, gain_query, gain_key, cotangent,
):
    x = inputs.reshape(256, 1024)
    dy = cotangent.reshape(256, 1024)
    freqs = theta ** (-(np.arange(32, dtype=np.float32) * 2.0) / 64)
    angles = np.arange(2048, dtype=np.float32)[:, None] * freqs.astype(np.float32)[None, :]
    cosine = jnp.asarray(np.tile(np.cos(angles), (1, 4)), F32)
    sine = jnp.asarray(np.tile(np.sin(angles), (1, 4)), F32)
    gains = [g[None] for g in (gain_query, gain_key, gain_attn, gain_ffn)]

    raw = call(
        block_kernel,
        [
            ((256, 1024), BF16), ((256, 1024), BF16), ((4, 32, 512), BF16), ((4, 2, 32, 1152), BF16),
            ((144, 1024), F32), ((32, 1024), F32), ((8, 1024), F32), ((4, 256, 1024), BF16),
        ],
        [ANY, ANY, SMEM] + [VMEM] * 6 + [ANY] * 3 + [VMEM] * 4,
        [ANY] * 2 + [VMEM] * 5 + [ANY],
        [
            ((4, 256, 1024), BF16), ((4, 256, 1024), BF16), ((8, 128, 512), BF16), ((8, 4, 32, 1024), BF16),
            ((8, 256, 256), BF16), ((8, 256, 256), BF16), ((8, 256, 128), BF16), ((8, 8, 512), F32),
            ((8, 256, 128), BF16), ((4, 8, 256, 128), BF16),
            ((4, 256, 1024), BF16), ((8, 2, 128, 1152), BF16), ((8, 144, 1024), BF16), ((1152, 1024), BF16),
            ((1024, 1152), BF16), ((4, 2, 128, 1152), BF16), ((4, 2, 128, 1152), BF16),
            ((8, 256, 128), F32), ((8, 256, 128), F32),
            ((4, 256, 1024), BF16), ((3, 256, 1024), BF16), ((3, 256, 1024), BF16),
            ((256, 1024), F32), ((256, 1024), F32), ((256, 1024), F32),
            ((4, 32, 512), BF16), ((4, 2, 32, 1152), BF16), ((8, 128), jnp.int32),
            ((256, 128), F32), ((256, 128), F32), ((4, 8, 128), jnp.int32),
            ((8, 256, 128), BF16), ((8, 8, 512), F32),
            ((4, 144, 1024), BF16), ((2, 144, 1024), BF16), ((2, 144, 1024), BF16),
            ((4, 128, 1152), BF16), ((2, 128, 1152), BF16), ((2, 128, 1152), BF16),
            ((4, 128, 1152), BF16), ((2, 128, 1152), BF16), ((2, 128, 1152), BF16),
            ((4, 128, 512), BF16), ((3, 128, 512), BF16), ((4, 32, 1024), BF16), ((3, 32, 1024), BF16),
            ((8, 1024), F32), ((4, 8, 1024), F32), ((8, 8, 1024), F32),
        ],
        0,
        (256, 32),
    )(x, dy, lengths, w_query, key_weight, value_weight, w_out, w_gate, w_up, w_down, cosine, sine, *gains)
    done = pl.pallas_call(
        finish_kernel,
        out_shape=[
            jax.ShapeDtypeStruct(shape, dtype)
            for shape, dtype in (
                ((256, 1024), BF16), ((256, 1024), BF16), ((32, 1024), F32), ((32, 512), F32),
                ((32, 512), F32), ((32, 1024), F32), ((32, 4608), F32), ((32, 4608), F32),
                ((144, 1024), F32), ((1, 1024), F32), ((1, 1024), F32), ((1, 64), F32), ((1, 64), F32),
            )
        ],
        in_specs=[VMEM] * 7,
        out_specs=[VMEM] * 13,
    )(*raw[:7])
    return (
        done[0].reshape(256, 1, 1024), done[1].reshape(256, 1, 1024), *done[2:9], *[g[0] for g in done[9:]],
    )


def rotary_tables(positions, width):
    half = width // 2
    freqs = theta ** (-(jnp.arange(half, dtype=jnp.float32) * 2.0) / width)
    angles = positions.astype(jnp.float32)[:, None] * freqs[None, :]
    cosine = jnp.concatenate([jnp.cos(angles), jnp.cos(angles)], axis=-1)
    sine = jnp.concatenate([jnp.sin(angles), jnp.sin(angles)], axis=-1)
    return (cosine, sine)


def rotate(v, cosine, sine):
    half = v.shape[-1] // 2
    turned = jnp.concatenate([-v[..., half:], v[..., :half]], axis=-1)
    return v * cosine + turned * sine


def rotate_back(grad, cosine, sine):
    half = grad.shape[-1] // 2
    moved = grad * sine
    return grad * cosine + jnp.concatenate([moved[..., half:], -moved[..., :half]], axis=-1)


def product(left, right):
    return jnp.dot(left, right, preferred_element_type=jnp.float32)


def left_product(left, right):
    return jnp.einsum("rd,rn->dn", left, right, preferred_element_type=jnp.float32)


def right_product(left, right):
    return jnp.einsum("rn,dn->rd", left, right, preferred_element_type=jnp.float32)


def rounded(v):
    return v.astype(jnp.bfloat16)


def split_rows(term, seq_size, batch_size):
    return term.reshape(
        seq_size, batch_size, term.shape[0] // (seq_size * batch_size), term.shape[1]
    )


def fold_sources(piece):
    return jnp.sum(piece, axis=1).reshape(-1, piece.shape[-1])


def general_body(
    inputs,
    lengths,
    w_query,
    key_weight,
    value_weight,
    w_out,
    w_gate,
    w_up,
    w_down,
    gain_attn,
    gain_ffn,
    gain_query,
    gain_key,
    cotangent,
):
    slice_len, seq_count, width = inputs.shape
    rows = slice_len * seq_count
    head_dim = gain_query.shape[0]
    kv_width = key_weight.shape[1]
    kv_heads = kv_width // head_dim
    q_heads = w_query.shape[1] // head_dim
    sequence_group = q_heads // kv_heads
    scale = head_dim ** (-0.5)
    cycle_size = lax.axis_size("seq")
    batch_size = lax.axis_size("batch")
    positions = lax.axis_index("seq") * slice_len + jnp.arange(slice_len, dtype=jnp.int32)
    cosine, sine = rotary_tables(positions, head_dim)
    cosine = cosine[:, None, None, :]
    sine = sine[:, None, None, :]
    shards = (w_query, key_weight, value_weight, w_out, w_gate, w_up, w_down)
    wq, key_matrix, value_matrix, wo, wg, wu, wd = (
        lax.all_gather(shards[0], ("seq", "batch"), axis=0, tiled=True),
        lax.all_gather(shards[1], ("seq", "batch"), axis=0, tiled=True),
        lax.all_gather(shards[2], ("seq", "batch"), axis=0, tiled=True),
        lax.all_gather(shards[3], ("seq", "batch"), axis=0, tiled=True),
        lax.all_gather(shards[4], ("seq", "batch"), axis=0, tiled=True),
        lax.all_gather(shards[5], ("seq", "batch"), axis=0, tiled=True),
        lax.all_gather(shards[6], ("seq", "batch"), axis=0, tiled=True),
    )
    stream = inputs.reshape(rows, width).astype(jnp.float32)
    factor_one = rms_factor(stream)
    normalized_input = rounded(stream * factor_one * gain_attn)
    query_pre = product(normalized_input, wq).reshape(slice_len, seq_count, q_heads, head_dim)
    key_before_rotation = product(normalized_input, key_matrix).reshape(
        slice_len, seq_count, kv_heads, head_dim
    )
    value_b = rounded(product(normalized_input, value_matrix)).reshape(
        slice_len, seq_count, kv_width
    )
    factor_q = rms_factor(query_pre)
    factor_k = rms_factor(key_before_rotation)
    query_b = rounded(rotate(query_pre * factor_q * gain_query, cosine, sine))
    key_b = rounded(rotate(key_before_rotation * factor_k * gain_key, cosine, sine)).reshape(
        slice_len, seq_count, kv_width
    )
    query_five = query_b.reshape(slice_len, seq_count, kv_heads, sequence_group, head_dim)

    def scores_of(keys, start):
        count = keys.shape[0]
        raw = (
            jnp.einsum(
                "tsgrd,csgd->sgrtc",
                query_five,
                keys.reshape(count, seq_count, kv_heads, head_dim),
                preferred_element_type=jnp.float32,
            )
            * scale
        )
        key_pos = start + jnp.arange(count, dtype=jnp.int32)
        causal = key_pos[None, :] <= positions[:, None]
        inside = key_pos[None, :] < lengths[:, None]
        valid = causal[None, :, :] & inside[:, None, :]
        return (raw, valid[:, None, None, :, :])

    state_shape = (seq_count, kv_heads, sequence_group, slice_len)
    shard_ids = jnp.arange(cycle_size, dtype=jnp.int32)
    top = jnp.full(state_shape, -1e30, jnp.float32)
    keys = lax.all_gather(key_b, "seq", axis=0, tiled=True)
    value_rows = lax.all_gather(value_b, "seq", axis=0, tiled=True)
    count = keys.shape[0]
    raw, valid = scores_of(keys, jnp.int32(0))
    masked = jnp.where(valid, raw, -jnp.inf)
    new_top = jnp.maximum(top, jnp.max(masked, axis=-1))
    probs = jnp.exp(masked - new_top[..., None])
    total = jnp.sum(probs, axis=-1)
    acc = jnp.einsum(
        "sgrtc,csgd->sgrtd",
        rounded(probs),
        value_rows.reshape(count, seq_count, kv_heads, head_dim),
        preferred_element_type=jnp.float32,
    )
    state = (new_top, total, acc)
    top, total, acc = state
    attn_out = acc / total[..., None]
    log_total = top + jnp.log(total)
    mixed_b = rounded(jnp.transpose(attn_out, (3, 0, 1, 2, 4)).reshape(rows, q_heads * head_dim))
    middle = stream + product(mixed_b, wo)
    factor_two = rms_factor(middle)
    normed_two = rounded(middle * factor_two * gain_ffn)
    gate = product(normed_two, wg)
    up_part = product(normed_two, wu)
    sigma = jax.nn.sigmoid(gate)
    swish = gate * sigma
    hidden_b = rounded(swish * up_part)
    result = middle + product(hidden_b, wd)
    output = rounded(result).reshape(slice_len, seq_count, width)
    wq, key_matrix, value_matrix, wo, wg, wu, wd = (
        lax.all_gather(shards[0], ("seq", "batch"), axis=0, tiled=True),
        lax.all_gather(shards[1], ("seq", "batch"), axis=0, tiled=True),
        lax.all_gather(shards[2], ("seq", "batch"), axis=0, tiled=True),
        lax.all_gather(shards[3], ("seq", "batch"), axis=0, tiled=True),
        lax.all_gather(shards[4], ("seq", "batch"), axis=0, tiled=True),
        lax.all_gather(shards[5], ("seq", "batch"), axis=0, tiled=True),
        lax.all_gather(shards[6], ("seq", "batch"), axis=0, tiled=True),
    )
    grad_res = cotangent.reshape(rows, width).astype(jnp.float32)
    grad_ffo = rounded(grad_res)
    grad_wd = left_product(hidden_b, grad_ffo)
    grad_hidden = right_product(grad_ffo, wd)
    grad_gate = rounded(grad_hidden * up_part * sigma * (1.0 + gate * (1.0 - sigma)))
    grad_up = rounded(grad_hidden * swish)
    grad_wg = left_product(normed_two, grad_gate)
    grad_wu = left_product(normed_two, grad_up)
    grad_normed_two = right_product(grad_gate, wg) + right_product(grad_up, wu)
    grad_gain_ffn = jnp.sum(grad_normed_two * middle * factor_two, axis=0)
    grad_middle = grad_res + norm_back(grad_normed_two * gain_ffn, middle, factor_two)
    grad_branch = rounded(grad_middle)
    grad_wo = left_product(mixed_b, grad_branch)
    grad_mixed = rounded(right_product(grad_branch, wo))
    grad_five = grad_mixed.reshape(slice_len, seq_count, kv_heads, sequence_group, head_dim)
    delta = jnp.sum(
        jnp.transpose(grad_five, (1, 2, 3, 0, 4)).astype(jnp.float32) * attn_out, axis=-1
    )
    gathered = (
        lax.all_gather(key_b, "seq", axis=0, tiled=True),
        lax.all_gather(value_b, "seq", axis=0, tiled=True),
    )

    def back_step(grad_query, item):
        index, keys, value_rows = item
        raw, valid = scores_of(keys, index * slice_len)
        probs = jnp.where(valid, jnp.exp(raw - log_total[..., None]), 0.0)
        key_four = keys.reshape(slice_len, seq_count, kv_heads, head_dim)
        value_four = value_rows.reshape(slice_len, seq_count, kv_heads, head_dim)
        grad_probs = jnp.einsum(
            "tsgrd,csgd->sgrtc", grad_five, value_four, preferred_element_type=jnp.float32
        )
        grad_score = rounded(probs * (grad_probs - delta[..., None]))
        grad_query = (
            grad_query
            + jnp.einsum(
                "sgrtc,csgd->tsgrd", grad_score, key_four, preferred_element_type=jnp.float32
            )
            * scale
        )
        key_term = (
            jnp.einsum(
                "sgrtc,tsgrd->csgd", grad_score, query_five, preferred_element_type=jnp.float32
            )
            * scale
        )
        value_term = jnp.einsum(
            "sgrtc,tsgrd->csgd", rounded(probs), grad_five, preferred_element_type=jnp.float32
        )
        return (
            grad_query,
            (
                key_term.reshape(slice_len, seq_count, kv_width),
                value_term.reshape(slice_len, seq_count, kv_width),
            ),
        )

    items = (
        shard_ids,
        gathered[0].reshape(cycle_size, slice_len, seq_count, kv_width),
        gathered[1].reshape(cycle_size, slice_len, seq_count, kv_width),
    )
    grad_query, terms = lax.scan(
        back_step,
        jnp.zeros((slice_len, seq_count, kv_heads, sequence_group, head_dim), jnp.float32),
        items,
    )
    key_terms = terms[0].reshape(cycle_size * slice_len, seq_count, kv_width)
    value_terms = terms[1].reshape(cycle_size * slice_len, seq_count, kv_width)
    grad_key, grad_value = (
        lax.psum_scatter(
            key_terms.astype(jnp.bfloat16), "seq", scatter_dimension=0, tiled=True
        ).astype(jnp.float32),
        lax.psum_scatter(
            value_terms.astype(jnp.bfloat16), "seq", scatter_dimension=0, tiled=True
        ).astype(jnp.float32),
    )
    grad_qr = (
        rounded(grad_query).astype(jnp.float32).reshape(slice_len, seq_count, q_heads, head_dim)
    )
    grad_qn = rotate_back(grad_qr, cosine, sine)
    grad_gain_query = jnp.sum(grad_qn * query_pre * factor_q, axis=(0, 1, 2))
    grad_qp = rounded(
        norm_back(grad_qn * gain_query, query_pre, factor_q).reshape(rows, q_heads * head_dim)
    )
    grad_kr = (
        rounded(grad_key).astype(jnp.float32).reshape(slice_len, seq_count, kv_heads, head_dim)
    )
    grad_kn = rotate_back(grad_kr, cosine, sine)
    grad_gain_key = jnp.sum(grad_kn * key_before_rotation * factor_k, axis=(0, 1, 2))
    grad_kp = rounded(
        norm_back(grad_kn * gain_key, key_before_rotation, factor_k).reshape(rows, kv_width)
    )
    grad_vp = rounded(grad_value).reshape(rows, kv_width)
    grad_wq = left_product(normalized_input, grad_qp)
    grad_wk = left_product(normalized_input, grad_kp)
    grad_wv = left_product(normalized_input, grad_vp)
    grad_normed = (
        right_product(grad_qp, wq)
        + right_product(grad_kp, key_matrix)
        + right_product(grad_vp, value_matrix)
    )
    grad_gain_attn = jnp.sum(grad_normed * stream * factor_one, axis=0)
    grad_stream = grad_middle + norm_back(grad_normed * gain_attn, stream, factor_one)
    spread = (
        lax.all_to_all(
            split_rows(grad_wq, cycle_size, batch_size).astype(jnp.bfloat16),
            "batch",
            split_axis=1,
            concat_axis=1,
            tiled=True,
        ).astype(jnp.float32),
        lax.all_to_all(
            split_rows(grad_wk, cycle_size, batch_size).astype(jnp.bfloat16),
            "batch",
            split_axis=1,
            concat_axis=1,
            tiled=True,
        ).astype(jnp.float32),
        lax.all_to_all(
            split_rows(grad_wv, cycle_size, batch_size).astype(jnp.bfloat16),
            "batch",
            split_axis=1,
            concat_axis=1,
            tiled=True,
        ).astype(jnp.float32),
        lax.all_to_all(
            split_rows(grad_wo, cycle_size, batch_size).astype(jnp.bfloat16),
            "batch",
            split_axis=1,
            concat_axis=1,
            tiled=True,
        ).astype(jnp.float32),
        lax.all_to_all(
            split_rows(grad_wg, cycle_size, batch_size).astype(jnp.bfloat16),
            "batch",
            split_axis=1,
            concat_axis=1,
            tiled=True,
        ).astype(jnp.float32),
        lax.all_to_all(
            split_rows(grad_wu, cycle_size, batch_size).astype(jnp.bfloat16),
            "batch",
            split_axis=1,
            concat_axis=1,
            tiled=True,
        ).astype(jnp.float32),
        lax.all_to_all(
            split_rows(grad_wd, cycle_size, batch_size).astype(jnp.bfloat16),
            "batch",
            split_axis=1,
            concat_axis=1,
            tiled=True,
        ).astype(jnp.float32),
    )
    partial_sums = [fold_sources(piece) for piece in spread]
    summed = (
        lax.psum_scatter(
            partial_sums[0].astype(jnp.bfloat16), "seq", scatter_dimension=0, tiled=True
        ).astype(jnp.float32),
        lax.psum_scatter(
            partial_sums[1].astype(jnp.bfloat16), "seq", scatter_dimension=0, tiled=True
        ).astype(jnp.float32),
        lax.psum_scatter(
            partial_sums[2].astype(jnp.bfloat16), "seq", scatter_dimension=0, tiled=True
        ).astype(jnp.float32),
        lax.psum_scatter(
            partial_sums[3].astype(jnp.bfloat16), "seq", scatter_dimension=0, tiled=True
        ).astype(jnp.float32),
        lax.psum_scatter(
            partial_sums[4].astype(jnp.bfloat16), "seq", scatter_dimension=0, tiled=True
        ).astype(jnp.float32),
        lax.psum_scatter(
            partial_sums[5].astype(jnp.bfloat16), "seq", scatter_dimension=0, tiled=True
        ).astype(jnp.float32),
        lax.psum_scatter(
            partial_sums[6].astype(jnp.bfloat16), "seq", scatter_dimension=0, tiled=True
        ).astype(jnp.float32),
    )
    gains = lax.psum(
        (grad_gain_attn, grad_gain_ffn, grad_gain_query, grad_gain_key), ("seq", "batch")
    )
    grad_inputs = rounded(grad_stream).reshape(slice_len, seq_count, width)
    return (
        output,
        grad_inputs,
        summed[0],
        summed[1],
        summed[2],
        summed[3],
        summed[4],
        summed[5],
        summed[6],
        gains[0],
        gains[1],
        gains[2],
        gains[3],
    )


def solution(mesh):
    sharded = P(("seq", "batch"), None)
    stream = P("seq", "batch", None)
    in_specs = (stream, P("batch")) + (sharded,) * 7 + (P(),) * 4 + (stream,)
    out_specs = (stream, stream) + (sharded,) * 7 + (P(),) * 4
    grouped = mesh.shape["seq"] == 8 and mesh.shape["batch"] == 4
    step = body if grouped else general_body
    return jax.shard_map(step, mesh=mesh, in_specs=in_specs, out_specs=out_specs, check_vma=False)
```
